32 devices in a mesh: dp: 8 (over z, x), mp: 4 (over y, core).
Axes of the slice: x: 2, y: 2, z: 4, core: 2. Of those that a mesh axis runs over, the one named last changes fastest.
Arguments:
- tokens: bfloat16 [12288, 768], P('dp'), may hold values from -6 to 6
- lengths: int32 [8], P('dp'), may hold values from 1 to 1536, 9216 in all
- horizontal: int32 [12288], P('dp'), may hold values from 0 to 63
- vertical: int32 [12288], P('dp'), may hold values from 0 to 63
- gain_attn: bfloat16 [768], replicated, may hold values from 0.5 to 1.5
- w_qkv: bfloat16 [3, 768, 768], P(None, None, 'mp'), may hold values from -0.21875 to 0.21875
- bias_tables: bfloat16 [96, 12], P(None, 'mp'), may hold values from -4 to 4
- w_output: bfloat16 [768, 768], P('mp'), may hold values from -1.75 to 1.75
- gain_ffn: bfloat16 [768], replicated, may hold values from 0.5 to 1.5
- w_inner: bfloat16 [768, 3072], P(None, 'mp'), may hold values from -0.21875 to 0.21875
- w_outer: bfloat16 [3072, 768], P('mp'), may hold values from -0.109375 to 0.109375
- cotangent: bfloat16 [12288, 768], P('dp'), may hold values from -6 to 6
Outputs:
- mixed: bfloat16 [12288, 768], P(('dp', 'mp'))
- input_grad: float32 [12288, 768], P(('dp', 'mp'))
- grad_qkv: float32 [3, 768, 768], P(None, 'dp', 'mp')
- grad_output: float32 [768, 768], P('mp', 'dp')
- grad_inner: float32 [768, 3072], P('dp', 'mp')
- grad_outer: float32 [3072, 768], P('mp', 'dp')
- grad_gain_attn: float32 [768], replicated
- grad_gain_ffn: float32 [768], replicated
- grad_tables: float32 [96, 12], P(None, 'mp')
The draws below stay inside these ranges and needn't reach their ends.
Inputs may be any that keep to these rules, and one draw needn't show every extreme that they name: `lengths`: live tokens of each document; the longest document has exactly 1536.
All inputs are finite; a program needn't handle non-finite values. No bound on the sum of `lengths` on one device may be relied on, other than what follows from the above.
Results may differ from the reference program's by a relative error of at most 0.015.
Values may be sent and summed in bfloat16 or wider, within the bound.
A program may use at most 192 MiB of HBM per device.

```python
import math
import jax
import jax.numpy as jnp
import numpy as np
from jax import lax

D = 768
HEADS = 12
HEAD_DIM = 64
FF = 3072
BUCKETS = 32
CODES = 64
ROWS = 1536
DOCS = 8
TOKENS = 12288


def place_ends(values, stream_key, low, largest):
    spot = [jax.random.randint(jax.random.fold_in(stream_key, axis), (), 0, length) for axis, length in enumerate(values.shape)]
    main_axis = values.shape.index(max(values.shape))
    beside = spot[:main_axis] + [(spot[main_axis] + 1) % values.shape[main_axis]] + spot[main_axis + 1:]
    return values.at[tuple(spot)].set(low).at[tuple(beside)].set(largest)


def shard_levels(stream_key, shape, shards, smallest, top_value):
    def one(position, shards_of):
        steps = jax.random.uniform(jax.random.fold_in(jax.random.fold_in(stream_key, 6), position), (shards_of,), jnp.float32, smallest / len(shards), top_value / len(shards))
        return jnp.repeat(jnp.exp(steps), shape[position] // shards_of).reshape((-1,) + (1,) * (len(shape) - position - 1))

    level = one(*shards[0])
    for cut in shards[1:]:
        level = level * one(*cut)
    return level


def profile(count, total, limit, lean):
    portions = [(1 << 20) // math.isqrt(rank ** lean) + 1 for rank in range(2, count + 1)]
    surplus, given = total - limit - (count - 1), [1] * (count - 1)
    while surplus > 0:
        free = [i for i in range(count - 1) if given[i] < limit]
        mass, remaining = sum([portions[i] for i in free]), surplus
        for i in free:
            more = min(limit - given[i], max(1, remaining * portions[i] // mass), surplus)
            given[i] = given[i] + more
            surplus = surplus - more
    return np.array([limit] + given)


def ragged(rng, amount, total, most, lean):
    if amount == 2:
        one = jax.random.randint(rng, (), max(1, total - most), min(most, total - 1) + 1)
        return jnp.stack([one, total - one])
    tallies = jnp.asarray(profile(amount, total, most, lean), jnp.int32)
    couples = (amount - 1) // 2
    giver, taker = tallies[1:1 + 2 * couples:2], tallies[2:2 + 2 * couples:2]
    margin = jnp.minimum(giver - 1, most - taker)
    moved = jax.random.randint(jax.random.fold_in(rng, 1), (couples,), 0, 1 << 20) % (margin + 1)
    tallies = tallies.at[1:1 + 2 * couples:2].set(giver - moved).at[2:2 + 2 * couples:2].set(taker + moved)
    return tallies[jax.random.permutation(jax.random.fold_in(rng, 2), amount)]


def noise(stream_key, dims, width, bound, split=(), kind=jnp.bfloat16):
    factor_of = shard_levels(stream_key, dims, split, -0.22, 0.18) if split else 1.0
    drawn = jax.random.normal(stream_key, dims, jnp.float32) * width * factor_of
    return jnp.minimum(jnp.maximum(drawn, -bound), bound).astype(kind)


def setup_inputs(seed: int = 0) -> dict:
    keys = jax.random.split(jax.random.key(seed), 13)
    tokens = noise(keys[0], (TOKENS, D), 1.0, 6.0, ((0, 8),))
    lengths = ragged(keys[1], DOCS, DOCS * ROWS * 3 // 4, ROWS, 2).astype(jnp.int32)
    horizontal = place_ends(jax.random.randint(keys[2], (TOKENS,), 0, CODES), jax.random.fold_in(keys[2], 1), 0, CODES - 1).astype(jnp.int32)
    vertical = place_ends(jax.random.randint(keys[3], (TOKENS,), 0, CODES), jax.random.fold_in(keys[3], 1), 0, CODES - 1).astype(jnp.int32)
    gain_attn = jnp.clip(1.0 + 0.1 * jax.random.normal(keys[4], (D,), jnp.float32), 0.5, 1.5).astype(jnp.bfloat16)
    w_qkv = noise(keys[5], (3, D, D), D ** -0.5, 0.21875, ((2, 4),))
    bias_tables = noise(keys[6], (3 * BUCKETS, HEADS), 1.0, 4.0, ((1, 4),))
    w_output = noise(keys[7], (D, D), (max(D * 24 // ROWS, 1)) ** -0.5, 1.75, ((0, 4),))
    gain_ffn = jnp.clip(1.0 + 0.1 * jax.random.normal(keys[8], (D,), jnp.float32), 0.5, 1.5).astype(jnp.bfloat16)
    w_inner = noise(keys[9], (D, FF), D ** -0.5, 0.21875, ((1, 4),))
    w_outer = noise(keys[10], (FF, D), FF ** -0.5, 0.109375, ((0, 4),))
    cotangent = noise(keys[11], (TOKENS, D), 1.0, 6.0, ((0, 8),))
    return {"tokens": tokens, "lengths": lengths, "horizontal": horizontal, "vertical": vertical, "gain_attn": gain_attn, "w_qkv": w_qkv, "bias_tables": bias_tables, "w_output": w_output, "gain_ffn": gain_ffn, "w_inner": w_inner, "w_outer": w_outer, "cotangent": cotangent}


epsilon = 1e-06
highest = lax.Precision.HIGHEST

@jax.custom_vjp
def low(v):
    return lax.optimization_barrier(v.astype(jnp.bfloat16)).astype(jnp.float32)

@jax.custom_vjp
def low_back(v):
    return v

def low_keep(v):
    return (low(v), None)

def low_pass(kept, grad):
    return (grad,)

def back_keep(v):
    return (v, None)

def back_low(kept, grad):
    return (low(grad),)
low.defvjp(low_keep, low_pass)
low_back.defvjp(back_keep, back_low)

def rms_norm(inputs, gain_vector):
    factor = lax.rsqrt(lax.optimization_barrier(jnp.mean(inputs * inputs, axis=-1, keepdims=True)) + epsilon)
    return inputs * factor * gain_vector

def forward(tokens, gain_attn, w_qkv, bias_tables, w_output, gain_ffn, w_inner, w_outer, lengths, horizontal, vertical):
    query_block = min(512, ROWS)
    half_count = BUCKETS // 2
    score_scale = HEAD_DIM ** (-0.5)

    def one_document(pieces):
        doc_tokens, doc_length, doc_horizontal, doc_vertical = pieces
        normed = low(rms_norm(doc_tokens, gain_attn))
        projected = jnp.einsum('id,kde->kie', normed, w_qkv, precision=highest)
        projected = low(low_back(projected))
        queries = projected[0].reshape(ROWS, HEADS, HEAD_DIM)
        key_rows = projected[1].reshape(ROWS, HEADS, HEAD_DIM)
        values = projected[2].reshape(ROWS, HEADS, HEAD_DIM)
        positions = jnp.arange(ROWS, dtype=jnp.int32)

        def attend(row_start):
            query_rows = lax.dynamic_slice_in_dim(queries, row_start, query_block, 0)
            row_ids = row_start + jnp.arange(query_block, dtype=jnp.int32)
            line_ids = jnp.clip(positions[None, :] - row_ids[:, None], -half_count, half_count - 1) + half_count
            across_rows = lax.dynamic_slice_in_dim(doc_horizontal, row_start, query_block, 0)
            upward_rows = lax.dynamic_slice_in_dim(doc_vertical, row_start, query_block, 0)
            across_ids = jnp.clip(doc_horizontal[None, :] - across_rows[:, None], -half_count, half_count - 1) + half_count + BUCKETS
            upward_ids = jnp.clip(doc_vertical[None, :] - upward_rows[:, None], -half_count, half_count - 1) + half_count + 2 * BUCKETS
            bias = bias_tables[line_ids] + bias_tables[across_ids] + bias_tables[upward_ids]
            logits = jnp.einsum('ihd,jhd->hij', query_rows, key_rows, precision=highest) * score_scale
            logits = low_back(logits + jnp.transpose(bias, (2, 0, 1)))
            logits = jnp.where((positions < doc_length)[None, None, :], logits, -1e+30)
            probs = low(jax.nn.softmax(logits, axis=-1))
            return jnp.einsum('hij,jhd->ihd', probs, values, precision=highest).reshape(query_block, D)
        starts = (jnp.arange(ROWS // query_block) * query_block).astype(jnp.int32)
        attended = lax.map(jax.checkpoint(attend), starts).reshape(ROWS, D)
        attended = low(low_back(attended))
        branch = low_back(jnp.dot(attended, w_output, precision=highest))
        hidden = doc_tokens + branch
        normed_ffn = low(rms_norm(hidden, gain_ffn))
        inner = low_back(jnp.dot(normed_ffn, w_inner, precision=highest))
        activated = low(jax.nn.gelu(inner))
        outer = low_back(jnp.dot(activated, w_outer, precision=highest))
        return hidden + outer
    result = lax.map(jax.checkpoint(one_document), (tokens.reshape(DOCS, ROWS, D), lengths, horizontal.reshape(DOCS, ROWS), vertical.reshape(DOCS, ROWS)))
    return result.reshape(TOKENS, D)

def reference(tokens, lengths, horizontal, vertical, gain_attn, w_qkv, bias_tables, w_output, gain_ffn, w_inner, w_outer, cotangent):

    def wrapped(tokens_f, gain_a, qkv_f, tables_f, output_f, gain_f, inner_f, outer_f):
        return forward(tokens_f, gain_a, qkv_f, tables_f, output_f, gain_f, inner_f, outer_f, lengths, horizontal, vertical)
    floats = (tokens.astype(jnp.float32), gain_attn.astype(jnp.float32), w_qkv.astype(jnp.float32), bias_tables.astype(jnp.float32), w_output.astype(jnp.float32), gain_ffn.astype(jnp.float32), w_inner.astype(jnp.float32), w_outer.astype(jnp.float32))
    result, backward = jax.vjp(wrapped, *floats)
    grads = backward(cotangent.astype(jnp.float32))
    return (result.astype(jnp.bfloat16), grads[0], grads[2], grads[4], grads[6], grads[7], grads[1], grads[5], grads[3])
```

```python
import functools
import jax
import jax.numpy as jnp
import numpy as np
from jax import lax
from jax.experimental import pallas as pl
from jax.experimental.pallas import tpu as pltpu
from jax.sharding import PartitionSpec as P

BUCKETS = 32
CODES = 64
HALF = BUCKETS // 2
EPSILON = 1e-06
DEAD = -1e9
CHUNK = 512
BLOCK = 128
BAND = 3 * BLOCK
WIDE = 6 * BLOCK
FAR = 64
MASK = 76
LSE = 80
MIB = 2**20

f32 = jnp.float32
bf16 = jnp.bfloat16


def expansion():
    offsets = np.arange(WIDE) - 2 * BLOCK
    line = np.clip(offsets, -HALF, HALF - 1) + HALF
    line[5 * BLOCK :] = 0
    wrapped = np.arange(BLOCK)
    wrapped = np.where(wrapped < CODES, wrapped, wrapped - BLOCK)
    plane = np.clip(wrapped, -HALF, HALF - 1) + HALF
    buckets = np.concatenate([line, BUCKETS + plane, 2 * BUCKETS + plane])
    return (np.arange(3 * BUCKETS)[:, None] == buckets[None, :]).astype(np.float32)


def collapse():
    buckets = np.argmax(expansion(), axis=0)
    buckets[5 * BLOCK + 1 : WIDE] = 0
    buckets = np.concatenate([buckets, np.zeros(BLOCK, int), np.full(BLOCK, BUCKETS - 1)])
    return (buckets[:, None] == np.arange(3 * BUCKETS)[None, :]).astype(np.float32)


def roll_rows(value, right):
    rows, width = value.shape
    index = lax.broadcasted_iota(jnp.int32, value.shape, 0)
    step = 1
    while step < rows:
        shift = step if right else width - step
        value = jnp.where((index // step) % 2 == 1, pltpu.roll(value, shift, 1), value)
        step *= 2
    return value


def dot(a, b):
    return jnp.dot(a, b, preferred_element_type=f32)


def dot_nt(a, b):
    return lax.dot_general(a, b, (((1,), (1,)), ((), ())), preferred_element_type=f32)


def split3(value):
    high = value.astype(bf16).astype(f32)
    rest = value - high
    middle = rest.astype(bf16).astype(f32)
    return high, middle, rest - middle


def prep_kernel(
    length_ref, tokens_ref, gain_ref, w_ref, codes_ref, tables_ref, expand_ref,
    normed_ref, q_ref, k_ref, kt_ref, v_ref, band_ref, band_t_ref,
    plane_ref, proj_ref,
):
    heads = q_ref.shape[0]
    step = pl.program_id(0)
    width = w_ref.shape[2]
    expanded = dot(tables_ref[...], expand_ref[...])

    @pl.when(step == 0)
    def _():
        rows = lax.broadcasted_iota(jnp.int32, (BLOCK, BLOCK), 0)
        lanes = lax.broadcasted_iota(jnp.int32, (BLOCK, BLOCK), 1)
        for h in range(heads):
            line = jnp.broadcast_to(expanded[h : h + 1, :WIDE], (BLOCK, WIDE))
            band = roll_rows(line, True)
            band_ref[h] = band
            band_t_ref[h] = band.T
            across = roll_rows(jnp.broadcast_to(expanded[h : h + 1, WIDE : WIDE + BLOCK], (BLOCK, BLOCK)), True)
            upward = roll_rows(jnp.broadcast_to(expanded[h : h + 1, WIDE + BLOCK :], (BLOCK, BLOCK)), True)
            plane = jnp.where(
                (rows < CODES) & (lanes < CODES), across, jnp.where((rows >= CODES) & (lanes >= CODES), upward, 0.0)
            )
            plane_ref[h] = plane.astype(bf16)
        proj_ref[...] = jnp.zeros_like(proj_ref)

    x = tokens_ref[...].astype(f32)
    factor = lax.rsqrt(jnp.mean(x * x, axis=-1, keepdims=True) + EPSILON)
    normed = (x * factor * gain_ref[...].astype(f32)).astype(bf16)
    normed_ref[...] = normed

    codes = codes_ref[...]
    codes_lines = lax.broadcasted_iota(jnp.int32, (BLOCK, CHUNK), 0)
    hot_t = jnp.where(
        codes_lines == jnp.broadcast_to(codes[0:1], (BLOCK, CHUNK)),
        1.0,
        jnp.where(codes_lines - CODES == jnp.broadcast_to(codes[1:2], (BLOCK, CHUNK)), 1.0, 0.0),
    )
    hot_f = hot_t.T
    hot = hot_f.astype(bf16)

    lanes = lax.broadcasted_iota(jnp.int32, (CHUNK, BLOCK), 1)
    rows = lax.broadcasted_iota(jnp.int32, (CHUNK, BLOCK), 0) + step * CHUNK
    block = rows // BLOCK
    blocks = pl.num_programs(0) * (CHUNK // BLOCK)
    start = jnp.clip(block - 1, 0, blocks - 3)
    far = (lanes >= FAR) & (lanes < MASK)
    far_left = far & (lanes - FAR < start)
    far_right = far & (lanes - FAR > start + 2)
    key_side = jnp.where(
        (far & (lanes - FAR == block))
        | ((lanes == MASK) & (rows >= length_ref[0]))
        | ((lanes >= LSE) & (lanes < LSE + 3)),
        1.0,
        0.0,
    )
    low = lanes < FAR

    def part(h):
        if h % 2 == 0:
            return proj_ref[:, h // 2 * BLOCK : h // 2 * BLOCK + BLOCK]
        return pltpu.roll(proj_ref[:, h // 2 * BLOCK : h // 2 * BLOCK + BLOCK], BLOCK - 64, 1)

    proj_ref[:, :width] = dot(normed, w_ref[0])
    for h in range(heads):
        left = expanded[h : h + 1, 0:1]
        right = expanded[h : h + 1, WIDE - BLOCK - 1 : WIDE - BLOCK]
        query_side = jnp.where(far_left, left, jnp.where(far_right, right, jnp.where(lanes == MASK, DEAD, 0.0)))
        q_ref[h, :, :BLOCK] = dot(hot, plane_ref[h]).astype(bf16)
        q_ref[h, :, BLOCK:] = jnp.where(low, part(h).astype(bf16).astype(f32) * 0.125, query_side).astype(bf16)
    proj_ref[:, :width] = dot(normed, w_ref[1])
    for h in range(heads):
        second = jnp.where(low, part(h), key_side)
        k_ref[h, :, :BLOCK] = hot
        k_ref[h, :, BLOCK:] = second.astype(bf16)
        kt_ref[h, :BLOCK, :] = hot_t.astype(bf16)
        kt_ref[h, BLOCK:, :] = second.T.astype(bf16)
    proj_ref[:, :width] = dot(normed, w_ref[2])
    for h in range(heads):
        v_ref[h] = jnp.where(low, part(h), 1.0).astype(bf16)


def prep(tokens, lengths, codes, gain, w_qkv, bias_tables):
    rows, model = tokens.shape
    heads = bias_tables.shape[1]
    tables = jnp.pad(bias_tables.T, ((0, 8 - heads), (0, 0)))
    expand = jnp.asarray(expansion(), bf16)
    full = pl.BlockSpec(memory_space=pltpu.VMEM)
    return pl.pallas_call(
        prep_kernel,
        grid=(rows // CHUNK,),
        in_specs=[
            pl.BlockSpec(memory_space=pltpu.SMEM),
            pl.BlockSpec((CHUNK, model), lambda i: (i, 0)),
            full,
            full,
            pl.BlockSpec((2, CHUNK), lambda i: (0, i)),
            full,
            full,
        ],
        out_specs=[
            pl.BlockSpec((CHUNK, model), lambda i: (i, 0)),
            pl.BlockSpec((heads, CHUNK, 256), lambda i: (0, i, 0)),
            pl.BlockSpec((heads, CHUNK, 256), lambda i: (0, i, 0)),
            pl.BlockSpec((heads, 256, CHUNK), lambda i: (0, 0, i)),
            pl.BlockSpec((heads, CHUNK, BLOCK), lambda i: (0, i, 0)),
            pl.BlockSpec((heads, BLOCK, WIDE), lambda i: (0, 0, 0)),
            pl.BlockSpec((heads, WIDE, BLOCK), lambda i: (0, 0, 0)),
        ],
        out_shape=[
            jax.ShapeDtypeStruct((rows, model), bf16),
            jax.ShapeDtypeStruct((heads, rows, 256), bf16),
            jax.ShapeDtypeStruct((heads, rows, 256), bf16),
            jax.ShapeDtypeStruct((heads, 256, rows), bf16),
            jax.ShapeDtypeStruct((heads, rows, BLOCK), bf16),
            jax.ShapeDtypeStruct((heads, BLOCK, WIDE), f32),
            jax.ShapeDtypeStruct((heads, WIDE, BLOCK), f32),
        ],
        scratch_shapes=[pltpu.VMEM((heads, BLOCK, BLOCK), bf16), pltpu.VMEM((CHUNK, 256), f32)],
        compiler_params=pltpu.CompilerParams(vmem_limit_bytes=40 * MIB),
        name="prep",
    )(lengths, tokens, gain.reshape(1, model), w_qkv, codes, tables, expand)


def attend_kernel(q_ref, kt_ref, v_ref, band_ref, w_ref, att_ref, qt_ref, partial_ref, s_ref):
    heads, _, keys = kt_ref.shape
    step = pl.program_id(0)
    blocks = keys // BLOCK
    low = lax.broadcasted_iota(jnp.int32, (CHUNK, BLOCK), 1) < FAR
    lanes = lax.broadcasted_iota(jnp.int32, (CHUNK, BLOCK), 1)
    results = []
    for h in range(heads):
        s_ref[...] = dot(q_ref[h], kt_ref[h])
        for p in range(CHUNK // BLOCK):
            block = step * (CHUNK // BLOCK) + p
            start = jnp.clip(block - 1, 0, blocks - 3)
            at = pl.ds(pl.multiple_of(start * BLOCK, BLOCK), BAND)
            of = pl.ds(pl.multiple_of((start - block + 2) * BLOCK, BLOCK), BAND)
            s_ref[p * BLOCK : (p + 1) * BLOCK, at] += band_ref[h, :, of]
        s = s_ref[...]
        top = jnp.max(s, axis=1, keepdims=True)
        weights = jnp.exp(s - top).astype(bf16)
        mixed = dot(weights, v_ref[h])
        sums = pltpu.roll(mixed, 64, 1)
        results.append(jnp.where(low, mixed / sums, 0.0))
        total = -(top + jnp.log(mixed[:, 64:65]))
        high, middle, rest = split3(total)
        second = q_ref[h, :, BLOCK:].astype(f32)
        second = jnp.where(
            lanes == LSE, high, jnp.where(lanes == LSE + 1, middle, jnp.where(lanes == LSE + 2, rest, second))
        )
        qt_ref[h, :BLOCK, :] = q_ref[h, :, :BLOCK].astype(f32).T.astype(bf16)
        qt_ref[h, BLOCK:, :] = second.T.astype(bf16)
    pairs = []
    for h in range(0, heads, 2):
        pair = results[h]
        if h + 1 < heads:
            pair = jnp.where(low, pair, pltpu.roll(results[h + 1], 64, 1))
        pairs.append(pair.astype(bf16))
    att = jnp.concatenate(pairs, axis=1)
    width = heads * 64
    att_ref[...] = att[:, :width]
    partial_ref[...] = dot(att[:, :width], w_ref[...]).astype(bf16)


def attend(q, kt, v, band, w_output):
    heads, rows, _ = q.shape
    width, model = w_output.shape
    full = pl.BlockSpec(memory_space=pltpu.VMEM)
    return pl.pallas_call(
        attend_kernel,
        grid=(rows // CHUNK,),
        in_specs=[pl.BlockSpec((heads, CHUNK, 256), lambda i: (0, i, 0)), full, full, full, full],
        out_specs=[
            pl.BlockSpec((CHUNK, width), lambda i: (i, 0)),
            pl.BlockSpec((heads, 256, CHUNK), lambda i: (0, 0, i)),
            pl.BlockSpec((CHUNK, model), lambda i: (i, 0)),
        ],
        out_shape=[
            jax.ShapeDtypeStruct((rows, width), bf16),
            jax.ShapeDtypeStruct((heads, 256, rows), bf16),
            jax.ShapeDtypeStruct((rows, model), bf16),
        ],
        scratch_shapes=[pltpu.VMEM((CHUNK, rows), f32)],
        compiler_params=pltpu.CompilerParams(vmem_limit_bytes=56 * MIB),
        name="attend",
    )(q, kt, v, band, w_output)


def back_kernel(
    ghl_ref, w_ref, att_ref, q_ref, qt_ref, k_ref, kt_ref, v_ref, band_t_ref,
    grad_ref, sums_ref,
    da_ref, dat_ref, s_ref, g_ref, pt_ref, gt_ref, dqt_ref, dk_ref, dv_ref, bands_ref, pad_ref,
):
    heads, rows, _ = k_ref.shape
    blocks = rows // BLOCK
    chunks = rows // CHUNK
    width = heads * 64
    lanes = lax.broadcasted_iota(jnp.int32, (CHUNK, BLOCK), 1)
    low = lanes < FAR
    pad_ref[...] = jnp.zeros_like(pad_ref)

    def prologue(c, carry):
        at = pl.ds(pl.multiple_of(c * CHUNK, CHUNK), CHUNK)
        pad_ref[:, :width] = dot_nt(ghl_ref[at, :], w_ref[...]).astype(bf16).astype(f32)
        pad_ref[:, 256 : 256 + width] = att_ref[at, :].astype(f32)
        for h in range(heads):
            base = h // 2 * BLOCK
            grad = pad_ref[:, base : base + BLOCK]
            out = pad_ref[:, 256 + base : 256 + base + BLOCK]
            if h % 2 == 1:
                grad = pltpu.roll(grad, 64, 1)
                out = pltpu.roll(out, 64, 1)
            total = -jnp.sum(jnp.where(low, grad * out, 0.0), axis=1, keepdims=True)
            high, middle, rest = split3(total)
            grad = jnp.where(
                low,
                grad,
                jnp.where(
                    lanes == FAR, high, jnp.where(lanes == FAR + 1, middle, jnp.where(lanes == FAR + 2, rest, 0.0))
                ),
            )
            da_ref[h, at, :] = grad.astype(bf16)
            dat_ref[h, :, at] = grad.T.astype(bf16)
        return carry

    lax.fori_loop(0, chunks, prologue, 0)
    dk_ref[...] = jnp.zeros_like(dk_ref)
    dv_ref[...] = jnp.zeros_like(dv_ref)
    bands_ref[...] = jnp.zeros_like(bands_ref)

    def main(i, carry):
        h = i // chunks
        c = i % chunks
        at = pl.ds(pl.multiple_of(c * CHUNK, CHUNK), CHUNK)
        s_ref[...] = dot(k_ref[h], qt_ref[h, :, at])
        for p in range(CHUNK // BLOCK):
            block = c * (CHUNK // BLOCK) + p
            start = jnp.clip(block - 1, 0, blocks - 3)
            keys = pl.ds(pl.multiple_of(start * BLOCK, BLOCK), BAND)
            of = pl.ds(pl.multiple_of((start - block + 2) * BLOCK, BLOCK), BAND)
            s_ref[keys, p * BLOCK : (p + 1) * BLOCK] += band_t_ref[h, of, :]
        probs = jnp.exp(s_ref[...])
        pt_ref[...] = probs.astype(bf16)
        gt_ref[...] = (probs * dot(v_ref[h], dat_ref[h, :, at])).astype(bf16)
        dv_ref[h] += dot(pt_ref[...], da_ref[h, at, :])
        dk_ref[h] += dot(gt_ref[...], q_ref[h, at, BLOCK:])
        dqt_ref[h, :, at] = dot(kt_ref[h], gt_ref[...])
        for p in range(CHUNK // BLOCK):
            block = c * (CHUNK // BLOCK) + p
            start = jnp.clip(block - 1, 0, blocks - 3)
            keys = pl.ds(pl.multiple_of(start * BLOCK, BLOCK), BAND)
            of = pl.ds(pl.multiple_of((start - block + 2) * BLOCK, BLOCK), BAND)
            bands_ref[h, of, :] += gt_ref[keys, p * BLOCK : (p + 1) * BLOCK].astype(f32)
        return carry

    lax.fori_loop(0, heads * chunks, main, 0)

    def pack(k, parts):
        merged = []
        for h in range(0, heads, 2):
            pair = parts[h]
            pair_low = lax.broadcasted_iota(jnp.int32, pair.shape, 1) < 64
            if h + 1 < heads:
                pair = jnp.where(pair_low, pair, pltpu.roll(parts[h + 1], 64, 1))
            merged.append(pair.astype(bf16))
        grad_ref[k] = jnp.concatenate(merged, axis=1)[:, :width]

    pack(0, [dqt_ref[h, BLOCK:, :].T * 0.125 for h in range(heads)])
    pack(1, [dk_ref[h] for h in range(heads)])
    pack(2, [dv_ref[h] for h in range(heads)])

    sums_ref[...] = jnp.zeros_like(sums_ref)
    lines16 = lax.broadcasted_iota(jnp.int32, (16, rows), 0)
    block = lax.broadcasted_iota(jnp.int32, (16, rows), 1) // BLOCK
    start = jnp.clip(block - 1, 0, blocks - 3)
    real = lines16 < blocks
    plane_rows = lax.broadcasted_iota(jnp.int32, (BLOCK, BLOCK), 0)
    plane_lanes = lax.broadcasted_iota(jnp.int32, (BLOCK, BLOCK), 1)

    def fold(value):
        total = value[:, :BLOCK]
        for b in range(1, value.shape[1] // BLOCK):
            total = total + value[:, b * BLOCK : (b + 1) * BLOCK]
        return jnp.sum(total, axis=0, keepdims=True)

    for h in range(heads):
        band = roll_rows(bands_ref[h].T, False)
        sums_ref[h : h + 1, :WIDE] = jnp.sum(band, axis=0, keepdims=True)
        spread = dqt_ref[h, :BLOCK, :]
        high = spread.astype(bf16)
        rest = (spread - high.astype(f32)).astype(bf16)
        hot = k_ref[h, :, :BLOCK]
        plane = (dot(high, hot) + dot(rest, hot)).T
        plane = jnp.where((plane_rows < CODES) == (plane_lanes < CODES), plane, 0.0)
        plane = roll_rows(plane, False)
        sums_ref[h : h + 1, WIDE : WIDE + BLOCK] = jnp.sum(plane[:CODES], axis=0, keepdims=True)
        sums_ref[h : h + 1, WIDE + BLOCK : WIDE + 2 * BLOCK] = jnp.sum(plane[CODES:], axis=0, keepdims=True)
        far = dqt_ref[h, BLOCK + FAR : BLOCK + FAR + 16, :]
        sums_ref[h : h + 1, WIDE + 2 * BLOCK : WIDE + 3 * BLOCK] = fold(jnp.where(real & (lines16 < start), far, 0.0))
        sums_ref[h : h + 1, WIDE + 3 * BLOCK :] = fold(jnp.where(real & (lines16 > start + 2), far, 0.0))


def attend_back(ghl, w_output, att, q, qt, k, kt, v, band_t):
    heads, rows, _ = q.shape
    full = pl.BlockSpec(memory_space=pltpu.VMEM)
    return pl.pallas_call(
        back_kernel,
        in_specs=[full] * 9,
        out_specs=[full] * 2,
        out_shape=[
            jax.ShapeDtypeStruct((3, rows, heads * 64), bf16),
            jax.ShapeDtypeStruct((8, WIDE + 4 * BLOCK), f32),
        ],
        scratch_shapes=[
            pltpu.VMEM((heads, rows, BLOCK), bf16),
            pltpu.VMEM((heads, BLOCK, rows), bf16),
            pltpu.VMEM((rows, CHUNK), f32),
            pltpu.VMEM((rows, CHUNK), f32),
            pltpu.VMEM((rows, CHUNK), bf16),
            pltpu.VMEM((rows, CHUNK), bf16),
            pltpu.VMEM((heads, 256, rows), f32),
            pltpu.VMEM((heads, rows, BLOCK), f32),
            pltpu.VMEM((heads, rows, BLOCK), f32),
            pltpu.VMEM((heads, WIDE, BLOCK), f32),
            pltpu.VMEM((CHUNK, 512), f32),
        ],
        compiler_params=pltpu.CompilerParams(vmem_limit_bytes=60 * MIB),
        name="attend_back",
    )(ghl, w_output, att, q, qt, k, kt, v, band_t)


def factor_of(rows):
    return lax.rsqrt(jnp.mean(rows * rows, axis=-1, keepdims=True) + EPSILON)


def norm_back(inputs, grad_normed, gain):
    factor = factor_of(inputs)
    hat = inputs * factor
    scaled = grad_normed * gain
    back = factor * (scaled - hat * jnp.mean(scaled * hat, axis=-1, keepdims=True))
    return back, jnp.sum(grad_normed * hat, axis=0)


def local(
    tokens, lengths, horizontal, vertical, gain_attn, w_qkv, bias_tables, w_output, gain_ffn, w_inner, w_outer, cotangent
):
    rows, model = tokens.shape
    heads = bias_tables.shape[1]
    width = w_qkv.shape[2]
    share = rows // lax.axis_size("mp")
    mp = lax.axis_index("mp")
    gain_a = gain_attn.astype(f32)
    gain_f = gain_ffn.astype(f32)
    codes = jnp.stack([horizontal, vertical])
    normed_a, q, k, kt, v, band, band_t = prep(tokens, lengths, codes, gain_attn, w_qkv, bias_tables)
    att, qt, partial = attend(q, kt, v, band, w_output)

    def mine(x):
        return lax.dynamic_slice_in_dim(x, mp * share, share, 0)

    def scatter(x):
        return lax.psum_scatter(x, "mp", scatter_dimension=0, tiled=True).astype(f32)

    def gather(x):
        return lax.all_gather(x, "mp", axis=0, tiled=True)

    tokens_share = mine(tokens).astype(f32)
    hidden = tokens_share + scatter(partial)
    normed_f = gather((hidden * factor_of(hidden) * gain_f).astype(bf16))
    inner = dot(normed_f, w_inner)
    gelu, gelu_back = jax.vjp(jax.nn.gelu, inner)
    activated = gelu.astype(bf16)
    partial_ffn = dot(activated, w_outer).astype(bf16)
    grad_act = dot_nt(cotangent, w_outer)
    grad_inner_low = gelu_back(grad_act)[0].astype(bf16)
    partial_norm = dot_nt(grad_inner_low, w_inner).astype(bf16)
    grad_outer = lax.dot_general(activated, cotangent, (((0,), (0,)), ((), ())), preferred_element_type=f32)
    grad_inner = lax.dot_general(normed_f, grad_inner_low, (((0,), (0,)), ((), ())), preferred_element_type=f32)
    mixed = (hidden + scatter(partial_ffn)).astype(bf16)
    back_f, gain_f_grad = norm_back(hidden, scatter(partial_norm), gain_f)
    grad_hidden = mine(cotangent).astype(f32) + back_f
    ghl = gather(grad_hidden.astype(bf16))
    grad_output = lax.dot_general(att, ghl, (((0,), (0,)), ((), ())), preferred_element_type=f32)
    grads, sums = attend_back(ghl, w_output, att, q, qt, k, kt, v, band_t)
    grad_qkv = lax.dot_general(normed_a, grads, (((0,), (1,)), ((), ())), preferred_element_type=f32)
    grad_qkv = jnp.transpose(grad_qkv, (1, 0, 2))
    partial_a = (dot_nt(grads[0], w_qkv[0]) + dot_nt(grads[1], w_qkv[1]) + dot_nt(grads[2], w_qkv[2])).astype(bf16)
    back_a, gain_a_grad = norm_back(tokens_share, scatter(partial_a), gain_a)
    input_grad = grad_hidden + back_a
    tables = lax.dot_general(
        jnp.asarray(collapse(), f32), sums[:heads], (((0,), (1,)), ((), ())), precision=lax.Precision.HIGHEST
    )
    gains = lax.psum(jnp.stack([gain_a_grad, gain_f_grad]), ("dp", "mp"))
    tables = lax.psum(tables, "dp")

    def spread(x, axis):
        return lax.psum_scatter(x, "dp", scatter_dimension=axis, tiled=True)

    return (
        mixed,
        input_grad,
        spread(grad_qkv, 1),
        spread(grad_output, 1),
        spread(grad_inner, 0),
        spread(grad_outer, 1),
        gains[0],
        gains[1],
        tables,
    )


def solution(mesh):
    return jax.shard_map(
        local,
        mesh=mesh,
        in_specs=(
            P("dp", None), P("dp"), P("dp"), P("dp"), P(), P(None, None, "mp"), P(None, "mp"), P("mp", None), P(),
            P(None, "mp"), P("mp", None), P("dp", None),
        ),
        out_specs=(
            P(("dp", "mp"), None), P(("dp", "mp"), None), P(None, "dp", "mp"), P("mp", "dp"), P("dp", "mp"),
            P("mp", "dp"), P(), P(), P(None, "mp"),
        ),
        check_vma=False,
    )
```

```python
import functools
import jax
import jax.numpy as jnp
import numpy as np
from jax import lax
from jax.experimental import pallas as pl
from jax.experimental.pallas import tpu as pltpu
from jax.sharding import PartitionSpec as P

BUCKETS = 32
CODES = 64
HALF = BUCKETS // 2
EPSILON = 1e-06
DEAD = -1e9
CHUNK = 512
BLOCK = 128
BAND = 3 * BLOCK
WIDE = 6 * BLOCK
FAR = 64
MASK = 76
LSE = 80
MIB = 2**20

f32 = jnp.float32
bf16 = jnp.bfloat16


def expansion():
    offsets = np.arange(WIDE) - 2 * BLOCK
    line = np.clip(offsets, -HALF, HALF - 1) + HALF
    line[5 * BLOCK :] = 0
    wrapped = np.arange(BLOCK)
    wrapped = np.where(wrapped < CODES, wrapped, wrapped - BLOCK)
    plane = np.clip(wrapped, -HALF, HALF - 1) + HALF
    buckets = np.concatenate([line, BUCKETS + plane, 2 * BUCKETS + plane])
    return (np.arange(3 * BUCKETS)[:, None] == buckets[None, :]).astype(np.float32)


def collapse():
    buckets = np.argmax(expansion(), axis=0)
    buckets[5 * BLOCK + 1 : WIDE] = 0
    buckets = np.concatenate([buckets, np.zeros(BLOCK, int), np.full(BLOCK, BUCKETS - 1)])
    return (buckets[:, None] == np.arange(3 * BUCKETS)[None, :]).astype(np.float32)


def roll_rows(value, right):
    rows, width = value.shape
    index = lax.broadcasted_iota(jnp.int32, value.shape, 0)
    step = 1
    while step < rows:
        shift = step if right else width - step
        value = jnp.where((index // step) % 2 == 1, pltpu.roll(value, shift, 1), value)
        step *= 2
    return value


def dot(a, b):
    return jnp.dot(a, b, preferred_element_type=f32)


def dot_nt(a, b):
    return lax.dot_general(a, b, (((1,), (1,)), ((), ())), preferred_element_type=f32)


def split3(value):
    high = value.astype(bf16).astype(f32)
    rest = value - high
    middle = rest.astype(bf16).astype(f32)
    return high, middle, rest - middle


def prep_kernel(
    length_ref, tokens_ref, gain_ref, w_ref, codes_ref, tables_ref, expand_ref,
    normed_ref, q_ref, k_ref, kt_ref, v_ref, band_ref, band_t_ref,
    plane_ref, proj_ref,
):
    heads = q_ref.shape[0]
    step = pl.program_id(0)
    width = w_ref.shape[2]
    expanded = dot(tables_ref[...], expand_ref[...])

    @pl.when(step == 0)
    def _():
        rows = lax.broadcasted_iota(jnp.int32, (BLOCK, BLOCK), 0)
        lanes = lax.broadcasted_iota(jnp.int32, (BLOCK, BLOCK), 1)
        for h in range(heads):
            line = jnp.broadcast_to(expanded[h : h + 1, :WIDE], (BLOCK, WIDE))
            band = roll_rows(line, True)
            band_ref[h] = band
            band_t_ref[h] = band.T
            across = roll_rows(jnp.broadcast_to(expanded[h : h + 1, WIDE : WIDE + BLOCK], (BLOCK, BLOCK)), True)
            upward = roll_rows(jnp.broadcast_to(expanded[h : h + 1, WIDE + BLOCK :], (BLOCK, BLOCK)), True)
            plane = jnp.where(
                (rows < CODES) & (lanes < CODES), across, jnp.where((rows >= CODES) & (lanes >= CODES), upward, 0.0)
            )
            plane_ref[h] = plane.astype(bf16)
        proj_ref[...] = jnp.zeros_like(proj_ref)

    x = tokens_ref[...].astype(f32)
    factor = lax.rsqrt(jnp.mean(x * x, axis=-1, keepdims=True) + EPSILON)
    normed = (x * factor * gain_ref[...].astype(f32)).astype(bf16)
    normed_ref[...] = normed

    codes = codes_ref[...]
    codes_lines = lax.broadcasted_iota(jnp.int32, (BLOCK, CHUNK), 0)
    hot_t = jnp.where(
        codes_lines == jnp.broadcast_to(codes[0:1], (BLOCK, CHUNK)),
        1.0,
        jnp.where(codes_lines - CODES == jnp.broadcast_to(codes[1:2], (BLOCK, CHUNK)), 1.0, 0.0),
    )
    hot_f = hot_t.T
    hot = hot_f.astype(bf16)

    lanes = lax.broadcasted_iota(jnp.int32, (CHUNK, BLOCK), 1)
    rows = lax.broadcasted_iota(jnp.int32, (CHUNK, BLOCK), 0) + step * CHUNK
    block = rows // BLOCK
    blocks = pl.num_programs(0) * (CHUNK // BLOCK)
    start = jnp.clip(block - 1, 0, blocks - 3)
    far = (lanes >= FAR) & (lanes < MASK)
    far_left = far & (lanes - FAR < start)
    far_right = far & (lanes - FAR > start + 2)
    key_side = jnp.where(
        (far & (lanes - FAR == block))
        | ((lanes == MASK) & (rows >= length_ref[0]))
        | ((lanes >= LSE) & (lanes < LSE + 3)),
        1.0,
        0.0,
    )
    low = lanes < FAR

    def part(h):
        if h % 2 == 0:
            return proj_ref[:, h // 2 * BLOCK : h // 2 * BLOCK + BLOCK]
        return pltpu.roll(proj_ref[:, h // 2 * BLOCK : h // 2 * BLOCK + BLOCK], BLOCK - 64, 1)

    proj_ref[:, :width] = dot(normed, w_ref[0])
    for h in range(heads):
        left = expanded[h : h + 1, 0:1]
        right = expanded[h : h + 1, WIDE - BLOCK - 1 : WIDE - BLOCK]
        query_side = jnp.where(far_left, left, jnp.where(far_right, right, jnp.where(lanes == MASK, DEAD, 0.0)))
        q_ref[h, :, :BLOCK] = dot(hot, plane_ref[h]).astype(bf16)
        q_ref[h, :, BLOCK:] = jnp.where(low, part(h).astype(bf16).astype(f32) * 0.125, query_side).astype(bf16)
    proj_ref[:, :width] = dot(normed, w_ref[1])
    for h in range(heads):
        second = jnp.where(low, part(h), key_side)
        k_ref[h, :, :BLOCK] = hot
        k_ref[h, :, BLOCK:] = second.astype(bf16)
        kt_ref[h, :BLOCK, :] = hot_t.astype(bf16)
        kt_ref[h, BLOCK:, :] = second.T.astype(bf16)
    proj_ref[:, :width] = dot(normed, w_ref[2])
    for h in range(heads):
        v_ref[h] = jnp.where(low, part(h), 1.0).astype(bf16)


def prep(tokens, lengths, codes, gain, w_qkv, bias_tables):
    rows, model = tokens.shape
    heads = bias_tables.shape[1]
    tables = jnp.pad(bias_tables.T, ((0, 8 - heads), (0, 0)))
    expand = jnp.asarray(expansion(), bf16)
    full = pl.BlockSpec(memory_space=pltpu.VMEM)
    return pl.pallas_call(
        prep_kernel,
        grid=(rows // CHUNK,),
        in_specs=[
            pl.BlockSpec(memory_space=pltpu.SMEM),
            pl.BlockSpec((CHUNK, model), lambda i: (i, 0)),
            full,
            full,
            pl.BlockSpec((2, CHUNK), lambda i: (0, i)),
            full,
            full,
        ],
        out_specs=[
            pl.BlockSpec((CHUNK, model), lambda i: (i, 0)),
            pl.BlockSpec((heads, CHUNK, 256), lambda i: (0, i, 0)),
            pl.BlockSpec((heads, CHUNK, 256), lambda i: (0, i, 0)),
            pl.BlockSpec((heads, 256, CHUNK), lambda i: (0, 0, i)),
            pl.BlockSpec((heads, CHUNK, BLOCK), lambda i: (0, i, 0)),
            pl.BlockSpec((heads, BLOCK, WIDE), lambda i: (0, 0, 0)),
            pl.BlockSpec((heads, WIDE, BLOCK), lambda i: (0, 0, 0)),
        ],
        out_shape=[
            jax.ShapeDtypeStruct((rows, model), bf16),
            jax.ShapeDtypeStruct((heads, rows, 256), bf16),
            jax.ShapeDtypeStruct((heads, rows, 256), bf16),
            jax.ShapeDtypeStruct((heads, 256, rows), bf16),
            jax.ShapeDtypeStruct((heads, rows, BLOCK), bf16),
            jax.ShapeDtypeStruct((heads, BLOCK, WIDE), f32),
            jax.ShapeDtypeStruct((heads, WIDE, BLOCK), f32),
        ],
        scratch_shapes=[pltpu.VMEM((heads, BLOCK, BLOCK), bf16), pltpu.VMEM((CHUNK, 256), f32)],
        compiler_params=pltpu.CompilerParams(vmem_limit_bytes=40 * MIB),
        name="prep",
    )(lengths, tokens, gain.reshape(1, model), w_qkv, codes, tables, expand)


def back_kernel(
    ghl_ref, w_ref, att_ref, q_ref, qt_ref, k_ref, kt_ref, v_ref, band_t_ref,
    grad_ref, sums_ref,
    da_ref, dat_ref, s_ref, pt_ref, gt_ref, dqt_ref, dk_ref, dv_ref, bands_ref, pad_ref,
):
    heads, rows, _ = k_ref.shape
    blocks = rows // BLOCK
    chunks = rows // CHUNK
    width = heads * 64
    lanes = lax.broadcasted_iota(jnp.int32, (CHUNK, BLOCK), 1)
    low = lanes < FAR
    pad_ref[...] = jnp.zeros_like(pad_ref)

    def prologue(c, carry):
        at = pl.ds(pl.multiple_of(c * CHUNK, CHUNK), CHUNK)
        pad_ref[:, :width] = dot_nt(ghl_ref[at, :], w_ref[...]).astype(bf16).astype(f32)
        pad_ref[:, 256 : 256 + width] = att_ref[at, :].astype(f32)
        for h in range(heads):
            base = h // 2 * BLOCK
            grad = pad_ref[:, base : base + BLOCK]
            out = pad_ref[:, 256 + base : 256 + base + BLOCK]
            if h % 2 == 1:
                grad = pltpu.roll(grad, 64, 1)
                out = pltpu.roll(out, 64, 1)
            total = -jnp.sum(jnp.where(low, grad * out, 0.0), axis=1, keepdims=True)
            high, middle, rest = split3(total)
            grad = jnp.where(
                low,
                grad,
                jnp.where(
                    lanes == FAR, high, jnp.where(lanes == FAR + 1, middle, jnp.where(lanes == FAR + 2, rest, 0.0))
                ),
            )
            da_ref[h, at, :] = grad.astype(bf16)
            dat_ref[h, :, at] = grad.T.astype(bf16)
        return carry

    lax.fori_loop(0, chunks, prologue, 0)
    dk_ref[...] = jnp.zeros_like(dk_ref)
    dv_ref[...] = jnp.zeros_like(dv_ref)
    bands_ref[...] = jnp.zeros_like(bands_ref)

    def main(i, carry):
        h = i // chunks
        c = i % chunks
        at = pl.ds(pl.multiple_of(c * CHUNK, CHUNK), CHUNK)
        s_ref[...] = dot(k_ref[h], qt_ref[h, c])
        for p in range(CHUNK // BLOCK):
            block = p * chunks + c
            start = jnp.clip(block - 1, 0, blocks - 3)
            keys = pl.ds(pl.multiple_of(start * BLOCK, BLOCK), BAND)
            of = pl.ds(pl.multiple_of((start - block + 2) * BLOCK, BLOCK), BAND)
            s_ref[keys, p * BLOCK : (p + 1) * BLOCK] += band_t_ref[h, of, :]
        probs = jnp.exp(s_ref[...])
        pt_ref[...] = probs.astype(bf16)
        gt_ref[...] = (probs * dot(v_ref[h], dat_ref[h, :, at])).astype(bf16)
        dv_ref[h] += dot(pt_ref[...], da_ref[h, at, :])
        places = [pl.ds(pl.multiple_of((p * chunks + c) * BLOCK, BLOCK), BLOCK) for p in range(CHUNK // BLOCK)]
        dk_ref[h] += dot(gt_ref[...], jnp.concatenate([q_ref[h, place, BLOCK:] for place in places], axis=0))
        dq = dot(kt_ref[h], gt_ref[...])
        for p in range(CHUNK // BLOCK):
            dqt_ref[h, :, places[p]] = dq[:, p * BLOCK : (p + 1) * BLOCK]
        for p in range(CHUNK // BLOCK):
            block = p * chunks + c
            start = jnp.clip(block - 1, 0, blocks - 3)
            keys = pl.ds(pl.multiple_of(start * BLOCK, BLOCK), BAND)
            of = pl.ds(pl.multiple_of((start - block + 2) * BLOCK, BLOCK), BAND)
            bands_ref[h, of, :] += gt_ref[keys, p * BLOCK : (p + 1) * BLOCK].astype(f32)
        return carry

    lax.fori_loop(0, heads * chunks, main, 0)

    def pack(k, parts):
        merged = []
        for h in range(0, heads, 2):
            pair = parts[h]
            pair_low = lax.broadcasted_iota(jnp.int32, pair.shape, 1) < 64
            if h + 1 < heads:
                pair = jnp.where(pair_low, pair, pltpu.roll(parts[h + 1], 64, 1))
            merged.append(pair.astype(bf16))
        grad_ref[k] = jnp.concatenate(merged, axis=1)[:, :width]

    pack(0, [dqt_ref[h, BLOCK:, :].T * 0.125 for h in range(heads)])
    pack(1, [dk_ref[h] for h in range(heads)])
    pack(2, [dv_ref[h] for h in range(heads)])

    sums_ref[...] = jnp.zeros_like(sums_ref)
    lines16 = lax.broadcasted_iota(jnp.int32, (16, rows), 0)
    block = lax.broadcasted_iota(jnp.int32, (16, rows), 1) // BLOCK
    start = jnp.clip(block - 1, 0, blocks - 3)
    real = lines16 < blocks
    plane_rows = lax.broadcasted_iota(jnp.int32, (BLOCK, BLOCK), 0)
    plane_lanes = lax.broadcasted_iota(jnp.int32, (BLOCK, BLOCK), 1)

    def fold(value):
        total = value[:, :BLOCK]
        for b in range(1, value.shape[1] // BLOCK):
            total = total + value[:, b * BLOCK : (b + 1) * BLOCK]
        return jnp.sum(total, axis=0, keepdims=True)

    for h in range(heads):
        band = roll_rows(bands_ref[h].T, False)
        sums_ref[h : h + 1, :WIDE] = jnp.sum(band, axis=0, keepdims=True)
        spread = dqt_ref[h, :BLOCK, :]
        high = spread.astype(bf16)
        rest = (spread - high.astype(f32)).astype(bf16)
        hot = k_ref[h, :, :BLOCK]
        plane = (dot(high, hot) + dot(rest, hot)).T
        plane = jnp.where((plane_rows < CODES) == (plane_lanes < CODES), plane, 0.0)
        plane = roll_rows(plane, False)
        sums_ref[h : h + 1, WIDE : WIDE + BLOCK] = jnp.sum(plane[:CODES], axis=0, keepdims=True)
        sums_ref[h : h + 1, WIDE + BLOCK : WIDE + 2 * BLOCK] = jnp.sum(plane[CODES:], axis=0, keepdims=True)
        far = dqt_ref[h, BLOCK + FAR : BLOCK + FAR + 16, :]
        sums_ref[h : h + 1, WIDE + 2 * BLOCK : WIDE + 3 * BLOCK] = fold(jnp.where(real & (lines16 < start), far, 0.0))
        sums_ref[h : h + 1, WIDE + 3 * BLOCK :] = fold(jnp.where(real & (lines16 > start + 2), far, 0.0))


def attend_back(ghl, w_output, att, q, qt, k, kt, v, band_t):
    heads, rows, _ = q.shape
    full = pl.BlockSpec(memory_space=pltpu.VMEM)
    return pl.pallas_call(
        back_kernel,
        in_specs=[full] * 9,
        out_specs=[full] * 2,
        out_shape=[
            jax.ShapeDtypeStruct((3, rows, heads * 64), bf16),
            jax.ShapeDtypeStruct((8, WIDE + 4 * BLOCK), f32),
        ],
        scratch_shapes=[
            pltpu.VMEM((heads, rows, BLOCK), bf16),
            pltpu.VMEM((heads, BLOCK, rows), bf16),
            pltpu.VMEM((rows, CHUNK), f32),
            pltpu.VMEM((rows, CHUNK), bf16),
            pltpu.VMEM((rows, CHUNK), bf16),
            pltpu.VMEM((heads, 256, rows), f32),
            pltpu.VMEM((heads, rows, BLOCK), f32),
            pltpu.VMEM((heads, rows, BLOCK), f32),
            pltpu.VMEM((heads, WIDE, BLOCK), f32),
            pltpu.VMEM((CHUNK, 512), f32),
        ],
        compiler_params=pltpu.CompilerParams(vmem_limit_bytes=60 * MIB),
        name="attend_back",
    )(ghl, w_output, att, q, qt, k, kt, v, band_t)


def mp_places():
    mp = lax.axis_index("mp")
    y, core = mp // 2, mp % 2
    return mp, y, core, y * 2 + (1 - core), (1 - y) * 2 + core


def remote(src, dst, send, recv, mp):
    return pltpu.make_async_remote_copy(
        src_ref=src,
        dst_ref=dst,
        send_sem=send,
        recv_sem=recv,
        device_id=(lax.axis_index("dp"), mp),
        device_id_type=pl.DeviceIdType.MESH,
    )


def meet():
    _, _, _, sibling, across = mp_places()
    barrier = pltpu.get_barrier_semaphore()
    for other in (sibling, across):
        pl.semaphore_signal(
            barrier, inc=1, device_id=(lax.axis_index("dp"), other), device_id_type=pl.DeviceIdType.MESH
        )
    pl.semaphore_wait(barrier, 2)


class Scatter:

    def __init__(self, part, near, out, far, send, recv):
        self.part, self.near, self.out, self.far, self.send, self.recv = part, near, out, far, send, recv

    def first(self, c):
        _, _, core, sibling, _ = mp_places()
        return remote(self.part.at[c, 1 - core], self.near.at[c], self.send.at[c, 0], self.recv.at[c, 0], sibling)

    def second(self, c):
        _, _, _, _, across = mp_places()
        return remote(self.out.at[c], self.far.at[c], self.send.at[c, 1], self.recv.at[c, 1], across)

    def start(self, c):
        self.first(c).start()

    def middle(self, c):
        _, y, core, _, _ = mp_places()
        self.first(c).wait_recv()
        self.out[c] = (self.part[c, core, 1 - y].astype(f32) + self.near[c, 1 - y].astype(f32)).astype(bf16)
        self.second(c).start()

    def finish(self, c):
        _, y, core, _, _ = mp_places()
        self.second(c).wait_recv()
        own = self.part[c, core, y].astype(f32) + self.near[c, y].astype(f32)
        return own + self.far[c].astype(f32)

    def drain(self, c):
        self.first(c).wait_send()
        self.second(c).wait_send()


class Gather:

    def __init__(self, full, send, recv):
        self.full, self.send, self.recv = full, send, recv

    def copy(self, c, kind):
        mp, _, _, sibling, across = mp_places()
        at = self.full.at[c, across if kind == 2 else mp]
        return remote(at, at, self.send.at[c, kind], self.recv.at[c, kind], across if kind == 1 else sibling)

    def start(self, c):
        self.copy(c, 1).start()
        self.copy(c, 0).start()

    def forward(self, c):
        self.copy(c, 1).wait_recv()
        self.copy(c, 2).start()

    def finish(self, c):
        self.copy(c, 0).wait_recv()
        self.copy(c, 2).wait_recv()

    def drain(self, c):
        for kind in range(3):
            self.copy(c, kind).wait_send()


def scatter_scratch(chunks, piece, model):
    return [
        pltpu.VMEM((chunks, 2, 2, piece, model), bf16),
        pltpu.VMEM((chunks, 2, piece, model), bf16),
        pltpu.VMEM((chunks, piece, model), bf16),
        pltpu.VMEM((chunks, piece, model), bf16),
        pltpu.SemaphoreType.DMA((chunks, 2)),
        pltpu.SemaphoreType.DMA((chunks, 2)),
    ]


def gather_scratch(chunks, piece, model):
    return [
        pltpu.VMEM((chunks, 4, piece, model), bf16),
        pltpu.SemaphoreType.DMA((chunks, 3)),
        pltpu.SemaphoreType.DMA((chunks, 3)),
    ]


ROOT = float(np.sqrt(2.0 / np.pi))
CUBE = 0.044715


def factor_of(rows):
    return lax.rsqrt(jnp.mean(rows * rows, axis=-1, keepdims=True) + EPSILON)


def main_kernel(
    q_ref, kt_ref, v_ref, band_ref, w_output_ref, tokens_ref, gain_ref, w_inner_ref, w_outer_ref, cot_ref,
    qt_ref, att_ref, hidden_ref, ffn_ref, grad_hidden_ref, ghl_out_ref, grad_outer_ref, grad_inner_ref, gain_sum_ref,
    s_ref, res_ref, low_ref, grad_low_ref, sum_ffn_ref, sum_norm_ref,
    *comm,
):
    heads, _, rows = kt_ref.shape
    pieces = 4
    chunks = rows // CHUNK
    blocks = rows // BLOCK
    width = heads * 64
    mp, _, _, _, _ = mp_places()
    attn = Scatter(*comm[0:6])
    norm = Scatter(*comm[6:12])
    normed = Gather(*comm[12:15])
    grads = Gather(*comm[15:18])
    low = lax.broadcasted_iota(jnp.int32, (CHUNK, BLOCK), 1) < FAR
    lanes = lax.broadcasted_iota(jnp.int32, (CHUNK, BLOCK), 1)
    gain = gain_ref[...].astype(f32)
    meet()

    def place(m, c):
        return pl.ds(pl.multiple_of((m * chunks + c) * BLOCK, BLOCK), BLOCK)

    def own(c):
        return pl.ds(pl.multiple_of(c * BLOCK, BLOCK), BLOCK)

    def hidden_of(c):
        hidden = tokens_ref[own(c), :].astype(f32) + attn.finish(c)
        hidden_ref[own(c), :] = hidden
        normed.full[c, mp] = (hidden * factor_of(hidden) * gain).astype(bf16)
        normed.start(c)

    def grad_of(c):
        grad_normed = norm.finish(c)
        hidden = hidden_ref[own(c), :]
        factor = factor_of(hidden)
        hat = hidden * factor
        scaled = grad_normed * gain
        back = factor * (scaled - hat * jnp.mean(scaled * hat, axis=-1, keepdims=True))
        grad = cot_ref[place(mp, c), :].astype(f32) + back
        grad_hidden_ref[own(c), :] = grad
        gain_sum_ref[0:1, :] += jnp.sum(grad_normed * hat, axis=0, keepdims=True)
        grads.full[c, mp] = grad.astype(bf16)
        grads.start(c)

    gain_sum_ref[...] = jnp.zeros_like(gain_sum_ref)

    def attend(t, carry):
        c = t // heads
        h = t % heads
        query = jnp.concatenate([q_ref[h, place(m, c), :] for m in range(pieces)], axis=0)
        s_ref[...] = dot(query, kt_ref[h])
        for m in range(pieces):
            block = m * chunks + c
            start = jnp.clip(block - 1, 0, blocks - 3)
            at = pl.ds(pl.multiple_of(start * BLOCK, BLOCK), BAND)
            of = pl.ds(pl.multiple_of((start - block + 2) * BLOCK, BLOCK), BAND)
            s_ref[m * BLOCK : (m + 1) * BLOCK, at] += band_ref[h, :, of]
        s = s_ref[...]
        top = jnp.max(s, axis=1, keepdims=True)
        weights = jnp.exp(s - top).astype(bf16)
        mixed = dot(weights, v_ref[h])
        sums = pltpu.roll(mixed, 64, 1)
        res_ref[h] = jnp.where(low, mixed / sums, 0.0)
        total = -(top + jnp.log(mixed[:, 64:65]))
        high, middle, rest = split3(total)
        second = query[:, BLOCK:].astype(f32)
        second = jnp.where(
            lanes == LSE, high, jnp.where(lanes == LSE + 1, middle, jnp.where(lanes == LSE + 2, rest, second))
        )
        qt_ref[h, c, :BLOCK, :] = query[:, :BLOCK].astype(f32).T.astype(bf16)
        qt_ref[h, c, BLOCK:, :] = second.T.astype(bf16)

        @pl.when((h == 0) & (c >= 1))
        def _():
            attn.middle(c - 1)

        @pl.when((h == 0) & (c >= 2))
        def _():
            hidden_of(c - 2)

        @pl.when(h == heads - 1)
        def _():
            pairs = []
            for g in range(0, heads, 2):
                pair = res_ref[g]
                if g + 1 < heads:
                    pair = jnp.where(low, pair, pltpu.roll(res_ref[g + 1], 64, 1))
                pairs.append(pair.astype(bf16))
            att = jnp.concatenate(pairs, axis=1)[:, :width]
            att_ref[c] = att
            partial = dot(att, w_output_ref[...]).astype(bf16)
            for m in range(pieces):
                attn.part[c, m % 2, m // 2] = partial[m * BLOCK : (m + 1) * BLOCK]
            attn.start(c)

        return carry

    lax.fori_loop(0, chunks * heads, attend, 0)
    normed.forward(0)
    hidden_of(1)

    steps = w_inner_ref.shape[1] // 256

    def feed(t, carry):
        c = t // steps
        b = t % steps

        @pl.when(b == 0)
        def _():
            normed.finish(c)

        at = pl.ds(pl.multiple_of(b * 256, 256), 256)
        x = jnp.concatenate([normed.full[c, m] for m in range(pieces)], axis=0)
        cot = jnp.concatenate([cot_ref[place(m, c), :] for m in range(pieces)], axis=0)
        inner = dot(x, w_inner_ref[:, at])
        grad_act = dot_nt(cot, w_outer_ref[at, :])
        square = inner * inner
        tanh = jnp.tanh(ROOT * inner * (1.0 + CUBE * square))
        half = 0.5 * (1.0 + tanh)
        slope = half + 0.5 * inner * (1.0 - tanh * tanh) * (ROOT + 3.0 * CUBE * ROOT * square)
        activated = (inner * half).astype(bf16)
        grad_low = (slope * grad_act).astype(bf16)
        low_ref[c, :, at] = activated
        grad_low_ref[c, :, at] = grad_low
        part_ffn = dot(activated, w_outer_ref[at, :])
        part_norm = dot_nt(grad_low, w_inner_ref[:, at])

        @pl.when(b == 0)
        def _():
            sum_ffn_ref[...] = part_ffn
            sum_norm_ref[...] = part_norm

        @pl.when(b > 0)
        def _():
            sum_ffn_ref[...] += part_ffn
            sum_norm_ref[...] += part_norm

        @pl.when((b == 0) & (c == 0))
        def _():
            attn.middle(2)

        @pl.when((b == 0) & (c >= 1))
        def _():
            norm.middle(c - 1)

        @pl.when((b == 1) & (c < 2))
        def _():
            normed.forward(c + 1)

        @pl.when((b == steps - 1) & (c == 0))
        def _():
            hidden_of(2)

        @pl.when((b == steps - 1) & (c >= 1))
        def _():
            grad_of(c - 1)

        @pl.when((b == 1) & (c == 2))
        def _():
            grads.forward(0)

        @pl.when(b == steps - 1)
        def _():
            for m in range(pieces):
                ffn_ref[place(m, c), :] = sum_ffn_ref[m * BLOCK : (m + 1) * BLOCK, :].astype(bf16)
                norm.part[c, m % 2, m // 2] = sum_norm_ref[m * BLOCK : (m + 1) * BLOCK, :].astype(bf16)
            norm.start(c)

        return carry

    lax.fori_loop(0, chunks * steps, feed, 0)

    def weights_of(b, carry):
        at = pl.ds(pl.multiple_of(b * 256, 256), 256)
        outer = jnp.zeros((256, cot_ref.shape[1]), f32)
        inner = jnp.zeros((cot_ref.shape[1], 256), f32)
        for c in range(chunks):
            x = jnp.concatenate([normed.full[c, m] for m in range(pieces)], axis=0)
            cot = jnp.concatenate([cot_ref[place(m, c), :] for m in range(pieces)], axis=0)
            outer = outer + dot_tn(low_ref[c, :, at], cot)
            inner = inner + dot_tn(x, grad_low_ref[c, :, at])
        grad_outer_ref[at, :] = outer.astype(grad_outer_ref.dtype)
        grad_inner_ref[:, at] = inner.astype(grad_inner_ref.dtype)

        @pl.when(b == 0)
        def _():
            norm.middle(2)
            grads.forward(1)

        @pl.when(b == steps - 1)
        def _():
            grad_of(2)

        return carry

    lax.fori_loop(0, steps, weights_of, 0)
    grads.forward(2)
    for c in range(chunks):
        grads.finish(c)
    ghl_out_ref[...] = grads.full[...]
    for c in range(chunks):
        attn.drain(c)
        norm.drain(c)
        normed.drain(c)
        grads.drain(c)


def dot_tn(a, b):
    return lax.dot_general(a, b, (((0,), (0,)), ((), ())), preferred_element_type=f32)


def main_call(q, kt, v, band, w_output, tokens_share, gain, w_inner, w_outer, cotangent):
    heads, rows, _ = q.shape
    width, model = w_output.shape
    share = tokens_share.shape[0]
    chunks = rows // CHUNK
    full = pl.BlockSpec(memory_space=pltpu.VMEM)
    comm = (
        scatter_scratch(chunks, BLOCK, model) * 2 + gather_scratch(chunks, BLOCK, model) * 2
    )
    return pl.pallas_call(
        main_kernel,
        in_specs=[full] * 10,
        out_specs=[full] * 9,
        out_shape=[
            jax.ShapeDtypeStruct((heads, chunks, 256, CHUNK), bf16),
            jax.ShapeDtypeStruct((chunks, CHUNK, width), bf16),
            jax.ShapeDtypeStruct((share, model), f32),
            jax.ShapeDtypeStruct((rows, model), bf16),
            jax.ShapeDtypeStruct((share, model), f32),
            jax.ShapeDtypeStruct((chunks, 4, BLOCK, model), bf16),
            jax.ShapeDtypeStruct((w_outer.shape[0], model), f32),
            jax.ShapeDtypeStruct((model, w_inner.shape[1]), f32),
            jax.ShapeDtypeStruct((8, model), f32),
        ],
        scratch_shapes=[
            pltpu.VMEM((CHUNK, rows), f32),
            pltpu.VMEM((heads, CHUNK, BLOCK), f32),
            pltpu.VMEM((chunks, CHUNK, w_inner.shape[1]), bf16),
            pltpu.VMEM((chunks, CHUNK, w_inner.shape[1]), bf16),
            pltpu.VMEM((CHUNK, model), f32),
            pltpu.VMEM((CHUNK, model), f32),
            *comm,
        ],
        compiler_params=pltpu.CompilerParams(
            vmem_limit_bytes=63 * MIB, collective_id=1, has_side_effects=True
        ),
        name="forward_and_feed",
    )(q, kt, v, band, w_output, tokens_share, gain.reshape(1, model), w_inner, w_outer, cotangent)


def norm_back(inputs, grad_normed, gain):
    factor = factor_of(inputs)
    hat = inputs * factor
    scaled = grad_normed * gain
    back = factor * (scaled - hat * jnp.mean(scaled * hat, axis=-1, keepdims=True))
    return back, jnp.sum(grad_normed * hat, axis=0)


def local(
    tokens, lengths, horizontal, vertical, gain_attn, w_qkv, bias_tables, w_output, gain_ffn, w_inner, w_outer, cotangent
):
    rows, model = tokens.shape
    heads = bias_tables.shape[1]
    width = w_qkv.shape[2]
    share = rows // lax.axis_size("mp")
    mp = lax.axis_index("mp")
    gain_a = gain_attn.astype(f32)
    codes = jnp.stack([horizontal, vertical])
    normed_a, q, k, kt, v, band, band_t = prep(tokens, lengths, codes, gain_attn, w_qkv, bias_tables)
    token_share = lax.dynamic_slice_in_dim(tokens, mp * share, share, 0)
    qt, att, hidden, partial_ffn, grad_hidden, ghl, grad_outer, grad_inner, gain_sums = main_call(
        q, kt, v, band, w_output, token_share, gain_ffn, w_inner, w_outer, cotangent
    )
    att = att.reshape(rows, width)
    ghl = ghl.reshape(rows, model)

    def scatter(x):
        return lax.psum_scatter(x, "mp", scatter_dimension=0, tiled=True).astype(f32)

    tokens_share = token_share.astype(f32)
    gain_f_grad = gain_sums[0]
    mixed = (hidden + scatter(partial_ffn)).astype(bf16)
    grad_output = lax.dot_general(att, ghl, (((0,), (0,)), ((), ())), preferred_element_type=f32)
    grads, sums = attend_back(ghl, w_output, att, q, qt, k, kt, v, band_t)
    grad_qkv = lax.dot_general(normed_a, grads, (((0,), (1,)), ((), ())), preferred_element_type=f32)
    grad_qkv = jnp.transpose(grad_qkv, (1, 0, 2))
    partial_a = (dot_nt(grads[0], w_qkv[0]) + dot_nt(grads[1], w_qkv[1]) + dot_nt(grads[2], w_qkv[2])).astype(bf16)
    back_a, gain_a_grad = norm_back(tokens_share, scatter(partial_a), gain_a)
    input_grad = grad_hidden + back_a
    tables = lax.dot_general(
        jnp.asarray(collapse(), f32), sums[:heads], (((0,), (1,)), ((), ())), precision=lax.Precision.HIGHEST
    )
    gains = lax.psum(jnp.stack([gain_a_grad, gain_f_grad]), ("dp", "mp"))
    tables = lax.psum(tables, "dp")

    def spread(x, axis):
        return lax.psum_scatter(x, "dp", scatter_dimension=axis, tiled=True)

    return (
        mixed,
        input_grad,
        spread(grad_qkv, 1),
        spread(grad_output, 1),
        spread(grad_inner, 0),
        spread(grad_outer, 1),
        gains[0],
        gains[1],
        tables,
    )


def solution(mesh):
    return jax.shard_map(
        local,
        mesh=mesh,
        in_specs=(
            P("dp", None), P("dp"), P("dp"), P("dp"), P(), P(None, None, "mp"), P(None, "mp"), P("mp", None), P(),
            P(None, "mp"), P("mp", None), P("dp", None),
        ),
        out_specs=(
            P(("dp", "mp"), None), P(("dp", "mp"), None), P(None, "dp", "mp"), P("mp", "dp"), P("dp", "mp"),
            P("mp", "dp"), P(), P(), P(None, "mp"),
        ),
        check_vma=False,
    )
```

```python
import functools
import jax
import jax.numpy as jnp
import numpy as np
from jax import lax
from jax.experimental import pallas as pl
from jax.experimental.pallas import tpu as pltpu
from jax.sharding import PartitionSpec as P

BUCKETS = 32
CODES = 64
HALF = BUCKETS // 2
EPSILON = 1e-06
DEAD = -1e9
CHUNK = 512
BLOCK = 128
BAND = 3 * BLOCK
WIDE = 6 * BLOCK
FAR = 64
MASK = 76
LSE = 80
MIB = 2**20

f32 = jnp.float32
bf16 = jnp.bfloat16


def expansion():
    offsets = np.arange(WIDE) - 2 * BLOCK
    line = np.clip(offsets, -HALF, HALF - 1) + HALF
    line[5 * BLOCK :] = 0
    wrapped = np.arange(BLOCK)
    wrapped = np.where(wrapped < CODES, wrapped, wrapped - BLOCK)
    plane = np.clip(wrapped, -HALF, HALF - 1) + HALF
    buckets = np.concatenate([line, BUCKETS + plane, 2 * BUCKETS + plane])
    return (np.arange(3 * BUCKETS)[:, None] == buckets[None, :]).astype(np.float32)


def collapse():
    buckets = np.argmax(expansion(), axis=0)
    buckets[5 * BLOCK + 1 : WIDE] = 0
    buckets = np.concatenate([buckets, np.zeros(BLOCK, int), np.full(BLOCK, BUCKETS - 1)])
    return (buckets[:, None] == np.arange(3 * BUCKETS)[None, :]).astype(np.float32)


def roll_rows(value, right):
    rows, width = value.shape
    index = lax.broadcasted_iota(jnp.int32, value.shape, 0)
    step = 1
    while step < rows:
        shift = step if right else width - step
        value = jnp.where((index // step) % 2 == 1, pltpu.roll(value, shift, 1), value)
        step *= 2
    return value


def dot(a, b):
    return jnp.dot(a, b, preferred_element_type=f32)


def dot_nt(a, b):
    return lax.dot_general(a, b, (((1,), (1,)), ((), ())), preferred_element_type=f32)


def split3(value):
    high = value.astype(bf16).astype(f32)
    rest = value - high
    middle = rest.astype(bf16).astype(f32)
    return high, middle, rest - middle


def prep_kernel(
    length_ref, tokens_ref, gain_ref, w_ref, codes_ref, tables_ref, expand_ref,
    normed_ref, q_ref, k_ref, kt_ref, v_ref, band_ref, band_t_ref,
    plane_ref, proj_ref,
):
    heads = q_ref.shape[0]
    step = pl.program_id(0)
    width = w_ref.shape[2]
    expanded = dot(tables_ref[...], expand_ref[...])

    @pl.when(step == 0)
    def _():
        rows = lax.broadcasted_iota(jnp.int32, (BLOCK, BLOCK), 0)
        lanes = lax.broadcasted_iota(jnp.int32, (BLOCK, BLOCK), 1)
        for h in range(heads):
            line = jnp.broadcast_to(expanded[h : h + 1, :WIDE], (BLOCK, WIDE))
            band = roll_rows(line, True)
            band_ref[h] = band
            band_t_ref[h] = band.T
            across = roll_rows(jnp.broadcast_to(expanded[h : h + 1, WIDE : WIDE + BLOCK], (BLOCK, BLOCK)), True)
            upward = roll_rows(jnp.broadcast_to(expanded[h : h + 1, WIDE + BLOCK :], (BLOCK, BLOCK)), True)
            plane = jnp.where(
                (rows < CODES) & (lanes < CODES), across, jnp.where((rows >= CODES) & (lanes >= CODES), upward, 0.0)
            )
            plane_ref[h] = plane.astype(bf16)
        proj_ref[...] = jnp.zeros_like(proj_ref)

    x = tokens_ref[...].astype(f32)
    factor = lax.rsqrt(jnp.mean(x * x, axis=-1, keepdims=True) + EPSILON)
    normed = (x * factor * gain_ref[...].astype(f32)).astype(bf16)
    normed_ref[...] = normed

    codes = codes_ref[...]
    codes_lines = lax.broadcasted_iota(jnp.int32, (BLOCK, CHUNK), 0)
    hot_t = jnp.where(
        codes_lines == jnp.broadcast_to(codes[0:1], (BLOCK, CHUNK)),
        1.0,
        jnp.where(codes_lines - CODES == jnp.broadcast_to(codes[1:2], (BLOCK, CHUNK)), 1.0, 0.0),
    )
    hot_f = hot_t.T
    hot = hot_f.astype(bf16)

    lanes = lax.broadcasted_iota(jnp.int32, (CHUNK, BLOCK), 1)
    rows = lax.broadcasted_iota(jnp.int32, (CHUNK, BLOCK), 0) + step * CHUNK
    block = rows // BLOCK
    blocks = pl.num_programs(0) * (CHUNK // BLOCK)
    start = jnp.clip(block - 1, 0, blocks - 3)
    far = (lanes >= FAR) & (lanes < MASK)
    far_left = far & (lanes - FAR < start)
    far_right = far & (lanes - FAR > start + 2)
    key_side = jnp.where(
        (far & (lanes - FAR == block))
        | ((lanes == MASK) & (rows >= length_ref[0]))
        | ((lanes >= LSE) & (lanes < LSE + 3)),
        1.0,
        0.0,
    )
    low = lanes < FAR

    def part(h):
        if h % 2 == 0:
            return proj_ref[:, h // 2 * BLOCK : h // 2 * BLOCK + BLOCK]
        return pltpu.roll(proj_ref[:, h // 2 * BLOCK : h // 2 * BLOCK + BLOCK], BLOCK - 64, 1)

    proj_ref[:, :width] = dot(normed, w_ref[0])
    for h in range(heads):
        left = expanded[h : h + 1, 0:1]
        right = expanded[h : h + 1, WIDE - BLOCK - 1 : WIDE - BLOCK]
        query_side = jnp.where(far_left, left, jnp.where(far_right, right, jnp.where(lanes == MASK, DEAD, 0.0)))
        q_ref[h, :, :BLOCK] = dot(hot, plane_ref[h]).astype(bf16)
        q_ref[h, :, BLOCK:] = jnp.where(low, part(h).astype(bf16).astype(f32) * 0.125, query_side).astype(bf16)
    proj_ref[:, :width] = dot(normed, w_ref[1])
    for h in range(heads):
        second = jnp.where(low, part(h), key_side)
        k_ref[h, :, :BLOCK] = hot
        k_ref[h, :, BLOCK:] = second.astype(bf16)
        kt_ref[h, :BLOCK, :] = hot_t.astype(bf16)
        kt_ref[h, BLOCK:, :] = second.T.astype(bf16)
    proj_ref[:, :width] = dot(normed, w_ref[2])
    for h in range(heads):
        v_ref[h] = jnp.where(low, part(h), 1.0).astype(bf16)


def prep(tokens, lengths, codes, gain, w_qkv, bias_tables):
    rows, model = tokens.shape
    heads = bias_tables.shape[1]
    tables = jnp.pad(bias_tables.T, ((0, 8 - heads), (0, 0)))
    expand = jnp.asarray(expansion(), bf16)
    full = pl.BlockSpec(memory_space=pltpu.VMEM)
    return pl.pallas_call(
        prep_kernel,
        grid=(rows // CHUNK,),
        in_specs=[
            pl.BlockSpec(memory_space=pltpu.SMEM),
            pl.BlockSpec((CHUNK, model), lambda i: (i, 0)),
            full,
            full,
            pl.BlockSpec((2, CHUNK), lambda i: (0, i)),
            full,
            full,
        ],
        out_specs=[
            pl.BlockSpec((CHUNK, model), lambda i: (i, 0)),
            pl.BlockSpec((heads, CHUNK, 256), lambda i: (0, i, 0)),
            pl.BlockSpec((heads, CHUNK, 256), lambda i: (0, i, 0)),
            pl.BlockSpec((heads, 256, CHUNK), lambda i: (0, 0, i)),
            pl.BlockSpec((heads, CHUNK, BLOCK), lambda i: (0, i, 0)),
            pl.BlockSpec((heads, BLOCK, WIDE), lambda i: (0, 0, 0)),
            pl.BlockSpec((heads, WIDE, BLOCK), lambda i: (0, 0, 0)),
        ],
        out_shape=[
            jax.ShapeDtypeStruct((rows, model), bf16),
            jax.ShapeDtypeStruct((heads, rows, 256), bf16),
            jax.ShapeDtypeStruct((heads, rows, 256), bf16),
            jax.ShapeDtypeStruct((heads, 256, rows), bf16),
            jax.ShapeDtypeStruct((heads, rows, BLOCK), bf16),
            jax.ShapeDtypeStruct((heads, BLOCK, WIDE), f32),
            jax.ShapeDtypeStruct((heads, WIDE, BLOCK), f32),
        ],
        scratch_shapes=[pltpu.VMEM((heads, BLOCK, BLOCK), bf16), pltpu.VMEM((CHUNK, 256), f32)],
        compiler_params=pltpu.CompilerParams(vmem_limit_bytes=40 * MIB),
        name="prep",
    )(lengths, tokens, gain.reshape(1, model), w_qkv, codes, tables, expand)


def mp_places():
    mp = lax.axis_index("mp")
    y, core = mp // 2, mp % 2
    return mp, y, core, y * 2 + (1 - core), (1 - y) * 2 + core


def remote(src, dst, send, recv, mp):
    return pltpu.make_async_remote_copy(
        src_ref=src,
        dst_ref=dst,
        send_sem=send,
        recv_sem=recv,
        device_id=(lax.axis_index("dp"), mp),
        device_id_type=pl.DeviceIdType.MESH,
    )


def meet():
    _, _, _, sibling, across = mp_places()
    barrier = pltpu.get_barrier_semaphore()
    for other in (sibling, across):
        pl.semaphore_signal(
            barrier, inc=1, device_id=(lax.axis_index("dp"), other), device_id_type=pl.DeviceIdType.MESH
        )
    pl.semaphore_wait(barrier, 2)


class Scatter:

    def __init__(self, part, near, out, far, send, recv):
        self.part, self.near, self.out, self.far, self.send, self.recv = part, near, out, far, send, recv

    def first(self, c):
        _, _, core, sibling, _ = mp_places()
        return remote(self.part.at[c, 1 - core], self.near.at[c], self.send.at[c, 0], self.recv.at[c, 0], sibling)

    def second(self, c):
        _, _, _, _, across = mp_places()
        return remote(self.out.at[c], self.far.at[c], self.send.at[c, 1], self.recv.at[c, 1], across)

    def start(self, c):
        self.first(c).start()

    def middle(self, c):
        _, y, core, _, _ = mp_places()
        self.first(c).wait_recv()
        self.out[c] = (self.part[c, core, 1 - y].astype(f32) + self.near[c, 1 - y].astype(f32)).astype(bf16)
        self.second(c).start()

    def finish(self, c):
        _, y, core, _, _ = mp_places()
        self.second(c).wait_recv()
        own = self.part[c, core, y].astype(f32) + self.near[c, y].astype(f32)
        return own + self.far[c].astype(f32)

    def drain(self, c):
        self.first(c).wait_send()
        self.second(c).wait_send()


class Gather:

    def __init__(self, full, send, recv):
        self.full, self.send, self.recv = full, send, recv

    def copy(self, c, kind):
        mp, _, _, sibling, across = mp_places()
        at = self.full.at[c, across if kind == 2 else mp]
        return remote(at, at, self.send.at[c, kind], self.recv.at[c, kind], across if kind == 1 else sibling)

    def start(self, c):
        self.copy(c, 1).start()
        self.copy(c, 0).start()

    def forward(self, c):
        self.copy(c, 1).wait_recv()
        self.copy(c, 2).start()

    def finish(self, c):
        self.copy(c, 0).wait_recv()
        self.copy(c, 2).wait_recv()

    def drain(self, c):
        for kind in range(3):
            self.copy(c, kind).wait_send()


def scatter_scratch(chunks, piece, model):
    return [
        pltpu.VMEM((chunks, 2, 2, piece, model), bf16),
        pltpu.VMEM((chunks, 2, piece, model), bf16),
        pltpu.VMEM((chunks, piece, model), bf16),
        pltpu.VMEM((chunks, piece, model), bf16),
        pltpu.SemaphoreType.DMA((chunks, 2)),
        pltpu.SemaphoreType.DMA((chunks, 2)),
    ]


def gather_scratch(chunks, piece, model):
    return [
        pltpu.VMEM((chunks, 4, piece, model), bf16),
        pltpu.SemaphoreType.DMA((chunks, 3)),
        pltpu.SemaphoreType.DMA((chunks, 3)),
    ]


ROOT = float(np.sqrt(2.0 / np.pi))
CUBE = 0.044715


def factor_of(rows):
    return lax.rsqrt(jnp.mean(rows * rows, axis=-1, keepdims=True) + EPSILON)


def main_kernel(
    fast,
    q_ref, kt_ref, v_ref, band_ref, w_output_ref, tokens_ref, gain_ref, w_inner_ref, w_outer_ref, cot_ref,
    qt_ref, att_ref, hidden_ref, ffn_ref, grad_hidden_ref, ghl_out_ref, grad_outer_ref, grad_inner_ref, gain_sum_ref,
    s_ref, res_ref, low_ref, grad_low_ref, sum_ffn_ref, sum_norm_ref,
    *comm,
):
    heads, _, rows = kt_ref.shape
    pieces = 4
    chunks = rows // CHUNK
    blocks = rows // BLOCK
    width = heads * 64
    mp, _, _, _, _ = mp_places()
    attn = Scatter(*comm[0:6])
    norm = Scatter(*comm[6:12])
    normed = Gather(*comm[12:15])
    grads = Gather(*comm[15:18])
    low = lax.broadcasted_iota(jnp.int32, (CHUNK, BLOCK), 1) < FAR
    lanes = lax.broadcasted_iota(jnp.int32, (CHUNK, BLOCK), 1)
    gain = gain_ref[...].astype(f32)
    meet()

    def place(m, c):
        return pl.ds(pl.multiple_of((m * chunks + c) * BLOCK, BLOCK), BLOCK)

    def own(c):
        return pl.ds(pl.multiple_of(c * BLOCK, BLOCK), BLOCK)

    def hidden_of(c):
        hidden = tokens_ref[own(c), :].astype(f32) + attn.finish(c)
        hidden_ref[own(c), :] = hidden
        normed.full[c, mp] = (hidden * factor_of(hidden) * gain).astype(bf16)
        normed.start(c)

    def grad_of(c):
        grad_normed = norm.finish(c)
        hidden = hidden_ref[own(c), :]
        factor = factor_of(hidden)
        hat = hidden * factor
        scaled = grad_normed * gain
        back = factor * (scaled - hat * jnp.mean(scaled * hat, axis=-1, keepdims=True))
        grad = cot_ref[place(mp, c), :].astype(f32) + back
        grad_hidden_ref[own(c), :] = grad
        gain_sum_ref[0:1, :] += jnp.sum(grad_normed * hat, axis=0, keepdims=True)
        grads.full[c, mp] = grad.astype(bf16)
        grads.start(c)

    gain_sum_ref[...] = jnp.zeros_like(gain_sum_ref)

    def attend(t, carry):
        c = t // heads
        h = t % heads
        query = jnp.concatenate([q_ref[h, place(m, c), :] for m in range(pieces)], axis=0)
        s_ref[...] = dot(query, kt_ref[h])
        for m in range(pieces):
            block = m * chunks + c
            start = jnp.clip(block - 1, 0, blocks - 3)
            at = pl.ds(pl.multiple_of(start * BLOCK, BLOCK), BAND)
            of = pl.ds(pl.multiple_of((start - block + 2) * BLOCK, BLOCK), BAND)
            s_ref[m * BLOCK : (m + 1) * BLOCK, at] += band_ref[h, :, of]
        s = s_ref[...]
        top = jnp.max(s, axis=1, keepdims=True)
        weights = jnp.exp(s - top).astype(bf16)
        mixed = dot(weights, v_ref[h])
        sums = pltpu.roll(mixed, 64, 1)
        res_ref[h] = jnp.where(low, mixed / sums, 0.0)
        total = -(top + jnp.log(mixed[:, 64:65]))
        high, middle, rest = split3(total)
        second = query[:, BLOCK:].astype(f32)
        second = jnp.where(
            lanes == LSE, high, jnp.where(lanes == LSE + 1, middle, jnp.where(lanes == LSE + 2, rest, second))
        )
        qt_ref[h, c, :BLOCK, :] = query[:, :BLOCK].astype(f32).T.astype(bf16)
        qt_ref[h, c, BLOCK:, :] = second.T.astype(bf16)

        @pl.when((h == 0) & (c >= 1))
        def _():
            attn.middle(c - 1)

        @pl.when((h == 0) & (c >= 2))
        def _():
            hidden_of(c - 2)

        @pl.when(h == heads - 1)
        def _():
            pairs = []
            for g in range(0, heads, 2):
                pair = res_ref[g]
                if g + 1 < heads:
                    pair = jnp.where(low, pair, pltpu.roll(res_ref[g + 1], 64, 1))
                pairs.append(pair.astype(bf16))
            att = jnp.concatenate(pairs, axis=1)[:, :width]
            att_ref[c] = att
            partial = dot(att, w_output_ref[...]).astype(bf16)
            for m in range(pieces):
                attn.part[c, m % 2, m // 2] = partial[m * BLOCK : (m + 1) * BLOCK]
            attn.start(c)

        return carry

    lax.fori_loop(0, chunks * heads, attend, 0)
    normed.forward(0)
    hidden_of(1)

    steps = w_inner_ref.shape[1] // 256

    def feed(t, carry):
        c = t // steps
        b = t % steps

        @pl.when(b == 0)
        def _():
            normed.finish(c)

        at = pl.ds(pl.multiple_of(b * 256, 256), 256)
        x = jnp.concatenate([normed.full[c, m] for m in range(pieces)], axis=0)
        cot = jnp.concatenate([cot_ref[place(m, c), :] for m in range(pieces)], axis=0)
        inner = dot(x, w_inner_ref[:, at])
        grad_act = dot_nt(cot, w_outer_ref[at, :])
        square = inner * inner
        tanh = jnp.tanh(ROOT * inner * (1.0 + CUBE * square))
        half = 0.5 * (1.0 + tanh)
        slope = half + 0.5 * inner * (1.0 - tanh * tanh) * (ROOT + 3.0 * CUBE * ROOT * square)
        activated = (inner * half).astype(bf16)
        grad_low = (slope * grad_act).astype(bf16)
        low_ref[c, :, at] = activated
        grad_low_ref[c, :, at] = grad_low
        part_ffn = dot(activated, w_outer_ref[at, :])
        part_norm = dot_nt(grad_low, w_inner_ref[:, at])

        @pl.when(b == 0)
        def _():
            sum_ffn_ref[...] = part_ffn
            sum_norm_ref[...] = part_norm

        @pl.when(b > 0)
        def _():
            sum_ffn_ref[...] += part_ffn
            sum_norm_ref[...] += part_norm

        @pl.when((b == 0) & (c == 0))
        def _():
            attn.middle(2)

        @pl.when((b == 0) & (c >= 1))
        def _():
            norm.middle(c - 1)

        @pl.when((b == 1) & (c < 2))
        def _():
            normed.forward(c + 1)

        @pl.when((b == steps - 1) & (c == 0))
        def _():
            hidden_of(2)

        @pl.when((b == steps - 1) & (c >= 1))
        def _():
            grad_of(c - 1)

        @pl.when((b == 1) & (c == 2))
        def _():
            grads.forward(0)

        @pl.when(b == steps - 1)
        def _():
            for m in range(pieces):
                ffn_ref[c, m % 2, m // 2] = sum_ffn_ref[m * BLOCK : (m + 1) * BLOCK, :].astype(bf16)
                norm.part[c, m % 2, m // 2] = sum_norm_ref[m * BLOCK : (m + 1) * BLOCK, :].astype(bf16)
            norm.start(c)

        return carry

    lax.fori_loop(0, chunks * steps, feed, 0)

    model = cot_ref.shape[1]

    def weights_of(b):
        at = slice(b * (model // 2), (b + 1) * (model // 2))
        outer = jnp.zeros((model // 2, low_ref.shape[2]), f32)
        inner = jnp.zeros((model // 2, low_ref.shape[2]), f32)
        for c in range(chunks):
            x = jnp.concatenate([normed.full[c, m, :, at] for m in range(pieces)], axis=0)
            cot = jnp.concatenate([cot_ref[place(m, c), at] for m in range(pieces)], axis=0)
            outer = outer + dot_tn(cot, low_ref[c])
            inner = inner + dot_tn(x, grad_low_ref[c])
        for ref, value in ((grad_outer_ref, outer), (grad_inner_ref, inner)):
            if fast:
                each = model // 8
                for r in range(4):
                    j = b * 4 + r
                    ref[j % 2, j // 2] = value[r * each : (r + 1) * each].astype(bf16)
            else:
                ref[at, :] = value

    weights_of(0)
    norm.middle(2)
    grads.forward(1)
    weights_of(1)
    grad_of(2)
    grads.forward(2)
    for c in range(chunks):
        grads.finish(c)
    ghl_out_ref[...] = grads.full[...]
    for c in range(chunks):
        attn.drain(c)
        norm.drain(c)
        normed.drain(c)
        grads.drain(c)


def dot_tn(a, b):
    return lax.dot_general(a, b, (((0,), (0,)), ((), ())), preferred_element_type=f32)


def main_call(fast, q, kt, v, band, w_output, tokens_share, gain, w_inner, w_outer, cotangent):
    heads, rows, _ = q.shape
    width, model = w_output.shape
    share = tokens_share.shape[0]
    chunks = rows // CHUNK
    full = pl.BlockSpec(memory_space=pltpu.VMEM)
    comm = (
        scatter_scratch(chunks, BLOCK, model) * 2 + gather_scratch(chunks, BLOCK, model) * 2
    )
    weights = jax.ShapeDtypeStruct((model, w_inner.shape[1]), f32)
    if fast:
        weights = jax.ShapeDtypeStruct((2, 4, model // 8, w_inner.shape[1]), bf16)
    return pl.pallas_call(
        functools.partial(main_kernel, fast),
        in_specs=[full] * 10,
        out_specs=[full] * 9,
        out_shape=[
            jax.ShapeDtypeStruct((heads, chunks, 256, CHUNK), bf16),
            jax.ShapeDtypeStruct((chunks, CHUNK, width), bf16),
            jax.ShapeDtypeStruct((share, model), f32),
            jax.ShapeDtypeStruct((chunks, 2, 2, BLOCK, model), bf16),
            jax.ShapeDtypeStruct((share, model), f32),
            jax.ShapeDtypeStruct((chunks, 4, BLOCK, model), bf16),
            weights,
            weights,
            jax.ShapeDtypeStruct((8, model), f32),
        ],
        scratch_shapes=[
            pltpu.VMEM((CHUNK, rows), f32),
            pltpu.VMEM((heads, CHUNK, BLOCK), f32),
            pltpu.VMEM((chunks, CHUNK, w_inner.shape[1]), bf16),
            pltpu.VMEM((chunks, CHUNK, w_inner.shape[1]), bf16),
            pltpu.VMEM((CHUNK, model), f32),
            pltpu.VMEM((CHUNK, model), f32),
            *comm,
        ],
        compiler_params=pltpu.CompilerParams(
            vmem_limit_bytes=63 * MIB, collective_id=1, has_side_effects=True
        ),
        name="forward_and_feed",
    )(q, kt, v, band, w_output, tokens_share, gain.reshape(1, model), w_inner, w_outer, cotangent)


def dp_places():
    dp = lax.axis_index("dp")
    return dp // 2, dp % 2


def remote_dp(src, dst, send, recv, dp):
    return pltpu.make_async_remote_copy(
        src_ref=src,
        dst_ref=dst,
        send_sem=send,
        recv_sem=recv,
        device_id=(dp, lax.axis_index("mp")),
        device_id_type=pl.DeviceIdType.MESH,
    )


def meet_all(fast):
    mp, _, _, sibling, across = mp_places()
    dp = lax.axis_index("dp")
    z, x = dp_places()
    others = [(dp, sibling), (dp, across)]
    if fast:
        others.append((z * 2 + 1 - x, mp))
        others.extend(((z + d) % 4 * 2 + x, mp) for d in (1, 2, 3))
    barrier = pltpu.get_barrier_semaphore()
    for other in others:
        pl.semaphore_signal(barrier, inc=1, device_id=other, device_id_type=pl.DeviceIdType.MESH)
    pl.semaphore_wait(barrier, len(others))


class Spread:

    def __init__(self, part, near, out, far, send, recv):
        self.part, self.near, self.out, self.far, self.send, self.recv = part, near, out, far, send, recv

    def first(self):
        z, x = dp_places()
        return remote_dp(self.part.at[1 - x], self.near, self.send.at[0], self.recv.at[0], z * 2 + 1 - x)

    def second(self, d):
        z, x = dp_places()
        to = (z + d) % 4
        return remote_dp(self.out.at[to], self.far.at[d - 1], self.send.at[d], self.recv.at[d], to * 2 + x)

    def start(self):
        self.first().start()

    def middle(self):
        z, x = dp_places()
        self.first().wait_recv()
        for d in range(1, 4):
            to = (z + d) % 4
            self.out[to] = (self.part[x, to].astype(f32) + self.near[to].astype(f32)).astype(bf16)
            self.second(d).start()

    def finish(self):
        z, x = dp_places()
        total = self.part[x, z].astype(f32) + self.near[z].astype(f32)
        for d in range(1, 4):
            self.second(d).wait_recv()
            total = total + self.far[d - 1].astype(f32)
        return total

    def drain(self):
        self.first().wait_send()
        for d in range(1, 4):
            self.second(d).wait_send()


def spread_scratch(rows, columns, lead=(), part=True):
    buffers = [pltpu.VMEM((*lead, 2, 4, rows, columns), bf16)] if part else []
    return buffers + [
        pltpu.VMEM((*lead, 4, rows, columns), bf16),
        pltpu.VMEM((*lead, 4, rows, columns), bf16),
        pltpu.VMEM((*lead, 3, rows, columns), bf16),
        pltpu.SemaphoreType.DMA((*lead, 4)),
        pltpu.SemaphoreType.DMA((*lead, 4)),
    ]


class Total:

    def __init__(self, value, near, far, across, send, recv):
        self.value, self.near, self.far, self.across, self.send, self.recv = value, near, far, across, send, recv

    def copy(self, kind):
        z, x = dp_places()
        mp, _, _, sibling, across = mp_places()
        send, recv = self.send.at[kind], self.recv.at[kind]
        if kind == 0:
            return remote_dp(self.value.at[0], self.near, send, recv, z * 2 + 1 - x)
        if kind < 4:
            return remote_dp(self.value.at[1], self.far.at[kind - 1], send, recv, (z + kind) % 4 * 2 + x)
        if kind == 4:
            return remote(self.value.at[2], self.across.at[0], send, recv, sibling)
        return remote(self.value.at[3], self.across.at[1], send, recv, across)

    def start(self):
        self.copy(0).start()

    def over_z(self):
        self.copy(0).wait_recv()
        self.value[1] = self.value[0] + self.near[...]
        for kind in range(1, 4):
            self.copy(kind).start()

    def over_core(self):
        total = self.value[1]
        for kind in range(1, 4):
            self.copy(kind).wait_recv()
            total = total + self.far[kind - 1]
        self.value[2] = total
        self.copy(4).start()

    def over_y(self):
        self.copy(4).wait_recv()
        self.value[3] = self.value[2] + self.across[0]
        self.copy(5).start()

    def finish(self):
        self.copy(5).wait_recv()
        return self.value[3] + self.across[1]

    def drain(self):
        for kind in range(6):
            self.copy(kind).wait_send()


def total_scratch(rows, columns):
    return [
        pltpu.VMEM((4, rows, columns), f32),
        pltpu.VMEM((rows, columns), f32),
        pltpu.VMEM((3, rows, columns), f32),
        pltpu.VMEM((2, rows, columns), f32),
        pltpu.SemaphoreType.DMA((6,)),
        pltpu.SemaphoreType.DMA((6,)),
    ]


def back_kernel(
    fast,
    ghl_ref, w_ref, att_ref, q_ref, qt_ref, k_ref, kt_ref, v_ref, band_t_ref,
    ffn_ref, hidden_ref, grad_hidden_ref, tokens_ref, normed_ref, w_qkv_ref, gain_ref, gain_sum_ref,
    outer_ref, inner_ref, collapse_ref,
    *rest,
):
    outs, scratch = rest[: 9 if fast else 6], rest[9 if fast else 6 :]
    if fast:
        mixed_ref, input_ref, o_qkv_ref, o_output_ref, o_inner_ref, o_outer_ref, o_gain_a_ref, o_gain_f_ref, o_tables_ref = outs
    else:
        mixed_ref, input_ref, o_qkv_ref, o_output_ref, o_sums_ref, o_gains_ref = outs
    da_ref, dat_ref, s_ref, pt_ref, gt_ref, dqt_ref, dk_ref, dv_ref, bands_ref, pad_ref, grads_ref, wt_ref, sums_ref = scratch[:13]
    comm = scratch[13:]
    heads, rows, _ = k_ref.shape
    blocks = rows // BLOCK
    chunks = rows // CHUNK
    pieces = CHUNK // BLOCK
    model = w_ref.shape[1]
    width = heads * 64
    feed = Scatter(ffn_ref, *comm[0:5])
    norm = Scatter(*comm[5:11])
    comm = comm[11:]
    if fast:
        outer = Spread(outer_ref, *comm[0:5])
        inner = Spread(inner_ref, *comm[5:10])
        output = Spread(*comm[10:16])
        qkv_refs = comm[16:22]
        small = Total(*comm[22:28])

        def qkv(h):
            return Spread(*[ref.at[h] for ref in qkv_refs])

    lanes = lax.broadcasted_iota(jnp.int32, (CHUNK, BLOCK), 1)
    low = lanes < FAR
    meet_all(fast)
    for c in range(chunks):
        feed.start(c)
    if fast:
        outer.start()
        inner.start()
    pad_ref[...] = jnp.zeros_like(pad_ref)
    sums_ref[...] = jnp.zeros_like(sums_ref)

    def own(c):
        return pl.ds(pl.multiple_of(c * BLOCK, BLOCK), BLOCK)

    def put(ref, first_row, value):
        each = model // 8
        for r in range(value.shape[0] // each):
            j = first_row // each + r
            ref[j % 2, j // 2] = value[r * each : (r + 1) * each].astype(bf16)

    def prologue(c, carry):
        at = pl.ds(pl.multiple_of(c * CHUNK, CHUNK), CHUNK)
        pad_ref[:, :width] = dot_nt(ghl_ref[at, :], w_ref[...]).astype(bf16).astype(f32)
        pad_ref[:, 256 : 256 + width] = att_ref[at, :].astype(f32)
        for h in range(heads):
            base = h // 2 * BLOCK
            grad = pad_ref[:, base : base + BLOCK]
            out = pad_ref[:, 256 + base : 256 + base + BLOCK]
            if h % 2 == 1:
                grad = pltpu.roll(grad, 64, 1)
                out = pltpu.roll(out, 64, 1)
            total = -jnp.sum(jnp.where(low, grad * out, 0.0), axis=1, keepdims=True)
            high, middle, last = split3(total)
            grad = jnp.where(
                low,
                grad,
                jnp.where(
                    lanes == FAR, high, jnp.where(lanes == FAR + 1, middle, jnp.where(lanes == FAR + 2, last, 0.0))
                ),
            )
            da_ref[h, at, :] = grad.astype(bf16)
            dat_ref[h, :, at] = grad.T.astype(bf16)
        return carry

    lax.fori_loop(0, chunks, prologue, 0)
    pad_ref[:, 256:] = jnp.zeros_like(pad_ref[:, 256:])
    for b in range(2):
        cols = slice(b * (model // 2), (b + 1) * (model // 2))
        grad_output = dot_tn(ghl_ref[:, cols], att_ref[...])
        if fast:
            padded = jnp.concatenate([grad_output, jnp.zeros((model // 2, 256 - width), f32)], axis=1)
            put(output.part, b * (model // 2), padded)
        else:
            o_output_ref[cols, :] = grad_output
    if fast:
        output.start()
    for k in range(3):
        turned = w_qkv_ref[k].astype(f32).T.astype(bf16)
        for h in range(heads):
            wt_ref[h, k * 64 : (k + 1) * 64, :] = turned[h * 64 : (h + 1) * 64]
    wt_ref[:, 192:, :] = jnp.zeros_like(wt_ref[:, 192:, :])

    lines16 = lax.broadcasted_iota(jnp.int32, (16, rows), 0)
    block16 = lax.broadcasted_iota(jnp.int32, (16, rows), 1) // BLOCK
    start16 = jnp.clip(block16 - 1, 0, blocks - 3)
    real = lines16 < blocks
    plane_rows = lax.broadcasted_iota(jnp.int32, (BLOCK, BLOCK), 0)
    plane_lanes = lax.broadcasted_iota(jnp.int32, (BLOCK, BLOCK), 1)
    tall_low = lax.broadcasted_iota(jnp.int32, (rows, BLOCK), 1) < 64

    def fold(value):
        total = value[:, :BLOCK]
        for b in range(1, value.shape[1] // BLOCK):
            total = total + value[:, b * BLOCK : (b + 1) * BLOCK]
        return jnp.sum(total, axis=0, keepdims=True)

    def head(h, carry):
        dk_ref[...] = jnp.zeros_like(dk_ref)
        dv_ref[...] = jnp.zeros_like(dv_ref)
        bands_ref[...] = jnp.zeros_like(bands_ref)

        def chunk(c, carry):
            at = pl.ds(pl.multiple_of(c * CHUNK, CHUNK), CHUNK)
            places = [pl.ds(pl.multiple_of((p * chunks + c) * BLOCK, BLOCK), BLOCK) for p in range(pieces)]
            bands = []
            for p in range(pieces):
                block = p * chunks + c
                start = jnp.clip(block - 1, 0, blocks - 3)
                keys = pl.ds(pl.multiple_of(start * BLOCK, BLOCK), BAND)
                of = pl.ds(pl.multiple_of((start - block + 2) * BLOCK, BLOCK), BAND)
                bands.append((keys, of))
            s_ref[...] = dot(k_ref[h], qt_ref[h, c])
            for p, (keys, of) in enumerate(bands):
                s_ref[keys, p * BLOCK : (p + 1) * BLOCK] += band_t_ref[h, of, :]
            probs = jnp.exp(s_ref[...])
            pt_ref[...] = probs.astype(bf16)
            gt_ref[...] = (probs * dot(v_ref[h], dat_ref[h, :, at])).astype(bf16)
            dv_ref[...] += dot(pt_ref[...], da_ref[h, at, :])
            dk_ref[...] += dot(gt_ref[...], jnp.concatenate([q_ref[h, place, BLOCK:] for place in places], axis=0))
            dq = dot(kt_ref[h], gt_ref[...])
            for p in range(pieces):
                dqt_ref[:, places[p]] = dq[:, p * BLOCK : (p + 1) * BLOCK]
            for p, (keys, of) in enumerate(bands):
                bands_ref[of, :] += gt_ref[keys, p * BLOCK : (p + 1) * BLOCK].astype(f32)

            for k in range(chunks):

                @pl.when((h == 0) & (c == k))
                def _(k=k):
                    feed.middle(k)

                @pl.when((h == 1) & (c == k))
                def _(k=k):
                    rows_of = slice(k * BLOCK, (k + 1) * BLOCK)
                    mixed_ref[rows_of, :] = (hidden_ref[rows_of, :] + feed.finish(k)).astype(bf16)

            if fast:

                @pl.when((h == 1) & (c == 0))
                def _():
                    outer.middle()

                @pl.when((h == 2) & (c == 0))
                def _():
                    inner.middle()

                @pl.when((h == 2) & (c == 1))
                def _():
                    output.middle()
                    qkv(0).middle()

            return carry

        lax.fori_loop(0, chunks, chunk, 0)

        dq = dqt_ref[BLOCK:, :].T * 0.125
        grads_ref[h, :, :BLOCK] = jnp.where(tall_low, dq, pltpu.roll(dk_ref[...], 64, 1)).astype(bf16)
        grads_ref[h, :, BLOCK:] = jnp.where(tall_low, dv_ref[...], 0.0).astype(bf16)
        for b in range(2):
            cols = slice(b * (model // 2), (b + 1) * (model // 2))
            grad_qkv = dot_tn(normed_ref[:, cols], grads_ref[h])
            if fast:
                put(qkv_refs[0].at[h], b * (model // 2), grad_qkv)
            else:
                o_qkv_ref[h, cols, :] = grad_qkv
        if fast:
            qkv(h).start()

        band = roll_rows(bands_ref[...].T, False)
        spread = dqt_ref[:BLOCK, :]
        high = spread.astype(bf16)
        last = (spread - high.astype(f32)).astype(bf16)
        hot = k_ref[h, :, :BLOCK]
        plane = (dot(high, hot) + dot(last, hot)).T
        plane = jnp.where((plane_rows < CODES) == (plane_lanes < CODES), plane, 0.0)
        plane = roll_rows(plane, False)
        far = dqt_ref[BLOCK + FAR : BLOCK + FAR + 16, :]
        line = jnp.concatenate(
            [
                jnp.sum(band, axis=0, keepdims=True),
                jnp.sum(plane[:CODES], axis=0, keepdims=True),
                jnp.sum(plane[CODES:], axis=0, keepdims=True),
                fold(jnp.where(real & (lines16 < start16), far, 0.0)),
                fold(jnp.where(real & (lines16 > start16 + 2), far, 0.0)),
            ],
            axis=1,
        )
        sums_ref[...] += jnp.where(lax.broadcasted_iota(jnp.int32, sums_ref.shape, 0) == h, line, 0.0)
        return carry

    lax.fori_loop(0, heads, head, 0)

    sums_ref[4:5, :model] = gain_sum_ref[0:1, :]
    gain = gain_ref[...].astype(f32)
    gain_total = jnp.zeros((1, model), f32)
    for c in range(chunks):
        for m in range(pieces):
            at = pl.ds((m * chunks + c) * BLOCK, BLOCK)
            partial = dot(grads_ref[0, at, :], wt_ref[0])
            for h in range(1, heads):
                partial = partial + dot(grads_ref[h, at, :], wt_ref[h])
            gain_total = gain_total + jnp.sum(partial * normed_ref[at, :].astype(f32), axis=0, keepdims=True)
            norm.part[c, m % 2, m // 2] = partial.astype(bf16)
        norm.start(c)
    sums_ref[3:4, :model] = gain_total / gain
    if fast:
        small.value[0] = sums_ref[...]
        small.start()
        outer_sum = outer.finish()
        o_outer_ref[...] = outer_sum.T
    for c in range(chunks):
        norm.middle(c)
    if fast:
        qkv(1).middle()
        small.over_z()
        o_inner_ref[...] = inner.finish()
        qkv(2).middle()
        o_output_ref[...] = output.finish()[:, :width].T
        small.over_core()
    for c in range(chunks):
        x = tokens_ref[own(c), :].astype(f32)
        grad_normed = norm.finish(c)
        factor = factor_of(x)
        hat = x * factor
        scaled = grad_normed * gain
        back = factor * (scaled - hat * jnp.mean(scaled * hat, axis=-1, keepdims=True))
        input_ref[own(c), :] = grad_hidden_ref[own(c), :] + back
        if fast and c == 0:
            small.over_y()
    if fast:
        each = model // 8
        low_each = lax.broadcasted_iota(jnp.int32, (each, BLOCK), 1) < 64
        parts = [qkv(h).finish() for h in range(heads)]
        for k in range(3):
            for h in range(0, heads, 2):
                at = slice(0, BLOCK) if k < 2 else slice(BLOCK, 2 * BLOCK)
                one = parts[h][:, at]
                one = pltpu.roll(one, 64, 1) if k == 1 else one
                if h + 1 < heads:
                    two = parts[h + 1][:, at]
                    two = two if k == 1 else pltpu.roll(two, 64, 1)
                    o_qkv_ref[k, :, h * 64 : (h + 2) * 64] = jnp.where(low_each, one, two)
                else:
                    o_qkv_ref[k, :, h * 64 :] = one[:, :64]
        totals = small.finish()
        o_gain_a_ref[...] = totals[3:4, :model]
        o_gain_f_ref[...] = totals[4:5, :model]
        high, middle, last = split3(small.value[2])
        tables = sum(dot_nt(collapse_ref[...], part.astype(bf16)) for part in (high, middle, last))
        o_tables_ref[...] = tables[:, :heads]
        outer.drain()
        inner.drain()
        output.drain()
        for h in range(heads):
            qkv(h).drain()
        small.drain()
    else:
        o_sums_ref[...] = sums_ref[...]
        o_gains_ref[...] = sums_ref[...]
    for c in range(chunks):
        feed.drain(c)
        norm.drain(c)


def back_call(fast, *args):
    ghl, w_output, att, q = args[:4]
    heads, rows, _ = q.shape
    width, model = w_output.shape
    share = args[10].shape[0]
    chunks = rows // CHUNK
    each = model // 8
    full = pl.BlockSpec(memory_space=pltpu.VMEM)
    sums = (8, WIDE + 4 * BLOCK)
    outs = [((share, model), bf16), ((share, model), f32)]
    if fast:
        hidden_units = args[17].shape[-1]
        outs += [
            ((3, each, width), f32), ((width, each), f32), ((each, hidden_units), f32), ((hidden_units, each), f32),
            ((1, model), f32), ((1, model), f32), ((3 * BUCKETS, heads), f32),
        ]
    else:
        outs += [((heads, model, 256), f32), ((model, width), f32), (sums, f32), (sums, f32)]
    scratch = [
        pltpu.VMEM((heads, rows, BLOCK), bf16),
        pltpu.VMEM((heads, BLOCK, rows), bf16),
        pltpu.VMEM((rows, CHUNK), f32),
        pltpu.VMEM((rows, CHUNK), bf16),
        pltpu.VMEM((rows, CHUNK), bf16),
        pltpu.VMEM((256, rows), f32),
        pltpu.VMEM((rows, BLOCK), f32),
        pltpu.VMEM((rows, BLOCK), f32),
        pltpu.VMEM((WIDE, BLOCK), f32),
        pltpu.VMEM((CHUNK, 512), f32),
        pltpu.VMEM((heads, rows, 256), bf16),
        pltpu.VMEM((heads, 256, model), bf16),
        pltpu.VMEM(sums, f32),
        *scatter_scratch(chunks, BLOCK, model)[1:],
        *scatter_scratch(chunks, BLOCK, model),
    ]
    if fast:
        scratch += [
            *spread_scratch(each, hidden_units, part=False),
            *spread_scratch(each, hidden_units, part=False),
            *spread_scratch(each, 256),
            *spread_scratch(each, 256, lead=(heads,)),
            *total_scratch(*sums),
        ]
    return pl.pallas_call(
        functools.partial(back_kernel, fast),
        in_specs=[full] * len(args),
        out_specs=[full] * len(outs),
        out_shape=[jax.ShapeDtypeStruct(*out) for out in outs],
        scratch_shapes=scratch,
        compiler_params=pltpu.CompilerParams(vmem_limit_bytes=63 * MIB, collective_id=2, has_side_effects=True),
        name="backward",
    )(*args)


def local(
    fast,
    tokens, lengths, horizontal, vertical, gain_attn, w_qkv, bias_tables, w_output, gain_ffn, w_inner, w_outer, cotangent,
):
    rows, model = tokens.shape
    heads = bias_tables.shape[1]
    width = w_qkv.shape[2]
    share = rows // lax.axis_size("mp")
    mp = lax.axis_index("mp")
    codes = jnp.stack([horizontal, vertical])
    normed_a, q, k, kt, v, band, band_t = prep(tokens, lengths, codes, gain_attn, w_qkv, bias_tables)
    token_share = lax.dynamic_slice_in_dim(tokens, mp * share, share, 0)
    qt, att, hidden, ffn, grad_hidden, ghl, grad_outer, grad_inner, gain_sums = main_call(
        fast, q, kt, v, band, w_output, token_share, gain_ffn, w_inner, w_outer, cotangent
    )
    outs = back_call(
        fast, ghl.reshape(rows, model), w_output, att.reshape(rows, width), q, qt, k, kt, v, band_t, ffn, hidden,
        grad_hidden, token_share, normed_a, w_qkv, gain_attn.reshape(1, model), gain_sums, grad_outer, grad_inner,
        jnp.asarray(collapse().T, bf16),
    )
    if fast:
        mixed, input_grad, qkv, output, inner, outer, gain_a, gain_f, tables = outs
        return mixed, input_grad, qkv, output, inner, outer, gain_a[0], gain_f[0], tables
    mixed, input_grad, qkv, output, sums, _ = outs
    qkv = qkv[:, :, : 3 * 64].reshape(heads, model, 3, 64).transpose(2, 1, 0, 3).reshape(3, model, width)
    gains = lax.psum(sums[3:5, :model], ("dp", "mp"))
    totals = lax.psum(sums[:heads], "dp")
    tables = lax.dot_general(
        jnp.asarray(collapse(), f32), totals, (((0,), (1,)), ((), ())), precision=lax.Precision.HIGHEST
    )

    def spread(x, axis):
        return lax.psum_scatter(x, "dp", scatter_dimension=axis, tiled=True)

    return (
        mixed, input_grad, spread(qkv, 1), spread(output.T, 1), spread(grad_inner, 0), spread(grad_outer.T, 1),
        gains[0], gains[1], tables,
    )


def solution(mesh):
    fast = mesh.shape["dp"] == 8
    return jax.shard_map(
        functools.partial(local, fast),
        mesh=mesh,
        in_specs=(
            P("dp", None), P("dp"), P("dp"), P("dp"), P(), P(None, None, "mp"), P(None, "mp"), P("mp", None), P(),
            P(None, "mp"), P("mp", None), P("dp", None),
        ),
        out_specs=(
            P(("dp", "mp"), None), P(("dp", "mp"), None), P(None, "dp", "mp"), P("mp", "dp"), P("dp", "mp"),
            P("mp", "dp"), P(), P(), P(None, "mp"),
        ),
        check_vma=False,
    )
```

```python
import functools
import jax
import jax.numpy as jnp
import numpy as np
from jax import lax
from jax.experimental import pallas as pl
from jax.experimental.pallas import tpu as pltpu
from jax.sharding import PartitionSpec as P

BUCKETS = 32
CODES = 64
HALF = BUCKETS // 2
EPSILON = 1e-06
DEAD = -1e9
CHUNK = 512
BLOCK = 128
BAND = 3 * BLOCK
WIDE = 6 * BLOCK
FAR = 64
MASK = 76
LSE = 80
MIB = 2**20

f32 = jnp.float32
bf16 = jnp.bfloat16


def expansion():
    offsets = np.arange(WIDE) - 2 * BLOCK
    line = np.clip(offsets, -HALF, HALF - 1) + HALF
    line[5 * BLOCK :] = 0
    wrapped = np.arange(BLOCK)
    wrapped = np.where(wrapped < CODES, wrapped, wrapped - BLOCK)
    plane = np.clip(wrapped, -HALF, HALF - 1) + HALF
    buckets = np.concatenate([line, BUCKETS + plane, 2 * BUCKETS + plane])
    return (np.arange(3 * BUCKETS)[:, None] == buckets[None, :]).astype(np.float32)


def collapse():
    buckets = np.argmax(expansion(), axis=0)
    buckets[5 * BLOCK + 1 : WIDE] = 0
    buckets = np.concatenate([buckets, np.zeros(BLOCK, int), np.full(BLOCK, BUCKETS - 1)])
    return (buckets[:, None] == np.arange(3 * BUCKETS)[None, :]).astype(np.float32)


def roll_rows(value, right):
    rows, width = value.shape
    index = lax.broadcasted_iota(jnp.int32, value.shape, 0)
    step = 1
    while step < rows:
        shift = step if right else width - step
        value = jnp.where((index // step) % 2 == 1, pltpu.roll(value, shift, 1), value)
        step *= 2
    return value


def dot(a, b):
    return jnp.dot(a, b, preferred_element_type=f32)


def dot_nt(a, b):
    return lax.dot_general(a, b, (((1,), (1,)), ((), ())), preferred_element_type=f32)


def split3(value):
    high = value.astype(bf16).astype(f32)
    rest = value - high
    middle = rest.astype(bf16).astype(f32)
    return high, middle, rest - middle


def dot_tn(a, b):
    return lax.dot_general(a, b, (((0,), (0,)), ((), ())), preferred_element_type=f32)


ROOT = float(np.sqrt(2.0 / np.pi))
CUBE = 0.044715


def factor_of(rows):
    return lax.rsqrt(jnp.mean(rows * rows, axis=-1, keepdims=True) + EPSILON)


def mp_places():
    mp = lax.axis_index("mp")
    y, core = mp // 2, mp % 2
    return mp, y, core, y * 2 + (1 - core), (1 - y) * 2 + core


def dp_places():
    dp = lax.axis_index("dp")
    return dp // 2, dp % 2


def remote(src, dst, send, recv, mp=None, dp=None):
    return pltpu.make_async_remote_copy(
        src_ref=src,
        dst_ref=dst,
        send_sem=send,
        recv_sem=recv,
        device_id=(lax.axis_index("dp") if dp is None else dp, lax.axis_index("mp") if mp is None else mp),
        device_id_type=pl.DeviceIdType.MESH,
    )


def meet(fast):
    mp, dp = lax.axis_index("mp"), lax.axis_index("dp")
    z, x = dp_places()
    others = [(dp, (mp + d) % 4) for d in (1, 2, 3)]
    if fast:
        others.append((z * 2 + 1 - x, mp))
        others.extend(((z + d) % 4 * 2 + x, mp) for d in (1, 2, 3))
    barrier = pltpu.get_barrier_semaphore()
    for other in others:
        pl.semaphore_signal(barrier, inc=1, device_id=other, device_id_type=pl.DeviceIdType.MESH)
    pl.semaphore_wait(barrier, len(others))


def run(index, count=1, size=BLOCK):
    return pl.ds(pl.multiple_of(index * size, size), count * size)


class Scatter:

    def __init__(self, part, near, far, send, recv):
        self.part, self.near, self.far, self.send, self.recv = part, near, far, send, recv

    def block(self, c, core, y):
        return (c * 2 + core) * 2 + y

    def put(self, c, m, value):
        self.part[run(self.block(c, m % 2, m // 2)), :] = value.astype(bf16)

    def first(self, c):
        _, _, core, sibling, _ = mp_places()
        src = self.part.at[run(self.block(c, 1 - core, 0), 2)]
        return remote(src, self.near.at[run(c * 2, 2)], self.send.at[c, 0], self.recv.at[c, 0], sibling)

    def second(self, c):
        _, y, core, _, across = mp_places()
        src = self.part.at[run(self.block(c, core, 1 - y))]
        return remote(src, self.far.at[run(c)], self.send.at[c, 1], self.recv.at[c, 1], across)

    def start(self, c):
        self.first(c).start()

    def middle(self, c):
        _, y, core, _, _ = mp_places()
        self.first(c).wait_recv()
        at = run(self.block(c, core, 1 - y))
        self.part[at, :] = (self.part[at, :].astype(f32) + self.near[run(c * 2 + 1 - y), :].astype(f32)).astype(bf16)
        self.second(c).start()

    def finish(self, c):
        _, y, core, _, _ = mp_places()
        self.second(c).wait_recv()
        own = self.part[run(self.block(c, core, y)), :].astype(f32) + self.near[run(c * 2 + y), :].astype(f32)
        return own + self.far[run(c), :].astype(f32)

    def drain(self, c):
        self.first(c).wait_send()
        self.second(c).wait_send()


class Gather:

    def __init__(self, full, send, recv, size=BLOCK):
        self.full, self.send, self.recv, self.size = full, send, recv, size

    def at(self, c, m):
        return run(c * 4 + m, 1, self.size)

    def copy(self, c, kind):
        mp, _, _, sibling, across = mp_places()
        at = self.full.at[self.at(c, across if kind == 2 else mp)]
        return remote(at, at, self.send.at[c, kind], self.recv.at[c, kind], across if kind == 1 else sibling)

    def start(self, c):
        self.copy(c, 1).start()
        self.copy(c, 0).start()

    def forward(self, c):
        self.copy(c, 1).wait_recv()
        self.copy(c, 2).start()

    def finish(self, c):
        self.copy(c, 0).wait_recv()
        self.copy(c, 2).wait_recv()

    def drain(self, c):
        for kind in range(3):
            self.copy(c, kind).wait_send()


class Exchange:

    def __init__(self, given, at, taken, send, recv):
        self.given, self.at, self.taken, self.send, self.recv = given, at, taken, send, recv

    def copy(self, c, d):
        mp = lax.axis_index("mp")
        dst = self.taken.at[run(c * 4 + mp)]
        src = self.given.at[self.at(c, d)]
        return remote(src, dst, self.send.at[c, d - 1], self.recv.at[c, d - 1], (mp + d) % 4)

    def start(self, c):
        for d in (2, 1, 3):
            self.copy(c, d).start()

    def finish(self, c):
        for d in (1, 2, 3):
            self.copy(c, d).wait_recv()

    def drain(self, c):
        for d in (1, 2, 3):
            self.copy(c, d).wait_send()


class Spread:

    def __init__(self, part, near, far, send, recv):
        self.part, self.near, self.far, self.send, self.recv = part, near, far, send, recv
        self.each = part.shape[0] // 8

    def at(self, index, count=1):
        return run(index, count, self.each)

    def put(self, first_row, value):
        for r in range(value.shape[0] // self.each):
            j = first_row // self.each + r
            rows = value[r * self.each : (r + 1) * self.each]
            self.part[self.at(j % 2 * 4 + j // 2), :] = rows.astype(bf16)

    def first(self):
        z, x = dp_places()
        src = self.part.at[self.at((1 - x) * 4, 4)]
        return remote(src, self.near, self.send.at[0], self.recv.at[0], dp=z * 2 + 1 - x)

    def second(self, d):
        z, x = dp_places()
        to = (z + d) % 4
        src = self.part.at[self.at(x * 4 + to)]
        return remote(src, self.far.at[self.at(d - 1)], self.send.at[d], self.recv.at[d], dp=to * 2 + x)

    def start(self):
        self.first().start()

    def middle(self):
        z, x = dp_places()
        self.first().wait_recv()
        for d in range(1, 4):
            to = (z + d) % 4
            at = self.at(x * 4 + to)
            self.part[at, :] = (self.part[at, :].astype(f32) + self.near[self.at(to), :].astype(f32)).astype(bf16)
            self.second(d).start()

    def finish(self):
        z, x = dp_places()
        total = self.part[self.at(x * 4 + z), :].astype(f32) + self.near[self.at(z), :].astype(f32)
        for d in range(1, 4):
            self.second(d).wait_recv()
            total = total + self.far[self.at(d - 1), :].astype(f32)
        return total

    def drain(self):
        self.first().wait_send()
        for d in range(1, 4):
            self.second(d).wait_send()


class Total:

    def __init__(self, value, near, far, across, send, recv):
        self.value, self.near, self.far, self.across, self.send, self.recv = value, near, far, across, send, recv

    def copy(self, kind):
        z, x = dp_places()
        mp, _, _, sibling, across = mp_places()
        send, recv = self.send.at[kind], self.recv.at[kind]
        if kind == 0:
            return remote(self.value.at[0], self.near, send, recv, dp=z * 2 + 1 - x)
        if kind < 4:
            return remote(self.value.at[1], self.far.at[kind - 1], send, recv, dp=(z + kind) % 4 * 2 + x)
        if kind == 4:
            return remote(self.value.at[2], self.across.at[0], send, recv, sibling)
        return remote(self.value.at[3], self.across.at[1], send, recv, across)

    def start(self):
        self.copy(0).start()

    def over_z(self):
        self.copy(0).wait_recv()
        self.value[1] = self.value[0] + self.near[...]
        for kind in range(1, 4):
            self.copy(kind).start()

    def over_core(self):
        total = self.value[1]
        for kind in range(1, 4):
            self.copy(kind).wait_recv()
            total = total + self.far[kind - 1]
        self.value[2] = total
        self.copy(4).start()

    def over_y(self):
        self.copy(4).wait_recv()
        self.value[3] = self.value[2] + self.across[0]
        self.copy(5).start()

    def finish(self):
        self.copy(5).wait_recv()
        return self.value[3] + self.across[1]

    def drain(self):
        for kind in range(6):
            self.copy(kind).wait_send()


def layer_kernel(
    fast,
    length_ref, across_ref, upward_ref, gain_a_ref, gain_f_ref, tables_ref, expand_ref, collapse_ref,
    tokens_hbm, w_qkv_hbm, w_output_hbm, w_inner_hbm, w_outer_hbm, cot_hbm,
    *rest,
):
    outs, scratch = rest[: 9 if fast else 7], rest[9 if fast else 7 :]
    if fast:
        mixed_ref, input_ref, o_qkv_ref, o_output_ref, o_inner_ref, o_outer_ref, o_gain_a_ref, o_gain_f_ref, o_tables_ref = outs
    else:
        mixed_ref, input_ref, o_qkv_ref, o_output_ref, o_inner_ref, o_outer_ref, o_sums_ref = outs
    (
        x1, share_ref, w_qkv_ref, w_inner_ref, w_outer_ref, cot_ref, load_sem,
        plane_ref, hot_ref, hot_t_ref, qa_ref, qb_ref, k2_ref, kt2_ref, v_ref, band_ref, band_t_ref, qt_ref,
        s_ref, res_ref, dv_ref, dqt_ref, bands_ref, dat_ref, sums_ref, gain_sum_ref,
        att_ref, ax_ref, att_send, att_recv,
        es_ref, ga_ref, es_send, es_recv,
        wo_ref, wo_send, wo_recv,
        nf_ref, nf_send, nf_recv,
        ghl_ref, ghl_send, ghl_recv,
        feed_part, feed_near, feed_far, feed_send, feed_recv,
        norm_part, norm_near, norm_far, norm_send, norm_recv,
        last_send, last_recv,
        low_ref, grad_low_ref, hidden_ref,
        *spreads,
    ) = scratch
    heads = tables_ref.shape[0]
    rows, model = x1.shape
    width = heads * 64
    units = w_inner_ref.shape[1]
    pieces = 4
    chunks = rows // CHUNK
    blocks = rows // BLOCK
    half_model = model // 2
    mp = lax.axis_index("mp")
    da_ref, dk_ref, wt_ref = qa_ref, res_ref, w_inner_ref

    att = Exchange(att_ref, lambda c, d: run(c * 4 + (mp + d) % 4), ax_ref, att_send, att_recv)
    grad_att = Exchange(es_ref, lambda c, d: run(c * 3 + d - 1), ga_ref, es_send, es_recv)
    wo = Gather(wo_ref, wo_send, wo_recv, width)
    normed = Gather(nf_ref, nf_send, nf_recv)
    grads = Gather(ghl_ref, ghl_send, ghl_recv)
    feed = Scatter(feed_part, feed_near, feed_far, feed_send, feed_recv)
    norm = Scatter(norm_part, norm_near, norm_far, norm_send, norm_recv)
    last = Scatter(norm_part, norm_near, norm_far, last_send, last_recv)
    if fast:
        outer = Spread(w_outer_ref, *spreads[0:4])
        inner = Spread(*spreads[4:9])
        output = Spread(*spreads[9:14])
        small = Total(*spreads[19:25])

        def qkv(h):
            return Spread(*[ref.at[h] for ref in spreads[14:19]])

    loads = [
        pltpu.make_async_copy(src, dst, load_sem.at[i])
        for i, (src, dst) in enumerate(
            [
                (tokens_hbm, x1),
                (w_qkv_hbm, w_qkv_ref),
                (w_output_hbm, wo_ref.at[wo.at(0, mp)]),
                (tokens_hbm.at[run(mp * chunks, chunks)], share_ref),
                (w_inner_hbm, w_inner_ref),
                (w_outer_hbm, w_outer_ref),
                (cot_hbm, cot_ref),
            ]
        )
    ]
    for load in loads:
        load.start()
    meet(fast)

    def place(m, c):
        return run(m * chunks + c)

    def window(m, c):
        block = m * chunks + c
        start = jnp.clip(block - 1, 0, blocks - 3)
        return start, start - block + 2


    expanded = dot(tables_ref[...], expand_ref[...])
    square_rows = lax.broadcasted_iota(jnp.int32, (BLOCK, BLOCK), 0)
    square_lanes = lax.broadcasted_iota(jnp.int32, (BLOCK, BLOCK), 1)
    for h in range(heads):
        line = jnp.broadcast_to(expanded[h : h + 1, :WIDE], (BLOCK, WIDE))
        band = roll_rows(line, True)
        band_ref[h] = band.astype(bf16)
        band_t_ref[h] = band.T.astype(bf16)
        across = roll_rows(jnp.broadcast_to(expanded[h : h + 1, WIDE : WIDE + BLOCK], (BLOCK, BLOCK)), True)
        upward = roll_rows(jnp.broadcast_to(expanded[h : h + 1, WIDE + BLOCK :], (BLOCK, BLOCK)), True)
        plane = jnp.where(
            (square_rows < CODES) & (square_lanes < CODES),
            across,
            jnp.where((square_rows >= CODES) & (square_lanes >= CODES), upward, 0.0),
        )
        plane_ref[h] = plane.astype(bf16)
    loads[2].wait()
    wo.start(0)
    loads[1].wait()
    loads[0].wait()
    gain_a = gain_a_ref[...].astype(f32)
    gain_f = gain_f_ref[...].astype(f32)
    lanes = lax.broadcasted_iota(jnp.int32, (CHUNK, BLOCK), 1)
    low = lanes < FAR

    def prepare(j, carry):
        at = run(j, 1, CHUNK)
        x = x1[at, :].astype(f32)
        normed_rows = (x * factor_of(x) * gain_a).astype(bf16)
        x1[at, :] = normed_rows
        codes_lines = lax.broadcasted_iota(jnp.int32, (BLOCK, CHUNK), 0)
        hot_t = jnp.where(
            codes_lines == jnp.broadcast_to(across_ref[:, at], (BLOCK, CHUNK)),
            1.0,
            jnp.where(codes_lines - CODES == jnp.broadcast_to(upward_ref[:, at], (BLOCK, CHUNK)), 1.0, 0.0),
        )
        hot = hot_t.T.astype(bf16)
        hot_t_ref[:, at] = hot_t.astype(bf16)
        hot_ref[at, :] = hot
        row = lax.broadcasted_iota(jnp.int32, (CHUNK, BLOCK), 0) + j * CHUNK
        block = row // BLOCK
        start = jnp.clip(block - 1, 0, blocks - 3)
        far = (lanes >= FAR) & (lanes < MASK)
        far_left = far & (lanes - FAR < start)
        far_right = far & (lanes - FAR > start + 2)
        key_side = jnp.where(
            (far & (lanes - FAR == block))
            | ((lanes == MASK) & (row >= length_ref[0]))
            | ((lanes >= LSE) & (lanes < LSE + 3)),
            1.0,
            0.0,
        )

        def part(h):
            columns = s_ref[:CHUNK, h // 2 * BLOCK : h // 2 * BLOCK + BLOCK]
            return columns if h % 2 == 0 else pltpu.roll(columns, 64, 1)

        s_ref[:CHUNK, :width] = dot(normed_rows, w_qkv_ref[0])
        for h in range(heads):
            left = expanded[h : h + 1, 0:1]
            right = expanded[h : h + 1, WIDE - BLOCK - 1 : WIDE - BLOCK]
            query_side = jnp.where(far_left, left, jnp.where(far_right, right, jnp.where(lanes == MASK, DEAD, 0.0)))
            qa_ref[h, at, :] = dot(hot, plane_ref[h]).astype(bf16)
            qb_ref[h, at, :] = jnp.where(low, part(h).astype(bf16).astype(f32) * 0.125, query_side).astype(bf16)
        s_ref[:CHUNK, :width] = dot(normed_rows, w_qkv_ref[1])
        for h in range(heads):
            second = jnp.where(low, part(h), key_side)
            k2_ref[h, at, :] = second.astype(bf16)
            kt2_ref[h, :, at] = second.T.astype(bf16)
        s_ref[:CHUNK, :width] = dot(normed_rows, w_qkv_ref[2])
        for h in range(heads):
            v_ref[h, at, :] = jnp.where(low, part(h), 1.0).astype(bf16)
        return carry

    s_ref[:CHUNK, :] = jnp.zeros_like(s_ref[:CHUNK, :])
    lax.fori_loop(0, chunks, prepare, 0)
    wo.forward(0)
    loads[3].wait()
    gain_sum_ref[...] = jnp.zeros_like(gain_sum_ref)
    sums_ref[...] = jnp.zeros_like(sums_ref)

    def hidden_of(c):
        att.finish(c)
        hidden = share_ref[run(c), :].astype(f32)
        for m in range(pieces):
            hidden = hidden + dot(ax_ref[run(c * 4 + m), :width], wo_ref[m * width : (m + 1) * width, :])
        hidden_ref[run(c), :] = hidden
        nf_ref[normed.at(c, mp), :] = (hidden * factor_of(hidden) * gain_f).astype(bf16)
        normed.start(c)

    def grad_of(c):
        grad_normed = norm.finish(c)
        hidden = hidden_ref[run(c), :]
        factor = factor_of(hidden)
        hat = hidden * factor
        scaled = grad_normed * gain_f
        back = factor * (scaled - hat * jnp.mean(scaled * hat, axis=-1, keepdims=True))
        grad = cot_ref[place(mp, c), :].astype(f32) + back
        input_ref[run(c), :] = grad
        gain_sum_ref[0:1, :] += jnp.sum(grad_normed * hat, axis=0, keepdims=True)
        grad_low = grad.astype(bf16)
        ghl_ref[grads.at(c, mp), :] = grad_low

        def of(m):
            value = dot_nt(grad_low, wo_ref[run(m, 1, width), :])
            return jnp.concatenate([value, jnp.zeros((BLOCK, 256 - width), f32)], axis=1).astype(bf16)

        ga_ref[run(c * 4 + mp), :] = of(mp)
        for d in (1, 2, 3):
            es_ref[run(c * 3 + d - 1), :] = of((mp + d) % 4)
        grad_att.start(c)
        grads.start(c)

    def attend(t, carry):
        c = t // heads
        h = t % heads
        query_far = jnp.concatenate([qa_ref[h, place(m, c), :] for m in range(pieces)], axis=0)
        query_near = jnp.concatenate([qb_ref[h, place(m, c), :] for m in range(pieces)], axis=0)
        query = jnp.concatenate([query_far, query_near], axis=1)
        for j in range(chunks):
            cols = slice(j * CHUNK, (j + 1) * CHUNK)
            s_ref[cols, :] = dot(query, jnp.concatenate([hot_t_ref[:, cols], kt2_ref[h, :, cols]], axis=0))
        for m in range(pieces):
            start, of = window(m, c)
            for i in range(3):
                panel = (start + i) // pieces
                s_ref[run(panel * 4 + m), run((start + i) % pieces)] += band_ref[h, :, run(of + i)].astype(f32)
        panels = [s_ref[j * CHUNK : (j + 1) * CHUNK, :] for j in range(chunks)]
        top = jnp.max(functools.reduce(jnp.maximum, panels), axis=1, keepdims=True)
        mixed = jnp.zeros((CHUNK, BLOCK), f32)
        for j in range(chunks):
            weights = jnp.exp(panels[j] - top).astype(bf16)
            mixed = mixed + dot(weights, v_ref[h, j * CHUNK : (j + 1) * CHUNK, :])
        res_ref[run(h, 1, CHUNK), :] = jnp.where(low, mixed / pltpu.roll(mixed, 64, 1), 0.0)
        high, middle, rest = split3(-(top + jnp.log(mixed[:, 64:65])))
        second = jnp.where(
            lanes == LSE,
            high,
            jnp.where(lanes == LSE + 1, middle, jnp.where(lanes == LSE + 2, rest, query_near.astype(f32))),
        )
        qt_ref[h, c, :BLOCK, :] = query_far.astype(f32).T.astype(bf16)
        qt_ref[h, c, BLOCK:, :] = second.T.astype(bf16)

        @pl.when(h == heads - 1)
        def _():
            pairs = []
            for g in range(0, heads, 2):
                pair = res_ref[g * CHUNK : (g + 1) * CHUNK, :]
                if g + 1 < heads:
                    pair = jnp.where(low, pair, pltpu.roll(res_ref[(g + 1) * CHUNK : (g + 2) * CHUNK, :], 64, 1))
                pairs.append(pair.astype(bf16))
            merged = jnp.concatenate(pairs, axis=1)
            att_ref[run(c, 1, CHUNK), :] = merged
            ax_ref[run(c * 4 + mp), :] = att_ref[run(c * 4 + mp), :]
            att.start(c)

        @pl.when(t == 4)
        def _():
            wo.finish(0)
            hidden_of(0)

        @pl.when(t == 6)
        def _():
            normed.forward(0)

        @pl.when(t == 7)
        def _():
            hidden_of(1)

        return carry

    lax.fori_loop(0, chunks * heads, attend, 0)
    for load in loads[4:]:
        load.wait()
    normed.finish(0)

    steps = units // 256

    def feed_step(t, carry):
        c = t // steps
        b = t % steps

        @pl.when((b == 0) & (c > 0))
        def _():
            normed.finish(c)

        at = run(b, 1, 256)
        x = nf_ref[run(c, 1, CHUNK), :]
        cot = jnp.concatenate([cot_ref[place(m, c), :] for m in range(pieces)], axis=0)
        inner_units = dot(x, w_inner_ref[:, at])
        grad_act = dot_nt(cot, w_outer_ref[at, :])
        square = inner_units * inner_units
        tanh = jnp.tanh(ROOT * inner_units * (1.0 + CUBE * square))
        half = 0.5 * (1.0 + tanh)
        slope = half + 0.5 * inner_units * (1.0 - tanh * tanh) * (ROOT + 3.0 * CUBE * ROOT * square)
        activated = (inner_units * half).astype(bf16)
        grad_low = (slope * grad_act).astype(bf16)
        low_ref[run(c, 1, CHUNK), at] = activated
        grad_low_ref[run(c, 1, CHUNK), at] = grad_low
        part_ffn = dot(activated, w_outer_ref[at, :])
        part_norm = dot_nt(grad_low, w_inner_ref[:, at])

        @pl.when(b == 0)
        def _():
            for p in range(chunks):
                s_ref[p * CHUNK : (p + 1) * CHUNK, :256] = part_ffn[:, p * 256 : (p + 1) * 256]
                s_ref[p * CHUNK : (p + 1) * CHUNK, 256:] = part_norm[:, p * 256 : (p + 1) * 256]

        @pl.when(b > 0)
        def _():
            for p in range(chunks):
                s_ref[p * CHUNK : (p + 1) * CHUNK, :256] += part_ffn[:, p * 256 : (p + 1) * 256]
                s_ref[p * CHUNK : (p + 1) * CHUNK, 256:] += part_norm[:, p * 256 : (p + 1) * 256]

        @pl.when(b == steps - 1)
        def _():
            for m in range(pieces):
                parts = [s_ref[p * CHUNK + m * BLOCK : p * CHUNK + (m + 1) * BLOCK, :] for p in range(chunks)]
                feed.put(c, m, jnp.concatenate([p[:, :256] for p in parts], axis=1))
                norm.put(c, m, jnp.concatenate([p[:, 256:] for p in parts], axis=1))
            norm.start(c)
            feed.start(c)

        @pl.when(t == 1)
        def _():
            normed.forward(1)

        @pl.when(t == 2)
        def _():
            hidden_of(2)

        @pl.when(t == 3)
        def _():
            norm.middle(0)

        @pl.when(t == 5)
        def _():
            normed.forward(2)

        @pl.when(t == 6)
        def _():
            norm.middle(1)

        @pl.when(t == 7)
        def _():
            grad_of(0)

        return carry

    lax.fori_loop(0, chunks * steps, feed_step, 0)

    def weights_of(is_outer):
        for b in range(2):
            at = slice(b * half_model, (b + 1) * half_model)
            total = jnp.zeros((half_model, units), f32)
            for c in range(chunks):
                if is_outer:
                    left = jnp.concatenate([cot_ref[place(m, c), at] for m in range(pieces)], axis=0)
                    total = total + dot_tn(left, low_ref[run(c, 1, CHUNK), :])
                else:
                    total = total + dot_tn(nf_ref[run(c, 1, CHUNK), at], grad_low_ref[run(c, 1, CHUNK), :])
            if fast:
                (outer if is_outer else inner).put(b * half_model, total)
            else:
                (o_outer_ref if is_outer else o_inner_ref)[at, :] = total

    weights_of(True)
    if fast:
        outer.start()
    norm.middle(2)
    grad_of(1)
    weights_of(False)
    for c in range(chunks):
        normed.drain(c)
    wt_ref[...] = jnp.zeros_like(wt_ref)
    for k in range(3):
        turned = w_qkv_ref[k].astype(f32).T.astype(bf16)
        for h in range(heads):
            wt_ref[h * 256 + k * 64 : h * 256 + (k + 1) * 64, :] = turned[h * 64 : (h + 1) * 64]

    def receive(c):
        grad_att.finish(c)
        at = run(c, 1, CHUNK)
        for h in range(heads):
            pair = slice(h // 2 * BLOCK, h // 2 * BLOCK + BLOCK)
            grad = ga_ref[at, pair].astype(f32)
            out = att_ref[at, pair].astype(f32)
            if h % 2 == 1:
                grad = pltpu.roll(grad, 64, 1)
                out = pltpu.roll(out, 64, 1)
            high, middle, rest = split3(-jnp.sum(jnp.where(low, grad * out, 0.0), axis=1, keepdims=True))
            grad = jnp.where(
                low,
                grad,
                jnp.where(
                    lanes == FAR, high, jnp.where(lanes == FAR + 1, middle, jnp.where(lanes == FAR + 2, rest, 0.0))
                ),
            )
            da_ref[h, at, :] = grad.astype(bf16)
            dat_ref[h, :, at] = grad.T.astype(bf16)

    lines16 = lax.broadcasted_iota(jnp.int32, (16, rows), 0)
    block16 = lax.broadcasted_iota(jnp.int32, (16, rows), 1) // BLOCK
    start16 = jnp.clip(block16 - 1, 0, blocks - 3)
    real = lines16 < blocks
    tall_low = lax.broadcasted_iota(jnp.int32, (rows, BLOCK), 1) < 64

    def fold(value):
        total = value[:, :BLOCK]
        for b in range(1, value.shape[1] // BLOCK):
            total = total + value[:, b * BLOCK : (b + 1) * BLOCK]
        return jnp.sum(total, axis=0, keepdims=True)

    def head(h, carry):
        dk_ref[...] = jnp.zeros_like(dk_ref)
        dv_ref[...] = jnp.zeros_like(dv_ref)
        bands_ref[...] = jnp.zeros_like(bands_ref)

        def chunk(c, carry):
            @pl.when(h == 0)
            def _():
                receive(c)

            at = run(c, 1, CHUNK)
            s_ref[...] = dot(jnp.concatenate([hot_ref[...], k2_ref[h]], axis=1), qt_ref[h, c])
            for m in range(pieces):
                start, of = window(m, c)
                s_ref[run(start, 3), m * BLOCK : (m + 1) * BLOCK] += band_t_ref[h, run(of, 3), :].astype(f32)
            probs = jnp.exp(s_ref[...])
            low_ref[:, :CHUNK] = probs.astype(bf16)
            grad_low_ref[:, :CHUNK] = (probs * dot(v_ref[h], dat_ref[h, :, at])).astype(bf16)
            probs_t = low_ref[:, :CHUNK]
            grad_t = grad_low_ref[:, :CHUNK]
            dv_ref[...] += dot(probs_t, da_ref[h, at, :])
            dk_ref[...] += dot(grad_t, jnp.concatenate([qb_ref[h, place(m, c), :] for m in range(pieces)], axis=0))
            dq_far = dot(hot_t_ref[...], grad_t)
            dq_near = dot(kt2_ref[h], grad_t)
            for m in range(pieces):
                dqt_ref[:BLOCK, place(m, c)] = dq_far[:, m * BLOCK : (m + 1) * BLOCK]
                dqt_ref[BLOCK:, place(m, c)] = dq_near[:, m * BLOCK : (m + 1) * BLOCK]
                start, of = window(m, c)
                bands_ref[run(of, 3), :] += grad_low_ref[run(start, 3), m * BLOCK : (m + 1) * BLOCK].astype(f32)

            def when(head_index, chunk_index):
                return pl.when((h == head_index) & (c == chunk_index))

            def mix(k):
                mixed_ref[run(k), :] = (hidden_ref[run(k), :] + feed.finish(k)).astype(bf16)

            @when(0, 0)
            def _():
                grad_of(2)

            @when(0, 1)
            def _():
                grads.forward(0)
                feed.middle(0)

            @when(0, 2)
            def _():
                grads.forward(1)
                feed.middle(1)

            @when(1, 0)
            def _():
                grads.forward(2)
                feed.middle(2)
                mix(0)
                if fast:
                    outer.middle()
                    inner.start()

            @when(1, 1)
            def _():
                mix(1)

            @when(1, 2)
            def _():
                mix(2)

            if fast:

                @when(2, 0)
                def _():
                    inner.middle()

                @when(2, 1)
                def _():
                    qkv(0).middle()

                @when(2, 2)
                def _():
                    output.middle()
                    qkv(1).middle()

            return carry

        lax.fori_loop(0, chunks, chunk, 0)

        dq = dqt_ref[BLOCK:, :].T * 0.125
        grads_of = run(h, 1, 256)
        nf_ref[:, grads_of] = jnp.concatenate(
            [jnp.where(tall_low, dq, pltpu.roll(dk_ref[...], 64, 1)), jnp.where(tall_low, dv_ref[...], 0.0)], axis=1
        ).astype(bf16)
        for b in range(2):
            cols = slice(b * half_model, (b + 1) * half_model)
            grad_qkv = dot_tn(x1[:, cols], nf_ref[:, grads_of])
            if fast:
                qkv(h).put(b * half_model, grad_qkv)
            else:
                o_qkv_ref[h, cols, :] = grad_qkv
        if fast:
            qkv(h).start()

        @pl.when(h == 1)
        def _():
            for c in range(chunks):
                grads.finish(c)
            for b in range(2):
                cols = slice(b * half_model, (b + 1) * half_model)
                grad_output = dot_tn(ghl_ref[:, cols], att_ref[...])
                if fast:
                    output.put(b * half_model, grad_output)
                else:
                    o_output_ref[cols, :] = grad_output[:, :width]
            if fast:
                output.start()

        band = roll_rows(bands_ref[...].T, False)
        spread = dqt_ref[:BLOCK, :]
        high = spread.astype(bf16)
        rest = (spread - high.astype(f32)).astype(bf16)
        plane = (dot(high, hot_ref[...]) + dot(rest, hot_ref[...])).T
        plane = jnp.where((square_rows < CODES) == (square_lanes < CODES), plane, 0.0)
        plane = roll_rows(plane, False)
        far = dqt_ref[BLOCK + FAR : BLOCK + FAR + 16, :]
        line = jnp.concatenate(
            [
                jnp.sum(band, axis=0, keepdims=True),
                jnp.sum(plane[:CODES], axis=0, keepdims=True),
                jnp.sum(plane[CODES:], axis=0, keepdims=True),
                fold(jnp.where(real & (lines16 < start16), far, 0.0)),
                fold(jnp.where(real & (lines16 > start16 + 2), far, 0.0)),
            ],
            axis=1,
        )
        sums_ref[...] += jnp.where(lax.broadcasted_iota(jnp.int32, sums_ref.shape, 0) == h, line, 0.0)
        return carry

    lax.fori_loop(0, heads, head, 0)

    for c in range(chunks):
        norm.drain(c)
    gain_total = jnp.zeros((1, model), f32)
    for c in range(chunks):
        for m in range(pieces):
            at = place(m, c)
            partial = dot(nf_ref[at, :], wt_ref[...])
            gain_total = gain_total + jnp.sum(partial * x1[at, :].astype(f32), axis=0, keepdims=True)
            last.put(c, m, partial)
        last.start(c)
    sums_ref[3:4, :model] = gain_total / gain_a
    sums_ref[4:5, :model] = gain_sum_ref[0:1, :]
    if fast:
        small.value[0] = sums_ref[...]
        small.start()
        o_outer_ref[...] = outer.finish()
    for c in range(chunks):
        last.middle(c)
    if fast:
        qkv(2).middle()
        small.over_z()
        o_inner_ref[...] = inner.finish()
        o_output_ref[...] = output.finish()[:, :width].T
        small.over_core()
    for c in range(chunks):
        x = share_ref[run(c), :].astype(f32)
        grad_normed = last.finish(c)
        factor = factor_of(x)
        hat = x * factor
        scaled = grad_normed * gain_a
        back = factor * (scaled - hat * jnp.mean(scaled * hat, axis=-1, keepdims=True))
        input_ref[run(c), :] += back
        if fast and c == 0:
            small.over_y()
    if fast:
        low_each = lax.broadcasted_iota(jnp.int32, (model // 8, BLOCK), 1) < 64
        parts = [qkv(h).finish() for h in range(heads)]
        for k in range(3):
            for h in range(0, heads, 2):
                at = slice(0, BLOCK) if k < 2 else slice(BLOCK, 2 * BLOCK)
                one = parts[h][:, at]
                one = pltpu.roll(one, 64, 1) if k == 1 else one
                if h + 1 < heads:
                    two = parts[h + 1][:, at]
                    two = two if k == 1 else pltpu.roll(two, 64, 1)
                    o_qkv_ref[k, :, h * 64 : (h + 2) * 64] = jnp.where(low_each, one, two)
                else:
                    o_qkv_ref[k, :, h * 64 :] = one[:, :64]
        totals = small.finish()
        o_gain_a_ref[...] = totals[3:4, :model]
        o_gain_f_ref[...] = totals[4:5, :model]
        per_head = small.value[2]
        tables = sum(dot_nt(part.astype(bf16), collapse_ref[...]) for part in split3(per_head))
        o_tables_ref[...] = tables[:heads]
        outer.drain()
        inner.drain()
        output.drain()
        for h in range(heads):
            qkv(h).drain()
        small.drain()
    else:
        o_sums_ref[...] = sums_ref[...]
    wo.drain(0)
    for c in range(chunks):
        for each in (att, grad_att, grads, feed, last):
            each.drain(c)


def spread_scratch(rows, columns, lead=(), own_part=True):
    buffers = [pltpu.VMEM((*lead, 8 * rows, columns), bf16)] if own_part else []
    return buffers + [
        pltpu.VMEM((*lead, 4 * rows, columns), bf16),
        pltpu.VMEM((*lead, 3 * rows, columns), bf16),
        pltpu.SemaphoreType.DMA((*lead, 4)),
        pltpu.SemaphoreType.DMA((*lead, 4)),
    ]


def local(
    fast,
    tokens, lengths, horizontal, vertical, gain_attn, w_qkv, bias_tables, w_output, gain_ffn, w_inner, w_outer, cotangent,
):
    rows, model = tokens.shape
    heads = bias_tables.shape[1]
    width = w_qkv.shape[2]
    units = w_inner.shape[1]
    share = rows // lax.axis_size("mp")
    chunks = rows // CHUNK
    each = model // 8
    sums = (8, WIDE + 4 * BLOCK)

    def dma(*shape):
        return pltpu.SemaphoreType.DMA(shape)

    def vmem(*shape, dtype=bf16):
        return pltpu.VMEM(shape, dtype)

    scratch = [
        vmem(rows, model), vmem(share, model), vmem(3, model, width), vmem(model, units), vmem(units, model),
        vmem(rows, model), dma(7),
        vmem(heads, BLOCK, BLOCK), vmem(rows, BLOCK), vmem(BLOCK, rows), vmem(heads, rows, BLOCK),
        vmem(heads, rows, BLOCK), vmem(heads, rows, BLOCK), vmem(heads, BLOCK, rows), vmem(heads, rows, BLOCK),
        vmem(heads, BLOCK, WIDE), vmem(heads, WIDE, BLOCK),
        vmem(heads, chunks, 256, CHUNK),
        vmem(rows, CHUNK, dtype=f32), vmem(heads * CHUNK, BLOCK, dtype=f32), vmem(rows, BLOCK, dtype=f32),
        vmem(256, rows, dtype=f32), vmem(WIDE, BLOCK, dtype=f32), vmem(heads, BLOCK, rows),
        vmem(*sums, dtype=f32), vmem(8, model, dtype=f32),
        vmem(rows, 256), vmem(rows, 256), dma(chunks, 3), dma(chunks, 3),
        vmem(chunks * 3 * BLOCK, 256), vmem(rows, 256), dma(chunks, 3), dma(chunks, 3),
        vmem(4 * width, model), dma(1, 3), dma(1, 3),
        vmem(rows, model), dma(chunks, 3), dma(chunks, 3),
        vmem(rows, model), dma(chunks, 3), dma(chunks, 3),
        vmem(rows, model), vmem(rows // 2, model), vmem(share, model), dma(chunks, 2), dma(chunks, 2),
        vmem(rows, model), vmem(rows // 2, model), vmem(share, model), dma(chunks, 2), dma(chunks, 2),
        dma(chunks, 2), dma(chunks, 2),
        vmem(rows, units), vmem(rows, units), vmem(share, model, dtype=f32),
    ]
    outs = [((share, model), bf16), ((share, model), f32)]
    if fast:
        outs += [
            ((3, each, width), f32), ((width, each), f32), ((each, units), f32), ((each, units), f32),
            ((1, model), f32), ((1, model), f32), ((heads, 3 * BUCKETS), f32),
        ]
        scratch += [
            *spread_scratch(each, units, own_part=False), *spread_scratch(each, units), *spread_scratch(each, 256),
            *spread_scratch(each, 256, lead=(heads,)),
            vmem(4, *sums, dtype=f32), vmem(*sums, dtype=f32), vmem(3, *sums, dtype=f32), vmem(2, *sums, dtype=f32),
            dma(6), dma(6),
        ]
    else:
        outs += [
            ((heads, model, 256), f32), ((model, width), f32), ((model, units), f32), ((model, units), f32), (sums, f32),
        ]
    full = pl.BlockSpec(memory_space=pltpu.VMEM)
    anywhere = pl.BlockSpec(memory_space=pl.ANY)
    results = pl.pallas_call(
        functools.partial(layer_kernel, fast),
        in_specs=[pl.BlockSpec(memory_space=pltpu.SMEM)] + [full] * 7 + [anywhere] * 6,
        out_specs=[full] * len(outs),
        out_shape=[jax.ShapeDtypeStruct(*out) for out in outs],
        scratch_shapes=scratch,
        compiler_params=pltpu.CompilerParams(vmem_limit_bytes=64 * MIB, collective_id=1, has_side_effects=True),
        name="layer",
    )(
        lengths, horizontal.reshape(1, rows), vertical.reshape(1, rows), gain_attn.reshape(1, model),
        gain_ffn.reshape(1, model), bias_tables.T, jnp.asarray(expansion(), bf16), jnp.asarray(collapse().T, bf16),
        tokens, w_qkv, w_output, w_inner, w_outer, cotangent,
    )
    if fast:
        mixed, input_grad, qkv, output, inner, outer, gain_a, gain_f, tables = results
        return mixed, input_grad, qkv, output, inner, outer.T, gain_a[0], gain_f[0], tables.T
    mixed, input_grad, qkv, output, inner, outer, sums = results
    qkv = qkv[:, :, : 3 * 64].reshape(heads, model, 3, 64).transpose(2, 1, 0, 3).reshape(3, model, width)
    gains = lax.psum(sums[3:5, :model], ("dp", "mp"))
    tables = lax.dot_general(
        jnp.asarray(collapse(), f32),
        lax.psum(sums[:heads], "dp"),
        (((0,), (1,)), ((), ())),
        precision=lax.Precision.HIGHEST,
    )

    def spread(x, axis):
        return lax.psum_scatter(x, "dp", scatter_dimension=axis, tiled=True)

    return (
        mixed, input_grad, spread(qkv, 1), spread(output.T, 1), spread(inner, 0), spread(outer.T, 1),
        gains[0], gains[1], tables,
    )


def solution(mesh):
    fast = mesh.shape["dp"] == 8
    return jax.shard_map(
        functools.partial(local, fast),
        mesh=mesh,
        in_specs=(
            P("dp", None), P("dp"), P("dp"), P("dp"), P(), P(None, None, "mp"), P(None, "mp"), P("mp", None), P(),
            P(None, "mp"), P("mp", None), P("dp", None),
        ),
        out_specs=(
            P(("dp", "mp"), None), P(("dp", "mp"), None), P(None, "dp", "mp"), P("mp", "dp"), P("dp", "mp"),
            P("mp", "dp"), P(), P(), P(None, "mp"),
        ),
        check_vma=False,
    )
```

```python
import functools
import jax
import jax.numpy as jnp
import numpy as np
from jax import lax
from jax.experimental import pallas as pl
from jax.experimental.pallas import tpu as pltpu
from jax.sharding import PartitionSpec as P

BUCKETS = 32
CODES = 64
HALF = BUCKETS // 2
EPSILON = 1e-06
DEAD = -1e9
CHUNK = 512
BLOCK = 128
BAND = 3 * BLOCK
WIDE = 6 * BLOCK
FAR = 64
MASK = 76
LSE = 80
MIB = 2**20

f32 = jnp.float32
bf16 = jnp.bfloat16


def line_bucket(columns):
    line = jnp.clip(columns - 2 * BLOCK, -HALF, HALF - 1) + HALF
    line = jnp.where(columns < 5 * BLOCK, line, 0)
    wrapped = columns % BLOCK
    wrapped = jnp.where(wrapped < CODES, wrapped, wrapped - BLOCK)
    plane = jnp.clip(wrapped, -HALF, HALF - 1) + HALF
    return jnp.where(
        columns < WIDE, line, jnp.where(columns < WIDE + BLOCK, BUCKETS + plane, 2 * BUCKETS + plane)
    )


def expansion():
    rows = lax.broadcasted_iota(jnp.int32, (3 * BUCKETS, WIDE + 2 * BLOCK), 0)
    columns = lax.broadcasted_iota(jnp.int32, (3 * BUCKETS, WIDE + 2 * BLOCK), 1)
    return jnp.where(rows == line_bucket(columns), 1.0, 0.0).astype(bf16)


def collapse():
    rows = lax.broadcasted_iota(jnp.int32, (3 * BUCKETS, WIDE + 4 * BLOCK), 0)
    columns = lax.broadcasted_iota(jnp.int32, (3 * BUCKETS, WIDE + 4 * BLOCK), 1)
    bucket = line_bucket(columns)
    bucket = jnp.where(columns == 5 * BLOCK, BUCKETS - 1, bucket)
    bucket = jnp.where(columns >= WIDE + 2 * BLOCK, 0, bucket)
    bucket = jnp.where(columns >= WIDE + 3 * BLOCK, BUCKETS - 1, bucket)
    return jnp.where(rows == bucket, 1.0, 0.0).astype(bf16)


def roll_rows(value, right):
    rows, width = value.shape
    index = lax.broadcasted_iota(jnp.int32, value.shape, 0)
    step = 1
    while step < rows:
        shift = step if right else width - step
        value = jnp.where((index // step) % 2 == 1, pltpu.roll(value, shift, 1), value)
        step *= 2
    return value


def dot(a, b):
    return jnp.dot(a, b, preferred_element_type=f32)


def dot_nt(a, b):
    return lax.dot_general(a, b, (((1,), (1,)), ((), ())), preferred_element_type=f32)


def split3(value):
    high = value.astype(bf16).astype(f32)
    rest = value - high
    middle = rest.astype(bf16).astype(f32)
    return high, middle, rest - middle


def dot_tn(a, b):
    return lax.dot_general(a, b, (((0,), (0,)), ((), ())), preferred_element_type=f32)


ROOT = float(np.sqrt(2.0 / np.pi))
CUBE = 0.044715


def factor_of(rows):
    return lax.rsqrt(jnp.mean(rows * rows, axis=-1, keepdims=True) + EPSILON)


def mp_places():
    mp = lax.axis_index("mp")
    y, core = mp // 2, mp % 2
    return mp, y, core, y * 2 + (1 - core), (1 - y) * 2 + core


def dp_places():
    dp = lax.axis_index("dp")
    return dp // 2, dp % 2


def remote(src, dst, send, recv, mp=None, dp=None):
    return pltpu.make_async_remote_copy(
        src_ref=src,
        dst_ref=dst,
        send_sem=send,
        recv_sem=recv,
        device_id=(lax.axis_index("dp") if dp is None else dp, lax.axis_index("mp") if mp is None else mp),
        device_id_type=pl.DeviceIdType.MESH,
    )


def beside(z):
    return z // 2 * 2 + 1 - z % 2


def meet(fast):
    mp, dp = lax.axis_index("mp"), lax.axis_index("dp")
    z, x = dp_places()
    others = [(dp, (mp + d) % 4) for d in (1, 2, 3)]
    if fast:
        others.extend([(z * 2 + 1 - x, mp), (beside(z) * 2 + x, mp), ((z + 2) % 4 * 2 + x, mp)])
    barrier = pltpu.get_barrier_semaphore()
    for other in others:
        pl.semaphore_signal(barrier, inc=1, device_id=other, device_id_type=pl.DeviceIdType.MESH)
    pl.semaphore_wait(barrier, len(others))


def run(index, count=1, size=BLOCK):
    return pl.ds(pl.multiple_of(index * size, size), count * size)


class Scatter:

    def __init__(self, part, near, far, send, recv):
        self.part, self.near, self.far, self.send, self.recv = part, near, far, send, recv

    def block(self, c, core, y):
        return (c * 2 + core) * 2 + y

    def put(self, c, m, value):
        self.part[run(self.block(c, m % 2, m // 2)), :] = value.astype(bf16)

    def first(self, c):
        _, _, core, sibling, _ = mp_places()
        src = self.part.at[run(self.block(c, 1 - core, 0), 2)]
        return remote(src, self.near.at[run(c * 2, 2)], self.send.at[c, 0], self.recv.at[c, 0], sibling)

    def second(self, c):
        _, y, core, _, across = mp_places()
        src = self.part.at[run(self.block(c, core, 1 - y))]
        return remote(src, self.far.at[run(c)], self.send.at[c, 1], self.recv.at[c, 1], across)

    def start(self, c):
        self.first(c).start()

    def middle(self, c):
        _, y, core, _, _ = mp_places()
        self.first(c).wait_recv()
        at = run(self.block(c, core, 1 - y))
        self.part[at, :] = (self.part[at, :].astype(f32) + self.near[run(c * 2 + 1 - y), :].astype(f32)).astype(bf16)
        self.second(c).start()

    def finish(self, c):
        _, y, core, _, _ = mp_places()
        self.second(c).wait_recv()
        own = self.part[run(self.block(c, core, y)), :].astype(f32) + self.near[run(c * 2 + y), :].astype(f32)
        return own + self.far[run(c), :].astype(f32)

    def drain(self, c):
        self.first(c).wait_send()
        self.second(c).wait_send()


class Gather:

    def __init__(self, full, send, recv, size=BLOCK):
        self.full, self.send, self.recv, self.size = full, send, recv, size

    def at(self, c, m):
        return run(c * 4 + m, 1, self.size)

    def copy(self, c, kind):
        mp, _, _, sibling, across = mp_places()
        at = self.full.at[self.at(c, across if kind == 2 else mp)]
        return remote(at, at, self.send.at[c, kind], self.recv.at[c, kind], across if kind == 1 else sibling)

    def start(self, c):
        self.copy(c, 1).start()
        self.copy(c, 0).start()

    def forward(self, c):
        self.copy(c, 1).wait_recv()
        self.copy(c, 2).start()

    def finish(self, c):
        self.copy(c, 0).wait_recv()
        self.copy(c, 2).wait_recv()

    def drain(self, c):
        for kind in range(3):
            self.copy(c, kind).wait_send()


class Exchange:

    def __init__(self, given, taken, size, send, recv):
        self.given, self.taken, self.size, self.send, self.recv = given, taken, size, send, recv

    def copy(self, c, d):
        mp = lax.axis_index("mp")
        src = self.given.at[run(c * 3 + d - 1, 1, self.size)]
        dst = self.taken.at[run(c * 4 + mp, 1, self.size)]
        return remote(src, dst, self.send.at[c, d - 1], self.recv.at[c, d - 1], (mp + d) % 4)

    def start(self, c):
        for d in (2, 1, 3):
            self.copy(c, d).start()

    def finish(self, c):
        for d in (1, 2, 3):
            self.copy(c, d).wait_recv()

    def drain(self, c):
        for d in (1, 2, 3):
            self.copy(c, d).wait_send()


class Spread:

    def __init__(self, part, near, pair, far, send, recv):
        self.part, self.near, self.pair, self.far, self.send, self.recv = part, near, pair, far, send, recv
        self.each = part.shape[0] // 8

    def at(self, index, count=1):
        return run(index, count, self.each)

    def put(self, first_row, value):
        for r in range(value.shape[0] // self.each):
            j = first_row // self.each + r
            rows = value[r * self.each : (r + 1) * self.each]
            self.part[self.at(j % 2 * 4 + j // 2 % 2 * 2 + j // 4), :] = rows.astype(bf16)

    def copy(self, kind):
        z, x = dp_places()
        send, recv = self.send.at[kind], self.recv.at[kind]
        if kind == 0:
            src = self.part.at[self.at((1 - x) * 4, 4)]
            return remote(src, self.near, send, recv, dp=z * 2 + 1 - x)
        if kind == 1:
            src = self.part.at[self.at(x * 4 + (1 - z % 2) * 2, 2)]
            return remote(src, self.pair, send, recv, dp=beside(z) * 2 + x)
        src = self.part.at[self.at(x * 4 + z % 2 * 2 + 1 - z // 2)]
        return remote(src, self.far, send, recv, dp=(z + 2) % 4 * 2 + x)

    def start(self):
        self.copy(0).start()

    def middle(self):
        z, x = dp_places()
        self.copy(0).wait_recv()
        at = self.at(x * 4 + (1 - z % 2) * 2, 2)
        near = self.near[self.at((1 - z % 2) * 2, 2), :].astype(f32)
        self.part[at, :] = (self.part[at, :].astype(f32) + near).astype(bf16)
        self.copy(1).start()

    def sum_of(self, half):
        z, x = dp_places()
        total = self.part[self.at(x * 4 + z % 2 * 2 + half), :].astype(f32)
        total = total + self.near[self.at(z % 2 * 2 + half), :].astype(f32)
        return total + self.pair[self.at(half), :].astype(f32)

    def third(self):
        z, x = dp_places()
        self.copy(1).wait_recv()
        self.part[self.at(x * 4 + z % 2 * 2 + 1 - z // 2), :] = self.sum_of(1 - z // 2).astype(bf16)
        self.copy(2).start()

    def finish(self):
        z, _ = dp_places()
        self.copy(2).wait_recv()
        return self.sum_of(z // 2) + self.far[...].astype(f32)

    def drain(self):
        for kind in range(3):
            self.copy(kind).wait_send()


class Total:

    def __init__(self, value, taken, send, recv):
        self.value, self.taken, self.send, self.recv = value, taken, send, recv

    def copy(self, kind):
        z, x = dp_places()
        _, _, _, sibling, across = mp_places()
        mp = {3: sibling, 4: across}.get(kind)
        dp = {0: z * 2 + 1 - x, 1: beside(z) * 2 + x, 2: (z + 2) % 4 * 2 + x}.get(kind)
        return remote(self.value.at[kind], self.taken.at[kind], self.send.at[kind], self.recv.at[kind], mp, dp)

    def start(self, value):
        self.value[0] = value
        self.copy(0).start()

    def turn(self, kind):
        self.copy(kind - 1).wait_recv()
        self.value[kind] = self.value[kind - 1] + self.taken[kind - 1]
        self.copy(kind).start()

    def finish(self):
        self.copy(4).wait_recv()
        return self.value[4] + self.taken[4]

    def drain(self):
        for kind in range(5):
            self.copy(kind).wait_send()


def layer_kernel(
    fast,
    length_ref, across_ref, upward_ref, gain_a_ref, gain_f_ref, tables_ref,
    tokens_hbm, w_qkv_hbm, w_output_hbm, w_inner_hbm, w_outer_hbm, cot_hbm,
    *rest,
):
    outs, scratch = rest[: 9 if fast else 7], rest[9 if fast else 7 :]
    if fast:
        mixed_ref, input_ref, o_qkv_ref, o_output_ref, o_inner_ref, o_outer_ref, o_gain_a_ref, o_gain_f_ref, o_tables_ref = outs
    else:
        mixed_ref, input_ref, o_qkv_ref, o_output_ref, o_inner_ref, o_outer_ref, o_sums_ref = outs
    (
        x1, w_qkv_ref, w_inner_ref, w_outer_ref, cot_ref, load_sem,
        codes_ref, plane_ref, hot_ref, hot_t_ref, qa_ref, qb_ref, k2_ref, kt2_ref, v_ref, band_ref, band_t_ref, qt_ref,
        s_ref, res_ref, dv_ref, dqt_ref, bands_ref, dat_ref, sums_ref, gain_sum_ref,
        att_ref, af_ref, att_send, att_recv,
        es_ref, ga_ref, es_send, es_recv,
        wo_ref, wo_send, wo_recv,
        nf_ref,
        ghl_ref, ghl_send, ghl_recv,
        feed_part, feed_send, feed_recv, norm_part, norm_send, norm_recv, last_send, last_recv, near_ref, far_ref,
        credit,
        low_ref, grad_low_ref, hidden_ref,
        *spreads,
    ) = scratch
    heads = tables_ref.shape[0]
    rows, model = x1.shape
    width = heads * 64
    units = w_inner_ref.shape[1]
    pieces = 4
    chunks = rows // CHUNK
    blocks = rows // BLOCK
    half_model = model // 2
    mp, _, _, sibling, across = mp_places()
    da_ref, dk_ref, wt_ref = qa_ref, res_ref, w_inner_ref

    att = Gather(af_ref, att_send, att_recv, CHUNK + CHUNK // 2)
    grad_att = Exchange(es_ref, ga_ref, BLOCK + BLOCK // 2, es_send, es_recv)
    wo = Gather(wo_ref, wo_send, wo_recv, width)
    grads = Gather(ghl_ref, ghl_send, ghl_recv)
    feed = Scatter(feed_part, near_ref, far_ref, feed_send, feed_recv)
    norm = Scatter(norm_part, near_ref, far_ref, norm_send, norm_recv)
    last = Scatter(norm_part, near_ref, far_ref, last_send, last_recv)
    if fast:
        outer = Spread(w_outer_ref, *spreads[0:5])
        inner = Spread(*spreads[5:11])
        output = Spread(*spreads[11:17])
        small = Total(*spreads[23:27])

        def qkv(h):
            return Spread(*[ref.at[h] for ref in spreads[17:23]])

    def place(m, c):
        return run(m * chunks + c)

    loads = [
        pltpu.make_async_copy(src, dst, load_sem.at[i])
        for i, (src, dst) in enumerate(
            [
                (tokens_hbm, x1),
                (w_qkv_hbm, w_qkv_ref),
                (w_output_hbm, wo_ref.at[wo.at(0, mp)]),
                (w_inner_hbm, w_inner_ref),
                (w_outer_hbm, w_outer_ref),
                (cot_hbm, cot_ref),
                *[(tokens_hbm.at[place(m, c)], low_ref.at[run(c * 4 + m)]) for c in range(chunks) for m in range(4)],
                (tokens_hbm.at[run(mp * chunks, chunks)], cot_ref.at[run(0, chunks)]),
            ]
        )
    ]
    for load in loads[:-1]:
        load.start()
    meet(fast)

    def window(m, c):
        block = m * chunks + c
        start = jnp.clip(block - 1, 0, blocks - 3)
        return start, start - block + 2


    expanded = dot(tables_ref[...], expansion())
    square_rows = lax.broadcasted_iota(jnp.int32, (BLOCK, BLOCK), 0)
    square_lanes = lax.broadcasted_iota(jnp.int32, (BLOCK, BLOCK), 1)
    for h in range(heads):
        line = jnp.broadcast_to(expanded[h : h + 1, :WIDE], (BLOCK, WIDE))
        band = roll_rows(line, True)
        band_ref[h] = band.astype(bf16)
        band_t_ref[h] = band.T.astype(bf16)
        level = roll_rows(jnp.broadcast_to(expanded[h : h + 1, WIDE : WIDE + BLOCK], (BLOCK, BLOCK)), True)
        upward = roll_rows(jnp.broadcast_to(expanded[h : h + 1, WIDE + BLOCK :], (BLOCK, BLOCK)), True)
        plane = jnp.where(
            (square_rows < CODES) & (square_lanes < CODES),
            level,
            jnp.where((square_rows >= CODES) & (square_lanes >= CODES), upward, 0.0),
        )
        plane_ref[h] = plane.astype(bf16)
    loads[2].wait()
    wo.start(0)
    loads[1].wait()
    loads[0].wait()
    gain_a = gain_a_ref[...].reshape(1, model).astype(f32)
    gain_f = gain_f_ref[...].reshape(1, model).astype(f32)
    codes_ref[0:1, :] = across_ref[...].reshape(1, rows)
    codes_ref[1:2, :] = upward_ref[...].reshape(1, rows)
    lanes = lax.broadcasted_iota(jnp.int32, (CHUNK, BLOCK), 1)
    low = lanes < FAR

    def prepare(j, carry):
        at = run(j, 1, CHUNK)
        x = x1[at, :].astype(f32)
        normed_rows = (x * factor_of(x) * gain_a).astype(bf16)
        x1[at, :] = normed_rows
        codes_lines = lax.broadcasted_iota(jnp.int32, (BLOCK, CHUNK), 0)
        hot_t = jnp.where(
            codes_lines == jnp.broadcast_to(codes_ref[0:1, at], (BLOCK, CHUNK)),
            1.0,
            jnp.where(codes_lines - CODES == jnp.broadcast_to(codes_ref[1:2, at], (BLOCK, CHUNK)), 1.0, 0.0),
        )
        hot = hot_t.T.astype(bf16)
        hot_t_ref[:, at] = hot_t.astype(bf16)
        hot_ref[at, :] = hot
        row = lax.broadcasted_iota(jnp.int32, (CHUNK, BLOCK), 0) + j * CHUNK
        block = row // BLOCK
        start = jnp.clip(block - 1, 0, blocks - 3)
        far = (lanes >= FAR) & (lanes < MASK)
        far_left = far & (lanes - FAR < start)
        far_right = far & (lanes - FAR > start + 2)
        key_side = jnp.where(
            (far & (lanes - FAR == block))
            | ((lanes == MASK) & (row >= length_ref[0]))
            | ((lanes >= LSE) & (lanes < LSE + 3)),
            1.0,
            0.0,
        )

        def part(h):
            columns = s_ref[:CHUNK, h // 2 * BLOCK : h // 2 * BLOCK + BLOCK]
            return columns if h % 2 == 0 else pltpu.roll(columns, 64, 1)

        s_ref[:CHUNK, :width] = dot_nt(normed_rows, w_qkv_ref[0])
        for h in range(heads):
            left = expanded[h : h + 1, 0:1]
            right = expanded[h : h + 1, WIDE - BLOCK - 1 : WIDE - BLOCK]
            query_side = jnp.where(far_left, left, jnp.where(far_right, right, jnp.where(lanes == MASK, DEAD, 0.0)))
            qa_ref[h, at, :] = dot(hot, plane_ref[h]).astype(bf16)
            qb_ref[h, at, :] = jnp.where(low, part(h).astype(bf16).astype(f32) * 0.125, query_side).astype(bf16)
        s_ref[:CHUNK, :width] = dot_nt(normed_rows, w_qkv_ref[1])
        for h in range(heads):
            second = jnp.where(low, part(h), key_side)
            k2_ref[h, at, :] = second.astype(bf16)
            kt2_ref[h, :, at] = second.T.astype(bf16)
        s_ref[:CHUNK, :width] = dot_nt(normed_rows, w_qkv_ref[2])
        for h in range(heads):
            v_ref[h, at, :] = jnp.where(low, part(h), 1.0).astype(bf16)
        return carry

    s_ref[:CHUNK, :] = jnp.zeros_like(s_ref[:CHUNK, :])
    lax.fori_loop(0, chunks, prepare, 0)
    wo.forward(0)
    gain_sum_ref[...] = jnp.zeros_like(gain_sum_ref)
    sums_ref[...] = jnp.zeros_like(sums_ref)

    half_low = lax.broadcasted_iota(jnp.int32, (CHUNK // 2, BLOCK), 1) < 64
    quarter_low = lax.broadcasted_iota(jnp.int32, (BLOCK // 2, BLOCK), 1) < 64

    def share_attended(c):
        at = run(c, 1, CHUNK)
        mine = att.at(c, mp).start
        third = att_ref[at, BLOCK:].astype(f32)
        af_ref[pl.ds(pl.multiple_of(mine, CHUNK // 2), CHUNK), :] = att_ref[at, :BLOCK]
        beside_it = jnp.where(half_low, third[: CHUNK // 2], pltpu.roll(third[CHUNK // 2 :], 64, 1)).astype(bf16)
        af_ref[pl.ds(pl.multiple_of(mine + CHUNK, CHUNK // 2), CHUNK // 2), :] = beside_it
        att.start(c)

    def hidden_of(c):
        att.finish(c)
        hidden = low_ref[run(c, 1, CHUNK), :].astype(f32)
        for m in range(pieces):
            first = (c * 4 + m) * (CHUNK + CHUNK // 2)
            pair = af_ref[pl.ds(pl.multiple_of(first, CHUNK // 2), CHUNK), :]
            third = af_ref[pl.ds(pl.multiple_of(first + CHUNK, CHUNK // 2), CHUNK // 2), :]
            third = jnp.concatenate([third, pltpu.roll(third.astype(f32), 64, 1).astype(bf16)], axis=0)
            weights = wo_ref[m * width : (m + 1) * width, :]
            hidden = hidden + dot(jnp.concatenate([pair, third[:, :64]], axis=1), weights)
        nf_ref[run(c, 1, CHUNK), :] = (hidden * factor_of(hidden) * gain_f).astype(bf16)
        for m in range(pieces):

            @pl.when(mp == m)
            def _(m=m):
                hidden_ref[run(c), :] = hidden[m * BLOCK : (m + 1) * BLOCK]

    def grad_of(c):
        grad_normed = norm.finish(c)
        hidden = hidden_ref[run(c), :]
        factor = factor_of(hidden)
        hat = hidden * factor
        scaled = grad_normed * gain_f
        back = factor * (scaled - hat * jnp.mean(scaled * hat, axis=-1, keepdims=True))
        grad = cot_ref[place(mp, c), :].astype(f32) + back
        input_ref[run(c), :] = grad
        gain_sum_ref[0:1, :] += jnp.sum(grad_normed * hat, axis=0, keepdims=True)
        grad_low = grad.astype(bf16)
        ghl_ref[grads.at(c, mp), :] = grad_low

        def of(m):
            value = dot_nt(grad_low, wo_ref[run(m, 1, width), :])
            third = jnp.concatenate([value[:, BLOCK:], jnp.zeros((BLOCK, 64), f32)], axis=1)
            third = jnp.where(quarter_low, third[: BLOCK // 2], pltpu.roll(third[BLOCK // 2 :], 64, 1))
            return jnp.concatenate([value[:, :BLOCK], third], axis=0).astype(bf16)

        size = BLOCK + BLOCK // 2
        ga_ref[run(c * 4 + mp, 1, size), :] = of(mp)
        for d in (1, 2, 3):
            es_ref[run(c * 3 + d - 1, 1, size), :] = of((mp + d) % 4)
        grad_att.start(c)

    def attend(t, carry):
        c = t // heads
        h = t % heads
        query_far = jnp.concatenate([qa_ref[h, place(m, c), :] for m in range(pieces)], axis=0)
        query_near = jnp.concatenate([qb_ref[h, place(m, c), :] for m in range(pieces)], axis=0)
        query = jnp.concatenate([query_far, query_near], axis=1)
        for j in range(chunks):
            cols = slice(j * CHUNK, (j + 1) * CHUNK)
            s_ref[cols, :] = dot(query, jnp.concatenate([hot_t_ref[:, cols], kt2_ref[h, :, cols]], axis=0))
        for m in range(pieces):
            start, of = window(m, c)
            for i in range(3):
                panel = (start + i) // pieces
                s_ref[run(panel * 4 + m), run((start + i) % pieces)] += band_ref[h, :, run(of + i)].astype(f32)
        panels = [s_ref[j * CHUNK : (j + 1) * CHUNK, :] for j in range(chunks)]
        top = jnp.max(functools.reduce(jnp.maximum, panels), axis=1, keepdims=True)
        mixed = jnp.zeros((CHUNK, BLOCK), f32)
        for j in range(chunks):
            weights = jnp.exp(panels[j] - top).astype(bf16)
            mixed = mixed + dot(weights, v_ref[h, j * CHUNK : (j + 1) * CHUNK, :])
        res_ref[run(h, 1, CHUNK), :] = jnp.where(low, mixed / pltpu.roll(mixed, 64, 1), 0.0)
        high, middle, rest = split3(-(top + jnp.log(mixed[:, 64:65])))
        second = jnp.where(
            lanes == LSE,
            high,
            jnp.where(lanes == LSE + 1, middle, jnp.where(lanes == LSE + 2, rest, query_near.astype(f32))),
        )
        qt_ref[h, c, :BLOCK, :] = query_far.astype(f32).T.astype(bf16)
        qt_ref[h, c, BLOCK:, :] = second.T.astype(bf16)

        @pl.when(h == heads - 1)
        def _():
            pairs = []
            for g in range(0, heads, 2):
                pair = res_ref[g * CHUNK : (g + 1) * CHUNK, :]
                if g + 1 < heads:
                    pair = jnp.where(low, pair, pltpu.roll(res_ref[(g + 1) * CHUNK : (g + 2) * CHUNK, :], 64, 1))
                pairs.append(pair.astype(bf16))
            merged = jnp.concatenate(pairs, axis=1)
            att_ref[run(c, 1, CHUNK), :] = merged
            share_attended(c)

        @pl.when(t == 4)
        def _():
            att.forward(0)

        @pl.when(t == 7)
        def _():
            att.forward(1)

        return carry

    lax.fori_loop(0, chunks * heads, attend, 0)
    for load in loads[3:-1]:
        load.wait()
    wo.finish(0)

    steps = units // 256

    def feed_step(t, carry):
        c = t // steps
        b = t % steps

        @pl.when(b == 0)
        def _():
            hidden_of(c)

        at = run(b, 1, 256)
        x = nf_ref[run(c, 1, CHUNK), :]
        cot = jnp.concatenate([cot_ref[place(m, c), :] for m in range(pieces)], axis=0)
        inner_units = dot(x, w_inner_ref[:, at])
        grad_act = dot_nt(cot, w_outer_ref[at, :])
        square = inner_units * inner_units
        tanh = jnp.tanh(ROOT * inner_units * (1.0 + CUBE * square))
        half = 0.5 * (1.0 + tanh)
        slope = half + 0.5 * inner_units * (1.0 - tanh * tanh) * (ROOT + 3.0 * CUBE * ROOT * square)
        activated = (inner_units * half).astype(bf16)
        grad_low = (slope * grad_act).astype(bf16)
        low_ref[run(c, 1, CHUNK), at] = activated
        grad_low_ref[run(c, 1, CHUNK), at] = grad_low
        part_ffn = dot(activated, w_outer_ref[at, :])
        part_norm = dot_nt(grad_low, w_inner_ref[:, at])

        @pl.when(b == 0)
        def _():
            for p in range(chunks):
                s_ref[p * CHUNK : (p + 1) * CHUNK, :256] = part_ffn[:, p * 256 : (p + 1) * 256]
                s_ref[p * CHUNK : (p + 1) * CHUNK, 256:] = part_norm[:, p * 256 : (p + 1) * 256]

        @pl.when(b > 0)
        def _():
            for p in range(chunks):
                s_ref[p * CHUNK : (p + 1) * CHUNK, :256] += part_ffn[:, p * 256 : (p + 1) * 256]
                s_ref[p * CHUNK : (p + 1) * CHUNK, 256:] += part_norm[:, p * 256 : (p + 1) * 256]

        @pl.when(b == steps - 1)
        def _():
            for m in range(pieces):
                parts = [s_ref[p * CHUNK + m * BLOCK : p * CHUNK + (m + 1) * BLOCK, :] for p in range(chunks)]
                feed.put(c, m, jnp.concatenate([p[:, :256] for p in parts], axis=1))
                norm.put(c, m, jnp.concatenate([p[:, 256:] for p in parts], axis=1))
            norm.start(c)

        @pl.when(t == 1)
        def _():
            att.forward(2)

        @pl.when(t == 3)
        def _():
            norm.middle(0)

        @pl.when(t == 6)
        def _():
            norm.middle(1)

        @pl.when(t == 7)
        def _():
            grad_of(0)

        return carry

    lax.fori_loop(0, chunks * steps, feed_step, 0)

    def weights_of(is_outer):
        for b in range(2):
            at = slice(b * half_model, (b + 1) * half_model)
            total = jnp.zeros((half_model, units), f32)
            for c in range(chunks):
                if is_outer:
                    left = jnp.concatenate([cot_ref[place(m, c), at] for m in range(pieces)], axis=0)
                    total = total + dot_tn(left, low_ref[run(c, 1, CHUNK), :])
                else:
                    total = total + dot_tn(nf_ref[run(c, 1, CHUNK), at], grad_low_ref[run(c, 1, CHUNK), :])
            if fast:
                (outer if is_outer else inner).put(b * half_model, total)
            else:
                (o_outer_ref if is_outer else o_inner_ref)[at, :] = total

    weights_of(True)
    if fast:
        outer.start()
    norm.middle(2)
    grad_of(1)
    weights_of(False)
    wt_ref[...] = jnp.zeros_like(wt_ref)
    for k in range(3):
        for h in range(heads):
            wt_ref[h * 256 + k * 64 : h * 256 + (k + 1) * 64, :] = w_qkv_ref[k, h * 64 : (h + 1) * 64, :]

    def receive(c):
        grad_att.finish(c)
        at = run(c, 1, CHUNK)
        pairs, thirds = [], []
        for m in range(pieces):
            first = (c * 4 + m) * (BLOCK + BLOCK // 2)
            pairs.append(ga_ref[pl.ds(pl.multiple_of(first, BLOCK // 2), BLOCK), :])
            third = ga_ref[pl.ds(pl.multiple_of(first + BLOCK, BLOCK // 2), BLOCK // 2), :].astype(f32)
            thirds.extend([third, pltpu.roll(third, 64, 1)])
        received = [jnp.concatenate(pairs, axis=0).astype(f32), jnp.concatenate(thirds, axis=0)]
        for h in range(heads):
            pair = slice(h // 2 * BLOCK, h // 2 * BLOCK + BLOCK)
            grad = received[h // 2]
            out = att_ref[at, pair].astype(f32)
            if h % 2 == 1:
                grad = pltpu.roll(grad, 64, 1)
                out = pltpu.roll(out, 64, 1)
            high, middle, rest = split3(-jnp.sum(jnp.where(low, grad * out, 0.0), axis=1, keepdims=True))
            grad = jnp.where(
                low,
                grad,
                jnp.where(
                    lanes == FAR, high, jnp.where(lanes == FAR + 1, middle, jnp.where(lanes == FAR + 2, rest, 0.0))
                ),
            )
            da_ref[h, at, :] = grad.astype(bf16)
            dat_ref[h, :, at] = grad.T.astype(bf16)

    lines16 = lax.broadcasted_iota(jnp.int32, (16, rows), 0)
    block16 = lax.broadcasted_iota(jnp.int32, (16, rows), 1) // BLOCK
    start16 = jnp.clip(block16 - 1, 0, blocks - 3)
    real = lines16 < blocks
    tall_low = lax.broadcasted_iota(jnp.int32, (rows, BLOCK), 1) < 64

    def fold(value):
        total = value[:, :BLOCK]
        for b in range(1, value.shape[1] // BLOCK):
            total = total + value[:, b * BLOCK : (b + 1) * BLOCK]
        return jnp.sum(total, axis=0, keepdims=True)

    def mix(k):
        mixed_ref[run(k), :] = (hidden_ref[run(k), :] + feed.finish(k)).astype(bf16)

    def head(h, carry):
        dk_ref[...] = jnp.zeros_like(dk_ref)
        dv_ref[...] = jnp.zeros_like(dv_ref)
        bands_ref[...] = jnp.zeros_like(bands_ref)

        def chunk(c, carry):
            @pl.when(h == 0)
            def _():
                receive(c)

            at = run(c, 1, CHUNK)
            s_ref[...] = dot(jnp.concatenate([hot_ref[...], k2_ref[h]], axis=1), qt_ref[h, c])
            for m in range(pieces):
                start, of = window(m, c)
                s_ref[run(start, 3), m * BLOCK : (m + 1) * BLOCK] += band_t_ref[h, run(of, 3), :].astype(f32)
            probs = jnp.exp(s_ref[...])
            low_ref[:, :CHUNK] = probs.astype(bf16)
            grad_low_ref[:, :CHUNK] = (probs * dot(v_ref[h], dat_ref[h, :, at])).astype(bf16)
            probs_t = low_ref[:, :CHUNK]
            grad_t = grad_low_ref[:, :CHUNK]
            dv_ref[...] += dot(probs_t, da_ref[h, at, :])
            dk_ref[...] += dot(grad_t, jnp.concatenate([qb_ref[h, place(m, c), :] for m in range(pieces)], axis=0))
            dq_far = dot(hot_t_ref[...], grad_t)
            dq_near = dot(kt2_ref[h], grad_t)
            for m in range(pieces):
                dqt_ref[:BLOCK, place(m, c)] = dq_far[:, m * BLOCK : (m + 1) * BLOCK]
                dqt_ref[BLOCK:, place(m, c)] = dq_near[:, m * BLOCK : (m + 1) * BLOCK]
                start, of = window(m, c)
                bands_ref[run(of, 3), :] += grad_low_ref[run(start, 3), m * BLOCK : (m + 1) * BLOCK].astype(f32)

            def when(head_index, chunk_index):
                return pl.when((h == head_index) & (c == chunk_index))

            @when(0, 0)
            def _():
                grad_of(2)

            @when(0, 1)
            def _():
                for k in range(chunks):
                    grads.start(k)

            @when(0, 2)
            def _():
                for k in range(chunks):
                    feed.start(k)
                if fast:
                    outer.middle()
                    inner.start()

            @when(1, 0)
            def _():
                grads.forward(0)

            @when(1, 1)
            def _():
                grads.forward(1)
                if fast:
                    outer.third()

            @when(1, 2)
            def _():
                grads.forward(2)
                feed.middle(0)

            @when(2, 0)
            def _():
                feed.middle(1)
                if fast:
                    inner.middle()

            @when(2, 1)
            def _():
                feed.middle(2)
                mix(0)
                if fast:
                    qkv(0).middle()
                    o_outer_ref[...] = outer.finish()

            @when(2, 2)
            def _():
                mix(1)
                if fast:
                    inner.third()
                    output.middle()
                    qkv(0).third()
                    qkv(1).middle()

            return carry

        lax.fori_loop(0, chunks, chunk, 0)

        dq = dqt_ref[BLOCK:, :].T * 0.125
        grads_of = run(h, 1, 256)
        nf_ref[:, grads_of] = jnp.concatenate(
            [jnp.where(tall_low, dq, pltpu.roll(dk_ref[...], 64, 1)), jnp.where(tall_low, dv_ref[...], 0.0)], axis=1
        ).astype(bf16)
        for b in range(2):
            cols = slice(b * half_model, (b + 1) * half_model)
            grad_qkv = dot_tn(x1[:, cols], nf_ref[:, grads_of])
            if fast:
                qkv(h).put(b * half_model, grad_qkv)
            else:
                o_qkv_ref[h, cols, :] = grad_qkv
        if fast:
            qkv(h).start()

        @pl.when(h == 1)
        def _():
            for c in range(chunks):
                grads.finish(c)
            for b in range(2):
                cols = slice(b * half_model, (b + 1) * half_model)
                grad_output = dot_tn(ghl_ref[:, cols], att_ref[...])
                if fast:
                    output.put(b * half_model, grad_output)
                else:
                    o_output_ref[cols, :] = grad_output[:, :width]
            if fast:
                output.start()

        band = roll_rows(bands_ref[...].T, False)
        spread = dqt_ref[:BLOCK, :]
        high = spread.astype(bf16)
        rest = (spread - high.astype(f32)).astype(bf16)
        plane = (dot(high, hot_ref[...]) + dot(rest, hot_ref[...])).T
        plane = jnp.where((square_rows < CODES) == (square_lanes < CODES), plane, 0.0)
        plane = roll_rows(plane, False)
        far = dqt_ref[BLOCK + FAR : BLOCK + FAR + 16, :]
        line = jnp.concatenate(
            [
                jnp.sum(band, axis=0, keepdims=True),
                jnp.sum(plane[:CODES], axis=0, keepdims=True),
                jnp.sum(plane[CODES:], axis=0, keepdims=True),
                fold(jnp.where(real & (lines16 < start16), far, 0.0)),
                fold(jnp.where(real & (lines16 > start16 + 2), far, 0.0)),
            ],
            axis=1,
        )
        sums_ref[...] += jnp.where(lax.broadcasted_iota(jnp.int32, sums_ref.shape, 0) == h, line, 0.0)
        return carry

    lax.fori_loop(0, heads, head, 0)

    mix(2)
    credits = [(sibling, credit.at[0]), (across, credit.at[1])]
    for other, sem in credits:
        pl.semaphore_signal(
            sem, inc=1, device_id=(lax.axis_index("dp"), other), device_id_type=pl.DeviceIdType.MESH
        )
    loads[-1].start()
    for c in range(chunks):
        norm.drain(c)
    gain_total = jnp.zeros((1, model), f32)
    for c in range(chunks):
        for m in range(pieces):
            at = place(m, c)
            partial = dot(nf_ref[at, :], wt_ref[...])
            gain_total = gain_total + jnp.sum(partial * x1[at, :].astype(f32), axis=0, keepdims=True)
            last.put(c, m, partial)
        if c == 0:
            for _, sem in credits:
                pl.semaphore_wait(sem, 1)
        last.start(c)
        if c > 0:
            last.middle(c - 1)
    sums_ref[3:4, :model] = gain_total / gain_a
    sums_ref[4:5, :model] = gain_sum_ref[0:1, :]
    if fast:
        small.start(sums_ref[...])
        output.third()
        qkv(1).third()
    last.middle(chunks - 1)
    if fast:
        qkv(2).middle()
        small.turn(1)
        o_inner_ref[...] = inner.finish()
        small.turn(2)
        o_output_ref[...] = output.finish()[:, :width].T
    loads[-1].wait()
    for c in range(chunks):
        x = cot_ref[run(c), :].astype(f32)
        grad_normed = last.finish(c)
        factor = factor_of(x)
        hat = x * factor
        scaled = grad_normed * gain_a
        back = factor * (scaled - hat * jnp.mean(scaled * hat, axis=-1, keepdims=True))
        input_ref[run(c), :] += back
        if fast and c == 0:
            small.turn(3)
            qkv(2).third()
        if fast and c == 1:
            small.turn(4)
    if fast:
        low_each = lax.broadcasted_iota(jnp.int32, (model // 8, BLOCK), 1) < 64
        parts = [qkv(h).finish() for h in range(heads)]
        for k in range(3):
            for h in range(0, heads, 2):
                at = slice(0, BLOCK) if k < 2 else slice(BLOCK, 2 * BLOCK)
                one = parts[h][:, at]
                one = pltpu.roll(one, 64, 1) if k == 1 else one
                if h + 1 < heads:
                    two = parts[h + 1][:, at]
                    two = two if k == 1 else pltpu.roll(two, 64, 1)
                    o_qkv_ref[k, :, h * 64 : (h + 2) * 64] = jnp.where(low_each, one, two)
                else:
                    o_qkv_ref[k, :, h * 64 :] = one[:, :64]
        totals = small.finish()
        o_gain_a_ref[...] = totals[3:4, :model].reshape(model)
        o_gain_f_ref[...] = totals[4:5, :model].reshape(model)
        buckets = collapse()
        tables = sum(dot_nt(part.astype(bf16), buckets) for part in split3(small.value[3]))
        o_tables_ref[...] = tables[:heads]
        outer.drain()
        inner.drain()
        output.drain()
        for h in range(heads):
            qkv(h).drain()
        small.drain()
    else:
        o_sums_ref[...] = sums_ref[...]
    wo.drain(0)
    for c in range(chunks):
        for each in (att, grad_att, grads, feed, last):
            each.drain(c)


def spread_scratch(rows, columns, lead=(), own_part=True):
    buffers = [pltpu.VMEM((*lead, 8 * rows, columns), bf16)] if own_part else []
    return buffers + [
        pltpu.VMEM((*lead, 4 * rows, columns), bf16),
        pltpu.VMEM((*lead, 2 * rows, columns), bf16),
        pltpu.VMEM((*lead, rows, columns), bf16),
        pltpu.SemaphoreType.DMA((*lead, 3)),
        pltpu.SemaphoreType.DMA((*lead, 3)),
    ]


def local(
    fast,
    tokens, lengths, horizontal, vertical, gain_attn, w_qkv, bias_tables, w_output, gain_ffn, w_inner, w_outer, cotangent,
):
    rows, model = tokens.shape
    heads = bias_tables.shape[1]
    width = w_qkv.shape[2]
    units = w_inner.shape[1]
    share = rows // lax.axis_size("mp")
    chunks = rows // CHUNK
    each = model // 8
    sums = (8, WIDE + 4 * BLOCK)

    def dma(*shape):
        return pltpu.SemaphoreType.DMA(shape)

    def vmem(*shape, dtype=bf16):
        return pltpu.VMEM(shape, dtype)

    scratch = [
        vmem(rows, model), vmem(3, width, model), vmem(model, units), vmem(units, model),
        vmem(rows, model), dma(7 + 4 * chunks),
        vmem(8, rows, dtype=jnp.int32), vmem(heads, BLOCK, BLOCK), vmem(rows, BLOCK), vmem(BLOCK, rows), vmem(heads, rows, BLOCK),
        vmem(heads, rows, BLOCK), vmem(heads, rows, BLOCK), vmem(heads, BLOCK, rows), vmem(heads, rows, BLOCK),
        vmem(heads, BLOCK, WIDE), vmem(heads, WIDE, BLOCK),
        vmem(heads, chunks, 256, CHUNK),
        vmem(rows, CHUNK, dtype=f32), vmem(heads * CHUNK, BLOCK, dtype=f32), vmem(rows, BLOCK, dtype=f32),
        vmem(256, rows, dtype=f32), vmem(WIDE, BLOCK, dtype=f32), vmem(heads, BLOCK, rows),
        vmem(*sums, dtype=f32), vmem(8, model, dtype=f32),
        vmem(rows, 256), vmem(6 * rows, BLOCK), dma(chunks, 3), dma(chunks, 3),
        vmem(chunks * 9 * BLOCK // 2, BLOCK), vmem(chunks * 6 * BLOCK, BLOCK), dma(chunks, 3), dma(chunks, 3),
        vmem(4 * width, model), dma(1, 3), dma(1, 3),
        vmem(rows, model),
        vmem(rows, model), dma(chunks, 3), dma(chunks, 3),
        vmem(rows, model), dma(chunks, 2), dma(chunks, 2), vmem(rows, model), dma(chunks, 2), dma(chunks, 2),
        dma(chunks, 2), dma(chunks, 2), vmem(rows // 2, model), vmem(share, model),
        pltpu.SemaphoreType.REGULAR((2,)),
        vmem(rows, units), vmem(rows, units), vmem(share, model, dtype=f32),
    ]
    outs = [((share, model), bf16), ((share, model), f32)]
    if fast:
        outs += [
            ((3, each, width), f32), ((width, each), f32), ((each, units), f32), ((each, units), f32),
            ((model,), f32), ((model,), f32), ((heads, 3 * BUCKETS), f32),
        ]
        scratch += [
            *spread_scratch(each, units, own_part=False), *spread_scratch(each, units), *spread_scratch(each, 256),
            *spread_scratch(each, 256, lead=(heads,)),
            vmem(5, *sums, dtype=f32), vmem(5, *sums, dtype=f32), dma(5), dma(5),
        ]
    else:
        outs += [
            ((heads, model, 256), f32), ((model, width), f32), ((model, units), f32), ((model, units), f32), (sums, f32),
        ]
    full = pl.BlockSpec(memory_space=pltpu.VMEM)
    anywhere = pl.BlockSpec(memory_space=pl.ANY)
    results = pl.pallas_call(
        functools.partial(layer_kernel, fast),
        in_specs=[pl.BlockSpec(memory_space=pltpu.SMEM)] + [full] * 5 + [anywhere] * 6,
        out_specs=[full] * len(outs),
        out_shape=[jax.ShapeDtypeStruct(*out) for out in outs],
        scratch_shapes=scratch,
        compiler_params=pltpu.CompilerParams(vmem_limit_bytes=64 * MIB, collective_id=1, has_side_effects=True),
        name="layer",
    )(
        lengths, horizontal, vertical, gain_attn, gain_ffn, bias_tables.T,
        tokens, jnp.swapaxes(w_qkv, 1, 2), w_output, w_inner, w_outer, cotangent,
    )
    if fast:
        mixed, input_grad, qkv, output, inner, outer, gain_a, gain_f, tables = results
        return mixed, input_grad, qkv, output, inner, outer.T, gain_a, gain_f, tables.T
    mixed, input_grad, qkv, output, inner, outer, sums = results
    qkv = qkv[:, :, : 3 * 64].reshape(heads, model, 3, 64).transpose(2, 1, 0, 3).reshape(3, model, width)
    gains = lax.psum(sums[3:5, :model], ("dp", "mp"))
    tables = lax.dot_general(
        collapse().astype(f32),
        lax.psum(sums[:heads], "dp"),
        (((1,), (1,)), ((), ())),
        precision=lax.Precision.HIGHEST,
    )

    def spread(x, axis):
        return lax.psum_scatter(x, "dp", scatter_dimension=axis, tiled=True)

    return (
        mixed, input_grad, spread(qkv, 1), spread(output.T, 1), spread(inner, 0), spread(outer.T, 1),
        gains[0], gains[1], tables,
    )


def solution(mesh):
    fast = mesh.shape["dp"] == 8
    return jax.shard_map(
        functools.partial(local, fast),
        mesh=mesh,
        in_specs=(
            P("dp", None), P("dp"), P("dp"), P("dp"), P(), P(None, None, "mp"), P(None, "mp"), P("mp", None), P(),
            P(None, "mp"), P("mp", None), P("dp", None),
        ),
        out_specs=(
            P(("dp", "mp"), None), P(("dp", "mp"), None), P(None, "dp", "mp"), P("mp", "dp"), P("dp", "mp"),
            P("mp", "dp"), P(), P(), P(None, "mp"),
        ),
        check_vma=False,
    )
```

```python
import functools
import jax
import jax.numpy as jnp
import numpy as np
from jax import lax
from jax.experimental import pallas as pl
from jax.experimental.pallas import tpu as pltpu
from jax.sharding import PartitionSpec as P

BUCKETS = 32
CODES = 64
HALF = BUCKETS // 2
EPSILON = 1e-06
DEAD = -1e9
CHUNK = 512
BLOCK = 128
BAND = 3 * BLOCK
WIDE = 6 * BLOCK
FAR = 64
MASK = 76
LSE = 80
MIB = 2**20

f32 = jnp.float32
bf16 = jnp.bfloat16


def line_bucket(columns):
    line = jnp.clip(columns - 2 * BLOCK, -HALF, HALF - 1) + HALF
    line = jnp.where(columns < 5 * BLOCK, line, 0)
    wrapped = columns % BLOCK
    wrapped = jnp.where(wrapped < CODES, wrapped, wrapped - BLOCK)
    plane = jnp.clip(wrapped, -HALF, HALF - 1) + HALF
    return jnp.where(
        columns < WIDE, line, jnp.where(columns < WIDE + BLOCK, BUCKETS + plane, 2 * BUCKETS + plane)
    )


def expansion():
    rows = lax.broadcasted_iota(jnp.int32, (3 * BUCKETS, WIDE + 2 * BLOCK), 0)
    columns = lax.broadcasted_iota(jnp.int32, (3 * BUCKETS, WIDE + 2 * BLOCK), 1)
    return jnp.where(rows == line_bucket(columns), 1.0, 0.0).astype(bf16)


def collapse():
    rows = lax.broadcasted_iota(jnp.int32, (3 * BUCKETS, WIDE + 4 * BLOCK), 0)
    columns = lax.broadcasted_iota(jnp.int32, (3 * BUCKETS, WIDE + 4 * BLOCK), 1)
    bucket = line_bucket(columns)
    bucket = jnp.where(columns == 5 * BLOCK, BUCKETS - 1, bucket)
    bucket = jnp.where(columns >= WIDE + 2 * BLOCK, 0, bucket)
    bucket = jnp.where(columns >= WIDE + 3 * BLOCK, BUCKETS - 1, bucket)
    return jnp.where(rows == bucket, 1.0, 0.0).astype(bf16)


def roll_rows(value, right):
    rows, width = value.shape
    index = lax.broadcasted_iota(jnp.int32, value.shape, 0)
    step = 1
    while step < rows:
        shift = step if right else width - step
        value = jnp.where((index // step) % 2 == 1, pltpu.roll(value, shift, 1), value)
        step *= 2
    return value


def dot(a, b):
    return jnp.dot(a, b, preferred_element_type=f32)


def dot_nt(a, b):
    return lax.dot_general(a, b, (((1,), (1,)), ((), ())), preferred_element_type=f32)


def split3(value):
    high = value.astype(bf16).astype(f32)
    rest = value - high
    middle = rest.astype(bf16).astype(f32)
    return high, middle, rest - middle


def dot_tn(a, b):
    return lax.dot_general(a, b, (((0,), (0,)), ((), ())), preferred_element_type=f32)


ROOT = float(np.sqrt(2.0 / np.pi))
CUBE = 0.044715


def factor_of(rows):
    return lax.rsqrt(jnp.mean(rows * rows, axis=-1, keepdims=True) + EPSILON)


def mp_places():
    mp = lax.axis_index("mp")
    y, core = mp // 2, mp % 2
    return mp, y, core, y * 2 + (1 - core), (1 - y) * 2 + core


def dp_places():
    dp = lax.axis_index("dp")
    return dp // 2, dp % 2


def remote(src, dst, send, recv, mp=None, dp=None):
    return pltpu.make_async_remote_copy(
        src_ref=src,
        dst_ref=dst,
        send_sem=send,
        recv_sem=recv,
        device_id=(lax.axis_index("dp") if dp is None else dp, lax.axis_index("mp") if mp is None else mp),
        device_id_type=pl.DeviceIdType.MESH,
    )


def beside(z):
    return z // 2 * 2 + 1 - z % 2


def meet(fast):
    mp, dp = lax.axis_index("mp"), lax.axis_index("dp")
    z, x = dp_places()
    others = [(dp, (mp + d) % 4) for d in (1, 2, 3)]
    if fast:
        others.extend([(z * 2 + 1 - x, mp), (beside(z) * 2 + x, mp), ((z + 2) % 4 * 2 + x, mp)])
    barrier = pltpu.get_barrier_semaphore()
    for other in others:
        pl.semaphore_signal(barrier, inc=1, device_id=other, device_id_type=pl.DeviceIdType.MESH)
    pl.semaphore_wait(barrier, len(others))


def run(index, count=1, size=BLOCK):
    return pl.ds(pl.multiple_of(index * size, size), count * size)


class Scatter:

    def __init__(self, part, near, far, send, recv):
        self.part, self.near, self.far, self.send, self.recv = part, near, far, send, recv

    def block(self, c, core, y):
        return (c * 2 + core) * 2 + y

    def put(self, c, m, value, columns=slice(None)):
        self.part[run(self.block(c, m % 2, m // 2)), columns] = value.astype(bf16)

    def first(self, c):
        _, _, core, sibling, _ = mp_places()
        src = self.part.at[run(self.block(c, 1 - core, 0), 2)]
        return remote(src, self.near.at[run(c * 2, 2)], self.send.at[c, 0], self.recv.at[c, 0], sibling)

    def second(self, c):
        _, y, core, _, across = mp_places()
        src = self.part.at[run(self.block(c, core, 1 - y))]
        return remote(src, self.far.at[run(c)], self.send.at[c, 1], self.recv.at[c, 1], across)

    def start(self, c):
        self.first(c).start()

    def middle(self, c):
        _, y, core, _, _ = mp_places()
        self.first(c).wait_recv()
        at = run(self.block(c, core, 1 - y))
        self.part[at, :] = (self.part[at, :].astype(f32) + self.near[run(c * 2 + 1 - y), :].astype(f32)).astype(bf16)
        self.second(c).start()

    def finish(self, c):
        _, y, core, _, _ = mp_places()
        self.second(c).wait_recv()
        own = self.part[run(self.block(c, core, y)), :].astype(f32) + self.near[run(c * 2 + y), :].astype(f32)
        return own + self.far[run(c), :].astype(f32)

    def drain(self, c):
        self.first(c).wait_send()
        self.second(c).wait_send()


class Gather:

    def __init__(self, full, send, recv, size=BLOCK):
        self.full, self.send, self.recv, self.size = full, send, recv, size

    def at(self, c, m):
        return run(c * 4 + m, 1, self.size)

    def copy(self, c, kind):
        mp, _, _, sibling, across = mp_places()
        at = self.full.at[self.at(c, across if kind == 2 else mp)]
        return remote(at, at, self.send.at[c, kind], self.recv.at[c, kind], across if kind == 1 else sibling)

    def start(self, c):
        self.copy(c, 1).start()
        self.copy(c, 0).start()

    def forward(self, c):
        self.copy(c, 1).wait_recv()
        self.copy(c, 2).start()

    def finish(self, c):
        self.copy(c, 0).wait_recv()
        self.copy(c, 2).wait_recv()

    def drain(self, c):
        for kind in range(3):
            self.copy(c, kind).wait_send()


class Exchange:

    def __init__(self, given, taken, size, send, recv):
        self.given, self.taken, self.size, self.send, self.recv = given, taken, size, send, recv

    def copy(self, c, d):
        mp = lax.axis_index("mp")
        src = self.given.at[run(c * 3 + d - 1, 1, self.size)]
        dst = self.taken.at[run(c * 4 + mp, 1, self.size)]
        return remote(src, dst, self.send.at[c, d - 1], self.recv.at[c, d - 1], (mp + d) % 4)

    def start(self, c):
        for d in (2, 1, 3):
            self.copy(c, d).start()

    def finish(self, c):
        for d in (1, 2, 3):
            self.copy(c, d).wait_recv()

    def drain(self, c):
        for d in (1, 2, 3):
            self.copy(c, d).wait_send()


class Spread:

    def __init__(self, part, near, pair, far, send, recv):
        self.part, self.near, self.pair, self.far, self.send, self.recv = part, near, pair, far, send, recv
        self.each = part.shape[0] // 8

    def at(self, index, count=1):
        return run(index, count, self.each)

    def put(self, first_row, value):
        for r in range(value.shape[0] // self.each):
            j = first_row // self.each + r
            rows = value[r * self.each : (r + 1) * self.each]
            self.part[self.at(j % 2 * 4 + j // 2 % 2 * 2 + j // 4), :] = rows.astype(bf16)

    def copy(self, kind):
        z, x = dp_places()
        send, recv = self.send.at[kind], self.recv.at[kind]
        if kind == 0:
            src = self.part.at[self.at((1 - x) * 4, 4)]
            return remote(src, self.near, send, recv, dp=z * 2 + 1 - x)
        if kind == 1:
            src = self.part.at[self.at(x * 4 + (1 - z % 2) * 2, 2)]
            return remote(src, self.pair, send, recv, dp=beside(z) * 2 + x)
        src = self.part.at[self.at(x * 4 + z % 2 * 2 + 1 - z // 2)]
        return remote(src, self.far, send, recv, dp=(z + 2) % 4 * 2 + x)

    def start(self):
        self.copy(0).start()

    def middle(self):
        z, x = dp_places()
        self.copy(0).wait_recv()
        at = self.at(x * 4 + (1 - z % 2) * 2, 2)
        near = self.near[self.at((1 - z % 2) * 2, 2), :].astype(f32)
        self.part[at, :] = (self.part[at, :].astype(f32) + near).astype(bf16)
        self.copy(1).start()

    def sum_of(self, half):
        z, x = dp_places()
        total = self.part[self.at(x * 4 + z % 2 * 2 + half), :].astype(f32)
        total = total + self.near[self.at(z % 2 * 2 + half), :].astype(f32)
        return total + self.pair[self.at(half), :].astype(f32)

    def third(self):
        z, x = dp_places()
        self.copy(1).wait_recv()
        self.part[self.at(x * 4 + z % 2 * 2 + 1 - z // 2), :] = self.sum_of(1 - z // 2).astype(bf16)
        self.copy(2).start()

    def finish(self):
        z, _ = dp_places()
        self.copy(2).wait_recv()
        return self.sum_of(z // 2) + self.far[...].astype(f32)

    def drain(self):
        for kind in range(3):
            self.copy(kind).wait_send()


class Total:

    def __init__(self, value, taken, send, recv):
        self.value, self.taken, self.send, self.recv = value, taken, send, recv

    def copy(self, kind):
        z, x = dp_places()
        _, _, _, sibling, across = mp_places()
        mp = {3: sibling, 4: across}.get(kind)
        dp = {0: z * 2 + 1 - x, 1: beside(z) * 2 + x, 2: (z + 2) % 4 * 2 + x}.get(kind)
        return remote(self.value.at[kind], self.taken.at[kind], self.send.at[kind], self.recv.at[kind], mp, dp)

    def start(self, value):
        self.value[0] = value
        self.copy(0).start()

    def turn(self, kind):
        self.copy(kind - 1).wait_recv()
        self.value[kind] = self.value[kind - 1] + self.taken[kind - 1]
        self.copy(kind).start()

    def finish(self):
        self.copy(4).wait_recv()
        return self.value[4] + self.taken[4]

    def drain(self):
        for kind in range(5):
            self.copy(kind).wait_send()


def layer_kernel(
    fast,
    length_ref, across_ref, upward_ref, gain_a_ref, gain_f_ref, tables_ref,
    tokens_hbm, w_qkv_hbm, w_output_hbm, w_inner_hbm, w_outer_hbm, cot_hbm,
    *rest,
):
    outs, scratch = rest[: 9 if fast else 7], rest[9 if fast else 7 :]
    if fast:
        mixed_ref, input_ref, o_qkv_ref, o_output_ref, o_inner_ref, o_outer_ref, o_gain_a_ref, o_gain_f_ref, o_tables_ref = outs
    else:
        mixed_ref, input_ref, o_qkv_ref, o_output_ref, o_inner_ref, o_outer_ref, o_sums_ref = outs
    (
        x1, w_qkv_ref, w_inner_ref, w_outer_ref, cot_ref, load_sem,
        codes_ref, plane_ref, hot_ref, hot_t_ref, qa_ref, qb_ref, k2_ref, kt2_ref, v_ref, band_ref, band_t_ref, qt_ref,
        s_ref, res_ref, dv_ref, dqt_ref, bands_ref, dat_ref, sums_ref, gain_sum_ref,
        att_ref, af_ref, att_send, att_recv,
        es_ref, ga_ref, es_send, es_recv,
        wo_ref, wo_send, wo_recv,
        nf_ref,
        ghl_ref, ghl_send, ghl_recv,
        feed_part, feed_send, feed_recv, norm_part, norm_send, norm_recv, last_send, last_recv, near_ref, far_ref,
        credit,
        low_ref, grad_low_ref, hidden_ref,
        *spreads,
    ) = scratch
    heads = tables_ref.shape[0]
    rows, model = x1.shape
    width = heads * 64
    units = w_inner_ref.shape[1]
    pieces = 4
    chunks = rows // CHUNK
    blocks = rows // BLOCK
    half_model = model // 2
    mp, _, _, sibling, across = mp_places()
    da_ref, dk_ref, wt_ref = qa_ref, res_ref, w_inner_ref

    att = Gather(af_ref, att_send, att_recv, CHUNK + CHUNK // 2)
    grad_att = Exchange(es_ref, ga_ref, BLOCK + BLOCK // 2, es_send, es_recv)
    wo = Gather(wo_ref, wo_send, wo_recv, width)
    grads = Gather(ghl_ref, ghl_send, ghl_recv)
    feed = Scatter(feed_part, near_ref, far_ref, feed_send, feed_recv)
    norm = Scatter(norm_part, near_ref, far_ref, norm_send, norm_recv)
    last = Scatter(norm_part, near_ref, far_ref, last_send, last_recv)
    if fast:
        outer = Spread(w_outer_ref, *spreads[0:5])
        inner = Spread(*spreads[5:11])
        output = Spread(*spreads[11:17])
        small = Total(*spreads[23:27])

        def qkv(h):
            return Spread(*[ref.at[h] for ref in spreads[17:23]])

    def place(m, c):
        return run(m * chunks + c)

    loads = [
        pltpu.make_async_copy(src, dst, load_sem.at[i])
        for i, (src, dst) in enumerate(
            [
                (tokens_hbm, x1),
                (w_qkv_hbm, w_qkv_ref),
                (w_output_hbm, wo_ref.at[wo.at(0, mp)]),
                (w_inner_hbm, w_inner_ref),
                (w_outer_hbm, w_outer_ref),
                (cot_hbm, cot_ref),
                *[(tokens_hbm.at[place(m, c)], low_ref.at[run(c * 4 + m)]) for c in range(chunks) for m in range(4)],
                (tokens_hbm.at[run(mp * chunks, chunks)], cot_ref.at[run(0, chunks)]),
            ]
        )
    ]
    for load in loads[:-1]:
        load.start()
    meet(fast)

    def window(m, c):
        block = m * chunks + c
        start = min(max(block - 1, 0), blocks - 3)
        return range(start, start + 3), 2 - block


    expanded = dot(tables_ref[...], expansion())
    square_rows = lax.broadcasted_iota(jnp.int32, (BLOCK, BLOCK), 0)
    square_lanes = lax.broadcasted_iota(jnp.int32, (BLOCK, BLOCK), 1)
    for h in range(heads):
        line = jnp.broadcast_to(expanded[h : h + 1, :WIDE], (BLOCK, WIDE))
        band = roll_rows(line, True)
        band_ref[h] = band.astype(bf16)
        band_t_ref[h] = band.T.astype(bf16)
        level = roll_rows(jnp.broadcast_to(expanded[h : h + 1, WIDE : WIDE + BLOCK], (BLOCK, BLOCK)), True)
        upward = roll_rows(jnp.broadcast_to(expanded[h : h + 1, WIDE + BLOCK :], (BLOCK, BLOCK)), True)
        plane = jnp.where(
            (square_rows < CODES) & (square_lanes < CODES),
            level,
            jnp.where((square_rows >= CODES) & (square_lanes >= CODES), upward, 0.0),
        )
        plane_ref[h] = plane.astype(bf16)
    loads[2].wait()
    wo.start(0)
    loads[1].wait()
    loads[0].wait()
    gain_a = gain_a_ref[...].reshape(1, model).astype(f32)
    gain_f = gain_f_ref[...].reshape(1, model).astype(f32)
    codes_ref[0:1, :] = across_ref[...].reshape(1, rows)
    codes_ref[1:2, :] = upward_ref[...].reshape(1, rows)
    lanes = lax.broadcasted_iota(jnp.int32, (CHUNK, BLOCK), 1)
    low = lanes < FAR

    def prepare(j, carry):
        at = run(j, 1, CHUNK)
        x = x1[at, :].astype(f32)
        normed_rows = (x * factor_of(x) * gain_a).astype(bf16)
        x1[at, :] = normed_rows
        codes_lines = lax.broadcasted_iota(jnp.int32, (BLOCK, CHUNK), 0)
        hot_t = jnp.where(
            codes_lines == jnp.broadcast_to(codes_ref[0:1, at], (BLOCK, CHUNK)),
            1.0,
            jnp.where(codes_lines - CODES == jnp.broadcast_to(codes_ref[1:2, at], (BLOCK, CHUNK)), 1.0, 0.0),
        )
        hot = hot_t.T.astype(bf16)
        hot_t_ref[:, at] = hot_t.astype(bf16)
        hot_ref[at, :] = hot
        row = lax.broadcasted_iota(jnp.int32, (CHUNK, BLOCK), 0) + j * CHUNK
        block = row // BLOCK
        start = jnp.clip(block - 1, 0, blocks - 3)
        far = (lanes >= FAR) & (lanes < MASK)
        far_left = far & (lanes - FAR < start)
        far_right = far & (lanes - FAR > start + 2)
        key_side = jnp.where(
            (far & (lanes - FAR == block))
            | ((lanes == MASK) & (row >= length_ref[0]))
            | ((lanes >= LSE) & (lanes < LSE + 3)),
            1.0,
            0.0,
        )

        def part(h):
            columns = s_ref[:CHUNK, h // 2 * BLOCK : h // 2 * BLOCK + BLOCK]
            return columns if h % 2 == 0 else pltpu.roll(columns, 64, 1)

        s_ref[:CHUNK, :width] = dot_nt(normed_rows, w_qkv_ref[0])
        for h in range(heads):
            left = expanded[h : h + 1, 0:1]
            right = expanded[h : h + 1, WIDE - BLOCK - 1 : WIDE - BLOCK]
            query_side = jnp.where(far_left, left, jnp.where(far_right, right, jnp.where(lanes == MASK, DEAD, 0.0)))
            qa_ref[h, at, :] = dot(hot, plane_ref[h]).astype(bf16)
            qb_ref[h, at, :] = jnp.where(low, part(h).astype(bf16).astype(f32) * 0.125, query_side).astype(bf16)
        s_ref[:CHUNK, :width] = dot_nt(normed_rows, w_qkv_ref[1])
        for h in range(heads):
            second = jnp.where(low, part(h), key_side)
            k2_ref[h, at, :] = second.astype(bf16)
            kt2_ref[h, :, at] = second.T.astype(bf16)
        s_ref[:CHUNK, :width] = dot_nt(normed_rows, w_qkv_ref[2])
        for h in range(heads):
            v_ref[h, at, :] = jnp.where(low, part(h), 1.0).astype(bf16)
        return carry

    s_ref[:CHUNK, :] = jnp.zeros_like(s_ref[:CHUNK, :])
    lax.fori_loop(0, chunks, prepare, 0)
    wo.forward(0)
    gain_sum_ref[...] = jnp.zeros_like(gain_sum_ref)
    sums_ref[...] = jnp.zeros_like(sums_ref)

    half_low = lax.broadcasted_iota(jnp.int32, (CHUNK // 2, BLOCK), 1) < 64
    quarter_low = lax.broadcasted_iota(jnp.int32, (BLOCK // 2, BLOCK), 1) < 64

    def share_attended(c):
        at = run(c, 1, CHUNK)
        mine = att.at(c, mp).start
        third = att_ref[at, BLOCK:].astype(f32)
        af_ref[pl.ds(pl.multiple_of(mine, CHUNK // 2), CHUNK), :] = att_ref[at, :BLOCK]
        beside_it = jnp.where(half_low, third[: CHUNK // 2], pltpu.roll(third[CHUNK // 2 :], 64, 1)).astype(bf16)
        af_ref[pl.ds(pl.multiple_of(mine + CHUNK, CHUNK // 2), CHUNK // 2), :] = beside_it
        att.start(c)

    def hidden_of(c):
        att.finish(c)
        hidden = low_ref[run(c, 1, CHUNK), :].astype(f32)
        for m in range(pieces):
            first = (c * 4 + m) * (CHUNK + CHUNK // 2)
            pair = af_ref[pl.ds(pl.multiple_of(first, CHUNK // 2), CHUNK), :]
            third = af_ref[pl.ds(pl.multiple_of(first + CHUNK, CHUNK // 2), CHUNK // 2), :]
            third = jnp.concatenate([third, pltpu.roll(third.astype(f32), 64, 1).astype(bf16)], axis=0)
            weights = wo_ref[m * width : (m + 1) * width, :]
            hidden = hidden + dot(jnp.concatenate([pair, third[:, :64]], axis=1), weights)
        nf_ref[run(c, 1, CHUNK), :] = (hidden * factor_of(hidden) * gain_f).astype(bf16)
        for m in range(pieces):

            @pl.when(mp == m)
            def _(m=m):
                hidden_ref[run(c), :] = hidden[m * BLOCK : (m + 1) * BLOCK]

    def grad_of(c):
        grad_normed = norm.finish(c)
        hidden = hidden_ref[run(c), :]
        factor = factor_of(hidden)
        hat = hidden * factor
        scaled = grad_normed * gain_f
        back = factor * (scaled - hat * jnp.mean(scaled * hat, axis=-1, keepdims=True))
        grad = cot_ref[place(mp, c), :].astype(f32) + back
        input_ref[run(c), :] = grad
        gain_sum_ref[0:1, :] += jnp.sum(grad_normed * hat, axis=0, keepdims=True)
        grad_low = grad.astype(bf16)
        ghl_ref[grads.at(c, mp), :] = grad_low

        def of(m):
            value = dot_nt(grad_low, wo_ref[run(m, 1, width), :])
            third = jnp.concatenate([value[:, BLOCK:], jnp.zeros((BLOCK, 64), f32)], axis=1)
            third = jnp.where(quarter_low, third[: BLOCK // 2], pltpu.roll(third[BLOCK // 2 :], 64, 1))
            return jnp.concatenate([value[:, :BLOCK], third], axis=0).astype(bf16)

        size = BLOCK + BLOCK // 2
        ga_ref[run(c * 4 + mp, 1, size), :] = of(mp)
        for d in (1, 2, 3):
            es_ref[run(c * 3 + d - 1, 1, size), :] = of((mp + d) % 4)
        grad_att.start(c)

    def attend(c, h, carry):
        query_far = jnp.concatenate([qa_ref[h, place(m, c), :] for m in range(pieces)], axis=0)
        query_near = jnp.concatenate([qb_ref[h, place(m, c), :] for m in range(pieces)], axis=0)
        query = jnp.concatenate([query_far, query_near], axis=1)
        tops, mixes = [], []
        for j in range(chunks):
            cols = slice(j * CHUNK, (j + 1) * CHUNK)
            s = dot(query, jnp.concatenate([hot_t_ref[:, cols], kt2_ref[h, :, cols]], axis=0))
            lines = []
            for m in range(pieces):
                near, shift = window(m, c)
                tiles = []
                for b in range(pieces):
                    tile = s[m * BLOCK : (m + 1) * BLOCK, b * BLOCK : (b + 1) * BLOCK]
                    if j * pieces + b in near:
                        at = (j * pieces + b + shift) * BLOCK
                        tile = tile + band_ref[h, :, at : at + BLOCK].astype(f32)
                    tiles.append(tile)
                lines.append(jnp.concatenate(tiles, axis=1))
            s = jnp.concatenate(lines, axis=0)
            tops.append(jnp.max(s, axis=1, keepdims=True))
            mixes.append(dot(jnp.exp(s - tops[j]).astype(bf16), v_ref[h, cols, :]))
        top = functools.reduce(jnp.maximum, tops)
        mixed = sum(mix * jnp.exp(part - top) for mix, part in zip(mixes, tops))
        res_ref[run(h, 1, CHUNK), :] = jnp.where(low, mixed / pltpu.roll(mixed, 64, 1), 0.0)
        high, middle, rest = split3(-(top + jnp.log(mixed[:, 64:65])))
        second = jnp.where(
            lanes == LSE,
            high,
            jnp.where(lanes == LSE + 1, middle, jnp.where(lanes == LSE + 2, rest, query_near.astype(f32))),
        )
        qt_ref[h, c, :BLOCK, :] = query_far.astype(f32).T.astype(bf16)
        qt_ref[h, c, BLOCK:, :] = second.T.astype(bf16)

        if c > 0:

            @pl.when(h == 1)
            def _():
                att.forward(c - 1)

        return carry

    for c in range(chunks):
        lax.fori_loop(0, heads, functools.partial(attend, c), 0)
        pairs = []
        for g in range(0, heads, 2):
            pair = res_ref[g * CHUNK : (g + 1) * CHUNK, :]
            if g + 1 < heads:
                pair = jnp.where(low, pair, pltpu.roll(res_ref[(g + 1) * CHUNK : (g + 2) * CHUNK, :], 64, 1))
            pairs.append(pair.astype(bf16))
        att_ref[run(c, 1, CHUNK), :] = jnp.concatenate(pairs, axis=1)
        share_attended(c)
    for load in loads[3:-1]:
        load.wait()
    wo.finish(0)

    steps = units // 256

    def feed_step(t, carry):
        c = t // steps
        b = t % steps

        @pl.when(b == 0)
        def _():
            hidden_of(c)

        at = run(b, 1, 256)
        x = nf_ref[run(c, 1, CHUNK), :]
        cot = jnp.concatenate([cot_ref[place(m, c), :] for m in range(pieces)], axis=0)
        inner_units = dot(x, w_inner_ref[:, at])
        grad_act = dot_nt(cot, w_outer_ref[at, :])
        square = inner_units * inner_units
        tanh = jnp.tanh(ROOT * inner_units * (1.0 + CUBE * square))
        half = 0.5 * (1.0 + tanh)
        slope = half + 0.5 * inner_units * (1.0 - tanh * tanh) * (ROOT + 3.0 * CUBE * ROOT * square)
        activated = (inner_units * half).astype(bf16)
        grad_low = (slope * grad_act).astype(bf16)
        low_ref[run(c, 1, CHUNK), at] = activated
        grad_low_ref[run(c, 1, CHUNK), at] = grad_low

        @pl.when(b == steps - 1)
        def _():
            chunk_rows = run(c, 1, CHUNK)
            for p in range(model // 256):
                cols = slice(p * 256, (p + 1) * 256)
                part_norm = dot_nt(grad_low_ref[chunk_rows, :], w_inner_ref[cols, :])
                part_ffn = dot(low_ref[chunk_rows, :], w_outer_ref[:, cols])
                for m in range(pieces):
                    norm.put(c, m, part_norm[m * BLOCK : (m + 1) * BLOCK], cols)
                    feed.put(c, m, part_ffn[m * BLOCK : (m + 1) * BLOCK], cols)
            norm.start(c)

        @pl.when(t == 1)
        def _():
            att.forward(2)

        @pl.when(t == 3)
        def _():
            norm.middle(0)

        @pl.when(t == 6)
        def _():
            norm.middle(1)

        @pl.when(t == 7)
        def _():
            grad_of(0)

        return carry

    lax.fori_loop(0, chunks * steps, feed_step, 0)

    def weights_of(is_outer):
        for b in range(2):
            at = slice(b * half_model, (b + 1) * half_model)
            total = jnp.zeros((half_model, units), f32)
            for c in range(chunks):
                if is_outer:
                    left = jnp.concatenate([cot_ref[place(m, c), at] for m in range(pieces)], axis=0)
                    total = total + dot_tn(left, low_ref[run(c, 1, CHUNK), :])
                else:
                    total = total + dot_tn(nf_ref[run(c, 1, CHUNK), at], grad_low_ref[run(c, 1, CHUNK), :])
            if fast:
                (outer if is_outer else inner).put(b * half_model, total)
            else:
                (o_outer_ref if is_outer else o_inner_ref)[at, :] = total

    weights_of(True)
    if fast:
        outer.start()
    norm.middle(2)
    grad_of(1)
    weights_of(False)
    wt_ref[...] = jnp.zeros_like(wt_ref)
    for k in range(3):
        for h in range(heads):
            wt_ref[h * 256 + k * 64 : h * 256 + (k + 1) * 64, :] = w_qkv_ref[k, h * 64 : (h + 1) * 64, :]

    def receive(c):
        grad_att.finish(c)
        at = run(c, 1, CHUNK)
        pairs, thirds = [], []
        for m in range(pieces):
            first = (c * 4 + m) * (BLOCK + BLOCK // 2)
            pairs.append(ga_ref[pl.ds(pl.multiple_of(first, BLOCK // 2), BLOCK), :])
            third = ga_ref[pl.ds(pl.multiple_of(first + BLOCK, BLOCK // 2), BLOCK // 2), :].astype(f32)
            thirds.extend([third, pltpu.roll(third, 64, 1)])
        received = [jnp.concatenate(pairs, axis=0).astype(f32), jnp.concatenate(thirds, axis=0)]
        for h in range(heads):
            pair = slice(h // 2 * BLOCK, h // 2 * BLOCK + BLOCK)
            grad = received[h // 2]
            out = att_ref[at, pair].astype(f32)
            if h % 2 == 1:
                grad = pltpu.roll(grad, 64, 1)
                out = pltpu.roll(out, 64, 1)
            high, middle, rest = split3(-jnp.sum(jnp.where(low, grad * out, 0.0), axis=1, keepdims=True))
            grad = jnp.where(
                low,
                grad,
                jnp.where(
                    lanes == FAR, high, jnp.where(lanes == FAR + 1, middle, jnp.where(lanes == FAR + 2, rest, 0.0))
                ),
            )
            da_ref[h, at, :] = grad.astype(bf16)
            dat_ref[h, :, at] = grad.T.astype(bf16)

    lines16 = lax.broadcasted_iota(jnp.int32, (16, rows), 0)
    block16 = lax.broadcasted_iota(jnp.int32, (16, rows), 1) // BLOCK
    start16 = jnp.clip(block16 - 1, 0, blocks - 3)
    real = lines16 < blocks
    tall_low = lax.broadcasted_iota(jnp.int32, (rows, BLOCK), 1) < 64

    def fold(value):
        total = value[:, :BLOCK]
        for b in range(1, value.shape[1] // BLOCK):
            total = total + value[:, b * BLOCK : (b + 1) * BLOCK]
        return jnp.sum(total, axis=0, keepdims=True)

    def mix(k):
        mixed_ref[run(k), :] = (hidden_ref[run(k), :] + feed.finish(k)).astype(bf16)

    def events(h, c):
        if c == 0:

            @pl.when(h == 0)
            def _():
                grad_of(2)

        if c == 1:

            @pl.when(h == 0)
            def _():
                for k in range(chunks):
                    grads.start(k)

        if c == 2:

            @pl.when(h == 0)
            def _():
                for k in range(chunks):
                    feed.start(k)
                if fast:
                    outer.middle()
                    inner.start()

        if c == 0:

            @pl.when(h == 1)
            def _():
                grads.forward(0)

        if c == 1:

            @pl.when(h == 1)
            def _():
                grads.forward(1)
                if fast:
                    outer.third()

        if c == 2:

            @pl.when(h == 1)
            def _():
                grads.forward(2)
                feed.middle(0)

        if c == 0:

            @pl.when(h == 2)
            def _():
                feed.middle(1)
                if fast:
                    inner.middle()

        if c == 1:

            @pl.when(h == 2)
            def _():
                feed.middle(2)
                mix(0)
                if fast:
                    qkv(0).middle()
                    o_outer_ref[...] = outer.finish()

        if c == 2:

            @pl.when(h == 2)
            def _():
                mix(1)
                if fast:
                    inner.third()
                    output.middle()
                    qkv(0).third()
                    qkv(1).middle()

    def head(h, carry):
        dk_ref[...] = jnp.zeros_like(dk_ref)
        dv_ref[...] = jnp.zeros_like(dv_ref)
        bands_ref[...] = jnp.zeros_like(bands_ref)

        for c in range(chunks):

            @pl.when(h == 0)
            def _(c=c):
                receive(c)

            at = slice(c * CHUNK, (c + 1) * CHUNK)
            query = jnp.concatenate([qb_ref[h, place(m, c), :] for m in range(pieces)], axis=0)
            for j in range(chunks):
                keys = slice(j * CHUNK, (j + 1) * CHUNK)
                s = dot(jnp.concatenate([hot_ref[keys, :], k2_ref[h, keys, :]], axis=1), qt_ref[h, c])
                columns = []
                for m in range(pieces):
                    near, shift = window(m, c)
                    tiles = []
                    for b in range(pieces):
                        tile = s[b * BLOCK : (b + 1) * BLOCK, m * BLOCK : (m + 1) * BLOCK]
                        if j * pieces + b in near:
                            of = (j * pieces + b + shift) * BLOCK
                            tile = tile + band_t_ref[h, of : of + BLOCK, :].astype(f32)
                        tiles.append(tile)
                    columns.append(jnp.concatenate(tiles, axis=0))
                probs = jnp.exp(jnp.concatenate(columns, axis=1))
                probs_t = probs.astype(bf16)
                grad_t = (probs * dot(v_ref[h, keys, :], dat_ref[h, :, at])).astype(bf16)
                grad_low_ref[keys, :CHUNK] = grad_t
                dv_ref[keys, :] += dot(probs_t, da_ref[h, at, :])
                dk_ref[keys, :] += dot(grad_t, query)
            dq = dot(jnp.concatenate([hot_t_ref[...], kt2_ref[h]], axis=0), grad_low_ref[:, :CHUNK])
            for m in range(pieces):
                dqt_ref[:, place(m, c)] = dq[:, m * BLOCK : (m + 1) * BLOCK]
                near, shift = window(m, c)
                of = slice((near.start + shift) * BLOCK, (near.stop + shift) * BLOCK)
                keys = slice(near.start * BLOCK, near.stop * BLOCK)
                bands_ref[of, :] += grad_low_ref[keys, m * BLOCK : (m + 1) * BLOCK].astype(f32)
            events(h, c)

        dq = dqt_ref[BLOCK:, :].T * 0.125
        grads_of = run(h, 1, 256)
        nf_ref[:, grads_of] = jnp.concatenate(
            [jnp.where(tall_low, dq, pltpu.roll(dk_ref[...], 64, 1)), jnp.where(tall_low, dv_ref[...], 0.0)], axis=1
        ).astype(bf16)
        for b in range(2):
            cols = slice(b * half_model, (b + 1) * half_model)
            grad_qkv = dot_tn(x1[:, cols], nf_ref[:, grads_of])
            if fast:
                qkv(h).put(b * half_model, grad_qkv)
            else:
                o_qkv_ref[h, cols, :] = grad_qkv
        if fast:
            qkv(h).start()

        @pl.when(h == 1)
        def _():
            for c in range(chunks):
                grads.finish(c)
            for b in range(2):
                cols = slice(b * half_model, (b + 1) * half_model)
                grad_output = dot_tn(ghl_ref[:, cols], att_ref[...])
                if fast:
                    output.put(b * half_model, grad_output)
                else:
                    o_output_ref[cols, :] = grad_output[:, :width]
            if fast:
                output.start()

        band = roll_rows(bands_ref[...].T, False)
        spread = dqt_ref[:BLOCK, :]
        high = spread.astype(bf16)
        rest = (spread - high.astype(f32)).astype(bf16)
        plane = (dot(high, hot_ref[...]) + dot(rest, hot_ref[...])).T
        plane = jnp.where((square_rows < CODES) == (square_lanes < CODES), plane, 0.0)
        plane = roll_rows(plane, False)
        far = dqt_ref[BLOCK + FAR : BLOCK + FAR + 16, :]
        line = jnp.concatenate(
            [
                jnp.sum(band, axis=0, keepdims=True),
                jnp.sum(plane[:CODES], axis=0, keepdims=True),
                jnp.sum(plane[CODES:], axis=0, keepdims=True),
                fold(jnp.where(real & (lines16 < start16), far, 0.0)),
                fold(jnp.where(real & (lines16 > start16 + 2), far, 0.0)),
            ],
            axis=1,
        )
        sums_ref[...] += jnp.where(lax.broadcasted_iota(jnp.int32, sums_ref.shape, 0) == h, line, 0.0)
        return carry

    lax.fori_loop(0, heads, head, 0)

    mix(2)
    credits = [(sibling, credit.at[0]), (across, credit.at[1])]
    for other, sem in credits:
        pl.semaphore_signal(
            sem, inc=1, device_id=(lax.axis_index("dp"), other), device_id_type=pl.DeviceIdType.MESH
        )
    loads[-1].start()
    for c in range(chunks):
        norm.drain(c)
    gain_total = jnp.zeros((1, model), f32)
    for c in range(chunks):
        for m in range(pieces):
            at = place(m, c)
            partial = dot(nf_ref[at, :], wt_ref[...])
            gain_total = gain_total + jnp.sum(partial * x1[at, :].astype(f32), axis=0, keepdims=True)
            last.put(c, m, partial)
        if c == 0:
            for _, sem in credits:
                pl.semaphore_wait(sem, 1)
        last.start(c)
        if c > 0:
            last.middle(c - 1)
    sums_ref[3:4, :model] = gain_total / gain_a
    sums_ref[4:5, :model] = gain_sum_ref[0:1, :]
    if fast:
        small.start(sums_ref[...])
        output.third()
        qkv(1).third()
    last.middle(chunks - 1)
    if fast:
        qkv(2).middle()
        small.turn(1)
        o_inner_ref[...] = inner.finish()
        small.turn(2)
        o_output_ref[...] = output.finish()[:, :width].T
    loads[-1].wait()
    for c in range(chunks):
        x = cot_ref[run(c), :].astype(f32)
        grad_normed = last.finish(c)
        factor = factor_of(x)
        hat = x * factor
        scaled = grad_normed * gain_a
        back = factor * (scaled - hat * jnp.mean(scaled * hat, axis=-1, keepdims=True))
        input_ref[run(c), :] += back
        if fast and c == 0:
            small.turn(3)
            qkv(2).third()
        if fast and c == 1:
            small.turn(4)
    if fast:
        low_each = lax.broadcasted_iota(jnp.int32, (model // 8, BLOCK), 1) < 64
        parts = [qkv(h).finish() for h in range(heads)]
        for k in range(3):
            for h in range(0, heads, 2):
                at = slice(0, BLOCK) if k < 2 else slice(BLOCK, 2 * BLOCK)
                one = parts[h][:, at]
                one = pltpu.roll(one, 64, 1) if k == 1 else one
                if h + 1 < heads:
                    two = parts[h + 1][:, at]
                    two = two if k == 1 else pltpu.roll(two, 64, 1)
                    o_qkv_ref[k, :, h * 64 : (h + 2) * 64] = jnp.where(low_each, one, two)
                else:
                    o_qkv_ref[k, :, h * 64 :] = one[:, :64]
        totals = small.finish()
        o_gain_a_ref[...] = totals[3:4, :model].reshape(model)
        o_gain_f_ref[...] = totals[4:5, :model].reshape(model)
        buckets = collapse()
        tables = sum(dot_nt(part.astype(bf16), buckets) for part in split3(small.value[3]))
        o_tables_ref[...] = tables[:heads]
        outer.drain()
        inner.drain()
        output.drain()
        for h in range(heads):
            qkv(h).drain()
        small.drain()
    else:
        o_sums_ref[...] = sums_ref[...]
    wo.drain(0)
    for c in range(chunks):
        for each in (att, grad_att, grads, feed, last):
            each.drain(c)


def spread_scratch(rows, columns, lead=(), own_part=True):
    buffers = [pltpu.VMEM((*lead, 8 * rows, columns), bf16)] if own_part else []
    return buffers + [
        pltpu.VMEM((*lead, 4 * rows, columns), bf16),
        pltpu.VMEM((*lead, 2 * rows, columns), bf16),
        pltpu.VMEM((*lead, rows, columns), bf16),
        pltpu.SemaphoreType.DMA((*lead, 3)),
        pltpu.SemaphoreType.DMA((*lead, 3)),
    ]


def local(
    fast,
    tokens, lengths, horizontal, vertical, gain_attn, w_qkv, bias_tables, w_output, gain_ffn, w_inner, w_outer, cotangent,
):
    rows, model = tokens.shape
    heads = bias_tables.shape[1]
    width = w_qkv.shape[2]
    units = w_inner.shape[1]
    share = rows // lax.axis_size("mp")
    chunks = rows // CHUNK
    each = model // 8
    sums = (8, WIDE + 4 * BLOCK)

    def dma(*shape):
        return pltpu.SemaphoreType.DMA(shape)

    def vmem(*shape, dtype=bf16):
        return pltpu.VMEM(shape, dtype)

    scratch = [
        vmem(rows, model), vmem(3, width, model), vmem(model, units), vmem(units, model),
        vmem(rows, model), dma(7 + 4 * chunks),
        vmem(8, rows, dtype=jnp.int32), vmem(heads, BLOCK, BLOCK), vmem(rows, BLOCK), vmem(BLOCK, rows), vmem(heads, rows, BLOCK),
        vmem(heads, rows, BLOCK), vmem(heads, rows, BLOCK), vmem(heads, BLOCK, rows), vmem(heads, rows, BLOCK),
        vmem(heads, BLOCK, WIDE), vmem(heads, WIDE, BLOCK),
        vmem(heads, chunks, 256, CHUNK),
        vmem(rows, CHUNK, dtype=f32), vmem(heads * CHUNK, BLOCK, dtype=f32), vmem(rows, BLOCK, dtype=f32),
        vmem(256, rows, dtype=f32), vmem(WIDE, BLOCK, dtype=f32), vmem(heads, BLOCK, rows),
        vmem(*sums, dtype=f32), vmem(8, model, dtype=f32),
        vmem(rows, 256), vmem(6 * rows, BLOCK), dma(chunks, 3), dma(chunks, 3),
        vmem(chunks * 9 * BLOCK // 2, BLOCK), vmem(chunks * 6 * BLOCK, BLOCK), dma(chunks, 3), dma(chunks, 3),
        vmem(4 * width, model), dma(1, 3), dma(1, 3),
        vmem(rows, model),
        vmem(rows, model), dma(chunks, 3), dma(chunks, 3),
        vmem(rows, model), dma(chunks, 2), dma(chunks, 2), vmem(rows, model), dma(chunks, 2), dma(chunks, 2),
        dma(chunks, 2), dma(chunks, 2), vmem(rows // 2, model), vmem(share, model),
        pltpu.SemaphoreType.REGULAR((2,)),
        vmem(rows, units), vmem(rows, units), vmem(share, model, dtype=f32),
    ]
    outs = [((share, model), bf16), ((share, model), f32)]
    if fast:
        outs += [
            ((3, each, width), f32), ((width, each), f32), ((each, units), f32), ((each, units), f32),
            ((model,), f32), ((model,), f32), ((heads, 3 * BUCKETS), f32),
        ]
        scratch += [
            *spread_scratch(each, units, own_part=False), *spread_scratch(each, units), *spread_scratch(each, 256),
            *spread_scratch(each, 256, lead=(heads,)),
            vmem(5, *sums, dtype=f32), vmem(5, *sums, dtype=f32), dma(5), dma(5),
        ]
    else:
        outs += [
            ((heads, model, 256), f32), ((model, width), f32), ((model, units), f32), ((model, units), f32), (sums, f32),
        ]
    full = pl.BlockSpec(memory_space=pltpu.VMEM)
    anywhere = pl.BlockSpec(memory_space=pl.ANY)
    results = pl.pallas_call(
        functools.partial(layer_kernel, fast),
        in_specs=[pl.BlockSpec(memory_space=pltpu.SMEM)] + [full] * 5 + [anywhere] * 6,
        out_specs=[full] * len(outs),
        out_shape=[jax.ShapeDtypeStruct(*out) for out in outs],
        scratch_shapes=scratch,
        compiler_params=pltpu.CompilerParams(vmem_limit_bytes=64 * MIB, collective_id=1, has_side_effects=True),
        name="layer",
    )(
        lengths, horizontal, vertical, gain_attn, gain_ffn, bias_tables.T,
        tokens, jnp.swapaxes(w_qkv, 1, 2), w_output, w_inner, w_outer, cotangent,
    )
    if fast:
        mixed, input_grad, qkv, output, inner, outer, gain_a, gain_f, tables = results
        return mixed, input_grad, qkv, output, inner, outer.T, gain_a, gain_f, tables.T
    mixed, input_grad, qkv, output, inner, outer, sums = results
    qkv = qkv[:, :, : 3 * 64].reshape(heads, model, 3, 64).transpose(2, 1, 0, 3).reshape(3, model, width)
    gains = lax.psum(sums[3:5, :model], ("dp", "mp"))
    tables = lax.dot_general(
        collapse().astype(f32),
        lax.psum(sums[:heads], "dp"),
        (((1,), (1,)), ((), ())),
        precision=lax.Precision.HIGHEST,
    )

    def spread(x, axis):
        return lax.psum_scatter(x, "dp", scatter_dimension=axis, tiled=True)

    return (
        mixed, input_grad, spread(qkv, 1), spread(output.T, 1), spread(inner, 0), spread(outer.T, 1),
        gains[0], gains[1], tables,
    )


def solution(mesh):
    fast = mesh.shape["dp"] == 8
    return jax.shard_map(
        functools.partial(local, fast),
        mesh=mesh,
        in_specs=(
            P("dp", None), P("dp"), P("dp"), P("dp"), P(), P(None, None, "mp"), P(None, "mp"), P("mp", None), P(),
            P(None, "mp"), P("mp", None), P("dp", None),
        ),
        out_specs=(
            P(("dp", "mp"), None), P(("dp", "mp"), None), P(None, "dp", "mp"), P("mp", "dp"), P("dp", "mp"),
            P("mp", "dp"), P(), P(), P(None, "mp"),
        ),
        check_vma=False,
    )
```

```python
import functools
import jax
import jax.numpy as jnp
import numpy as np
from jax import lax
from jax.experimental import pallas as pl
from jax.experimental.pallas import tpu as pltpu
from jax.sharding import PartitionSpec as P

BUCKETS = 32
CODES = 64
HALF = BUCKETS // 2
EPSILON = 1e-06
DEAD = -1e9
CHUNK = 512
BLOCK = 128
BAND = 3 * BLOCK
WIDE = 6 * BLOCK
FAR = 64
MASK = 76
LSE = 80
MIB = 2**20

f32 = jnp.float32
bf16 = jnp.bfloat16


def line_bucket(columns):
    line = jnp.clip(columns - 2 * BLOCK, -HALF, HALF - 1) + HALF
    line = jnp.where(columns < 5 * BLOCK, line, 0)
    wrapped = columns % BLOCK
    wrapped = jnp.where(wrapped < CODES, wrapped, wrapped - BLOCK)
    plane = jnp.clip(wrapped, -HALF, HALF - 1) + HALF
    return jnp.where(
        columns < WIDE, line, jnp.where(columns < WIDE + BLOCK, BUCKETS + plane, 2 * BUCKETS + plane)
    )


def expansion():
    rows = lax.broadcasted_iota(jnp.int32, (3 * BUCKETS, WIDE + 2 * BLOCK), 0)
    columns = lax.broadcasted_iota(jnp.int32, (3 * BUCKETS, WIDE + 2 * BLOCK), 1)
    return jnp.where(rows == line_bucket(columns), 1.0, 0.0).astype(bf16)


def collapse():
    rows = lax.broadcasted_iota(jnp.int32, (3 * BUCKETS, WIDE + 4 * BLOCK), 0)
    columns = lax.broadcasted_iota(jnp.int32, (3 * BUCKETS, WIDE + 4 * BLOCK), 1)
    bucket = line_bucket(columns)
    bucket = jnp.where(columns == 5 * BLOCK, BUCKETS - 1, bucket)
    bucket = jnp.where(columns >= WIDE + 2 * BLOCK, 0, bucket)
    bucket = jnp.where(columns >= WIDE + 3 * BLOCK, BUCKETS - 1, bucket)
    return jnp.where(rows == bucket, 1.0, 0.0).astype(bf16)


def roll_rows(value, right):
    rows, width = value.shape
    index = lax.broadcasted_iota(jnp.int32, value.shape, 0)
    step = 1
    while step < rows:
        shift = step if right else width - step
        value = jnp.where((index // step) % 2 == 1, pltpu.roll(value, shift, 1), value)
        step *= 2
    return value


def dot(a, b):
    return jnp.dot(a, b, preferred_element_type=f32)


def dot_nt(a, b):
    return lax.dot_general(a, b, (((1,), (1,)), ((), ())), preferred_element_type=f32)


def split3(value):
    high = value.astype(bf16).astype(f32)
    rest = value - high
    middle = rest.astype(bf16).astype(f32)
    return high, middle, rest - middle


def dot_tn(a, b):
    return lax.dot_general(a, b, (((0,), (0,)), ((), ())), preferred_element_type=f32)


ROOT = float(np.sqrt(2.0 / np.pi))
CUBE = 0.044715


def factor_of(rows):
    return lax.rsqrt(jnp.mean(rows * rows, axis=-1, keepdims=True) + EPSILON)


def mp_places():
    mp = lax.axis_index("mp")
    y, core = mp // 2, mp % 2
    return mp, y, core, y * 2 + (1 - core), (1 - y) * 2 + core


def dp_places():
    dp = lax.axis_index("dp")
    return dp // 2, dp % 2


def remote(src, dst, send, recv, mp=None, dp=None):
    return pltpu.make_async_remote_copy(
        src_ref=src,
        dst_ref=dst,
        send_sem=send,
        recv_sem=recv,
        device_id=(lax.axis_index("dp") if dp is None else dp, lax.axis_index("mp") if mp is None else mp),
        device_id_type=pl.DeviceIdType.MESH,
    )


def beside(z):
    return z // 2 * 2 + 1 - z % 2


def meet(fast):
    mp, dp = lax.axis_index("mp"), lax.axis_index("dp")
    others = [(dp, (mp + d) % 4) for d in (1, 2, 3)]
    if fast:
        others.extend(((dp + d) % 8, mp) for d in range(1, 8))
    barrier = pltpu.get_barrier_semaphore()
    for other in others:
        pl.semaphore_signal(barrier, inc=1, device_id=other, device_id_type=pl.DeviceIdType.MESH)
    pl.semaphore_wait(barrier, len(others))


def run(index, count=1, size=BLOCK):
    return pl.ds(pl.multiple_of(index * size, size), count * size)


class Scatter:

    def __init__(self, part, near, far, send, recv):
        self.part, self.near, self.far, self.send, self.recv = part, near, far, send, recv

    def block(self, c, core, y):
        return (c * 2 + core) * 2 + y

    def put(self, c, m, value, columns=slice(None)):
        self.part[run(self.block(c, m % 2, m // 2)), columns] = value.astype(bf16)

    def first(self, c):
        _, _, core, sibling, _ = mp_places()
        src = self.part.at[run(self.block(c, 1 - core, 0), 2)]
        return remote(src, self.near.at[run(c * 2, 2)], self.send.at[c, 0], self.recv.at[c, 0], sibling)

    def second(self, c):
        _, y, core, _, across = mp_places()
        src = self.part.at[run(self.block(c, core, 1 - y))]
        return remote(src, self.far.at[run(c)], self.send.at[c, 1], self.recv.at[c, 1], across)

    def start(self, c):
        self.first(c).start()

    def middle(self, c):
        _, y, core, _, _ = mp_places()
        self.first(c).wait_recv()
        at = run(self.block(c, core, 1 - y))
        self.part[at, :] = (self.part[at, :].astype(f32) + self.near[run(c * 2 + 1 - y), :].astype(f32)).astype(bf16)
        self.second(c).start()

    def finish(self, c):
        _, y, core, _, _ = mp_places()
        self.second(c).wait_recv()
        own = self.part[run(self.block(c, core, y)), :].astype(f32) + self.near[run(c * 2 + y), :].astype(f32)
        return own + self.far[run(c), :].astype(f32)

    def drain(self, c):
        self.first(c).wait_send()
        self.second(c).wait_send()


class Gather:

    def __init__(self, full, send, recv, size=BLOCK):
        self.full, self.send, self.recv, self.size = full, send, recv, size

    def at(self, c, m):
        return run(c * 4 + m, 1, self.size)

    def copy(self, c, kind):
        mp, _, _, sibling, across = mp_places()
        at = self.full.at[self.at(c, across if kind == 2 else mp)]
        return remote(at, at, self.send.at[c, kind], self.recv.at[c, kind], across if kind == 1 else sibling)

    def start(self, c):
        self.copy(c, 1).start()
        self.copy(c, 0).start()

    def forward(self, c):
        self.copy(c, 1).wait_recv()
        self.copy(c, 2).start()

    def finish(self, c):
        self.copy(c, 0).wait_recv()
        self.copy(c, 2).wait_recv()

    def drain(self, c):
        for kind in range(3):
            self.copy(c, kind).wait_send()


class Exchange:

    def __init__(self, given, taken, size, send, recv):
        self.given, self.taken, self.size, self.send, self.recv = given, taken, size, send, recv

    def copy(self, c, d):
        mp = lax.axis_index("mp")
        src = self.given.at[run(c * 3 + d - 1, 1, self.size)]
        dst = self.taken.at[run(c * 4 + mp, 1, self.size)]
        return remote(src, dst, self.send.at[c, d - 1], self.recv.at[c, d - 1], (mp + d) % 4)

    def start(self, c):
        for d in (2, 1, 3):
            self.copy(c, d).start()

    def finish(self, c):
        for d in (1, 2, 3):
            self.copy(c, d).wait_recv()

    def drain(self, c):
        for d in (1, 2, 3):
            self.copy(c, d).wait_send()


class Spread:

    def __init__(self, part, near, pair, far, send, recv):
        self.part, self.near, self.pair, self.far, self.send, self.recv = part, near, pair, far, send, recv
        self.each = part.shape[0] // 8

    def at(self, index, count=1):
        return run(index, count, self.each)

    def put(self, first_row, value):
        for r in range(value.shape[0] // self.each):
            j = first_row // self.each + r
            rows = value[r * self.each : (r + 1) * self.each]
            self.part[self.at(j % 2 * 4 + j // 2 % 2 * 2 + j // 4), :] = rows.astype(bf16)

    def copy(self, kind):
        z, x = dp_places()
        send, recv = self.send.at[kind], self.recv.at[kind]
        if kind == 0:
            src = self.part.at[self.at((1 - x) * 4, 4)]
            return remote(src, self.near, send, recv, dp=z * 2 + 1 - x)
        if kind == 1:
            src = self.part.at[self.at(x * 4 + (1 - z % 2) * 2, 2)]
            return remote(src, self.pair, send, recv, dp=beside(z) * 2 + x)
        src = self.part.at[self.at(x * 4 + z % 2 * 2 + 1 - z // 2)]
        return remote(src, self.far, send, recv, dp=(z + 2) % 4 * 2 + x)

    def start(self):
        self.copy(0).start()

    def middle(self):
        z, x = dp_places()
        self.copy(0).wait_recv()
        at = self.at(x * 4 + (1 - z % 2) * 2, 2)
        near = self.near[self.at((1 - z % 2) * 2, 2), :].astype(f32)
        self.part[at, :] = (self.part[at, :].astype(f32) + near).astype(bf16)
        self.copy(1).start()

    def sum_of(self, half):
        z, x = dp_places()
        total = self.part[self.at(x * 4 + z % 2 * 2 + half), :].astype(f32)
        total = total + self.near[self.at(z % 2 * 2 + half), :].astype(f32)
        return total + self.pair[self.at(half), :].astype(f32)

    def third(self):
        z, x = dp_places()
        self.copy(1).wait_recv()
        self.part[self.at(x * 4 + z % 2 * 2 + 1 - z // 2), :] = self.sum_of(1 - z // 2).astype(bf16)
        self.copy(2).start()

    def finish(self):
        z, _ = dp_places()
        self.copy(2).wait_recv()
        return self.sum_of(z // 2) + self.far[...].astype(f32)

    def drain(self):
        for kind in range(3):
            self.copy(kind).wait_send()


class Direct:

    def __init__(self, part, taken, send, recv):
        self.part, self.taken, self.send, self.recv = part, taken, send, recv
        self.each = part.shape[0] // 8

    put = Spread.put

    def at(self, index, count=1):
        return run(index, count, self.each)

    def block(self, dp):
        return self.at(dp % 2 * 4 + dp // 2 % 2 * 2 + dp // 4)

    def copy(self, d):
        to = (lax.axis_index("dp") + d) % 8
        src = self.part.at[self.block(to)]
        return remote(src, self.taken.at[run(d - 1, 1, self.each)], self.send.at[d - 1], self.recv.at[d - 1], dp=to)

    def start(self):
        for d in (4, 3, 5, 2, 6, 1, 7):
            self.copy(d).start()

    def finish(self):
        total = self.part[self.block(lax.axis_index("dp")), :].astype(f32)
        for d in range(1, 8):
            self.copy(d).wait_recv()
            total = total + self.taken[run(d - 1, 1, self.each), :].astype(f32)
        return total

    def drain(self):
        for d in range(1, 8):
            self.copy(d).wait_send()


class Total:

    def __init__(self, value, taken, send, recv):
        self.value, self.taken, self.send, self.recv = value, taken, send, recv

    def copy(self, kind):
        mp, dp = lax.axis_index("mp"), lax.axis_index("dp")
        send, recv = self.send.at[kind], self.recv.at[kind]
        if kind < 7:
            return remote(self.value.at[0], self.taken.at[kind], send, recv, dp=(dp + kind + 1) % 8)
        return remote(self.value.at[1], self.taken.at[kind], send, recv, mp=(mp + kind - 6) % 4)

    def start(self):
        for kind in range(7):
            self.copy(kind).start()

    def turn(self):
        total = self.value[0]
        for kind in range(7):
            self.copy(kind).wait_recv()
            total = total + self.taken[kind]
        self.value[1] = total
        for kind in range(7, 10):
            self.copy(kind).start()

    def finish(self):
        total = self.value[1]
        for kind in range(7, 10):
            self.copy(kind).wait_recv()
            total = total + self.taken[kind]
        return total

    def drain(self):
        for kind in range(10):
            self.copy(kind).wait_send()


def layer_kernel(
    fast,
    length_ref, across_ref, upward_ref, gain_a_ref, gain_f_ref, tables_ref,
    tokens_hbm, w_qkv_hbm, w_output_hbm, w_inner_hbm, w_outer_hbm, cot_hbm,
    *rest,
):
    outs, scratch = rest[: 9 if fast else 7], rest[9 if fast else 7 :]
    if fast:
        mixed_ref, input_ref, o_qkv_ref, o_output_ref, o_inner_ref, o_outer_ref, o_gain_a_ref, o_gain_f_ref, o_tables_ref = outs
    else:
        mixed_ref, input_ref, o_qkv_ref, o_output_ref, o_inner_ref, o_outer_ref, o_sums_ref = outs
    (
        x1, w_qkv_ref, w_inner_ref, w_outer_ref, cot_ref, load_sem,
        codes_ref, plane_ref, hot_ref, hot_t_ref, qa_ref, qb_ref, k2_ref, kt2_ref, v_ref, band_ref, band_t_ref, qt_ref,
        s_ref, res_ref, dv_ref, dqt_ref, bands_ref, dat_ref, sums_ref, gain_sum_ref, collapse_ref,
        att_ref, af_ref, att_send, att_recv,
        es_ref, ga_ref, es_send, es_recv,
        wo_ref, wo_send, wo_recv,
        nf_ref,
        ghl_ref, ghl_send, ghl_recv,
        feed_part, feed_send, feed_recv, norm_part, norm_send, norm_recv, last_send, last_recv, near_ref, far_ref,
        credit,
        low_ref, grad_low_ref, hidden_ref,
        *spreads,
    ) = scratch
    heads = tables_ref.shape[0]
    rows, model = x1.shape
    width = heads * 64
    units = w_inner_ref.shape[1]
    pieces = 4
    chunks = rows // CHUNK
    blocks = rows // BLOCK
    half_model = model // 2
    mp, _, _, sibling, across = mp_places()
    da_ref, dk_ref, wt_ref = qa_ref, res_ref, w_inner_ref

    att = Gather(af_ref, att_send, att_recv, CHUNK + CHUNK // 2)
    grad_att = Exchange(es_ref, ga_ref, BLOCK + BLOCK // 2, es_send, es_recv)
    wo = Gather(wo_ref, wo_send, wo_recv, width)
    grads = Gather(ghl_ref, ghl_send, ghl_recv)
    feed = Scatter(feed_part, near_ref, far_ref, feed_send, feed_recv)
    norm = Scatter(norm_part, near_ref, far_ref, norm_send, norm_recv)
    last = Scatter(norm_part, near_ref, far_ref, last_send, last_recv)
    if fast:
        outer = Spread(w_outer_ref, *spreads[0:5])
        inner = Spread(*spreads[5:11])
        output = Spread(*spreads[11:17])
        qkv_last = Direct(*spreads[23:27])
        small = Total(*spreads[27:31])

        def qkv(h):
            return Spread(*[ref.at[h] for ref in spreads[17:23]])

    def place(m, c):
        return run(m * chunks + c)

    loads = [
        pltpu.make_async_copy(src, dst, load_sem.at[i])
        for i, (src, dst) in enumerate(
            [
                (tokens_hbm, x1),
                (w_qkv_hbm, w_qkv_ref),
                (w_output_hbm, wo_ref.at[wo.at(0, mp)]),
                (w_inner_hbm, w_inner_ref),
                (w_outer_hbm, w_outer_ref),
                (cot_hbm, cot_ref),
                *[(tokens_hbm.at[place(m, c)], low_ref.at[run(c * 4 + m)]) for c in range(chunks) for m in range(4)],
                (tokens_hbm.at[run(mp * chunks, chunks)], cot_ref.at[run(0, chunks)]),
            ]
        )
    ]
    for load in loads[:-1]:
        load.start()
    meet(fast)

    def window(m, c):
        block = m * chunks + c
        start = min(max(block - 1, 0), blocks - 3)
        return range(start, start + 3), 2 - block


    expanded = dot(tables_ref[...], expansion())
    square_rows = lax.broadcasted_iota(jnp.int32, (BLOCK, BLOCK), 0)
    square_lanes = lax.broadcasted_iota(jnp.int32, (BLOCK, BLOCK), 1)
    for h in range(heads):
        line = jnp.broadcast_to(expanded[h : h + 1, :WIDE], (BLOCK, WIDE))
        band = roll_rows(line, True)
        band_ref[h] = band.astype(bf16)
        band_t_ref[h] = band.T.astype(bf16)
        level = roll_rows(jnp.broadcast_to(expanded[h : h + 1, WIDE : WIDE + BLOCK], (BLOCK, BLOCK)), True)
        upward = roll_rows(jnp.broadcast_to(expanded[h : h + 1, WIDE + BLOCK :], (BLOCK, BLOCK)), True)
        plane = jnp.where(
            (square_rows < CODES) & (square_lanes < CODES),
            level,
            jnp.where((square_rows >= CODES) & (square_lanes >= CODES), upward, 0.0),
        )
        plane_ref[h] = plane.astype(bf16)
    loads[2].wait()
    wo.start(0)
    loads[1].wait()
    loads[0].wait()
    gain_a = gain_a_ref[...].reshape(1, model).astype(f32)
    gain_f = gain_f_ref[...].reshape(1, model).astype(f32)
    codes_ref[0:1, :] = across_ref[...].reshape(1, rows)
    codes_ref[1:2, :] = upward_ref[...].reshape(1, rows)
    lanes = lax.broadcasted_iota(jnp.int32, (CHUNK, BLOCK), 1)
    low = lanes < FAR

    def prepare(j, carry):
        at = run(j, 1, CHUNK)
        x = x1[at, :].astype(f32)
        normed_rows = (x * factor_of(x) * gain_a).astype(bf16)
        x1[at, :] = normed_rows
        codes_lines = lax.broadcasted_iota(jnp.int32, (BLOCK, CHUNK), 0)
        hot_t = jnp.where(
            codes_lines == jnp.broadcast_to(codes_ref[0:1, at], (BLOCK, CHUNK)),
            1.0,
            jnp.where(codes_lines - CODES == jnp.broadcast_to(codes_ref[1:2, at], (BLOCK, CHUNK)), 1.0, 0.0),
        )
        hot = hot_t.T.astype(bf16)
        hot_t_ref[:, at] = hot_t.astype(bf16)
        hot_ref[at, :] = hot
        row = lax.broadcasted_iota(jnp.int32, (CHUNK, BLOCK), 0) + j * CHUNK
        block = row // BLOCK
        start = jnp.clip(block - 1, 0, blocks - 3)
        far = (lanes >= FAR) & (lanes < MASK)
        far_left = far & (lanes - FAR < start)
        far_right = far & (lanes - FAR > start + 2)
        key_side = jnp.where(
            (far & (lanes - FAR == block))
            | ((lanes == MASK) & (row >= length_ref[0]))
            | ((lanes >= LSE) & (lanes < LSE + 3)),
            1.0,
            0.0,
        )

        def part(h):
            columns = s_ref[:CHUNK, h // 2 * BLOCK : h // 2 * BLOCK + BLOCK]
            return columns if h % 2 == 0 else pltpu.roll(columns, 64, 1)

        s_ref[:CHUNK, :width] = dot_nt(normed_rows, w_qkv_ref[0])
        for h in range(heads):
            left = expanded[h : h + 1, 0:1]
            right = expanded[h : h + 1, WIDE - BLOCK - 1 : WIDE - BLOCK]
            query_side = jnp.where(far_left, left, jnp.where(far_right, right, jnp.where(lanes == MASK, DEAD, 0.0)))
            qa_ref[h, at, :] = dot(hot, plane_ref[h]).astype(bf16)
            qb_ref[h, at, :] = jnp.where(low, part(h).astype(bf16).astype(f32) * 0.125, query_side).astype(bf16)
        s_ref[:CHUNK, :width] = dot_nt(normed_rows, w_qkv_ref[1])
        for h in range(heads):
            second = jnp.where(low, part(h), key_side)
            k2_ref[h, at, :] = second.astype(bf16)
            kt2_ref[h, :, at] = second.T.astype(bf16)
        s_ref[:CHUNK, :width] = dot_nt(normed_rows, w_qkv_ref[2])
        for h in range(heads):
            v_ref[h, at, :] = jnp.where(low, part(h), 1.0).astype(bf16)
        return carry

    s_ref[:CHUNK, :] = jnp.zeros_like(s_ref[:CHUNK, :])
    lax.fori_loop(0, chunks, prepare, 0)
    wo.forward(0)
    gain_sum_ref[...] = jnp.zeros_like(gain_sum_ref)
    sums_ref[...] = jnp.zeros_like(sums_ref)
    collapse_ref[...] = collapse()

    half_low = lax.broadcasted_iota(jnp.int32, (CHUNK // 2, BLOCK), 1) < 64
    quarter_low = lax.broadcasted_iota(jnp.int32, (BLOCK // 2, BLOCK), 1) < 64

    def share_attended(c):
        at = run(c, 1, CHUNK)
        mine = att.at(c, mp).start
        third = att_ref[at, BLOCK:].astype(f32)
        af_ref[pl.ds(pl.multiple_of(mine, CHUNK // 2), CHUNK), :] = att_ref[at, :BLOCK]
        beside_it = jnp.where(half_low, third[: CHUNK // 2], pltpu.roll(third[CHUNK // 2 :], 64, 1)).astype(bf16)
        af_ref[pl.ds(pl.multiple_of(mine + CHUNK, CHUNK // 2), CHUNK // 2), :] = beside_it
        att.start(c)

    def hidden_of(c):
        att.finish(c)
        hidden = low_ref[run(c, 1, CHUNK), :].astype(f32)
        for m in range(pieces):
            first = (c * 4 + m) * (CHUNK + CHUNK // 2)
            pair = af_ref[pl.ds(pl.multiple_of(first, CHUNK // 2), CHUNK), :]
            third = af_ref[pl.ds(pl.multiple_of(first + CHUNK, CHUNK // 2), CHUNK // 2), :]
            third = jnp.concatenate([third, pltpu.roll(third.astype(f32), 64, 1).astype(bf16)], axis=0)
            weights = wo_ref[m * width : (m + 1) * width, :]
            hidden = hidden + dot(jnp.concatenate([pair, third[:, :64]], axis=1), weights)
        nf_ref[run(c, 1, CHUNK), :] = (hidden * factor_of(hidden) * gain_f).astype(bf16)
        for m in range(pieces):

            @pl.when(mp == m)
            def _(m=m):
                hidden_ref[run(c), :] = hidden[m * BLOCK : (m + 1) * BLOCK]

    def grad_of(c):
        grad_normed = norm.finish(c)
        hidden = hidden_ref[run(c), :]
        factor = factor_of(hidden)
        hat = hidden * factor
        scaled = grad_normed * gain_f
        back = factor * (scaled - hat * jnp.mean(scaled * hat, axis=-1, keepdims=True))
        grad = cot_ref[place(mp, c), :].astype(f32) + back
        input_ref[run(c), :] = grad
        gain_sum_ref[0:1, :] += jnp.sum(grad_normed * hat, axis=0, keepdims=True)
        grad_low = grad.astype(bf16)
        ghl_ref[grads.at(c, mp), :] = grad_low

        def of(m):
            value = dot_nt(grad_low, wo_ref[run(m, 1, width), :])
            third = jnp.concatenate([value[:, BLOCK:], jnp.zeros((BLOCK, 64), f32)], axis=1)
            third = jnp.where(quarter_low, third[: BLOCK // 2], pltpu.roll(third[BLOCK // 2 :], 64, 1))
            return jnp.concatenate([value[:, :BLOCK], third], axis=0).astype(bf16)

        size = BLOCK + BLOCK // 2
        ga_ref[run(c * 4 + mp, 1, size), :] = of(mp)
        for d in (1, 2, 3):
            es_ref[run(c * 3 + d - 1, 1, size), :] = of((mp + d) % 4)
        grad_att.start(c)

    def attend(c, h, carry):
        query_far = jnp.concatenate([qa_ref[h, place(m, c), :] for m in range(pieces)], axis=0)
        query_near = jnp.concatenate([qb_ref[h, place(m, c), :] for m in range(pieces)], axis=0)
        query = jnp.concatenate([query_far, query_near], axis=1)
        tops, mixes = [], []
        for j in range(chunks):
            cols = slice(j * CHUNK, (j + 1) * CHUNK)
            s = dot(query, jnp.concatenate([hot_t_ref[:, cols], kt2_ref[h, :, cols]], axis=0))
            lines = []
            for m in range(pieces):
                near, shift = window(m, c)
                tiles = []
                for b in range(pieces):
                    tile = s[m * BLOCK : (m + 1) * BLOCK, b * BLOCK : (b + 1) * BLOCK]
                    if j * pieces + b in near:
                        at = (j * pieces + b + shift) * BLOCK
                        tile = tile + band_ref[h, :, at : at + BLOCK].astype(f32)
                    tiles.append(tile)
                lines.append(jnp.concatenate(tiles, axis=1))
            s = jnp.concatenate(lines, axis=0)
            tops.append(jnp.max(s, axis=1, keepdims=True))
            mixes.append(dot(jnp.exp(s - tops[j]).astype(bf16), v_ref[h, cols, :]))
        top = functools.reduce(jnp.maximum, tops)
        mixed = sum(mix * jnp.exp(part - top) for mix, part in zip(mixes, tops))
        res_ref[run(h, 1, CHUNK), :] = jnp.where(low, mixed / pltpu.roll(mixed, 64, 1), 0.0)
        high, middle, rest = split3(-(top + jnp.log(mixed[:, 64:65])))
        second = jnp.where(
            lanes == LSE,
            high,
            jnp.where(lanes == LSE + 1, middle, jnp.where(lanes == LSE + 2, rest, query_near.astype(f32))),
        )
        qt_ref[h, c, :BLOCK, :] = query_far.astype(f32).T.astype(bf16)
        qt_ref[h, c, BLOCK:, :] = second.T.astype(bf16)

        return carry

    for c in range(chunks):
        lax.fori_loop(0, heads, functools.partial(attend, c), 0)
        if c > 0:
            att.forward(c - 1)
        pairs = []
        for g in range(0, heads, 2):
            pair = res_ref[g * CHUNK : (g + 1) * CHUNK, :]
            if g + 1 < heads:
                pair = jnp.where(low, pair, pltpu.roll(res_ref[(g + 1) * CHUNK : (g + 2) * CHUNK, :], 64, 1))
            pairs.append(pair.astype(bf16))
        att_ref[run(c, 1, CHUNK), :] = jnp.concatenate(pairs, axis=1)
        share_attended(c)
    for load in loads[3:-1]:
        load.wait()
    wo.finish(0)

    steps = units // 256

    def feed_step(t, carry):
        c = t // steps
        b = t % steps

        @pl.when(b == 0)
        def _():
            hidden_of(c)

        at = run(b, 1, 256)
        x = nf_ref[run(c, 1, CHUNK), :]
        cot = jnp.concatenate([cot_ref[place(m, c), :] for m in range(pieces)], axis=0)
        inner_units = dot(x, w_inner_ref[:, at])
        grad_act = dot_nt(cot, w_outer_ref[at, :])
        square = inner_units * inner_units
        tanh = jnp.tanh(ROOT * inner_units * (1.0 + CUBE * square))
        half = 0.5 * (1.0 + tanh)
        slope = half + 0.5 * inner_units * (1.0 - tanh * tanh) * (ROOT + 3.0 * CUBE * ROOT * square)
        activated = (inner_units * half).astype(bf16)
        grad_low = (slope * grad_act).astype(bf16)
        low_ref[run(c, 1, CHUNK), at] = activated
        grad_low_ref[run(c, 1, CHUNK), at] = grad_low

        @pl.when(b == steps - 1)
        def _():
            chunk_rows = run(c, 1, CHUNK)
            for p in range(model // 256):
                cols = slice(p * 256, (p + 1) * 256)
                part_norm = dot_nt(grad_low_ref[chunk_rows, :], w_inner_ref[cols, :])
                part_ffn = dot(low_ref[chunk_rows, :], w_outer_ref[:, cols])
                for m in range(pieces):
                    norm.put(c, m, part_norm[m * BLOCK : (m + 1) * BLOCK], cols)
                    feed.put(c, m, part_ffn[m * BLOCK : (m + 1) * BLOCK], cols)
            norm.start(c)

        @pl.when(t == 2)
        def _():
            att.forward(2)

        @pl.when(t == 3)
        def _():
            norm.middle(0)

        @pl.when(t == 6)
        def _():
            norm.middle(1)

        @pl.when(t == 7)
        def _():
            grad_of(0)

        return carry

    lax.fori_loop(0, chunks * steps, feed_step, 0)

    def weights_of(is_outer):
        for b in range(2):
            at = slice(b * half_model, (b + 1) * half_model)
            total = jnp.zeros((half_model, units), f32)
            for c in range(chunks):
                if is_outer:
                    left = jnp.concatenate([cot_ref[place(m, c), at] for m in range(pieces)], axis=0)
                    total = total + dot_tn(left, low_ref[run(c, 1, CHUNK), :])
                else:
                    total = total + dot_tn(nf_ref[run(c, 1, CHUNK), at], grad_low_ref[run(c, 1, CHUNK), :])
            if fast:
                (outer if is_outer else inner).put(b * half_model, total)
            else:
                (o_outer_ref if is_outer else o_inner_ref)[at, :] = total

    weights_of(True)
    if fast:
        outer.start()
    norm.middle(2)
    weights_of(False)
    if fast:
        inner.start()
    grad_of(1)
    wt_ref[...] = jnp.zeros_like(wt_ref)
    for k in range(3):
        for h in range(heads):
            wt_ref[h * 256 + k * 64 : h * 256 + (k + 1) * 64, :] = w_qkv_ref[k, h * 64 : (h + 1) * 64, :]

    def receive(c):
        grad_att.finish(c)
        at = run(c, 1, CHUNK)
        pairs, thirds = [], []
        for m in range(pieces):
            first = (c * 4 + m) * (BLOCK + BLOCK // 2)
            pairs.append(ga_ref[pl.ds(pl.multiple_of(first, BLOCK // 2), BLOCK), :])
            third = ga_ref[pl.ds(pl.multiple_of(first + BLOCK, BLOCK // 2), BLOCK // 2), :].astype(f32)
            thirds.extend([third, pltpu.roll(third, 64, 1)])
        received = [jnp.concatenate(pairs, axis=0).astype(f32), jnp.concatenate(thirds, axis=0)]
        for h in range(heads):
            pair = slice(h // 2 * BLOCK, h // 2 * BLOCK + BLOCK)
            grad = received[h // 2]
            out = att_ref[at, pair].astype(f32)
            if h % 2 == 1:
                grad = pltpu.roll(grad, 64, 1)
                out = pltpu.roll(out, 64, 1)
            high, middle, rest = split3(-jnp.sum(jnp.where(low, grad * out, 0.0), axis=1, keepdims=True))
            grad = jnp.where(
                low,
                grad,
                jnp.where(
                    lanes == FAR, high, jnp.where(lanes == FAR + 1, middle, jnp.where(lanes == FAR + 2, rest, 0.0))
                ),
            )
            da_ref[h, at, :] = grad.astype(bf16)
            dat_ref[h, :, at] = grad.T.astype(bf16)

    lines16 = lax.broadcasted_iota(jnp.int32, (16, rows), 0)
    block16 = lax.broadcasted_iota(jnp.int32, (16, rows), 1) // BLOCK
    start16 = jnp.clip(block16 - 1, 0, blocks - 3)
    real = lines16 < blocks
    tall_low = lax.broadcasted_iota(jnp.int32, (rows, BLOCK), 1) < 64

    def fold(value):
        total = value[:, :BLOCK]
        for b in range(1, value.shape[1] // BLOCK):
            total = total + value[:, b * BLOCK : (b + 1) * BLOCK]
        return jnp.sum(total, axis=0, keepdims=True)

    def mix(k):
        mixed_ref[run(k), :] = (hidden_ref[run(k), :] + feed.finish(k)).astype(bf16)

    def events(h, c, j):
        due = {
            (0, 0, 2): [lambda: grad_of(2)],
            (0, 1, 2): [lambda: grads.start(0)],
            (0, 2, 2): [lambda: grads.start(1)],
            (1, 0, 2): [lambda: grads.forward(0), lambda: grads.start(2), lambda: grads.forward(1)],
            (1, 1, 2): [lambda: feed.start(0), lambda: feed.start(1), lambda: feed.start(2)],
            (1, 2, 2): [lambda: grads.forward(2), lambda: feed.middle(0), lambda: feed.middle(1)],
            (2, 0, 2): [lambda: feed.middle(2)],
            (2, 1, 2): [lambda: mix(0), lambda: mix(1)],
            (2, 2, 2): [lambda: mix(2)],
        }
        if fast:
            for at, what in {
                (1, 1, 2): [outer.middle],
                (1, 2, 2): [inner.middle],
                (2, 0, 2): [outer.third, lambda: qkv(0).middle()],
                (2, 1, 2): [inner.third, lambda: qkv(0).third()],
                (2, 2, 2): [lambda: qkv(1).middle(), output.middle],
            }.items():
                due[at] = due.get(at, []) + what
        for (head_due, chunk_due, panel_due), what in due.items():
            if (chunk_due, panel_due) == (c, j):

                @pl.when(h == head_due)
                def _(what=what):
                    for each in what:
                        each()

    def leave(h, spread):
        grads_of = run(h, 1, 256)
        for b in range(2):
            cols = slice(b * half_model, (b + 1) * half_model)
            grad_qkv = dot_tn(x1[:, cols], nf_ref[:, grads_of])
            if fast:
                spread.put(b * half_model, grad_qkv)
            else:
                o_qkv_ref[h, cols, :] = grad_qkv
        if fast:
            spread.start()

    def leave_tables(h):
        band = roll_rows(bands_ref[...].T, False)
        spread = dqt_ref[:BLOCK, :]
        high = spread.astype(bf16)
        rest = (spread - high.astype(f32)).astype(bf16)
        plane = (dot(high, hot_ref[...]) + dot(rest, hot_ref[...])).T
        plane = jnp.where((square_rows < CODES) == (square_lanes < CODES), plane, 0.0)
        plane = roll_rows(plane, False)
        far = dqt_ref[BLOCK + FAR : BLOCK + FAR + 16, :]
        line = jnp.concatenate(
            [
                jnp.sum(band, axis=0, keepdims=True),
                jnp.sum(plane[:CODES], axis=0, keepdims=True),
                jnp.sum(plane[CODES:], axis=0, keepdims=True),
                fold(jnp.where(real & (lines16 < start16), far, 0.0)),
                fold(jnp.where(real & (lines16 > start16 + 2), far, 0.0)),
            ],
            axis=1,
        )
        sums_ref[...] += jnp.where(lax.broadcasted_iota(jnp.int32, sums_ref.shape, 0) == h, line, 0.0)

    def head(h, carry):
        dk_ref[...] = jnp.zeros_like(dk_ref)
        dv_ref[...] = jnp.zeros_like(dv_ref)
        bands_ref[...] = jnp.zeros_like(bands_ref)

        for c in range(chunks):

            @pl.when(h == 0)
            def _(c=c):
                receive(c)

            at = slice(c * CHUNK, (c + 1) * CHUNK)
            query = jnp.concatenate([qb_ref[h, place(m, c), :] for m in range(pieces)], axis=0)
            for j in range(chunks):
                keys = slice(j * CHUNK, (j + 1) * CHUNK)
                s = dot(jnp.concatenate([hot_ref[keys, :], k2_ref[h, keys, :]], axis=1), qt_ref[h, c])
                columns = []
                for m in range(pieces):
                    near, shift = window(m, c)
                    tiles = []
                    for b in range(pieces):
                        tile = s[b * BLOCK : (b + 1) * BLOCK, m * BLOCK : (m + 1) * BLOCK]
                        if j * pieces + b in near:
                            of = (j * pieces + b + shift) * BLOCK
                            tile = tile + band_t_ref[h, of : of + BLOCK, :].astype(f32)
                        tiles.append(tile)
                    columns.append(jnp.concatenate(tiles, axis=0))
                probs = jnp.exp(jnp.concatenate(columns, axis=1))
                probs_t = probs.astype(bf16)
                grad_t = (probs * dot(v_ref[h, keys, :], dat_ref[h, :, at])).astype(bf16)
                grad_low_ref[keys, :CHUNK] = grad_t
                dv_ref[keys, :] += dot(probs_t, da_ref[h, at, :])
                dk_ref[keys, :] += dot(grad_t, query)
                if j < chunks - 1:
                    events(h, c, j)
            dq = dot(jnp.concatenate([hot_t_ref[...], kt2_ref[h]], axis=0), grad_low_ref[:, :CHUNK])
            for m in range(pieces):
                dqt_ref[:, place(m, c)] = dq[:, m * BLOCK : (m + 1) * BLOCK]
                near, shift = window(m, c)
                of = slice((near.start + shift) * BLOCK, (near.stop + shift) * BLOCK)
                keys = slice(near.start * BLOCK, near.stop * BLOCK)
                bands_ref[of, :] += grad_low_ref[keys, m * BLOCK : (m + 1) * BLOCK].astype(f32)
            events(h, c, chunks - 1)

        dq = dqt_ref[BLOCK:, :].T * 0.125
        grads_of = run(h, 1, 256)
        nf_ref[:, grads_of] = jnp.concatenate(
            [jnp.where(tall_low, dq, pltpu.roll(dk_ref[...], 64, 1)), jnp.where(tall_low, dv_ref[...], 0.0)], axis=1
        ).astype(bf16)

        @pl.when(h < heads - 1)
        def _():
            leave(h, qkv(h) if fast else None)
            leave_tables(h)

        @pl.when(h == 1)
        def _():
            for c in range(chunks):
                grads.finish(c)
            for b in range(2):
                cols = slice(b * half_model, (b + 1) * half_model)
                grad_output = dot_tn(ghl_ref[:, cols], att_ref[...])
                if fast:
                    output.put(b * half_model, grad_output)
                else:
                    o_output_ref[cols, :] = grad_output[:, :width]
            if fast:
                output.start()

        return carry

    lax.fori_loop(0, heads, head, 0)

    credits = [(sibling, credit.at[0]), (across, credit.at[1])]
    for other, sem in credits:
        pl.semaphore_signal(
            sem, inc=1, device_id=(lax.axis_index("dp"), other), device_id_type=pl.DeviceIdType.MESH
        )
    leave(heads - 1, qkv_last if fast else None)
    loads[-1].start()
    for c in range(chunks):
        norm.drain(c)
    gain_total = jnp.zeros((1, model), f32)
    for c in range(chunks):
        for m in range(pieces):
            at = place(m, c)
            partial = dot(nf_ref[at, :], wt_ref[...])
            gain_total = gain_total + jnp.sum(partial * x1[at, :].astype(f32), axis=0, keepdims=True)
            last.put(c, m, partial)
        if c == 0:
            for _, sem in credits:
                pl.semaphore_wait(sem, 1)
        last.start(c)
        if c > 0:
            last.middle(c - 1)
    leave_tables(heads - 1)
    last.middle(chunks - 1)
    gain_total = gain_total / gain_a
    tables = sum(dot_nt(part.astype(bf16), collapse_ref[...]) for part in split3(sums_ref[...]))[:heads]
    if fast:
        lines = model // BLOCK
        small.value[0] = jnp.zeros_like(small.value[0])
        for i in range(lines):
            lane = slice(i * BLOCK, (i + 1) * BLOCK)
            small.value[0, i : i + 1, :] = gain_total[:, lane]
            small.value[0, lines + i : lines + i + 1, :] = gain_sum_ref[0:1, lane]
        small.value[0, 2 * lines : 2 * lines + heads, : 3 * BUCKETS] = tables
        small.start()
        output.third()
        qkv(1).third()
        o_outer_ref[...] = outer.finish()
        small.turn()
        o_output_ref[...] = output.finish()[:, :width].T
    loads[-1].wait()
    for c in range(chunks):
        x = cot_ref[run(c), :].astype(f32)
        grad_normed = last.finish(c)
        factor = factor_of(x)
        hat = x * factor
        scaled = grad_normed * gain_a
        back = factor * (scaled - hat * jnp.mean(scaled * hat, axis=-1, keepdims=True))
        input_ref[run(c), :] += back
    if fast:
        o_inner_ref[...] = inner.finish()
    if fast:
        low_each = lax.broadcasted_iota(jnp.int32, (model // 8, BLOCK), 1) < 64
        parts = [(qkv(h) if h < heads - 1 else qkv_last).finish() for h in range(heads)]
        for k in range(3):
            for h in range(0, heads, 2):
                at = slice(0, BLOCK) if k < 2 else slice(BLOCK, 2 * BLOCK)
                one = parts[h][:, at]
                one = pltpu.roll(one, 64, 1) if k == 1 else one
                if h + 1 < heads:
                    two = parts[h + 1][:, at]
                    two = two if k == 1 else pltpu.roll(two, 64, 1)
                    o_qkv_ref[k, :, h * 64 : (h + 2) * 64] = jnp.where(low_each, one, two)
                else:
                    o_qkv_ref[k, :, h * 64 :] = one[:, :64]
        totals = small.finish()
        for i in range(lines):
            o_gain_a_ref[i * BLOCK : (i + 1) * BLOCK] = totals[i : i + 1].reshape(BLOCK)
            o_gain_f_ref[i * BLOCK : (i + 1) * BLOCK] = totals[lines + i : lines + i + 1].reshape(BLOCK)
        o_tables_ref[...] = small.value[1, 2 * lines : 2 * lines + heads, : 3 * BUCKETS]
        outer.drain()
        inner.drain()
        output.drain()
        for h in range(heads - 1):
            qkv(h).drain()
        qkv_last.drain()
        small.drain()
    else:
        o_sums_ref[...] = jnp.zeros_like(o_sums_ref)
        o_sums_ref[0:1, :] = gain_total
        o_sums_ref[1:2, :] = gain_sum_ref[0:1, :]
        o_sums_ref[2 : 2 + heads, : 3 * BUCKETS] = tables
    wo.drain(0)
    for c in range(chunks):
        for each in (att, grad_att, grads, feed, last):
            each.drain(c)


def spread_scratch(rows, columns, lead=(), own_part=True):
    buffers = [pltpu.VMEM((*lead, 8 * rows, columns), bf16)] if own_part else []
    return buffers + [
        pltpu.VMEM((*lead, 4 * rows, columns), bf16),
        pltpu.VMEM((*lead, 2 * rows, columns), bf16),
        pltpu.VMEM((*lead, rows, columns), bf16),
        pltpu.SemaphoreType.DMA((*lead, 3)),
        pltpu.SemaphoreType.DMA((*lead, 3)),
    ]


def hand_over_kernel(*refs):
    count = len(refs) // 2
    for i in range(count):
        refs[count + i][...] = refs[i][...]


def hand_over(results):
    full = pl.BlockSpec(memory_space=pltpu.VMEM)
    return pl.pallas_call(
        hand_over_kernel,
        in_specs=[full] * len(results),
        out_specs=[full] * len(results),
        out_shape=[jax.ShapeDtypeStruct(each.shape, each.dtype) for each in results],
        name="hand_over",
    )(*results)


def local(
    fast,
    tokens, lengths, horizontal, vertical, gain_attn, w_qkv, bias_tables, w_output, gain_ffn, w_inner, w_outer, cotangent,
):
    rows, model = tokens.shape
    heads = bias_tables.shape[1]
    width = w_qkv.shape[2]
    units = w_inner.shape[1]
    share = rows // lax.axis_size("mp")
    chunks = rows // CHUNK
    each = model // 8
    sums = (8, WIDE + 4 * BLOCK)

    def dma(*shape):
        return pltpu.SemaphoreType.DMA(shape)

    def vmem(*shape, dtype=bf16):
        return pltpu.VMEM(shape, dtype)

    scratch = [
        vmem(rows, model), vmem(3, width, model), vmem(model, units), vmem(units, model),
        vmem(rows, model), dma(7 + 4 * chunks),
        vmem(8, rows, dtype=jnp.int32), vmem(heads, BLOCK, BLOCK), vmem(rows, BLOCK), vmem(BLOCK, rows), vmem(heads, rows, BLOCK),
        vmem(heads, rows, BLOCK), vmem(heads, rows, BLOCK), vmem(heads, BLOCK, rows), vmem(heads, rows, BLOCK),
        vmem(heads, BLOCK, WIDE), vmem(heads, WIDE, BLOCK),
        vmem(heads, chunks, 256, CHUNK),
        vmem(CHUNK, 256, dtype=f32), vmem(heads * CHUNK, BLOCK, dtype=f32), vmem(rows, BLOCK, dtype=f32),
        vmem(256, rows, dtype=f32), vmem(WIDE, BLOCK, dtype=f32), vmem(heads, BLOCK, rows),
        vmem(*sums, dtype=f32), vmem(8, model, dtype=f32), vmem(3 * BUCKETS, sums[1]),
        vmem(rows, 256), vmem(6 * rows, BLOCK), dma(chunks, 3), dma(chunks, 3),
        vmem(chunks * 9 * BLOCK // 2, BLOCK), vmem(chunks * 6 * BLOCK, BLOCK), dma(chunks, 3), dma(chunks, 3),
        vmem(4 * width, model), dma(1, 3), dma(1, 3),
        vmem(rows, model),
        vmem(rows, model), dma(chunks, 3), dma(chunks, 3),
        vmem(rows, model), dma(chunks, 2), dma(chunks, 2), vmem(rows, model), dma(chunks, 2), dma(chunks, 2),
        dma(chunks, 2), dma(chunks, 2), vmem(rows // 2, model), vmem(share, model),
        pltpu.SemaphoreType.REGULAR((2,)),
        vmem(rows, units), vmem(rows, units), vmem(share, model, dtype=f32),
    ]
    outs = [((share, model), bf16), ((share, model), f32)]
    if fast:
        outs += [
            ((3, each, width), f32), ((width, each), f32), ((each, units), f32), ((each, units), f32),
            ((model,), f32), ((model,), f32), ((heads, 3 * BUCKETS), f32),
        ]
        scratch += [
            *spread_scratch(each, units, own_part=False), *spread_scratch(each, units), *spread_scratch(each, 256),
            *spread_scratch(each, 256, lead=(heads - 1,)),
            vmem(8 * each, 256), vmem(7 * each, 256), dma(7), dma(7),
            vmem(2, 16, BLOCK, dtype=f32), vmem(10, 16, BLOCK, dtype=f32), dma(10), dma(10),
        ]
    else:
        outs += [
            ((heads, model, 256), f32), ((model, width), f32), ((model, units), f32), ((model, units), f32), ((8, model), f32),
        ]
    full = pl.BlockSpec(memory_space=pltpu.VMEM)
    anywhere = pl.BlockSpec(memory_space=pl.ANY)
    results = pl.pallas_call(
        functools.partial(layer_kernel, fast),
        in_specs=[pl.BlockSpec(memory_space=pltpu.SMEM)] + [full] * 5 + [anywhere] * 6,
        out_specs=[full] * len(outs),
        out_shape=[jax.ShapeDtypeStruct(*out) for out in outs],
        scratch_shapes=scratch,
        compiler_params=pltpu.CompilerParams(vmem_limit_bytes=64 * MIB, collective_id=1, has_side_effects=True),
        name="layer",
    )(
        lengths, horizontal, vertical, gain_attn, gain_ffn, bias_tables.T,
        tokens, jnp.swapaxes(w_qkv, 1, 2), w_output, w_inner, w_outer, cotangent,
    )
    if fast:
        mixed, input_grad, qkv, output, inner, outer, gain_a, gain_f, tables = hand_over(results)
        return mixed, input_grad, qkv, output, inner, outer.T, gain_a, gain_f, tables.T
    mixed, input_grad, qkv, output, inner, outer, sums = results
    qkv = qkv[:, :, : 3 * 64].reshape(heads, model, 3, 64).transpose(2, 1, 0, 3).reshape(3, model, width)
    gains = lax.psum(sums[:2], ("dp", "mp"))
    tables = lax.psum(sums[2 : 2 + heads, : 3 * BUCKETS], "dp").T

    def spread(x, axis):
        return lax.psum_scatter(x, "dp", scatter_dimension=axis, tiled=True)

    return (
        mixed, input_grad, spread(qkv, 1), spread(output.T, 1), spread(inner, 0), spread(outer.T, 1),
        gains[0], gains[1], tables,
    )


def solution(mesh):
    fast = mesh.shape["dp"] == 8
    return jax.shard_map(
        functools.partial(local, fast),
        mesh=mesh,
        in_specs=(
            P("dp", None), P("dp"), P("dp"), P("dp"), P(), P(None, None, "mp"), P(None, "mp"), P("mp", None), P(),
            P(None, "mp"), P("mp", None), P("dp", None),
        ),
        out_specs=(
            P(("dp", "mp"), None), P(("dp", "mp"), None), P(None, "dp", "mp"), P("mp", "dp"), P("dp", "mp"),
            P("mp", "dp"), P(), P(), P(None, "mp"),
        ),
        check_vma=False,
    )
```

```python
import functools
import jax
import jax.numpy as jnp
import numpy as np
from jax import lax
from jax.experimental import pallas as pl
from jax.experimental.pallas import tpu as pltpu
from jax.sharding import PartitionSpec as P

BUCKETS = 32
CODES = 64
HALF = BUCKETS // 2
EPSILON = 1e-06
DEAD = -1e9
CHUNK = 512
BLOCK = 128
BAND = 3 * BLOCK
WIDE = 6 * BLOCK
FAR = 64
MASK = 76
LSE = 80
MIB = 2**20

f32 = jnp.float32
bf16 = jnp.bfloat16


def line_bucket(columns):
    line = jnp.clip(columns - 2 * BLOCK, -HALF, HALF - 1) + HALF
    line = jnp.where(columns < 5 * BLOCK, line, 0)
    wrapped = columns % BLOCK
    wrapped = jnp.where(wrapped < CODES, wrapped, wrapped - BLOCK)
    plane = jnp.clip(wrapped, -HALF, HALF - 1) + HALF
    return jnp.where(
        columns < WIDE, line, jnp.where(columns < WIDE + BLOCK, BUCKETS + plane, 2 * BUCKETS + plane)
    )


def expansion():
    rows = lax.broadcasted_iota(jnp.int32, (3 * BUCKETS, WIDE + 2 * BLOCK), 0)
    columns = lax.broadcasted_iota(jnp.int32, (3 * BUCKETS, WIDE + 2 * BLOCK), 1)
    return jnp.where(rows == line_bucket(columns), 1.0, 0.0).astype(bf16)


def collapse():
    rows = lax.broadcasted_iota(jnp.int32, (3 * BUCKETS, WIDE + 4 * BLOCK), 0)
    columns = lax.broadcasted_iota(jnp.int32, (3 * BUCKETS, WIDE + 4 * BLOCK), 1)
    bucket = line_bucket(columns)
    bucket = jnp.where(columns == 5 * BLOCK, BUCKETS - 1, bucket)
    bucket = jnp.where(columns >= WIDE + 2 * BLOCK, 0, bucket)
    bucket = jnp.where(columns >= WIDE + 3 * BLOCK, BUCKETS - 1, bucket)
    return jnp.where(rows == bucket, 1.0, 0.0).astype(bf16)


def roll_rows(value, right):
    rows, width = value.shape
    index = lax.broadcasted_iota(jnp.int32, value.shape, 0)
    step = 1
    while step < rows:
        shift = step if right else width - step
        value = jnp.where((index // step) % 2 == 1, pltpu.roll(value, shift, 1), value)
        step *= 2
    return value


def dot(a, b):
    return jnp.dot(a, b, preferred_element_type=f32)


def dot_nt(a, b):
    return lax.dot_general(a, b, (((1,), (1,)), ((), ())), preferred_element_type=f32)


def split3(value):
    high = value.astype(bf16).astype(f32)
    rest = value - high
    middle = rest.astype(bf16).astype(f32)
    return high, middle, rest - middle


def dot_tn(a, b):
    return lax.dot_general(a, b, (((0,), (0,)), ((), ())), preferred_element_type=f32)


ROOT = float(np.sqrt(2.0 / np.pi))
CUBE = 0.044715


def factor_of(rows):
    return lax.rsqrt(jnp.mean(rows * rows, axis=-1, keepdims=True) + EPSILON)


def mp_places():
    mp = lax.axis_index("mp")
    y, core = mp // 2, mp % 2
    return mp, y, core, y * 2 + (1 - core), (1 - y) * 2 + core


def dp_places():
    dp = lax.axis_index("dp")
    return dp // 2, dp % 2


def remote(src, dst, send, recv, mp=None, dp=None):
    return pltpu.make_async_remote_copy(
        src_ref=src,
        dst_ref=dst,
        send_sem=send,
        recv_sem=recv,
        device_id=(lax.axis_index("dp") if dp is None else dp, lax.axis_index("mp") if mp is None else mp),
        device_id_type=pl.DeviceIdType.MESH,
    )


def beside(z):
    return z // 2 * 2 + 1 - z % 2


def meet(fast):
    mp, dp = lax.axis_index("mp"), lax.axis_index("dp")
    others = [(dp, (mp + d) % 4) for d in (1, 2, 3)]
    if fast:
        others.extend(((dp + d) % 8, mp) for d in range(1, 8))
    barrier = pltpu.get_barrier_semaphore()
    for other in others:
        pl.semaphore_signal(barrier, inc=1, device_id=other, device_id_type=pl.DeviceIdType.MESH)
    return lambda: pl.semaphore_wait(barrier, len(others))


def run(index, count=1, size=BLOCK):
    return pl.ds(pl.multiple_of(index * size, size), count * size)


class Scatter:

    def __init__(self, part, near, far, send, recv):
        self.part, self.near, self.far, self.send, self.recv = part, near, far, send, recv

    def block(self, c, core, y):
        return (c * 2 + core) * 2 + y

    def put(self, c, m, value, columns=slice(None)):
        self.part[run(self.block(c, m % 2, m // 2)), columns] = value.astype(bf16)

    def first(self, c):
        _, _, core, sibling, _ = mp_places()
        src = self.part.at[run(self.block(c, 1 - core, 0), 2)]
        return remote(src, self.near.at[run(c * 2, 2)], self.send.at[c, 0], self.recv.at[c, 0], sibling)

    def second(self, c):
        _, y, core, _, across = mp_places()
        src = self.part.at[run(self.block(c, core, 1 - y))]
        return remote(src, self.far.at[run(c)], self.send.at[c, 1], self.recv.at[c, 1], across)

    def start(self, c):
        self.first(c).start()

    def middle(self, c):
        _, y, core, _, _ = mp_places()
        self.first(c).wait_recv()
        at = run(self.block(c, core, 1 - y))
        self.part[at, :] = (self.part[at, :].astype(f32) + self.near[run(c * 2 + 1 - y), :].astype(f32)).astype(bf16)
        self.second(c).start()

    def finish(self, c):
        _, y, core, _, _ = mp_places()
        self.second(c).wait_recv()
        own = self.part[run(self.block(c, core, y)), :].astype(f32) + self.near[run(c * 2 + y), :].astype(f32)
        return own + self.far[run(c), :].astype(f32)

    def drain(self, c):
        self.first(c).wait_send()
        self.second(c).wait_send()


class Gather:

    def __init__(self, full, send, recv, size=BLOCK):
        self.full, self.send, self.recv, self.size = full, send, recv, size

    def at(self, c, m):
        return run(c * 4 + m, 1, self.size)

    def copy(self, c, kind):
        mp, _, _, sibling, across = mp_places()
        at = self.full.at[self.at(c, across if kind == 2 else mp)]
        return remote(at, at, self.send.at[c, kind], self.recv.at[c, kind], across if kind == 1 else sibling)

    def start(self, c):
        self.copy(c, 1).start()
        self.copy(c, 0).start()

    def forward(self, c):
        self.copy(c, 1).wait_recv()
        self.copy(c, 2).start()

    def finish(self, c):
        self.copy(c, 0).wait_recv()
        self.copy(c, 2).wait_recv()

    def drain(self, c):
        for kind in range(3):
            self.copy(c, kind).wait_send()


class Exchange:

    def __init__(self, given, taken, size, send, recv):
        self.given, self.taken, self.size, self.send, self.recv = given, taken, size, send, recv

    def copy(self, c, d):
        mp = lax.axis_index("mp")
        src = self.given.at[run(c * 3 + d - 1, 1, self.size)]
        dst = self.taken.at[run(c * 4 + mp, 1, self.size)]
        return remote(src, dst, self.send.at[c, d - 1], self.recv.at[c, d - 1], (mp + d) % 4)

    def start(self, c):
        for d in (2, 1, 3):
            self.copy(c, d).start()

    def finish(self, c):
        for d in (1, 2, 3):
            self.copy(c, d).wait_recv()

    def drain(self, c):
        for d in (1, 2, 3):
            self.copy(c, d).wait_send()


class Spread:

    def __init__(self, part, near, pair, far, send, recv):
        self.part, self.near, self.pair, self.far, self.send, self.recv = part, near, pair, far, send, recv
        self.each = part.shape[0] // 8

    def at(self, index, count=1):
        return run(index, count, self.each)

    def put(self, first_row, value):
        for r in range(value.shape[0] // self.each):
            j = first_row // self.each + r
            rows = value[r * self.each : (r + 1) * self.each]
            self.part[self.at(j % 2 * 4 + j // 2 % 2 * 2 + j // 4), :] = rows.astype(bf16)

    def copy(self, kind):
        z, x = dp_places()
        send, recv = self.send.at[kind], self.recv.at[kind]
        if kind == 0:
            src = self.part.at[self.at((1 - x) * 4, 4)]
            return remote(src, self.near, send, recv, dp=z * 2 + 1 - x)
        if kind == 1:
            src = self.part.at[self.at(x * 4 + (1 - z % 2) * 2, 2)]
            return remote(src, self.pair, send, recv, dp=beside(z) * 2 + x)
        src = self.part.at[self.at(x * 4 + z % 2 * 2 + 1 - z // 2)]
        return remote(src, self.far, send, recv, dp=(z + 2) % 4 * 2 + x)

    def start(self):
        self.copy(0).start()

    def middle(self):
        z, x = dp_places()
        self.copy(0).wait_recv()
        at = self.at(x * 4 + (1 - z % 2) * 2, 2)
        near = self.near[self.at((1 - z % 2) * 2, 2), :].astype(f32)
        self.part[at, :] = (self.part[at, :].astype(f32) + near).astype(bf16)
        self.copy(1).start()

    def sum_of(self, half):
        z, x = dp_places()
        total = self.part[self.at(x * 4 + z % 2 * 2 + half), :].astype(f32)
        total = total + self.near[self.at(z % 2 * 2 + half), :].astype(f32)
        return total + self.pair[self.at(half), :].astype(f32)

    def third(self):
        z, x = dp_places()
        self.copy(1).wait_recv()
        self.part[self.at(x * 4 + z % 2 * 2 + 1 - z // 2), :] = self.sum_of(1 - z // 2).astype(bf16)
        self.copy(2).start()

    def finish(self):
        z, _ = dp_places()
        self.copy(2).wait_recv()
        return self.sum_of(z // 2) + self.far[...].astype(f32)

    def drain(self):
        for kind in range(3):
            self.copy(kind).wait_send()


class Direct:

    def __init__(self, part, taken, send, recv):
        self.part, self.taken, self.send, self.recv = part, taken, send, recv
        self.each = part.shape[0] // 8

    put = Spread.put

    def at(self, index, count=1):
        return run(index, count, self.each)

    def block(self, dp):
        return self.at(dp % 2 * 4 + dp // 2 % 2 * 2 + dp // 4)

    def copy(self, d):
        to = (lax.axis_index("dp") + d) % 8
        src = self.part.at[self.block(to)]
        return remote(src, self.taken.at[run(d - 1, 1, self.each)], self.send.at[d - 1], self.recv.at[d - 1], dp=to)

    def start(self):
        for d in (4, 3, 5, 2, 6, 1, 7):
            self.copy(d).start()

    def finish(self):
        total = self.part[self.block(lax.axis_index("dp")), :].astype(f32)
        for d in range(1, 8):
            self.copy(d).wait_recv()
            total = total + self.taken[run(d - 1, 1, self.each), :].astype(f32)
        return total

    def drain(self):
        for d in range(1, 8):
            self.copy(d).wait_send()


class Total:

    def __init__(self, value, taken, send, recv):
        self.value, self.taken, self.send, self.recv = value, taken, send, recv

    def copy(self, kind):
        mp, dp = lax.axis_index("mp"), lax.axis_index("dp")
        send, recv = self.send.at[kind], self.recv.at[kind]
        if kind < 7:
            return remote(self.value.at[0], self.taken.at[kind], send, recv, dp=(dp + kind + 1) % 8)
        return remote(self.value.at[1], self.taken.at[kind], send, recv, mp=(mp + kind - 6) % 4)

    def start(self):
        for kind in range(7):
            self.copy(kind).start()

    def turn(self):
        total = self.value[0]
        for kind in range(7):
            self.copy(kind).wait_recv()
            total = total + self.taken[kind]
        self.value[1] = total
        for kind in range(7, 10):
            self.copy(kind).start()

    def finish(self):
        total = self.value[1]
        for kind in range(7, 10):
            self.copy(kind).wait_recv()
            total = total + self.taken[kind]
        return total

    def drain(self):
        for kind in range(10):
            self.copy(kind).wait_send()


def layer_kernel(
    fast,
    length_ref, across_ref, upward_ref, gain_a_ref, gain_f_ref, tables_ref,
    tokens_hbm, w_qkv_hbm, w_output_hbm, w_inner_hbm, w_outer_hbm, cot_hbm,
    *rest,
):
    outs, scratch = rest[: 9 if fast else 7], rest[9 if fast else 7 :]
    if fast:
        mixed_ref, input_ref, o_qkv_ref, o_output_ref, o_inner_ref, o_outer_ref, o_gain_a_ref, o_gain_f_ref, o_tables_ref = outs
    else:
        mixed_ref, input_ref, o_qkv_ref, o_output_ref, o_inner_ref, o_outer_ref, o_sums_ref = outs
    (
        x1, w_qkv_ref, w_inner_ref, w_outer_ref, cot_ref, load_sem,
        codes_ref, plane_ref, hot_ref, hot_t_ref, qa_ref, qb_ref, k2_ref, kt2_ref, v_ref, band_ref, band_t_ref, qt_ref,
        s_ref, res_ref, dv_ref, dqt_ref, bands_ref, dat_ref, sums_ref, gain_sum_ref, collapse_ref,
        att_ref, af_ref, att_send, att_recv,
        es_ref, ga_ref, es_send, es_recv,
        wo_ref, wo_send, wo_recv, wo_t_ref,
        nf_ref,
        ghl_ref, ghl_send, ghl_recv,
        feed_part, feed_send, feed_recv, norm_part, norm_send, norm_recv, last_send, last_recv, near_ref, far_ref,
        credit,
        low_ref, grad_low_ref, hidden_ref,
        *spreads,
    ) = scratch
    heads = tables_ref.shape[0]
    rows, model = x1.shape
    width = heads * 64
    units = w_inner_ref.shape[1]
    pieces = 4
    chunks = rows // CHUNK
    blocks = rows // BLOCK
    half_model = model // 2
    mp, _, _, sibling, across = mp_places()
    da_ref, dk_ref, wt_ref = qa_ref, res_ref, w_inner_ref

    att = Gather(af_ref, att_send, att_recv, CHUNK + CHUNK // 2)
    grad_att = Exchange(es_ref, ga_ref, BLOCK + BLOCK // 2, es_send, es_recv)
    wo = Gather(wo_ref, wo_send, wo_recv, width)
    grads = Gather(ghl_ref, ghl_send, ghl_recv)
    feed = Scatter(feed_part, near_ref, far_ref, feed_send, feed_recv)
    norm = Scatter(norm_part, near_ref, far_ref, norm_send, norm_recv)
    last = Scatter(norm_part, near_ref, far_ref, last_send, last_recv)
    if fast:
        outer = Spread(w_outer_ref, *spreads[0:5])
        inner = Spread(*spreads[5:11])
        output = Spread(*spreads[11:17])
        qkv_last = Direct(*spreads[23:27])
        small = Total(*spreads[27:31])

        def qkv(h):
            return Spread(*[ref.at[h] for ref in spreads[17:23]])

    def place(m, c):
        return run(m * chunks + c)

    loads = [
        pltpu.make_async_copy(src, dst, load_sem.at[i])
        for i, (src, dst) in enumerate(
            [
                (tokens_hbm, x1),
                (w_qkv_hbm, w_qkv_ref),
                (w_output_hbm, wo_ref.at[wo.at(0, mp)]),
                (w_inner_hbm, w_inner_ref),
                (w_outer_hbm, w_outer_ref),
                (cot_hbm, cot_ref),
                *[(tokens_hbm.at[place(m, c)], low_ref.at[run(c * 4 + m)]) for c in range(chunks) for m in range(4)],
                (tokens_hbm.at[run(mp * chunks, chunks)], cot_ref.at[run(0, chunks)]),
            ]
        )
    ]
    for load in loads[:-1]:
        load.start()
    everyone_is_here = meet(fast)

    def window(m, c):
        block = m * chunks + c
        start = min(max(block - 1, 0), blocks - 3)
        return range(start, start + 3), 2 - block


    expanded = dot(tables_ref[...], expansion())
    square_rows = lax.broadcasted_iota(jnp.int32, (BLOCK, BLOCK), 0)
    square_lanes = lax.broadcasted_iota(jnp.int32, (BLOCK, BLOCK), 1)
    for h in range(heads):
        line = jnp.broadcast_to(expanded[h : h + 1, :WIDE], (BLOCK, WIDE))
        band = roll_rows(line, True)
        band_ref[h] = band.astype(bf16)
        band_t_ref[h] = band.T.astype(bf16)
        level = roll_rows(jnp.broadcast_to(expanded[h : h + 1, WIDE : WIDE + BLOCK], (BLOCK, BLOCK)), True)
        upward = roll_rows(jnp.broadcast_to(expanded[h : h + 1, WIDE + BLOCK :], (BLOCK, BLOCK)), True)
        plane = jnp.where(
            (square_rows < CODES) & (square_lanes < CODES),
            level,
            jnp.where((square_rows >= CODES) & (square_lanes >= CODES), upward, 0.0),
        )
        plane_ref[h] = plane.astype(bf16)
    everyone_is_here()
    loads[2].wait()
    wo.start(0)
    loads[1].wait()
    loads[0].wait()
    gain_a = gain_a_ref[...].reshape(1, model).astype(f32)
    gain_f = gain_f_ref[...].reshape(1, model).astype(f32)
    codes_ref[0:1, :] = across_ref[...].reshape(1, rows)
    codes_ref[1:2, :] = upward_ref[...].reshape(1, rows)
    lanes = lax.broadcasted_iota(jnp.int32, (CHUNK, BLOCK), 1)
    low = lanes < FAR

    def prepare(j, carry):
        at = run(j, 1, CHUNK)
        x = x1[at, :].astype(f32)
        normed_rows = (x * factor_of(x) * gain_a).astype(bf16)
        x1[at, :] = normed_rows
        codes_lines = lax.broadcasted_iota(jnp.int32, (BLOCK, CHUNK), 0)
        hot_t = jnp.where(
            codes_lines == jnp.broadcast_to(codes_ref[0:1, at], (BLOCK, CHUNK)),
            1.0,
            jnp.where(codes_lines - CODES == jnp.broadcast_to(codes_ref[1:2, at], (BLOCK, CHUNK)), 1.0, 0.0),
        )
        hot = hot_t.T.astype(bf16)
        hot_t_ref[:, at] = hot_t.astype(bf16)
        hot_ref[at, :] = hot
        row = lax.broadcasted_iota(jnp.int32, (CHUNK, BLOCK), 0) + j * CHUNK
        block = row // BLOCK
        start = jnp.clip(block - 1, 0, blocks - 3)
        far = (lanes >= FAR) & (lanes < MASK)
        far_left = far & (lanes - FAR < start)
        far_right = far & (lanes - FAR > start + 2)
        key_side = jnp.where(
            (far & (lanes - FAR == block))
            | ((lanes == MASK) & (row >= length_ref[0]))
            | ((lanes >= LSE) & (lanes < LSE + 3)),
            1.0,
            0.0,
        )

        def part(h):
            columns = s_ref[:CHUNK, h // 2 * BLOCK : h // 2 * BLOCK + BLOCK]
            return columns if h % 2 == 0 else pltpu.roll(columns, 64, 1)

        s_ref[:CHUNK, :width] = dot_nt(normed_rows, w_qkv_ref[0])
        for h in range(heads):
            left = expanded[h : h + 1, 0:1]
            right = expanded[h : h + 1, WIDE - BLOCK - 1 : WIDE - BLOCK]
            query_side = jnp.where(far_left, left, jnp.where(far_right, right, jnp.where(lanes == MASK, DEAD, 0.0)))
            qa_ref[h, at, :] = dot(hot, plane_ref[h]).astype(bf16)
            qb_ref[h, at, :] = jnp.where(low, part(h).astype(bf16).astype(f32) * 0.125, query_side).astype(bf16)
        s_ref[:CHUNK, :width] = dot_nt(normed_rows, w_qkv_ref[1])
        for h in range(heads):
            second = jnp.where(low, part(h), key_side)
            k2_ref[h, at, :] = second.astype(bf16)
            kt2_ref[h, :, at] = second.T.astype(bf16)
        s_ref[:CHUNK, :width] = dot_nt(normed_rows, w_qkv_ref[2])
        for h in range(heads):
            v_ref[h, at, :] = jnp.where(low, part(h), 1.0).astype(bf16)
        return carry

    s_ref[:CHUNK, :] = jnp.zeros_like(s_ref[:CHUNK, :])
    lax.fori_loop(0, chunks, prepare, 0)
    wo.forward(0)
    gain_sum_ref[...] = jnp.zeros_like(gain_sum_ref)
    sums_ref[...] = jnp.zeros_like(sums_ref)
    collapse_ref[...] = collapse()

    half_low = lax.broadcasted_iota(jnp.int32, (CHUNK // 2, BLOCK), 1) < 64
    quarter_low = lax.broadcasted_iota(jnp.int32, (BLOCK // 2, BLOCK), 1) < 64

    def share_attended(c):
        at = run(c, 1, CHUNK)
        mine = att.at(c, mp).start
        third = att_ref[at, BLOCK:].astype(f32)
        af_ref[pl.ds(pl.multiple_of(mine, CHUNK // 2), CHUNK), :] = att_ref[at, :BLOCK]
        beside_it = jnp.where(half_low, third[: CHUNK // 2], pltpu.roll(third[CHUNK // 2 :], 64, 1)).astype(bf16)
        af_ref[pl.ds(pl.multiple_of(mine + CHUNK, CHUNK // 2), CHUNK // 2), :] = beside_it
        att.start(c)

    def hidden_of(c):
        att.finish(c)
        hidden = low_ref[run(c, 1, CHUNK), :].astype(f32)
        for m in range(pieces):
            first = (c * 4 + m) * (CHUNK + CHUNK // 2)
            pair = af_ref[pl.ds(pl.multiple_of(first, CHUNK // 2), CHUNK), :]
            third = af_ref[pl.ds(pl.multiple_of(first + CHUNK, CHUNK // 2), CHUNK // 2), :]
            third = jnp.concatenate([third, pltpu.roll(third.astype(f32), 64, 1).astype(bf16)], axis=0)
            weights = wo_ref[m * width : (m + 1) * width, :]
            hidden = hidden + dot(jnp.concatenate([pair, third[:, :64]], axis=1), weights)
        nf_ref[run(c, 1, CHUNK), :] = (hidden * factor_of(hidden) * gain_f).astype(bf16)
        for m in range(pieces):

            @pl.when(mp == m)
            def _(m=m):
                hidden_ref[run(c), :] = hidden[m * BLOCK : (m + 1) * BLOCK]

    def grad_of(c):
        grad_normed = norm.finish(c)
        hidden = hidden_ref[run(c), :]
        factor = factor_of(hidden)
        hat = hidden * factor
        scaled = grad_normed * gain_f
        back = factor * (scaled - hat * jnp.mean(scaled * hat, axis=-1, keepdims=True))
        grad = cot_ref[place(mp, c), :].astype(f32) + back
        input_ref[run(c), :] = grad
        gain_sum_ref[0:1, :] += jnp.sum(grad_normed * hat, axis=0, keepdims=True)
        grad_low = grad.astype(bf16)
        ghl_ref[grads.at(c, mp), :] = grad_low

        size = BLOCK + BLOCK // 2
        every = dot(grad_low, wo_t_ref[...])
        for m in range(pieces):
            third = every[:, m * 256 + BLOCK : (m + 1) * 256]
            third = jnp.where(quarter_low, third[: BLOCK // 2], pltpu.roll(third[BLOCK // 2 :], 64, 1))
            value = jnp.concatenate([every[:, m * 256 : m * 256 + BLOCK], third], axis=0).astype(bf16)

            @pl.when(mp == m)
            def _(value=value):
                ga_ref[run(c * 4 + mp, 1, size), :] = value

            @pl.when(mp != m)
            def _(value=value, m=m):
                es_ref[run(c * 3 + (m - mp + 4) % 4 - 1, 1, size), :] = value

        grad_att.start(c)

    def attend(c, h, carry):
        query_far = jnp.concatenate([qa_ref[h, place(m, c), :] for m in range(pieces)], axis=0)
        query_near = jnp.concatenate([qb_ref[h, place(m, c), :] for m in range(pieces)], axis=0)
        query = jnp.concatenate([query_far, query_near], axis=1)
        tops, mixes = [], []
        for j in range(chunks):
            cols = slice(j * CHUNK, (j + 1) * CHUNK)
            s = dot(query, jnp.concatenate([hot_t_ref[:, cols], kt2_ref[h, :, cols]], axis=0))
            lines = []
            for m in range(pieces):
                near, shift = window(m, c)
                tiles = []
                for b in range(pieces):
                    tile = s[m * BLOCK : (m + 1) * BLOCK, b * BLOCK : (b + 1) * BLOCK]
                    if j * pieces + b in near:
                        at = (j * pieces + b + shift) * BLOCK
                        tile = tile + band_ref[h, :, at : at + BLOCK].astype(f32)
                    tiles.append(tile)
                lines.append(jnp.concatenate(tiles, axis=1))
            s = jnp.concatenate(lines, axis=0)
            tops.append(jnp.max(s, axis=1, keepdims=True))
            mixes.append(dot(jnp.exp(s - tops[j]).astype(bf16), v_ref[h, cols, :]))
        top = functools.reduce(jnp.maximum, tops)
        mixed = sum(mix * jnp.exp(part - top) for mix, part in zip(mixes, tops))
        res_ref[run(h, 1, CHUNK), :] = jnp.where(low, mixed / pltpu.roll(mixed, 64, 1), 0.0)
        high, middle, rest = split3(-(top + jnp.log(mixed[:, 64:65])))
        second = jnp.where(
            lanes == LSE,
            high,
            jnp.where(lanes == LSE + 1, middle, jnp.where(lanes == LSE + 2, rest, query_near.astype(f32))),
        )
        qt_ref[h, c, :BLOCK, :] = query_far.astype(f32).T.astype(bf16)
        qt_ref[h, c, BLOCK:, :] = second.T.astype(bf16)

        return carry

    for c in range(chunks):
        lax.fori_loop(0, heads, functools.partial(attend, c), 0)
        if c > 0:
            att.forward(c - 1)
        if c == 1:
            wo.finish(0)
            for m in range(pieces):
                turned = wo_ref[m * width : (m + 1) * width, :].astype(f32).T
                wo_t_ref[:, m * 256 : m * 256 + width] = turned.astype(bf16)
                wo_t_ref[:, m * 256 + width : (m + 1) * 256] = jnp.zeros((model, 256 - width), bf16)
        pairs = []
        for g in range(0, heads, 2):
            pair = res_ref[g * CHUNK : (g + 1) * CHUNK, :]
            if g + 1 < heads:
                pair = jnp.where(low, pair, pltpu.roll(res_ref[(g + 1) * CHUNK : (g + 2) * CHUNK, :], 64, 1))
            pairs.append(pair.astype(bf16))
        att_ref[run(c, 1, CHUNK), :] = jnp.concatenate(pairs, axis=1)
        share_attended(c)
    for load in loads[3:-1]:
        load.wait()
    outer_t = w_outer_ref[...].astype(f32).T.astype(bf16)
    inner_t = w_inner_ref[...].astype(f32).T.astype(bf16)
    for r in range(units // BLOCK):
        qa_ref[r // 2, run(r % 2, 1, model), :] = outer_t[:, r * BLOCK : (r + 1) * BLOCK]
        dat_ref[r // 2, :, r % 2 * model : (r % 2 + 1) * model] = inner_t[r * BLOCK : (r + 1) * BLOCK, :]

    steps = units // 256

    def feed_step(t, carry):
        c = t // steps
        b = t % steps

        @pl.when(b == 0)
        def _():
            hidden_of(c)

        at = run(b, 1, 256)
        x = nf_ref[run(c, 1, CHUNK), :]
        cot = jnp.concatenate([cot_ref[place(m, c), :] for m in range(pieces)], axis=0)
        inner_units = dot(x, w_inner_ref[:, at])
        grad_act = dot(cot, jnp.concatenate([qa_ref[b, :model, :], qa_ref[b, model:, :]], axis=1))
        square = inner_units * inner_units
        tanh = jnp.tanh(ROOT * inner_units * (1.0 + CUBE * square))
        half = 0.5 * (1.0 + tanh)
        slope = half + 0.5 * inner_units * (1.0 - tanh * tanh) * (ROOT + 3.0 * CUBE * ROOT * square)
        activated = (inner_units * half).astype(bf16)
        grad_low = (slope * grad_act).astype(bf16)
        low_ref[run(c, 1, CHUNK), at] = activated
        grad_low_ref[run(c, 1, CHUNK), at] = grad_low

        @pl.when(b == steps - 1)
        def _():
            chunk_rows = run(c, 1, CHUNK)
            for p in range(model // 256):
                cols = slice(p * 256, (p + 1) * 256)
                turned = [
                    dat_ref[r // 2, :, r % 2 * model + p * 256 : r % 2 * model + (p + 1) * 256] for r in range(units // BLOCK)
                ]
                part_norm = dot(grad_low_ref[chunk_rows, :], jnp.concatenate(turned, axis=0))
                part_ffn = dot(low_ref[chunk_rows, :], w_outer_ref[:, cols])
                for m in range(pieces):
                    norm.put(c, m, part_norm[m * BLOCK : (m + 1) * BLOCK], cols)
                    feed.put(c, m, part_ffn[m * BLOCK : (m + 1) * BLOCK], cols)
            norm.start(c)

        @pl.when(t == 2)
        def _():
            att.forward(2)

        @pl.when(t == 3)
        def _():
            norm.middle(0)

        @pl.when(t == 6)
        def _():
            norm.middle(1)

        @pl.when(t == 7)
        def _():
            grad_of(0)

        return carry

    lax.fori_loop(0, chunks * steps, feed_step, 0)

    def weights_of(is_outer):
        for b in range(2):
            at = slice(b * half_model, (b + 1) * half_model)
            total = jnp.zeros((half_model, units), f32)
            for c in range(chunks):
                if is_outer:
                    left = jnp.concatenate([cot_ref[place(m, c), at] for m in range(pieces)], axis=0)
                    total = total + dot_tn(left, low_ref[run(c, 1, CHUNK), :])
                else:
                    total = total + dot_tn(nf_ref[run(c, 1, CHUNK), at], grad_low_ref[run(c, 1, CHUNK), :])
            if fast:
                (outer if is_outer else inner).put(b * half_model, total)
            else:
                (o_outer_ref if is_outer else o_inner_ref)[at, :] = total

    weights_of(True)
    if fast:
        outer.start()
    norm.middle(2)
    weights_of(False)
    if fast:
        inner.start()
    grad_of(1)
    wt_ref[...] = jnp.zeros_like(wt_ref)
    for k in range(3):
        for h in range(heads):
            wt_ref[h * 256 + k * 64 : h * 256 + (k + 1) * 64, :] = w_qkv_ref[k, h * 64 : (h + 1) * 64, :]

    def receive(c):
        grad_att.finish(c)
        at = run(c, 1, CHUNK)
        pairs, thirds = [], []
        for m in range(pieces):
            first = (c * 4 + m) * (BLOCK + BLOCK // 2)
            pairs.append(ga_ref[pl.ds(pl.multiple_of(first, BLOCK // 2), BLOCK), :])
            third = ga_ref[pl.ds(pl.multiple_of(first + BLOCK, BLOCK // 2), BLOCK // 2), :].astype(f32)
            thirds.extend([third, pltpu.roll(third, 64, 1)])
        received = [jnp.concatenate(pairs, axis=0).astype(f32), jnp.concatenate(thirds, axis=0)]
        for h in range(heads):
            pair = slice(h // 2 * BLOCK, h // 2 * BLOCK + BLOCK)
            grad = received[h // 2]
            out = att_ref[at, pair].astype(f32)
            if h % 2 == 1:
                grad = pltpu.roll(grad, 64, 1)
                out = pltpu.roll(out, 64, 1)
            high, middle, rest = split3(-jnp.sum(jnp.where(low, grad * out, 0.0), axis=1, keepdims=True))
            grad = jnp.where(
                low,
                grad,
                jnp.where(
                    lanes == FAR, high, jnp.where(lanes == FAR + 1, middle, jnp.where(lanes == FAR + 2, rest, 0.0))
                ),
            )
            da_ref[h, at, :] = grad.astype(bf16)
            dat_ref[h, :, at] = grad.T.astype(bf16)

    lines16 = lax.broadcasted_iota(jnp.int32, (16, rows), 0)
    block16 = lax.broadcasted_iota(jnp.int32, (16, rows), 1) // BLOCK
    start16 = jnp.clip(block16 - 1, 0, blocks - 3)
    real = lines16 < blocks
    tall_low = lax.broadcasted_iota(jnp.int32, (rows, BLOCK), 1) < 64

    def fold(value):
        total = value[:, :BLOCK]
        for b in range(1, value.shape[1] // BLOCK):
            total = total + value[:, b * BLOCK : (b + 1) * BLOCK]
        return jnp.sum(total, axis=0, keepdims=True)

    def mix(k):
        mixed_ref[run(k), :] = (hidden_ref[run(k), :] + feed.finish(k)).astype(bf16)

    def events(h, c, j):
        due = {
            (0, 0, 2): [lambda: grad_of(2)],
            (0, 1, 2): [lambda: grads.start(0)],
            (0, 2, 2): [lambda: grads.start(1)],
            (1, 0, 2): [lambda: grads.forward(0), lambda: grads.start(2), lambda: grads.forward(1)],
            (1, 1, 2): [lambda: feed.start(0), lambda: feed.start(1), lambda: feed.start(2)],
            (1, 2, 2): [lambda: grads.forward(2), lambda: feed.middle(0), lambda: feed.middle(1)],
            (2, 0, 2): [lambda: feed.middle(2)],
            (2, 1, 2): [lambda: mix(0), lambda: mix(1)],
            (2, 2, 2): [lambda: mix(2)],
        }
        if fast:
            for at, what in {
                (1, 1, 2): [outer.middle],
                (1, 2, 2): [inner.middle],
                (2, 0, 2): [outer.third, lambda: qkv(0).middle()],
                (2, 1, 2): [inner.third, lambda: qkv(0).third()],
                (2, 2, 2): [lambda: qkv(1).middle(), output.middle],
            }.items():
                due[at] = due.get(at, []) + what
        for (head_due, chunk_due, panel_due), what in due.items():
            if (chunk_due, panel_due) == (c, j):

                @pl.when(h == head_due)
                def _(what=what):
                    for each in what:
                        each()

    def leave(h, spread):
        grads_of = run(h, 1, 256)
        grad_qkv = dot_tn(nf_ref[:, grads_of], x1[...]).T
        if fast:
            spread.put(0, grad_qkv)
        else:
            o_qkv_ref[h] = grad_qkv
        if fast:
            spread.start()

    def leave_tables(h):
        band = roll_rows(bands_ref[...].T, False)
        spread = dqt_ref[:BLOCK, :]
        high = spread.astype(bf16)
        rest = (spread - high.astype(f32)).astype(bf16)
        plane = (dot(high, hot_ref[...]) + dot(rest, hot_ref[...])).T
        plane = jnp.where((square_rows < CODES) == (square_lanes < CODES), plane, 0.0)
        plane = roll_rows(plane, False)
        far = dqt_ref[BLOCK + FAR : BLOCK + FAR + 16, :]
        line = jnp.concatenate(
            [
                jnp.sum(band, axis=0, keepdims=True),
                jnp.sum(plane[:CODES], axis=0, keepdims=True),
                jnp.sum(plane[CODES:], axis=0, keepdims=True),
                fold(jnp.where(real & (lines16 < start16), far, 0.0)),
                fold(jnp.where(real & (lines16 > start16 + 2), far, 0.0)),
            ],
            axis=1,
        )
        sums_ref[...] += jnp.where(lax.broadcasted_iota(jnp.int32, sums_ref.shape, 0) == h, line, 0.0)

    def head(h, carry):
        dk_ref[...] = jnp.zeros_like(dk_ref)
        dv_ref[...] = jnp.zeros_like(dv_ref)
        bands_ref[...] = jnp.zeros_like(bands_ref)

        for c in range(chunks):

            @pl.when(h == 0)
            def _(c=c):
                receive(c)

            at = slice(c * CHUNK, (c + 1) * CHUNK)
            query = jnp.concatenate([qb_ref[h, place(m, c), :] for m in range(pieces)], axis=0)
            for j in range(chunks):
                keys = slice(j * CHUNK, (j + 1) * CHUNK)
                s = dot(jnp.concatenate([hot_ref[keys, :], k2_ref[h, keys, :]], axis=1), qt_ref[h, c])
                columns = []
                for m in range(pieces):
                    near, shift = window(m, c)
                    tiles = []
                    for b in range(pieces):
                        tile = s[b * BLOCK : (b + 1) * BLOCK, m * BLOCK : (m + 1) * BLOCK]
                        if j * pieces + b in near:
                            of = (j * pieces + b + shift) * BLOCK
                            tile = tile + band_t_ref[h, of : of + BLOCK, :].astype(f32)
                        tiles.append(tile)
                    columns.append(jnp.concatenate(tiles, axis=0))
                probs = jnp.exp(jnp.concatenate(columns, axis=1))
                probs_t = probs.astype(bf16)
                grad_t = (probs * dot(v_ref[h, keys, :], dat_ref[h, :, at])).astype(bf16)
                grad_low_ref[keys, :CHUNK] = grad_t
                dv_ref[keys, :] += dot(probs_t, da_ref[h, at, :])
                dk_ref[keys, :] += dot(grad_t, query)
                if j < chunks - 1:
                    events(h, c, j)
            dq = dot(jnp.concatenate([hot_t_ref[...], kt2_ref[h]], axis=0), grad_low_ref[:, :CHUNK])
            for m in range(pieces):
                dqt_ref[:, place(m, c)] = dq[:, m * BLOCK : (m + 1) * BLOCK]
                near, shift = window(m, c)
                of = slice((near.start + shift) * BLOCK, (near.stop + shift) * BLOCK)
                keys = slice(near.start * BLOCK, near.stop * BLOCK)
                bands_ref[of, :] += grad_low_ref[keys, m * BLOCK : (m + 1) * BLOCK].astype(f32)
            events(h, c, chunks - 1)

        dq = dqt_ref[BLOCK:, :].T * 0.125
        grads_of = run(h, 1, 256)
        nf_ref[:, grads_of] = jnp.concatenate(
            [jnp.where(tall_low, dq, pltpu.roll(dk_ref[...], 64, 1)), jnp.where(tall_low, dv_ref[...], 0.0)], axis=1
        ).astype(bf16)

        @pl.when(h < heads - 1)
        def _():
            leave(h, qkv(h) if fast else None)
            leave_tables(h)

        @pl.when(h == 1)
        def _():
            for c in range(chunks):
                grads.finish(c)
            grad_output = dot_tn(att_ref[...], ghl_ref[...]).T
            if fast:
                output.put(0, grad_output)
            else:
                o_output_ref[...] = grad_output[:, :width]
            if fast:
                output.start()

        return carry

    lax.fori_loop(0, heads, head, 0)

    credits = [(sibling, credit.at[0]), (across, credit.at[1])]
    for other, sem in credits:
        pl.semaphore_signal(
            sem, inc=1, device_id=(lax.axis_index("dp"), other), device_id_type=pl.DeviceIdType.MESH
        )
    leave(heads - 1, qkv_last if fast else None)
    loads[-1].start()
    for c in range(chunks):
        norm.drain(c)
    gain_total = jnp.zeros((1, model), f32)
    for c in range(chunks):
        at = [place(m, c) for m in range(pieces)]
        grad_rows = jnp.concatenate([nf_ref[rows_of, :] for rows_of in at], axis=0)
        sums = []
        for p in range(model // 256):
            cols = slice(p * 256, (p + 1) * 256)
            partial = dot(grad_rows, wt_ref[:, cols])
            normed_rows = jnp.concatenate([x1[rows_of, cols] for rows_of in at], axis=0)
            sums.append(jnp.sum(partial * normed_rows.astype(f32), axis=0, keepdims=True))
            for m in range(pieces):
                last.put(c, m, partial[m * BLOCK : (m + 1) * BLOCK], cols)
        gain_total = gain_total + jnp.concatenate(sums, axis=1)
        if c == 0:
            for _, sem in credits:
                pl.semaphore_wait(sem, 1)
        last.start(c)
        if c > 0:
            last.middle(c - 1)
    leave_tables(heads - 1)
    last.middle(chunks - 1)
    gain_total = gain_total / gain_a
    tables = sum(dot_nt(part.astype(bf16), collapse_ref[...]) for part in split3(sums_ref[...]))[:heads]
    if fast:
        lines = model // BLOCK
        small.value[0] = jnp.zeros_like(small.value[0])
        for i in range(lines):
            lane = slice(i * BLOCK, (i + 1) * BLOCK)
            small.value[0, i : i + 1, :] = gain_total[:, lane]
            small.value[0, lines + i : lines + i + 1, :] = gain_sum_ref[0:1, lane]
        small.value[0, 2 * lines : 2 * lines + heads, : 3 * BUCKETS] = tables
        small.start()
        output.third()
        qkv(1).third()
        o_outer_ref[...] = outer.finish()
        small.turn()
        o_output_ref[...] = output.finish()[:, :width].T
    loads[-1].wait()
    for c in range(chunks):
        x = cot_ref[run(c), :].astype(f32)
        grad_normed = last.finish(c)
        factor = factor_of(x)
        hat = x * factor
        scaled = grad_normed * gain_a
        back = factor * (scaled - hat * jnp.mean(scaled * hat, axis=-1, keepdims=True))
        input_ref[run(c), :] += back
    if fast:
        o_inner_ref[...] = inner.finish()
    if fast:
        low_each = lax.broadcasted_iota(jnp.int32, (model // 8, BLOCK), 1) < 64
        parts = [(qkv(h) if h < heads - 1 else qkv_last).finish() for h in range(heads)]
        for k in range(3):
            for h in range(0, heads, 2):
                at = slice(0, BLOCK) if k < 2 else slice(BLOCK, 2 * BLOCK)
                one = parts[h][:, at]
                one = pltpu.roll(one, 64, 1) if k == 1 else one
                if h + 1 < heads:
                    two = parts[h + 1][:, at]
                    two = two if k == 1 else pltpu.roll(two, 64, 1)
                    o_qkv_ref[k, :, h * 64 : (h + 2) * 64] = jnp.where(low_each, one, two)
                else:
                    o_qkv_ref[k, :, h * 64 :] = one[:, :64]
        totals = small.finish()
        for i in range(lines):
            o_gain_a_ref[i * BLOCK : (i + 1) * BLOCK] = totals[i : i + 1].reshape(BLOCK)
            o_gain_f_ref[i * BLOCK : (i + 1) * BLOCK] = totals[lines + i : lines + i + 1].reshape(BLOCK)
        o_tables_ref[...] = small.value[1, 2 * lines : 2 * lines + heads, : 3 * BUCKETS]
        outer.drain()
        inner.drain()
        output.drain()
        for h in range(heads - 1):
            qkv(h).drain()
        qkv_last.drain()
        small.drain()
    else:
        o_sums_ref[...] = jnp.zeros_like(o_sums_ref)
        o_sums_ref[0:1, :] = gain_total
        o_sums_ref[1:2, :] = gain_sum_ref[0:1, :]
        o_sums_ref[2 : 2 + heads, : 3 * BUCKETS] = tables
    wo.drain(0)
    for c in range(chunks):
        for each in (att, grad_att, grads, feed, last):
            each.drain(c)


def spread_scratch(rows, columns, lead=(), own_part=True):
    buffers = [pltpu.VMEM((*lead, 8 * rows, columns), bf16)] if own_part else []
    return buffers + [
        pltpu.VMEM((*lead, 4 * rows, columns), bf16),
        pltpu.VMEM((*lead, 2 * rows, columns), bf16),
        pltpu.VMEM((*lead, rows, columns), bf16),
        pltpu.SemaphoreType.DMA((*lead, 3)),
        pltpu.SemaphoreType.DMA((*lead, 3)),
    ]


def hand_over_kernel(*refs):
    count = len(refs) // 2
    for i in range(count):
        refs[count + i][...] = refs[i][...]


def hand_over(results):
    full = pl.BlockSpec(memory_space=pltpu.VMEM)
    return pl.pallas_call(
        hand_over_kernel,
        in_specs=[full] * len(results),
        out_specs=[full] * len(results),
        out_shape=[jax.ShapeDtypeStruct(each.shape, each.dtype) for each in results],
        name="hand_over",
    )(*results)


def local(
    fast,
    tokens, lengths, horizontal, vertical, gain_attn, w_qkv, bias_tables, w_output, gain_ffn, w_inner, w_outer, cotangent,
):
    rows, model = tokens.shape
    heads = bias_tables.shape[1]
    width = w_qkv.shape[2]
    units = w_inner.shape[1]
    share = rows // lax.axis_size("mp")
    chunks = rows // CHUNK
    each = model // 8
    sums = (8, WIDE + 4 * BLOCK)

    def dma(*shape):
        return pltpu.SemaphoreType.DMA(shape)

    def vmem(*shape, dtype=bf16):
        return pltpu.VMEM(shape, dtype)

    scratch = [
        vmem(rows, model), vmem(3, width, model), vmem(model, units), vmem(units, model),
        vmem(rows, model), dma(7 + 4 * chunks),
        vmem(8, rows, dtype=jnp.int32), vmem(heads, BLOCK, BLOCK), vmem(rows, BLOCK), vmem(BLOCK, rows), vmem(heads, rows, BLOCK),
        vmem(heads, rows, BLOCK), vmem(heads, rows, BLOCK), vmem(heads, BLOCK, rows), vmem(heads, rows, BLOCK),
        vmem(heads, BLOCK, WIDE), vmem(heads, WIDE, BLOCK),
        vmem(heads, chunks, 256, CHUNK),
        vmem(CHUNK, 256, dtype=f32), vmem(heads * CHUNK, BLOCK, dtype=f32), vmem(rows, BLOCK, dtype=f32),
        vmem(256, rows, dtype=f32), vmem(WIDE, BLOCK, dtype=f32), vmem(heads, BLOCK, rows),
        vmem(*sums, dtype=f32), vmem(8, model, dtype=f32), vmem(3 * BUCKETS, sums[1]),
        vmem(rows, 256), vmem(6 * rows, BLOCK), dma(chunks, 3), dma(chunks, 3),
        vmem(chunks * 9 * BLOCK // 2, BLOCK), vmem(chunks * 6 * BLOCK, BLOCK), dma(chunks, 3), dma(chunks, 3),
        vmem(4 * width, model), dma(1, 3), dma(1, 3), vmem(model, 4 * 256),
        vmem(rows, model),
        vmem(rows, model), dma(chunks, 3), dma(chunks, 3),
        vmem(rows, model), dma(chunks, 2), dma(chunks, 2), vmem(rows, model), dma(chunks, 2), dma(chunks, 2),
        dma(chunks, 2), dma(chunks, 2), vmem(rows // 2, model), vmem(share, model),
        pltpu.SemaphoreType.REGULAR((2,)),
        vmem(rows, units), vmem(rows, units), vmem(share, model, dtype=f32),
    ]
    outs = [((share, model), bf16), ((share, model), f32)]
    if fast:
        outs += [
            ((3, each, width), f32), ((width, each), f32), ((each, units), f32), ((each, units), f32),
            ((model,), f32), ((model,), f32), ((heads, 3 * BUCKETS), f32),
        ]
        scratch += [
            *spread_scratch(each, units, own_part=False), *spread_scratch(each, units), *spread_scratch(each, 256),
            *spread_scratch(each, 256, lead=(heads - 1,)),
            vmem(8 * each, 256), vmem(7 * each, 256), dma(7), dma(7),
            vmem(2, 16, BLOCK, dtype=f32), vmem(10, 16, BLOCK, dtype=f32), dma(10), dma(10),
        ]
    else:
        outs += [
            ((heads, model, 256), f32), ((model, width), f32), ((model, units), f32), ((model, units), f32), ((8, model), f32),
        ]
    full = pl.BlockSpec(memory_space=pltpu.VMEM)
    anywhere = pl.BlockSpec(memory_space=pl.ANY)
    results = pl.pallas_call(
        functools.partial(layer_kernel, fast),
        in_specs=[pl.BlockSpec(memory_space=pltpu.SMEM)] + [full] * 5 + [anywhere] * 6,
        out_specs=[full] * len(outs),
        out_shape=[jax.ShapeDtypeStruct(*out) for out in outs],
        scratch_shapes=scratch,
        compiler_params=pltpu.CompilerParams(vmem_limit_bytes=64 * MIB, collective_id=1, has_side_effects=True),
        name="layer",
    )(
        lengths, horizontal, vertical, gain_attn, gain_ffn, bias_tables.T,
        tokens, jnp.swapaxes(w_qkv, 1, 2), w_output, w_inner, w_outer, cotangent,
    )
    if fast:
        mixed, input_grad, qkv, output, inner, outer, gain_a, gain_f, tables = hand_over(results)
        return mixed, input_grad, qkv, output, inner, outer.T, gain_a, gain_f, tables.T
    mixed, input_grad, qkv, output, inner, outer, sums = results
    qkv = qkv[:, :, : 3 * 64].reshape(heads, model, 3, 64).transpose(2, 1, 0, 3).reshape(3, model, width)
    gains = lax.psum(sums[:2], ("dp", "mp"))
    tables = lax.psum(sums[2 : 2 + heads, : 3 * BUCKETS], "dp").T

    def spread(x, axis):
        return lax.psum_scatter(x, "dp", scatter_dimension=axis, tiled=True)

    return (
        mixed, input_grad, spread(qkv, 1), spread(output.T, 1), spread(inner, 0), spread(outer.T, 1),
        gains[0], gains[1], tables,
    )


def solution(mesh):
    fast = mesh.shape["dp"] == 8
    return jax.shard_map(
        functools.partial(local, fast),
        mesh=mesh,
        in_specs=(
            P("dp", None), P("dp"), P("dp"), P("dp"), P(), P(None, None, "mp"), P(None, "mp"), P("mp", None), P(),
            P(None, "mp"), P("mp", None), P("dp", None),
        ),
        out_specs=(
            P(("dp", "mp"), None), P(("dp", "mp"), None), P(None, "dp", "mp"), P("mp", "dp"), P("dp", "mp"),
            P("mp", "dp"), P(), P(), P(None, "mp"),
        ),
        check_vma=False,
    )
```

```python
import functools
import jax
import jax.numpy as jnp
import numpy as np
from jax import lax
from jax.experimental import pallas as pl
from jax.experimental.pallas import tpu as pltpu
from jax.sharding import PartitionSpec as P

BUCKETS = 32
CODES = 64
HALF = BUCKETS // 2
EPSILON = 1e-06
DEAD = -1e9
CHUNK = 512
BLOCK = 128
BAND = 3 * BLOCK
WIDE = 6 * BLOCK
FAR = 64
MASK = 76
LSE = 80
MIB = 2**20

f32 = jnp.float32
bf16 = jnp.bfloat16


def line_bucket(columns):
    line = jnp.clip(columns - 2 * BLOCK, -HALF, HALF - 1) + HALF
    line = jnp.where(columns < 5 * BLOCK, line, 0)
    wrapped = columns % BLOCK
    wrapped = jnp.where(wrapped < CODES, wrapped, wrapped - BLOCK)
    plane = jnp.clip(wrapped, -HALF, HALF - 1) + HALF
    return jnp.where(
        columns < WIDE, line, jnp.where(columns < WIDE + BLOCK, BUCKETS + plane, 2 * BUCKETS + plane)
    )


def expansion():
    rows = lax.broadcasted_iota(jnp.int32, (3 * BUCKETS, WIDE + 2 * BLOCK), 0)
    columns = lax.broadcasted_iota(jnp.int32, (3 * BUCKETS, WIDE + 2 * BLOCK), 1)
    return jnp.where(rows == line_bucket(columns), 1.0, 0.0).astype(bf16)


def collapse():
    rows = lax.broadcasted_iota(jnp.int32, (3 * BUCKETS, WIDE + 4 * BLOCK), 0)
    columns = lax.broadcasted_iota(jnp.int32, (3 * BUCKETS, WIDE + 4 * BLOCK), 1)
    bucket = line_bucket(columns)
    bucket = jnp.where(columns == 5 * BLOCK, BUCKETS - 1, bucket)
    bucket = jnp.where(columns >= WIDE + 2 * BLOCK, 0, bucket)
    bucket = jnp.where(columns >= WIDE + 3 * BLOCK, BUCKETS - 1, bucket)
    return jnp.where(rows == bucket, 1.0, 0.0).astype(bf16)


def roll_rows(value, right):
    rows, width = value.shape
    index = lax.broadcasted_iota(jnp.int32, value.shape, 0)
    step = 1
    while step < rows:
        shift = step if right else width - step
        value = jnp.where((index // step) % 2 == 1, pltpu.roll(value, shift, 1), value)
        step *= 2
    return value


def dot(a, b):
    return jnp.dot(a, b, preferred_element_type=f32)


def dot_nt(a, b):
    return lax.dot_general(a, b, (((1,), (1,)), ((), ())), preferred_element_type=f32)


def split3(value):
    high = value.astype(bf16).astype(f32)
    rest = value - high
    middle = rest.astype(bf16).astype(f32)
    return high, middle, rest - middle


def dot_tn(a, b):
    return lax.dot_general(a, b, (((0,), (0,)), ((), ())), preferred_element_type=f32)


ROOT = float(np.sqrt(2.0 / np.pi))
CUBE = 0.044715


def factor_of(rows):
    return lax.rsqrt(jnp.mean(rows * rows, axis=-1, keepdims=True) + EPSILON)


def mp_places():
    mp = lax.axis_index("mp")
    y, core = mp // 2, mp % 2
    return mp, y, core, y * 2 + (1 - core), (1 - y) * 2 + core


def dp_places():
    dp = lax.axis_index("dp")
    return dp // 2, dp % 2


def remote(src, dst, send, recv, mp=None, dp=None):
    return pltpu.make_async_remote_copy(
        src_ref=src,
        dst_ref=dst,
        send_sem=send,
        recv_sem=recv,
        device_id=(lax.axis_index("dp") if dp is None else dp, lax.axis_index("mp") if mp is None else mp),
        device_id_type=pl.DeviceIdType.MESH,
    )


def beside(z):
    return z // 2 * 2 + 1 - z % 2


def meet(fast):
    mp, dp = lax.axis_index("mp"), lax.axis_index("dp")
    others = [(dp, (mp + d) % 4) for d in (1, 2, 3)]
    if fast:
        others.extend(((dp + d) % 8, mp) for d in range(1, 8))
    barrier = pltpu.get_barrier_semaphore()
    for other in others:
        pl.semaphore_signal(barrier, inc=1, device_id=other, device_id_type=pl.DeviceIdType.MESH)
    return lambda: pl.semaphore_wait(barrier, len(others))


def run(index, count=1, size=BLOCK):
    return pl.ds(pl.multiple_of(index * size, size), count * size)


class Scatter:

    def __init__(self, part, near, far, send, recv):
        self.part, self.near, self.far, self.send, self.recv = part, near, far, send, recv

    def block(self, c, core, y):
        return (c * 2 + core) * 2 + y

    def put(self, c, m, value, columns=slice(None)):
        self.part[run(self.block(c, m % 2, m // 2)), columns] = value.astype(bf16)

    def first(self, c):
        _, _, core, sibling, _ = mp_places()
        src = self.part.at[run(self.block(c, 1 - core, 0), 2)]
        return remote(src, self.near.at[run(c * 2, 2)], self.send.at[c, 0], self.recv.at[c, 0], sibling)

    def second(self, c):
        _, y, core, _, across = mp_places()
        src = self.part.at[run(self.block(c, core, 1 - y))]
        return remote(src, self.far.at[run(c)], self.send.at[c, 1], self.recv.at[c, 1], across)

    def start(self, c):
        self.first(c).start()

    def middle(self, c):
        _, y, core, _, _ = mp_places()
        self.first(c).wait_recv()
        at = run(self.block(c, core, 1 - y))
        self.part[at, :] = (self.part[at, :].astype(f32) + self.near[run(c * 2 + 1 - y), :].astype(f32)).astype(bf16)
        self.second(c).start()

    def finish(self, c):
        _, y, core, _, _ = mp_places()
        self.second(c).wait_recv()
        own = self.part[run(self.block(c, core, y)), :].astype(f32) + self.near[run(c * 2 + y), :].astype(f32)
        return own + self.far[run(c), :].astype(f32)

    def drain(self, c):
        self.first(c).wait_send()
        self.second(c).wait_send()


class Gather:

    def __init__(self, full, send, recv, size=BLOCK):
        self.full, self.send, self.recv, self.size = full, send, recv, size

    def at(self, c, m):
        return run(c * 4 + m, 1, self.size)

    def copy(self, c, kind):
        mp, _, _, sibling, across = mp_places()
        at = self.full.at[self.at(c, across if kind == 2 else mp)]
        return remote(at, at, self.send.at[c, kind], self.recv.at[c, kind], across if kind == 1 else sibling)

    def start(self, c):
        self.copy(c, 1).start()
        self.copy(c, 0).start()

    def forward(self, c):
        self.copy(c, 1).wait_recv()
        self.copy(c, 2).start()

    def finish(self, c):
        self.copy(c, 0).wait_recv()
        self.copy(c, 2).wait_recv()

    def drain(self, c):
        for kind in range(3):
            self.copy(c, kind).wait_send()


class Exchange:

    def __init__(self, given, taken, size, send, recv):
        self.given, self.taken, self.size, self.send, self.recv = given, taken, size, send, recv

    def copy(self, c, d):
        mp = lax.axis_index("mp")
        src = self.given.at[run(c * 3 + d - 1, 1, self.size)]
        dst = self.taken.at[run(c * 4 + mp, 1, self.size)]
        return remote(src, dst, self.send.at[c, d - 1], self.recv.at[c, d - 1], (mp + d) % 4)

    def start(self, c):
        for d in (2, 1, 3):
            self.copy(c, d).start()

    def finish(self, c):
        for d in (1, 2, 3):
            self.copy(c, d).wait_recv()

    def drain(self, c):
        for d in (1, 2, 3):
            self.copy(c, d).wait_send()


class Spread:

    def __init__(self, part, near, pair, far, send, recv):
        self.part, self.near, self.pair, self.far, self.send, self.recv = part, near, pair, far, send, recv
        self.each = part.shape[0] // 8

    def at(self, index, count=1):
        return run(index, count, self.each)

    def put(self, first_row, value):
        for r in range(value.shape[0] // self.each):
            j = first_row // self.each + r
            rows = value[r * self.each : (r + 1) * self.each]
            self.part[self.at(j % 2 * 4 + j // 2 % 2 * 2 + j // 4), :] = rows.astype(bf16)

    def copy(self, kind):
        z, x = dp_places()
        send, recv = self.send.at[kind], self.recv.at[kind]
        if kind == 0:
            src = self.part.at[self.at((1 - x) * 4, 4)]
            return remote(src, self.near, send, recv, dp=z * 2 + 1 - x)
        if kind == 1:
            src = self.part.at[self.at(x * 4 + (1 - z % 2) * 2, 2)]
            return remote(src, self.pair, send, recv, dp=beside(z) * 2 + x)
        src = self.part.at[self.at(x * 4 + z % 2 * 2 + 1 - z // 2)]
        return remote(src, self.far, send, recv, dp=(z + 2) % 4 * 2 + x)

    def start(self):
        self.copy(0).start()

    def middle(self):
        z, x = dp_places()
        self.copy(0).wait_recv()
        at = self.at(x * 4 + (1 - z % 2) * 2, 2)
        near = self.near[self.at((1 - z % 2) * 2, 2), :].astype(f32)
        self.part[at, :] = (self.part[at, :].astype(f32) + near).astype(bf16)
        self.copy(1).start()

    def sum_of(self, half):
        z, x = dp_places()
        total = self.part[self.at(x * 4 + z % 2 * 2 + half), :].astype(f32)
        total = total + self.near[self.at(z % 2 * 2 + half), :].astype(f32)
        return total + self.pair[self.at(half), :].astype(f32)

    def third(self):
        z, x = dp_places()
        self.copy(1).wait_recv()
        self.part[self.at(x * 4 + z % 2 * 2 + 1 - z // 2), :] = self.sum_of(1 - z // 2).astype(bf16)
        self.copy(2).start()

    def finish(self):
        z, _ = dp_places()
        self.copy(2).wait_recv()
        return self.sum_of(z // 2) + self.far[...].astype(f32)

    def drain(self):
        for kind in range(3):
            self.copy(kind).wait_send()


class Direct:

    def __init__(self, part, taken, send, recv):
        self.part, self.taken, self.send, self.recv = part, taken, send, recv
        self.each = part.shape[0] // 8

    put = Spread.put

    def at(self, index, count=1):
        return run(index, count, self.each)

    def block(self, dp):
        return self.at(dp % 2 * 4 + dp // 2 % 2 * 2 + dp // 4)

    def copy(self, d):
        to = (lax.axis_index("dp") + d) % 8
        src = self.part.at[self.block(to)]
        return remote(src, self.taken.at[run(d - 1, 1, self.each)], self.send.at[d - 1], self.recv.at[d - 1], dp=to)

    def start(self):
        for d in (4, 3, 5, 2, 6, 1, 7):
            self.copy(d).start()

    def finish(self):
        total = self.part[self.block(lax.axis_index("dp")), :].astype(f32)
        for d in range(1, 8):
            self.copy(d).wait_recv()
            total = total + self.taken[run(d - 1, 1, self.each), :].astype(f32)
        return total

    def drain(self):
        for d in range(1, 8):
            self.copy(d).wait_send()


class Total:

    def __init__(self, value, taken, send, recv):
        self.value, self.taken, self.send, self.recv = value, taken, send, recv

    def copy(self, kind):
        mp, dp = lax.axis_index("mp"), lax.axis_index("dp")
        send, recv = self.send.at[kind], self.recv.at[kind]
        if kind < 7:
            return remote(self.value.at[0], self.taken.at[kind], send, recv, dp=(dp + kind + 1) % 8)
        return remote(self.value.at[1], self.taken.at[kind], send, recv, mp=(mp + kind - 6) % 4)

    def start(self):
        for kind in range(7):
            self.copy(kind).start()

    def turn(self):
        total = self.value[0]
        for kind in range(7):
            self.copy(kind).wait_recv()
            total = total + self.taken[kind]
        self.value[1] = total
        for kind in range(7, 10):
            self.copy(kind).start()

    def finish(self):
        total = self.value[1]
        for kind in range(7, 10):
            self.copy(kind).wait_recv()
            total = total + self.taken[kind]
        return total

    def drain(self):
        for kind in range(10):
            self.copy(kind).wait_send()


def layer_kernel(
    fast,
    length_ref, across_ref, upward_ref, gain_a_ref, gain_f_ref, tables_ref,
    tokens_hbm, w_qkv_hbm, w_output_hbm, w_inner_hbm, w_outer_hbm, cot_hbm,
    *rest,
):
    outs, scratch = rest[: 9 if fast else 7], rest[9 if fast else 7 :]
    if fast:
        mixed_ref, input_ref, o_qkv_ref, o_output_ref, o_inner_ref, o_outer_ref, o_gain_a_ref, o_gain_f_ref, o_tables_ref = outs
    else:
        mixed_ref, input_ref, o_qkv_ref, o_output_ref, o_inner_ref, o_outer_ref, o_sums_ref = outs
    (
        x1, w_qkv_ref, w_inner_ref, w_outer_ref, cot_ref, load_sem,
        codes_ref, plane_ref, hot_ref, hot_t_ref, qa_ref, qb_ref, k2_ref, kt2_ref, v_ref, band_ref, band_t_ref, qt_ref,
        s_ref, res_ref, dv_ref, dqt_ref, bands_ref, dat_ref, sums_ref, gain_sum_ref, collapse_ref,
        att_ref, af_ref, att_send, att_recv,
        es_ref, ga_ref, es_send, es_recv,
        wo_ref, wo_send, wo_recv, wo_t_ref,
        nf_ref,
        ghl_ref, ghl_send, ghl_recv,
        feed_part, feed_send, feed_recv, norm_part, norm_send, norm_recv, last_send, last_recv, near_ref, far_ref,
        credit,
        low_ref, grad_low_ref, hidden_ref,
        *spreads,
    ) = scratch
    heads = tables_ref.shape[0]
    rows, model = x1.shape
    width = heads * 64
    units = w_inner_ref.shape[1]
    pieces = 4
    chunks = rows // CHUNK
    blocks = rows // BLOCK
    half_model = model // 2
    mp, _, _, sibling, across = mp_places()
    da_ref, dk_ref, wt_ref = qa_ref, res_ref, w_inner_ref

    att = Gather(af_ref, att_send, att_recv, CHUNK + CHUNK // 2)
    grad_att = Exchange(es_ref, ga_ref, BLOCK + BLOCK // 2, es_send, es_recv)
    wo = Gather(wo_ref, wo_send, wo_recv, width)
    grads = Gather(ghl_ref, ghl_send, ghl_recv)
    feed = Scatter(feed_part, near_ref, far_ref, feed_send, feed_recv)
    norm = Scatter(norm_part, near_ref, far_ref, norm_send, norm_recv)
    last = Scatter(norm_part, near_ref, far_ref, last_send, last_recv)
    if fast:
        outer = Spread(w_outer_ref, *spreads[0:5])
        inner = Spread(*spreads[5:11])
        output = Spread(*spreads[11:17])
        qkv_last = Direct(*spreads[23:27])
        small = Total(*spreads[27:31])

        def qkv(h):
            return Spread(*[ref.at[h] for ref in spreads[17:23]])

    def place(m, c):
        return run(m * chunks + c)

    loads = [
        pltpu.make_async_copy(src, dst, load_sem.at[i])
        for i, (src, dst) in enumerate(
            [
                (tokens_hbm, x1),
                (w_qkv_hbm, w_qkv_ref),
                (w_output_hbm, wo_ref.at[wo.at(0, mp)]),
                (w_inner_hbm, w_inner_ref),
                (w_outer_hbm, w_outer_ref),
                (cot_hbm, cot_ref),
                *[(tokens_hbm.at[place(m, c)], low_ref.at[run(c * 4 + m)]) for c in range(chunks) for m in range(4)],
                (tokens_hbm.at[run(mp * chunks, chunks)], cot_ref.at[run(0, chunks)]),
            ]
        )
    ]
    for load in loads[:-1]:
        load.start()
    everyone_is_here = meet(fast)

    def window(m, c):
        block = m * chunks + c
        start = min(max(block - 1, 0), blocks - 3)
        return range(start, start + 3), 2 - block


    expanded = dot(tables_ref[...], expansion())
    square_rows = lax.broadcasted_iota(jnp.int32, (BLOCK, BLOCK), 0)
    square_lanes = lax.broadcasted_iota(jnp.int32, (BLOCK, BLOCK), 1)
    for h in range(heads):
        line = jnp.broadcast_to(expanded[h : h + 1, :WIDE], (BLOCK, WIDE))
        band = roll_rows(line, True)
        band_ref[h] = band.astype(bf16)
        band_t_ref[h] = band.T.astype(bf16)
        level = roll_rows(jnp.broadcast_to(expanded[h : h + 1, WIDE : WIDE + BLOCK], (BLOCK, BLOCK)), True)
        upward = roll_rows(jnp.broadcast_to(expanded[h : h + 1, WIDE + BLOCK :], (BLOCK, BLOCK)), True)
        plane = jnp.where(
            (square_rows < CODES) & (square_lanes < CODES),
            level,
            jnp.where((square_rows >= CODES) & (square_lanes >= CODES), upward, 0.0),
        )
        plane_ref[h] = plane.astype(bf16)
    everyone_is_here()
    loads[2].wait()
    wo.start(0)
    loads[1].wait()
    loads[0].wait()
    gain_a = gain_a_ref[...].reshape(1, model).astype(f32)
    gain_f = gain_f_ref[...].reshape(1, model).astype(f32)
    codes_ref[0:1, :] = across_ref[...].reshape(1, rows)
    codes_ref[1:2, :] = upward_ref[...].reshape(1, rows)
    lanes = lax.broadcasted_iota(jnp.int32, (CHUNK, BLOCK), 1)
    low = lanes < FAR

    def prepare(j, carry):
        at = run(j, 1, CHUNK)
        x = x1[at, :].astype(f32)
        normed_rows = (x * factor_of(x) * gain_a).astype(bf16)
        x1[at, :] = normed_rows
        codes_lines = lax.broadcasted_iota(jnp.int32, (BLOCK, CHUNK), 0)
        hot_t = jnp.where(
            codes_lines == jnp.broadcast_to(codes_ref[0:1, at], (BLOCK, CHUNK)),
            1.0,
            jnp.where(codes_lines - CODES == jnp.broadcast_to(codes_ref[1:2, at], (BLOCK, CHUNK)), 1.0, 0.0),
        )
        hot = hot_t.T.astype(bf16)
        hot_t_ref[:, at] = hot_t.astype(bf16)
        hot_ref[at, :] = hot
        row = lax.broadcasted_iota(jnp.int32, (CHUNK, BLOCK), 0) + j * CHUNK
        block = row // BLOCK
        start = jnp.clip(block - 1, 0, blocks - 3)
        far = (lanes >= FAR) & (lanes < MASK)
        far_left = far & (lanes - FAR < start)
        far_right = far & (lanes - FAR > start + 2)
        key_side = jnp.where(
            (far & (lanes - FAR == block))
            | ((lanes == MASK) & (row >= length_ref[0]))
            | ((lanes >= LSE) & (lanes < LSE + 3)),
            1.0,
            0.0,
        )

        def part(h):
            columns = s_ref[:CHUNK, h // 2 * BLOCK : h // 2 * BLOCK + BLOCK]
            return columns if h % 2 == 0 else pltpu.roll(columns, 64, 1)

        s_ref[:CHUNK, :width] = dot_nt(normed_rows, w_qkv_ref[0])
        for h in range(heads):
            left = expanded[h : h + 1, 0:1]
            right = expanded[h : h + 1, WIDE - BLOCK - 1 : WIDE - BLOCK]
            query_side = jnp.where(far_left, left, jnp.where(far_right, right, jnp.where(lanes == MASK, DEAD, 0.0)))
            qa_ref[h, at, :] = dot(hot, plane_ref[h]).astype(bf16)
            qb_ref[h, at, :] = jnp.where(low, part(h).astype(bf16).astype(f32) * 0.125, query_side).astype(bf16)
        s_ref[:CHUNK, :width] = dot_nt(normed_rows, w_qkv_ref[1])
        for h in range(heads):
            second = jnp.where(low, part(h), key_side)
            k2_ref[h, at, :] = second.astype(bf16)
            kt2_ref[h, :, at] = second.T.astype(bf16)
        s_ref[:CHUNK, :width] = dot_nt(normed_rows, w_qkv_ref[2])
        for h in range(heads):
            v_ref[h, at, :] = jnp.where(low, part(h), 1.0).astype(bf16)
        return carry

    s_ref[:CHUNK, :] = jnp.zeros_like(s_ref[:CHUNK, :])
    lax.fori_loop(0, chunks, prepare, 0)
    wo.forward(0)
    gain_sum_ref[...] = jnp.zeros_like(gain_sum_ref)
    sums_ref[...] = jnp.zeros_like(sums_ref)
    collapse_ref[...] = collapse()

    half_low = lax.broadcasted_iota(jnp.int32, (CHUNK // 2, BLOCK), 1) < 64
    quarter_low = lax.broadcasted_iota(jnp.int32, (BLOCK // 2, BLOCK), 1) < 64

    def share_attended(c):
        at = run(c, 1, CHUNK)
        mine = att.at(c, mp).start
        third = att_ref[at, BLOCK:].astype(f32)
        af_ref[pl.ds(pl.multiple_of(mine, CHUNK // 2), CHUNK), :] = att_ref[at, :BLOCK]
        beside_it = jnp.where(half_low, third[: CHUNK // 2], pltpu.roll(third[CHUNK // 2 :], 64, 1)).astype(bf16)
        af_ref[pl.ds(pl.multiple_of(mine + CHUNK, CHUNK // 2), CHUNK // 2), :] = beside_it
        att.start(c)

    def hidden_of(c):
        att.finish(c)
        hidden = low_ref[run(c, 1, CHUNK), :].astype(f32)
        for m in range(pieces):
            first = (c * 4 + m) * (CHUNK + CHUNK // 2)
            pair = af_ref[pl.ds(pl.multiple_of(first, CHUNK // 2), CHUNK), :]
            third = af_ref[pl.ds(pl.multiple_of(first + CHUNK, CHUNK // 2), CHUNK // 2), :]
            third = jnp.concatenate([third, pltpu.roll(third.astype(f32), 64, 1).astype(bf16)], axis=0)
            weights = wo_ref[m * width : (m + 1) * width, :]
            hidden = hidden + dot(jnp.concatenate([pair, third[:, :64]], axis=1), weights)
        nf_ref[run(c, 1, CHUNK), :] = (hidden * factor_of(hidden) * gain_f).astype(bf16)
        for m in range(pieces):

            @pl.when(mp == m)
            def _(m=m):
                hidden_ref[run(c), :] = hidden[m * BLOCK : (m + 1) * BLOCK]

    def grad_of(c):
        grad_normed = norm.finish(c)
        hidden = hidden_ref[run(c), :]
        factor = factor_of(hidden)
        hat = hidden * factor
        scaled = grad_normed * gain_f
        back = factor * (scaled - hat * jnp.mean(scaled * hat, axis=-1, keepdims=True))
        grad = cot_ref[place(mp, c), :].astype(f32) + back
        input_ref[run(c), :] = grad
        gain_sum_ref[0:1, :] += jnp.sum(grad_normed * hat, axis=0, keepdims=True)
        grad_low = grad.astype(bf16)
        ghl_ref[grads.at(c, mp), :] = grad_low

        size = BLOCK + BLOCK // 2
        every = dot(grad_low, wo_t_ref[...])
        for m in range(pieces):
            third = every[:, m * 256 + BLOCK : (m + 1) * 256]
            third = jnp.where(quarter_low, third[: BLOCK // 2], pltpu.roll(third[BLOCK // 2 :], 64, 1))
            value = jnp.concatenate([every[:, m * 256 : m * 256 + BLOCK], third], axis=0).astype(bf16)

            @pl.when(mp == m)
            def _(value=value):
                ga_ref[run(c * 4 + mp, 1, size), :] = value

            @pl.when(mp != m)
            def _(value=value, m=m):
                es_ref[run(c * 3 + (m - mp + 4) % 4 - 1, 1, size), :] = value

        grad_att.start(c)

    def attend(c, h, carry):
        query_far = jnp.concatenate([qa_ref[h, place(m, c), :] for m in range(pieces)], axis=0)
        query_near = jnp.concatenate([qb_ref[h, place(m, c), :] for m in range(pieces)], axis=0)
        query = jnp.concatenate([query_far, query_near], axis=1)
        tops, mixes = [], []
        for j in range(chunks):
            cols = slice(j * CHUNK, (j + 1) * CHUNK)
            s = dot(query, jnp.concatenate([hot_t_ref[:, cols], kt2_ref[h, :, cols]], axis=0))
            lines = []
            for m in range(pieces):
                near, shift = window(m, c)
                tiles = []
                for b in range(pieces):
                    tile = s[m * BLOCK : (m + 1) * BLOCK, b * BLOCK : (b + 1) * BLOCK]
                    if j * pieces + b in near:
                        at = (j * pieces + b + shift) * BLOCK
                        tile = tile + band_ref[h, :, at : at + BLOCK].astype(f32)
                    tiles.append(tile)
                lines.append(jnp.concatenate(tiles, axis=1))
            s = jnp.concatenate(lines, axis=0)
            tops.append(jnp.max(s, axis=1, keepdims=True))
            mixes.append(dot(jnp.exp(s - tops[j]).astype(bf16), v_ref[h, cols, :]))
        top = functools.reduce(jnp.maximum, tops)
        mixed = sum(mix * jnp.exp(part - top) for mix, part in zip(mixes, tops))
        res_ref[run(h, 1, CHUNK), :] = jnp.where(low, mixed / pltpu.roll(mixed, 64, 1), 0.0)
        high, middle, rest = split3(-(top + jnp.log(mixed[:, 64:65])))
        second = jnp.where(
            lanes == LSE,
            high,
            jnp.where(lanes == LSE + 1, middle, jnp.where(lanes == LSE + 2, rest, query_near.astype(f32))),
        )
        qt_ref[h, c, :BLOCK, :] = query_far.astype(f32).T.astype(bf16)
        qt_ref[h, c, BLOCK:, :] = second.T.astype(bf16)

        return carry

    for c in range(chunks):
        lax.fori_loop(0, heads, functools.partial(attend, c), 0)
        if c > 0:
            att.forward(c - 1)
        if c == 1:
            wo.finish(0)
            for m in range(pieces):
                turned = wo_ref[m * width : (m + 1) * width, :].astype(f32).T
                wo_t_ref[:, m * 256 : m * 256 + width] = turned.astype(bf16)
                wo_t_ref[:, m * 256 + width : (m + 1) * 256] = jnp.zeros((model, 256 - width), bf16)
        pairs = []
        for g in range(0, heads, 2):
            pair = res_ref[g * CHUNK : (g + 1) * CHUNK, :]
            if g + 1 < heads:
                pair = jnp.where(low, pair, pltpu.roll(res_ref[(g + 1) * CHUNK : (g + 2) * CHUNK, :], 64, 1))
            pairs.append(pair.astype(bf16))
        att_ref[run(c, 1, CHUNK), :] = jnp.concatenate(pairs, axis=1)
        share_attended(c)
    for load in loads[3:-1]:
        load.wait()
    outer_t = w_outer_ref[...].astype(f32).T.astype(bf16)
    inner_t = w_inner_ref[...].astype(f32).T.astype(bf16)
    for r in range(units // BLOCK):
        qa_ref[r // 2, run(r % 2, 1, model), :] = outer_t[:, r * BLOCK : (r + 1) * BLOCK]
        dat_ref[r // 2, :, r % 2 * model : (r % 2 + 1) * model] = inner_t[r * BLOCK : (r + 1) * BLOCK, :]

    steps = units // 256

    def feed_step(t, carry):
        c = t // steps
        b = t % steps

        @pl.when(b == 0)
        def _():
            hidden_of(c)

        at = run(b, 1, 256)
        x = nf_ref[run(c, 1, CHUNK), :]
        cot = jnp.concatenate([cot_ref[place(m, c), :] for m in range(pieces)], axis=0)
        inner_units = dot(x, w_inner_ref[:, at])
        grad_act = dot(cot, jnp.concatenate([qa_ref[b, :model, :], qa_ref[b, model:, :]], axis=1))
        square = inner_units * inner_units
        tanh = jnp.tanh(ROOT * inner_units * (1.0 + CUBE * square))
        half = 0.5 * (1.0 + tanh)
        slope = half + 0.5 * inner_units * (1.0 - tanh * tanh) * (ROOT + 3.0 * CUBE * ROOT * square)
        activated = (inner_units * half).astype(bf16)
        grad_low = (slope * grad_act).astype(bf16)
        low_ref[run(c, 1, CHUNK), at] = activated
        grad_low_ref[run(c, 1, CHUNK), at] = grad_low

        @pl.when(b == steps - 1)
        def _():
            chunk_rows = run(c, 1, CHUNK)
            for p in range(model // 256):
                cols = slice(p * 256, (p + 1) * 256)
                turned = [
                    dat_ref[r // 2, :, r % 2 * model + p * 256 : r % 2 * model + (p + 1) * 256] for r in range(units // BLOCK)
                ]
                part_norm = dot(grad_low_ref[chunk_rows, :], jnp.concatenate(turned, axis=0))
                part_ffn = dot(low_ref[chunk_rows, :], w_outer_ref[:, cols])
                for m in range(pieces):
                    norm.put(c, m, part_norm[m * BLOCK : (m + 1) * BLOCK], cols)
                    feed.put(c, m, part_ffn[m * BLOCK : (m + 1) * BLOCK], cols)
            norm.start(c)

        @pl.when(t == 2)
        def _():
            att.forward(2)

        @pl.when(t == 3)
        def _():
            norm.middle(0)

        @pl.when(t == 6)
        def _():
            norm.middle(1)

        @pl.when(t == 7)
        def _():
            grad_of(0)

        return carry

    lax.fori_loop(0, chunks * steps, feed_step, 0)

    def weights_of(is_outer):
        for b in range(2):
            at = slice(b * half_model, (b + 1) * half_model)
            total = jnp.zeros((half_model, units), f32)
            for c in range(chunks):
                if is_outer:
                    left = jnp.concatenate([cot_ref[place(m, c), at] for m in range(pieces)], axis=0)
                    total = total + dot_tn(left, low_ref[run(c, 1, CHUNK), :])
                else:
                    total = total + dot_tn(nf_ref[run(c, 1, CHUNK), at], grad_low_ref[run(c, 1, CHUNK), :])
            if fast:
                (outer if is_outer else inner).put(b * half_model, total)
            else:
                (o_outer_ref if is_outer else o_inner_ref)[at, :] = total

    weights_of(True)
    if fast:
        outer.start()
    norm.middle(2)
    weights_of(False)
    if fast:
        inner.start()
    grad_of(1)
    wt_ref[...] = jnp.zeros_like(wt_ref)
    for k in range(3):
        for h in range(heads):
            wt_ref[h * 256 + k * 64 : h * 256 + (k + 1) * 64, :] = w_qkv_ref[k, h * 64 : (h + 1) * 64, :]

    def receive(c):
        grad_att.finish(c)
        at = run(c, 1, CHUNK)
        pairs, thirds = [], []
        for m in range(pieces):
            first = (c * 4 + m) * (BLOCK + BLOCK // 2)
            pairs.append(ga_ref[pl.ds(pl.multiple_of(first, BLOCK // 2), BLOCK), :])
            third = ga_ref[pl.ds(pl.multiple_of(first + BLOCK, BLOCK // 2), BLOCK // 2), :].astype(f32)
            thirds.extend([third, pltpu.roll(third, 64, 1)])
        received = [jnp.concatenate(pairs, axis=0).astype(f32), jnp.concatenate(thirds, axis=0)]
        for h in range(heads):
            pair = slice(h // 2 * BLOCK, h // 2 * BLOCK + BLOCK)
            grad = received[h // 2]
            out = att_ref[at, pair].astype(f32)
            if h % 2 == 1:
                grad = pltpu.roll(grad, 64, 1)
                out = pltpu.roll(out, 64, 1)
            high, middle, rest = split3(-jnp.sum(jnp.where(low, grad * out, 0.0), axis=1, keepdims=True))
            grad = jnp.where(
                low,
                grad,
                jnp.where(
                    lanes == FAR, high, jnp.where(lanes == FAR + 1, middle, jnp.where(lanes == FAR + 2, rest, 0.0))
                ),
            )
            da_ref[h, at, :] = grad.astype(bf16)
            dat_ref[h, :, at] = grad.T.astype(bf16)

    lines16 = lax.broadcasted_iota(jnp.int32, (16, rows), 0)
    block16 = lax.broadcasted_iota(jnp.int32, (16, rows), 1) // BLOCK
    start16 = jnp.clip(block16 - 1, 0, blocks - 3)
    real = lines16 < blocks
    tall_low = lax.broadcasted_iota(jnp.int32, (rows, BLOCK), 1) < 64

    def fold(value):
        total = value[:, :BLOCK]
        for b in range(1, value.shape[1] // BLOCK):
            total = total + value[:, b * BLOCK : (b + 1) * BLOCK]
        return jnp.sum(total, axis=0, keepdims=True)

    def mix(k):
        mixed_ref[run(k), :] = (hidden_ref[run(k), :] + feed.finish(k)).astype(bf16)

    def events(h, c, j):
        due = {
            (0, 0, 2): [lambda: grad_of(2)],
            (0, 1, 2): [lambda: grads.start(0)],
            (0, 2, 2): [lambda: grads.start(1)],
            (1, 0, 2): [lambda: grads.forward(0), lambda: grads.start(2), lambda: grads.forward(1)],
            (1, 1, 2): [lambda: feed.start(0), lambda: feed.start(1), lambda: feed.start(2)],
            (1, 2, 2): [lambda: grads.forward(2), lambda: feed.middle(0), lambda: feed.middle(1)],
            (2, 0, 2): [lambda: feed.middle(2)],
            (2, 1, 2): [lambda: mix(0), lambda: mix(1)],
            (2, 2, 2): [lambda: mix(2)],
        }
        if fast:
            for at, what in {
                (0, 2, 2): [outer.middle],
                (1, 1, 2): [outer.third, inner.middle],
                (1, 2, 2): [lambda: qkv(0).middle()],
                (2, 0, 2): [inner.third],
                (2, 1, 2): [lambda: qkv(0).third()],
                (2, 2, 2): [lambda: qkv(1).middle(), output.middle],
            }.items():
                due[at] = due.get(at, []) + what
        for (head_due, chunk_due, panel_due), what in due.items():
            if (chunk_due, panel_due) == (c, j):

                @pl.when(h == head_due)
                def _(what=what):
                    for each in what:
                        each()

    def leave(h, spread):
        grads_of = run(h, 1, 256)
        grad_qkv = dot_tn(nf_ref[:, grads_of], x1[...]).T
        if fast:
            spread.put(0, grad_qkv)
        else:
            o_qkv_ref[h] = grad_qkv
        if fast:
            spread.start()

    def leave_tables(h):
        band = roll_rows(bands_ref[...].T, False)
        spread = dqt_ref[:BLOCK, :]
        high = spread.astype(bf16)
        rest = (spread - high.astype(f32)).astype(bf16)
        plane = (dot(high, hot_ref[...]) + dot(rest, hot_ref[...])).T
        plane = jnp.where((square_rows < CODES) == (square_lanes < CODES), plane, 0.0)
        plane = roll_rows(plane, False)
        far = dqt_ref[BLOCK + FAR : BLOCK + FAR + 16, :]
        line = jnp.concatenate(
            [
                jnp.sum(band, axis=0, keepdims=True),
                jnp.sum(plane[:CODES], axis=0, keepdims=True),
                jnp.sum(plane[CODES:], axis=0, keepdims=True),
                fold(jnp.where(real & (lines16 < start16), far, 0.0)),
                fold(jnp.where(real & (lines16 > start16 + 2), far, 0.0)),
            ],
            axis=1,
        )
        sums_ref[...] += jnp.where(lax.broadcasted_iota(jnp.int32, sums_ref.shape, 0) == h, line, 0.0)

    def head(h, carry):
        dk_ref[...] = jnp.zeros_like(dk_ref)
        dv_ref[...] = jnp.zeros_like(dv_ref)
        bands_ref[...] = jnp.zeros_like(bands_ref)

        for c in range(chunks):

            @pl.when(h == 0)
            def _(c=c):
                receive(c)

            at = slice(c * CHUNK, (c + 1) * CHUNK)
            query = jnp.concatenate([qb_ref[h, place(m, c), :] for m in range(pieces)], axis=0)
            for j in range(chunks):
                keys = slice(j * CHUNK, (j + 1) * CHUNK)
                s = dot(jnp.concatenate([hot_ref[keys, :], k2_ref[h, keys, :]], axis=1), qt_ref[h, c])
                columns = []
                for m in range(pieces):
                    near, shift = window(m, c)
                    tiles = []
                    for b in range(pieces):
                        tile = s[b * BLOCK : (b + 1) * BLOCK, m * BLOCK : (m + 1) * BLOCK]
                        if j * pieces + b in near:
                            of = (j * pieces + b + shift) * BLOCK
                            tile = tile + band_t_ref[h, of : of + BLOCK, :].astype(f32)
                        tiles.append(tile)
                    columns.append(jnp.concatenate(tiles, axis=0))
                probs = jnp.exp(jnp.concatenate(columns, axis=1))
                probs_t = probs.astype(bf16)
                grad_t = (probs * dot(v_ref[h, keys, :], dat_ref[h, :, at])).astype(bf16)
                grad_low_ref[keys, :CHUNK] = grad_t
                dv_ref[keys, :] += dot(probs_t, da_ref[h, at, :])
                dk_ref[keys, :] += dot(grad_t, query)
                if j < chunks - 1:
                    events(h, c, j)
            dq = dot(jnp.concatenate([hot_t_ref[...], kt2_ref[h]], axis=0), grad_low_ref[:, :CHUNK])
            for m in range(pieces):
                dqt_ref[:, place(m, c)] = dq[:, m * BLOCK : (m + 1) * BLOCK]
                near, shift = window(m, c)
                of = slice((near.start + shift) * BLOCK, (near.stop + shift) * BLOCK)
                keys = slice(near.start * BLOCK, near.stop * BLOCK)
                bands_ref[of, :] += grad_low_ref[keys, m * BLOCK : (m + 1) * BLOCK].astype(f32)
            events(h, c, chunks - 1)

        dq = dqt_ref[BLOCK:, :].T * 0.125
        grads_of = run(h, 1, 256)
        nf_ref[:, grads_of] = jnp.concatenate(
            [jnp.where(tall_low, dq, pltpu.roll(dk_ref[...], 64, 1)), jnp.where(tall_low, dv_ref[...], 0.0)], axis=1
        ).astype(bf16)

        @pl.when(h < heads - 1)
        def _():
            leave(h, qkv(h) if fast else None)
            leave_tables(h)

        @pl.when(h == 1)
        def _():
            for c in range(chunks):
                grads.finish(c)
            grad_output = dot_tn(att_ref[...], ghl_ref[...]).T
            if fast:
                output.put(0, grad_output)
            else:
                o_output_ref[...] = grad_output[:, :width]
            if fast:
                output.start()

        return carry

    lax.fori_loop(0, heads, head, 0)

    credits = [(sibling, credit.at[0]), (across, credit.at[1])]
    for other, sem in credits:
        pl.semaphore_signal(
            sem, inc=1, device_id=(lax.axis_index("dp"), other), device_id_type=pl.DeviceIdType.MESH
        )
    leave(heads - 1, qkv_last if fast else None)
    loads[-1].start()
    for c in range(chunks):
        norm.drain(c)
    gain_total = jnp.zeros((1, model), f32)
    for c in range(chunks):
        at = [place(m, c) for m in range(pieces)]
        grad_rows = jnp.concatenate([nf_ref[rows_of, :] for rows_of in at], axis=0)
        sums = []
        for p in range(model // 256):
            cols = slice(p * 256, (p + 1) * 256)
            partial = dot(grad_rows, wt_ref[:, cols])
            normed_rows = jnp.concatenate([x1[rows_of, cols] for rows_of in at], axis=0)
            sums.append(jnp.sum(partial * normed_rows.astype(f32), axis=0, keepdims=True))
            for m in range(pieces):
                last.put(c, m, partial[m * BLOCK : (m + 1) * BLOCK], cols)
        gain_total = gain_total + jnp.concatenate(sums, axis=1)
        if c == 0:
            for _, sem in credits:
                pl.semaphore_wait(sem, 1)
        last.start(c)
        if c > 0:
            last.middle(c - 1)
    leave_tables(heads - 1)
    last.middle(chunks - 1)
    gain_total = gain_total / gain_a
    tables = sum(dot_nt(part.astype(bf16), collapse_ref[...]) for part in split3(sums_ref[...]))[:heads]
    if fast:
        lines = model // BLOCK
        small.value[0] = jnp.zeros_like(small.value[0])
        for i in range(lines):
            lane = slice(i * BLOCK, (i + 1) * BLOCK)
            small.value[0, i : i + 1, :] = gain_total[:, lane]
            small.value[0, lines + i : lines + i + 1, :] = gain_sum_ref[0:1, lane]
        small.value[0, 2 * lines : 2 * lines + heads, : 3 * BUCKETS] = tables
        small.start()
        output.third()
        qkv(1).third()
        o_outer_ref[...] = outer.finish()
        small.turn()
        o_output_ref[...] = output.finish()[:, :width].T
    loads[-1].wait()
    for c in range(chunks):
        x = cot_ref[run(c), :].astype(f32)
        grad_normed = last.finish(c)
        factor = factor_of(x)
        hat = x * factor
        scaled = grad_normed * gain_a
        back = factor * (scaled - hat * jnp.mean(scaled * hat, axis=-1, keepdims=True))
        input_ref[run(c), :] += back
    if fast:
        o_inner_ref[...] = inner.finish()
    if fast:
        low_each = lax.broadcasted_iota(jnp.int32, (model // 8, BLOCK), 1) < 64
        parts = [(qkv(h) if h < heads - 1 else qkv_last).finish() for h in range(heads)]
        for k in range(3):
            for h in range(0, heads, 2):
                at = slice(0, BLOCK) if k < 2 else slice(BLOCK, 2 * BLOCK)
                one = parts[h][:, at]
                one = pltpu.roll(one, 64, 1) if k == 1 else one
                if h + 1 < heads:
                    two = parts[h + 1][:, at]
                    two = two if k == 1 else pltpu.roll(two, 64, 1)
                    o_qkv_ref[k, :, h * 64 : (h + 2) * 64] = jnp.where(low_each, one, two)
                else:
                    o_qkv_ref[k, :, h * 64 :] = one[:, :64]
        totals = small.finish()
        for i in range(lines):
            o_gain_a_ref[i * BLOCK : (i + 1) * BLOCK] = totals[i : i + 1].reshape(BLOCK)
            o_gain_f_ref[i * BLOCK : (i + 1) * BLOCK] = totals[lines + i : lines + i + 1].reshape(BLOCK)
        o_tables_ref[...] = small.value[1, 2 * lines : 2 * lines + heads, : 3 * BUCKETS]
        outer.drain()
        inner.drain()
        output.drain()
        for h in range(heads - 1):
            qkv(h).drain()
        qkv_last.drain()
        small.drain()
    else:
        o_sums_ref[...] = jnp.zeros_like(o_sums_ref)
        o_sums_ref[0:1, :] = gain_total
        o_sums_ref[1:2, :] = gain_sum_ref[0:1, :]
        o_sums_ref[2 : 2 + heads, : 3 * BUCKETS] = tables
    wo.drain(0)
    for c in range(chunks):
        for each in (att, grad_att, grads, feed, last):
            each.drain(c)


def spread_scratch(rows, columns, lead=(), own_part=True):
    buffers = [pltpu.VMEM((*lead, 8 * rows, columns), bf16)] if own_part else []
    return buffers + [
        pltpu.VMEM((*lead, 4 * rows, columns), bf16),
        pltpu.VMEM((*lead, 2 * rows, columns), bf16),
        pltpu.VMEM((*lead, rows, columns), bf16),
        pltpu.SemaphoreType.DMA((*lead, 3)),
        pltpu.SemaphoreType.DMA((*lead, 3)),
    ]


def hand_over_kernel(*refs):
    count = len(refs) // 2
    for i in range(count):
        refs[count + i][...] = refs[i][...]


def hand_over(results):
    full = pl.BlockSpec(memory_space=pltpu.VMEM)
    return pl.pallas_call(
        hand_over_kernel,
        in_specs=[full] * len(results),
        out_specs=[full] * len(results),
        out_shape=[jax.ShapeDtypeStruct(each.shape, each.dtype) for each in results],
        name="hand_over",
    )(*results)


def local(
    fast,
    tokens, lengths, horizontal, vertical, gain_attn, w_qkv, bias_tables, w_output, gain_ffn, w_inner, w_outer, cotangent,
):
    rows, model = tokens.shape
    heads = bias_tables.shape[1]
    width = w_qkv.shape[2]
    units = w_inner.shape[1]
    share = rows // lax.axis_size("mp")
    chunks = rows // CHUNK
    each = model // 8
    sums = (8, WIDE + 4 * BLOCK)

    def dma(*shape):
        return pltpu.SemaphoreType.DMA(shape)

    def vmem(*shape, dtype=bf16):
        return pltpu.VMEM(shape, dtype)

    scratch = [
        vmem(rows, model), vmem(3, width, model), vmem(model, units), vmem(units, model),
        vmem(rows, model), dma(7 + 4 * chunks),
        vmem(8, rows, dtype=jnp.int32), vmem(heads, BLOCK, BLOCK), vmem(rows, BLOCK), vmem(BLOCK, rows), vmem(heads, rows, BLOCK),
        vmem(heads, rows, BLOCK), vmem(heads, rows, BLOCK), vmem(heads, BLOCK, rows), vmem(heads, rows, BLOCK),
        vmem(heads, BLOCK, WIDE), vmem(heads, WIDE, BLOCK),
        vmem(heads, chunks, 256, CHUNK),
        vmem(CHUNK, 256, dtype=f32), vmem(heads * CHUNK, BLOCK, dtype=f32), vmem(rows, BLOCK, dtype=f32),
        vmem(256, rows, dtype=f32), vmem(WIDE, BLOCK, dtype=f32), vmem(heads, BLOCK, rows),
        vmem(*sums, dtype=f32), vmem(8, model, dtype=f32), vmem(3 * BUCKETS, sums[1]),
        vmem(rows, 256), vmem(6 * rows, BLOCK), dma(chunks, 3), dma(chunks, 3),
        vmem(chunks * 9 * BLOCK // 2, BLOCK), vmem(chunks * 6 * BLOCK, BLOCK), dma(chunks, 3), dma(chunks, 3),
        vmem(4 * width, model), dma(1, 3), dma(1, 3), vmem(model, 4 * 256),
        vmem(rows, model),
        vmem(rows, model), dma(chunks, 3), dma(chunks, 3),
        vmem(rows, model), dma(chunks, 2), dma(chunks, 2), vmem(rows, model), dma(chunks, 2), dma(chunks, 2),
        dma(chunks, 2), dma(chunks, 2), vmem(rows // 2, model), vmem(share, model),
        pltpu.SemaphoreType.REGULAR((2,)),
        vmem(rows, units), vmem(rows, units), vmem(share, model, dtype=f32),
    ]
    outs = [((share, model), bf16), ((share, model), f32)]
    if fast:
        outs += [
            ((3, each, width), f32), ((width, each), f32), ((each, units), f32), ((each, units), f32),
            ((model,), f32), ((model,), f32), ((heads, 3 * BUCKETS), f32),
        ]
        scratch += [
            *spread_scratch(each, units, own_part=False), *spread_scratch(each, units), *spread_scratch(each, 256),
            *spread_scratch(each, 256, lead=(heads - 1,)),
            vmem(8 * each, 256), vmem(7 * each, 256), dma(7), dma(7),
            vmem(2, 16, BLOCK, dtype=f32), vmem(10, 16, BLOCK, dtype=f32), dma(10), dma(10),
        ]
    else:
        outs += [
            ((heads, model, 256), f32), ((model, width), f32), ((model, units), f32), ((model, units), f32), ((8, model), f32),
        ]
    full = pl.BlockSpec(memory_space=pltpu.VMEM)
    anywhere = pl.BlockSpec(memory_space=pl.ANY)
    results = pl.pallas_call(
        functools.partial(layer_kernel, fast),
        in_specs=[pl.BlockSpec(memory_space=pltpu.SMEM)] + [full] * 5 + [anywhere] * 6,
        out_specs=[full] * len(outs),
        out_shape=[jax.ShapeDtypeStruct(*out) for out in outs],
        scratch_shapes=scratch,
        compiler_params=pltpu.CompilerParams(vmem_limit_bytes=64 * MIB, collective_id=1, has_side_effects=True),
        name="layer",
    )(
        lengths, horizontal, vertical, gain_attn, gain_ffn, bias_tables.T,
        tokens, jnp.swapaxes(w_qkv, 1, 2), w_output, w_inner, w_outer, cotangent,
    )
    if fast:
        mixed, input_grad, qkv, output, inner, outer, gain_a, gain_f, tables = hand_over(results)
        return mixed, input_grad, qkv, output, inner, outer.T, gain_a, gain_f, tables.T
    mixed, input_grad, qkv, output, inner, outer, sums = results
    qkv = qkv[:, :, : 3 * 64].reshape(heads, model, 3, 64).transpose(2, 1, 0, 3).reshape(3, model, width)
    gains = lax.psum(sums[:2], ("dp", "mp"))
    tables = lax.psum(sums[2 : 2 + heads, : 3 * BUCKETS], "dp").T

    def spread(x, axis):
        return lax.psum_scatter(x, "dp", scatter_dimension=axis, tiled=True)

    return (
        mixed, input_grad, spread(qkv, 1), spread(output.T, 1), spread(inner, 0), spread(outer.T, 1),
        gains[0], gains[1], tables,
    )


def solution(mesh):
    fast = mesh.shape["dp"] == 8
    return jax.shard_map(
        functools.partial(local, fast),
        mesh=mesh,
        in_specs=(
            P("dp", None), P("dp"), P("dp"), P("dp"), P(), P(None, None, "mp"), P(None, "mp"), P("mp", None), P(),
            P(None, "mp"), P("mp", None), P("dp", None),
        ),
        out_specs=(
            P(("dp", "mp"), None), P(("dp", "mp"), None), P(None, "dp", "mp"), P("mp", "dp"), P("dp", "mp"),
            P("mp", "dp"), P(), P(), P(None, "mp"),
        ),
        check_vma=False,
    )
```

```python
import functools
import jax
import jax.numpy as jnp
import numpy as np
from jax import lax
from jax.experimental import pallas as pl
from jax.experimental.pallas import tpu as pltpu
from jax.sharding import PartitionSpec as P

BUCKETS = 32
CODES = 64
HALF = BUCKETS // 2
EPSILON = 1e-06
DEAD = -1e9
CHUNK = 512
BLOCK = 128
BAND = 3 * BLOCK
WIDE = 6 * BLOCK
FAR = 64
MASK = 76
LSE = 80
MIB = 2**20

f32 = jnp.float32
bf16 = jnp.bfloat16


def line_bucket(columns):
    line = jnp.clip(columns - 2 * BLOCK, -HALF, HALF - 1) + HALF
    line = jnp.where(columns < 5 * BLOCK, line, 0)
    wrapped = columns % BLOCK
    wrapped = jnp.where(wrapped < CODES, wrapped, wrapped - BLOCK)
    plane = jnp.clip(wrapped, -HALF, HALF - 1) + HALF
    return jnp.where(
        columns < WIDE, line, jnp.where(columns < WIDE + BLOCK, BUCKETS + plane, 2 * BUCKETS + plane)
    )


def expansion():
    rows = lax.broadcasted_iota(jnp.int32, (3 * BUCKETS, WIDE + 2 * BLOCK), 0)
    columns = lax.broadcasted_iota(jnp.int32, (3 * BUCKETS, WIDE + 2 * BLOCK), 1)
    return jnp.where(rows == line_bucket(columns), 1.0, 0.0).astype(bf16)


def collapse():
    rows = lax.broadcasted_iota(jnp.int32, (3 * BUCKETS, WIDE + 4 * BLOCK), 0)
    columns = lax.broadcasted_iota(jnp.int32, (3 * BUCKETS, WIDE + 4 * BLOCK), 1)
    bucket = line_bucket(columns)
    bucket = jnp.where(columns == 5 * BLOCK, BUCKETS - 1, bucket)
    bucket = jnp.where(columns >= WIDE + 2 * BLOCK, 0, bucket)
    bucket = jnp.where(columns >= WIDE + 3 * BLOCK, BUCKETS - 1, bucket)
    return jnp.where(rows == bucket, 1.0, 0.0).astype(bf16)


def roll_rows(value, right):
    rows, width = value.shape
    index = lax.broadcasted_iota(jnp.int32, value.shape, 0)
    step = 1
    while step < rows:
        shift = step if right else width - step
        value = jnp.where((index // step) % 2 == 1, pltpu.roll(value, shift, 1), value)
        step *= 2
    return value


def dot(a, b):
    return jnp.dot(a, b, preferred_element_type=f32)


def dot_nt(a, b):
    return lax.dot_general(a, b, (((1,), (1,)), ((), ())), preferred_element_type=f32)


def split3(value):
    high = value.astype(bf16).astype(f32)
    rest = value - high
    middle = rest.astype(bf16).astype(f32)
    return high, middle, rest - middle


def dot_tn(a, b):
    return lax.dot_general(a, b, (((0,), (0,)), ((), ())), preferred_element_type=f32)


ROOT = float(np.sqrt(2.0 / np.pi))
CUBE = 0.044715


def factor_of(rows):
    return lax.rsqrt(jnp.mean(rows * rows, axis=-1, keepdims=True) + EPSILON)


def mp_places():
    mp = lax.axis_index("mp")
    y, core = mp // 2, mp % 2
    return mp, y, core, y * 2 + (1 - core), (1 - y) * 2 + core


def dp_places():
    dp = lax.axis_index("dp")
    return dp // 2, dp % 2


def remote(src, dst, send, recv, mp=None, dp=None):
    return pltpu.make_async_remote_copy(
        src_ref=src,
        dst_ref=dst,
        send_sem=send,
        recv_sem=recv,
        device_id=(lax.axis_index("dp") if dp is None else dp, lax.axis_index("mp") if mp is None else mp),
        device_id_type=pl.DeviceIdType.MESH,
    )


def beside(z):
    return z // 2 * 2 + 1 - z % 2


def meet(fast):
    mp, dp = lax.axis_index("mp"), lax.axis_index("dp")
    others = [(dp, (mp + d) % 4) for d in (1, 2, 3)]
    if fast:
        others.extend(((dp + d) % 8, mp) for d in range(1, 8))
    barrier = pltpu.get_barrier_semaphore()
    for other in others:
        pl.semaphore_signal(barrier, inc=1, device_id=other, device_id_type=pl.DeviceIdType.MESH)
    return lambda: pl.semaphore_wait(barrier, len(others))


def run(index, count=1, size=BLOCK):
    return pl.ds(pl.multiple_of(index * size, size), count * size)


class Scatter:

    def __init__(self, part, near, far, send, recv):
        self.part, self.near, self.far, self.send, self.recv = part, near, far, send, recv

    def block(self, c, core, y):
        return (c * 2 + core) * 2 + y

    def put(self, c, m, value, columns=slice(None)):
        self.part[run(self.block(c, m % 2, m // 2)), columns] = value.astype(bf16)

    def first(self, c):
        _, _, core, sibling, _ = mp_places()
        src = self.part.at[run(self.block(c, 1 - core, 0), 2)]
        return remote(src, self.near.at[run(c * 2, 2)], self.send.at[c, 0], self.recv.at[c, 0], sibling)

    def second(self, c):
        _, y, core, _, across = mp_places()
        src = self.part.at[run(self.block(c, core, 1 - y))]
        return remote(src, self.far.at[run(c)], self.send.at[c, 1], self.recv.at[c, 1], across)

    def start(self, c):
        self.first(c).start()

    def middle(self, c):
        _, y, core, _, _ = mp_places()
        self.first(c).wait_recv()
        at = run(self.block(c, core, 1 - y))
        self.part[at, :] = (self.part[at, :].astype(f32) + self.near[run(c * 2 + 1 - y), :].astype(f32)).astype(bf16)
        self.second(c).start()

    def finish(self, c):
        _, y, core, _, _ = mp_places()
        self.second(c).wait_recv()
        own = self.part[run(self.block(c, core, y)), :].astype(f32) + self.near[run(c * 2 + y), :].astype(f32)
        return own + self.far[run(c), :].astype(f32)

    def drain(self, c):
        self.first(c).wait_send()
        self.second(c).wait_send()


class Gather:

    def __init__(self, full, send, recv, size=BLOCK):
        self.full, self.send, self.recv, self.size = full, send, recv, size

    def at(self, c, m):
        return run(c * 4 + m, 1, self.size)

    def copy(self, c, kind):
        mp, _, _, sibling, across = mp_places()
        at = self.full.at[self.at(c, across if kind == 2 else mp)]
        return remote(at, at, self.send.at[c, kind], self.recv.at[c, kind], across if kind == 1 else sibling)

    def start(self, c):
        self.copy(c, 1).start()
        self.copy(c, 0).start()

    def forward(self, c):
        self.copy(c, 1).wait_recv()
        self.copy(c, 2).start()

    def finish(self, c):
        self.copy(c, 0).wait_recv()
        self.copy(c, 2).wait_recv()

    def drain(self, c):
        for kind in range(3):
            self.copy(c, kind).wait_send()


class Exchange:

    def __init__(self, given, taken, size, send, recv):
        self.given, self.taken, self.size, self.send, self.recv = given, taken, size, send, recv

    def copy(self, c, d):
        mp = lax.axis_index("mp")
        src = self.given.at[run(c * 3 + d - 1, 1, self.size)]
        dst = self.taken.at[run(c * 4 + mp, 1, self.size)]
        return remote(src, dst, self.send.at[c, d - 1], self.recv.at[c, d - 1], (mp + d) % 4)

    def start(self, c):
        for d in (2, 1, 3):
            self.copy(c, d).start()

    def finish(self, c):
        for d in (1, 2, 3):
            self.copy(c, d).wait_recv()

    def drain(self, c):
        for d in (1, 2, 3):
            self.copy(c, d).wait_send()


class Spread:

    def __init__(self, part, near, pair, far, send, recv):
        self.part, self.near, self.pair, self.far, self.send, self.recv = part, near, pair, far, send, recv
        self.each = part.shape[0] // 8

    def at(self, index, count=1):
        return run(index, count, self.each)

    def put(self, first_row, value):
        for r in range(value.shape[0] // self.each):
            j = first_row // self.each + r
            rows = value[r * self.each : (r + 1) * self.each]
            self.part[self.at(j % 2 * 4 + j // 2 % 2 * 2 + j // 4), :] = rows.astype(bf16)

    def copy(self, kind):
        z, x = dp_places()
        send, recv = self.send.at[kind], self.recv.at[kind]
        if kind == 0:
            src = self.part.at[self.at((1 - x) * 4, 4)]
            return remote(src, self.near, send, recv, dp=z * 2 + 1 - x)
        if kind == 1:
            src = self.part.at[self.at(x * 4 + (1 - z % 2) * 2, 2)]
            return remote(src, self.pair, send, recv, dp=beside(z) * 2 + x)
        src = self.part.at[self.at(x * 4 + z % 2 * 2 + 1 - z // 2)]
        return remote(src, self.far, send, recv, dp=(z + 2) % 4 * 2 + x)

    def start(self):
        self.copy(0).start()

    def middle(self):
        z, x = dp_places()
        self.copy(0).wait_recv()
        at = self.at(x * 4 + (1 - z % 2) * 2, 2)
        near = self.near[self.at((1 - z % 2) * 2, 2), :].astype(f32)
        self.part[at, :] = (self.part[at, :].astype(f32) + near).astype(bf16)
        self.copy(1).start()

    def sum_of(self, half):
        z, x = dp_places()
        total = self.part[self.at(x * 4 + z % 2 * 2 + half), :].astype(f32)
        total = total + self.near[self.at(z % 2 * 2 + half), :].astype(f32)
        return total + self.pair[self.at(half), :].astype(f32)

    def third(self):
        z, x = dp_places()
        self.copy(1).wait_recv()
        self.part[self.at(x * 4 + z % 2 * 2 + 1 - z // 2), :] = self.sum_of(1 - z // 2).astype(bf16)
        self.copy(2).start()

    def finish(self):
        z, _ = dp_places()
        self.copy(2).wait_recv()
        return self.sum_of(z // 2) + self.far[...].astype(f32)

    def drain(self):
        for kind in range(3):
            self.copy(kind).wait_send()


class Direct:

    def __init__(self, part, taken, send, recv):
        self.part, self.taken, self.send, self.recv = part, taken, send, recv
        self.each = part.shape[0] // 8

    put = Spread.put

    def at(self, index, count=1):
        return run(index, count, self.each)

    def block(self, dp):
        return self.at(dp % 2 * 4 + dp // 2 % 2 * 2 + dp // 4)

    def copy(self, d):
        to = (lax.axis_index("dp") + d) % 8
        src = self.part.at[self.block(to)]
        return remote(src, self.taken.at[run(d - 1, 1, self.each)], self.send.at[d - 1], self.recv.at[d - 1], dp=to)

    def start(self):
        for d in (4, 3, 5, 2, 6, 1, 7):
            self.copy(d).start()

    def finish(self):
        total = self.part[self.block(lax.axis_index("dp")), :].astype(f32)
        for d in range(1, 8):
            self.copy(d).wait_recv()
            total = total + self.taken[run(d - 1, 1, self.each), :].astype(f32)
        return total

    def drain(self):
        for d in range(1, 8):
            self.copy(d).wait_send()


class Total:

    def __init__(self, value, taken, send, recv):
        self.value, self.taken, self.send, self.recv = value, taken, send, recv

    def copy(self, kind):
        mp, dp = lax.axis_index("mp"), lax.axis_index("dp")
        send, recv = self.send.at[kind], self.recv.at[kind]
        if kind < 7:
            return remote(self.value.at[0], self.taken.at[kind], send, recv, dp=(dp + kind + 1) % 8)
        return remote(self.value.at[1], self.taken.at[kind], send, recv, mp=(mp + kind - 6) % 4)

    def start(self):
        for kind in range(7):
            self.copy(kind).start()

    def turn(self):
        total = self.value[0]
        for kind in range(7):
            self.copy(kind).wait_recv()
            total = total + self.taken[kind]
        self.value[1] = total
        for kind in range(7, 10):
            self.copy(kind).start()

    def finish(self):
        total = self.value[1]
        for kind in range(7, 10):
            self.copy(kind).wait_recv()
            total = total + self.taken[kind]
        return total

    def drain(self):
        for kind in range(10):
            self.copy(kind).wait_send()


def layer_kernel(
    fast,
    length_ref, across_ref, upward_ref, gain_a_ref, gain_f_ref, tables_ref,
    tokens_hbm, w_qkv_hbm, w_output_hbm, w_inner_hbm, w_outer_hbm, cot_hbm,
    *rest,
):
    outs, scratch = rest[: 9 if fast else 7], rest[9 if fast else 7 :]
    if fast:
        mixed_ref, input_ref, o_qkv_ref, o_output_ref, o_inner_ref, o_outer_ref, o_gain_a_ref, o_gain_f_ref, o_tables_ref = outs
    else:
        mixed_ref, input_ref, o_qkv_ref, o_output_ref, o_inner_ref, o_outer_ref, o_sums_ref = outs
    (
        x1, w_qkv_ref, w_inner_ref, w_outer_ref, cot_ref, load_sem,
        codes_ref, plane_ref, hot_ref, hot_t_ref, qa_ref, qb_ref, k2_ref, kt2_ref, v_ref, band_ref, band_t_ref, qt_ref,
        s_ref, res_ref, dv_ref, dqt_ref, bands_ref, dat_ref, sums_ref, gain_sum_ref, collapse_ref,
        att_ref, af_ref, att_send, att_recv,
        es_ref, ga_ref, es_send, es_recv,
        wo_ref, wo_send, wo_recv, wo_t_ref,
        nf_ref,
        ghl_ref, ghl_send, ghl_recv,
        feed_part, feed_send, feed_recv, norm_part, norm_send, norm_recv, last_send, last_recv, near_ref, far_ref,
        credit,
        low_ref, grad_low_ref, hidden_ref,
        *spreads,
    ) = scratch
    heads = tables_ref.shape[0]
    rows, model = x1.shape
    width = heads * 64
    units = w_inner_ref.shape[1]
    pieces = 4
    chunks = rows // CHUNK
    blocks = rows // BLOCK
    half_model = model // 2
    mp, _, _, sibling, across = mp_places()
    da_ref, dk_ref, wt_ref = qa_ref, res_ref, w_inner_ref

    att = Gather(af_ref, att_send, att_recv, CHUNK + CHUNK // 2)
    grad_att = Exchange(es_ref, ga_ref, BLOCK + BLOCK // 2, es_send, es_recv)
    wo = Gather(wo_ref, wo_send, wo_recv, width)
    grads = Gather(ghl_ref, ghl_send, ghl_recv)
    feed = Scatter(feed_part, near_ref, far_ref, feed_send, feed_recv)
    norm = Scatter(norm_part, near_ref, far_ref, norm_send, norm_recv)
    last = Scatter(norm_part, near_ref, far_ref, last_send, last_recv)
    if fast:
        outer = Spread(w_outer_ref, *spreads[0:5])
        inner = Spread(*spreads[5:11])
        output = Spread(*spreads[11:17])
        qkv_last = Direct(*spreads[23:27])
        small = Total(*spreads[27:31])

        def qkv(h):
            return Spread(*[ref.at[h] for ref in spreads[17:23]])

    def place(m, c):
        return run(m * chunks + c)

    loads = [
        pltpu.make_async_copy(src, dst, load_sem.at[i])
        for i, (src, dst) in enumerate(
            [
                (tokens_hbm, x1),
                (w_qkv_hbm, w_qkv_ref),
                (w_output_hbm, wo_ref.at[wo.at(0, mp)]),
                (w_inner_hbm, w_inner_ref),
                (w_outer_hbm, w_outer_ref),
                (cot_hbm, cot_ref),
                *[(tokens_hbm.at[place(m, c)], low_ref.at[run(c * 4 + m)]) for c in range(chunks) for m in range(4)],
                (tokens_hbm.at[run(mp * chunks, chunks)], cot_ref.at[run(0, chunks)]),
            ]
        )
    ]
    for load in loads[:-1]:
        load.start()
    everyone_is_here = meet(fast)

    def window(m, c):
        block = m * chunks + c
        start = min(max(block - 1, 0), blocks - 3)
        return range(start, start + 3), 2 - block


    expanded = dot(tables_ref[...], expansion())
    square_rows = lax.broadcasted_iota(jnp.int32, (BLOCK, BLOCK), 0)
    square_lanes = lax.broadcasted_iota(jnp.int32, (BLOCK, BLOCK), 1)
    for h in range(heads):
        line = jnp.broadcast_to(expanded[h : h + 1, :WIDE], (BLOCK, WIDE))
        band = roll_rows(line, True)
        band_ref[h] = band.astype(bf16)
        band_t_ref[h] = band.T.astype(bf16)
        level = roll_rows(jnp.broadcast_to(expanded[h : h + 1, WIDE : WIDE + BLOCK], (BLOCK, BLOCK)), True)
        upward = roll_rows(jnp.broadcast_to(expanded[h : h + 1, WIDE + BLOCK :], (BLOCK, BLOCK)), True)
        plane = jnp.where(
            (square_rows < CODES) & (square_lanes < CODES),
            level,
            jnp.where((square_rows >= CODES) & (square_lanes >= CODES), upward, 0.0),
        )
        plane_ref[h] = plane.astype(bf16)
    everyone_is_here()
    loads[2].wait()
    wo.start(0)
    loads[1].wait()
    loads[0].wait()
    gain_a = gain_a_ref[...].reshape(1, model).astype(f32)
    gain_f = gain_f_ref[...].reshape(1, model).astype(f32)
    codes_ref[0:1, :] = across_ref[...].reshape(1, rows)
    codes_ref[1:2, :] = upward_ref[...].reshape(1, rows)
    lanes = lax.broadcasted_iota(jnp.int32, (CHUNK, BLOCK), 1)
    low = lanes < FAR

    def prepare(j, carry):
        at = run(j, 1, CHUNK)
        x = x1[at, :].astype(f32)
        normed_rows = (x * factor_of(x) * gain_a).astype(bf16)
        x1[at, :] = normed_rows
        codes_lines = lax.broadcasted_iota(jnp.int32, (BLOCK, CHUNK), 0)
        hot_t = jnp.where(
            codes_lines == jnp.broadcast_to(codes_ref[0:1, at], (BLOCK, CHUNK)),
            1.0,
            jnp.where(codes_lines - CODES == jnp.broadcast_to(codes_ref[1:2, at], (BLOCK, CHUNK)), 1.0, 0.0),
        )
        hot = hot_t.T.astype(bf16)
        hot_t_ref[:, at] = hot_t.astype(bf16)
        hot_ref[at, :] = hot
        row = lax.broadcasted_iota(jnp.int32, (CHUNK, BLOCK), 0) + j * CHUNK
        block = row // BLOCK
        start = jnp.clip(block - 1, 0, blocks - 3)
        far = (lanes >= FAR) & (lanes < MASK)
        far_left = far & (lanes - FAR < start)
        far_right = far & (lanes - FAR > start + 2)
        key_side = jnp.where(
            (far & (lanes - FAR == block))
            | ((lanes == MASK) & (row >= length_ref[0]))
            | ((lanes >= LSE) & (lanes < LSE + 3)),
            1.0,
            0.0,
        )

        def part(h):
            columns = s_ref[:CHUNK, h // 2 * BLOCK : h // 2 * BLOCK + BLOCK]
            return columns if h % 2 == 0 else pltpu.roll(columns, 64, 1)

        s_ref[:CHUNK, :width] = dot_nt(normed_rows, w_qkv_ref[0])
        for h in range(heads):
            left = expanded[h : h + 1, 0:1]
            right = expanded[h : h + 1, WIDE - BLOCK - 1 : WIDE - BLOCK]
            query_side = jnp.where(far_left, left, jnp.where(far_right, right, jnp.where(lanes == MASK, DEAD, 0.0)))
            qa_ref[h, at, :] = dot(hot, plane_ref[h]).astype(bf16)
            qb_ref[h, at, :] = jnp.where(low, part(h).astype(bf16).astype(f32) * 0.125, query_side).astype(bf16)
        s_ref[:CHUNK, :width] = dot_nt(normed_rows, w_qkv_ref[1])
        for h in range(heads):
            second = jnp.where(low, part(h), key_side)
            k2_ref[h, at, :] = second.astype(bf16)
            kt2_ref[h, :, at] = second.T.astype(bf16)
        s_ref[:CHUNK, :width] = dot_nt(normed_rows, w_qkv_ref[2])
        for h in range(heads):
            v_ref[h, at, :] = jnp.where(low, part(h), 1.0).astype(bf16)
        return carry

    s_ref[:CHUNK, :] = jnp.zeros_like(s_ref[:CHUNK, :])
    lax.fori_loop(0, chunks, prepare, 0)
    wo.forward(0)
    gain_sum_ref[...] = jnp.zeros_like(gain_sum_ref)
    sums_ref[...] = jnp.zeros_like(sums_ref)
    collapse_ref[...] = collapse()

    half_low = lax.broadcasted_iota(jnp.int32, (CHUNK // 2, BLOCK), 1) < 64
    quarter_low = lax.broadcasted_iota(jnp.int32, (BLOCK // 2, BLOCK), 1) < 64

    def share_attended(c):
        at = run(c, 1, CHUNK)
        mine = att.at(c, mp).start
        third = att_ref[at, BLOCK:].astype(f32)
        af_ref[pl.ds(pl.multiple_of(mine, CHUNK // 2), CHUNK), :] = att_ref[at, :BLOCK]
        beside_it = jnp.where(half_low, third[: CHUNK // 2], pltpu.roll(third[CHUNK // 2 :], 64, 1)).astype(bf16)
        af_ref[pl.ds(pl.multiple_of(mine + CHUNK, CHUNK // 2), CHUNK // 2), :] = beside_it
        att.start(c)

    def hidden_of(c):
        att.finish(c)
        hidden = low_ref[run(c, 1, CHUNK), :].astype(f32)
        for m in range(pieces):
            first = (c * 4 + m) * (CHUNK + CHUNK // 2)
            pair = af_ref[pl.ds(pl.multiple_of(first, CHUNK // 2), CHUNK), :]
            third = af_ref[pl.ds(pl.multiple_of(first + CHUNK, CHUNK // 2), CHUNK // 2), :]
            third = jnp.concatenate([third, pltpu.roll(third.astype(f32), 64, 1).astype(bf16)], axis=0)
            weights = wo_ref[m * width : (m + 1) * width, :]
            hidden = hidden + dot(jnp.concatenate([pair, third[:, :64]], axis=1), weights)
        nf_ref[run(c, 1, CHUNK), :] = (hidden * factor_of(hidden) * gain_f).astype(bf16)
        for m in range(pieces):

            @pl.when(mp == m)
            def _(m=m):
                hidden_ref[run(c), :] = hidden[m * BLOCK : (m + 1) * BLOCK]

    def grad_of(c):
        grad_normed = norm.finish(c)
        hidden = hidden_ref[run(c), :]
        factor = factor_of(hidden)
        hat = hidden * factor
        scaled = grad_normed * gain_f
        back = factor * (scaled - hat * jnp.mean(scaled * hat, axis=-1, keepdims=True))
        grad = cot_ref[place(mp, c), :].astype(f32) + back
        input_ref[run(c), :] = grad
        gain_sum_ref[0:1, :] += jnp.sum(grad_normed * hat, axis=0, keepdims=True)
        grad_low = grad.astype(bf16)
        ghl_ref[grads.at(c, mp), :] = grad_low

        size = BLOCK + BLOCK // 2
        every = dot(grad_low, wo_t_ref[...])
        for m in range(pieces):
            third = every[:, m * 256 + BLOCK : (m + 1) * 256]
            third = jnp.where(quarter_low, third[: BLOCK // 2], pltpu.roll(third[BLOCK // 2 :], 64, 1))
            value = jnp.concatenate([every[:, m * 256 : m * 256 + BLOCK], third], axis=0).astype(bf16)

            @pl.when(mp == m)
            def _(value=value):
                ga_ref[run(c * 4 + mp, 1, size), :] = value

            @pl.when(mp != m)
            def _(value=value, m=m):
                es_ref[run(c * 3 + (m - mp + 4) % 4 - 1, 1, size), :] = value

        grad_att.start(c)

    def attend(c, h, carry):
        query_far = jnp.concatenate([qa_ref[h, place(m, c), :] for m in range(pieces)], axis=0)
        query_near = jnp.concatenate([qb_ref[h, place(m, c), :] for m in range(pieces)], axis=0)
        query = jnp.concatenate([query_far, query_near], axis=1)
        tops, mixes = [], []
        for j in range(chunks):
            cols = slice(j * CHUNK, (j + 1) * CHUNK)
            s = dot(query, jnp.concatenate([hot_t_ref[:, cols], kt2_ref[h, :, cols]], axis=0))
            lines = []
            for m in range(pieces):
                near, shift = window(m, c)
                tiles = []
                for b in range(pieces):
                    tile = s[m * BLOCK : (m + 1) * BLOCK, b * BLOCK : (b + 1) * BLOCK]
                    if j * pieces + b in near:
                        at = (j * pieces + b + shift) * BLOCK
                        tile = tile + band_ref[h, :, at : at + BLOCK].astype(f32)
                    tiles.append(tile)
                lines.append(jnp.concatenate(tiles, axis=1))
            s = jnp.concatenate(lines, axis=0)
            tops.append(jnp.max(s, axis=1, keepdims=True))
            mixes.append(dot(jnp.exp(s - tops[j]).astype(bf16), v_ref[h, cols, :]))
        top = functools.reduce(jnp.maximum, tops)
        mixed = sum(mix * jnp.exp(part - top) for mix, part in zip(mixes, tops))
        res_ref[run(h, 1, CHUNK), :] = jnp.where(low, mixed / pltpu.roll(mixed, 64, 1), 0.0)
        high, middle, rest = split3(-(top + jnp.log(mixed[:, 64:65])))
        second = jnp.where(
            lanes == LSE,
            high,
            jnp.where(lanes == LSE + 1, middle, jnp.where(lanes == LSE + 2, rest, query_near.astype(f32))),
        )
        qt_ref[h, c, :BLOCK, :] = query_far.astype(f32).T.astype(bf16)
        qt_ref[h, c, BLOCK:, :] = second.T.astype(bf16)

        return carry

    for c in range(chunks):
        lax.fori_loop(0, heads, functools.partial(attend, c), 0)
        if c > 0:
            att.forward(c - 1)
        if c == 1:
            wo.finish(0)
            for m in range(pieces):
                turned = wo_ref[m * width : (m + 1) * width, :].astype(f32).T
                wo_t_ref[:, m * 256 : m * 256 + width] = turned.astype(bf16)
                wo_t_ref[:, m * 256 + width : (m + 1) * 256] = jnp.zeros((model, 256 - width), bf16)
        pairs = []
        for g in range(0, heads, 2):
            pair = res_ref[g * CHUNK : (g + 1) * CHUNK, :]
            if g + 1 < heads:
                pair = jnp.where(low, pair, pltpu.roll(res_ref[(g + 1) * CHUNK : (g + 2) * CHUNK, :], 64, 1))
            pairs.append(pair.astype(bf16))
        att_ref[run(c, 1, CHUNK), :] = jnp.concatenate(pairs, axis=1)
        share_attended(c)
    for load in loads[3:-1]:
        load.wait()
    outer_t = w_outer_ref[...].astype(f32).T.astype(bf16)
    inner_t = w_inner_ref[...].astype(f32).T.astype(bf16)
    for r in range(units // BLOCK):
        qa_ref[r // 2, run(r % 2, 1, model), :] = outer_t[:, r * BLOCK : (r + 1) * BLOCK]
        dat_ref[r // 2, :, r % 2 * model : (r % 2 + 1) * model] = inner_t[r * BLOCK : (r + 1) * BLOCK, :]

    steps = units // 256

    def feed_step(t, carry):
        c = t // steps
        b = t % steps

        @pl.when(b == 0)
        def _():
            hidden_of(c)

        at = run(b, 1, 256)
        x = nf_ref[run(c, 1, CHUNK), :]
        cot = jnp.concatenate([cot_ref[place(m, c), :] for m in range(pieces)], axis=0)
        inner_units = dot(x, w_inner_ref[:, at])
        grad_act = dot(cot, jnp.concatenate([qa_ref[b, :model, :], qa_ref[b, model:, :]], axis=1))
        square = inner_units * inner_units
        tanh = jnp.tanh(ROOT * inner_units * (1.0 + CUBE * square))
        half = 0.5 * (1.0 + tanh)
        slope = half + 0.5 * inner_units * (1.0 - tanh * tanh) * (ROOT + 3.0 * CUBE * ROOT * square)
        activated = (inner_units * half).astype(bf16)
        grad_low = (slope * grad_act).astype(bf16)
        low_ref[run(c, 1, CHUNK), at] = activated
        grad_low_ref[run(c, 1, CHUNK), at] = grad_low

        @pl.when(b == steps - 1)
        def _():
            chunk_rows = run(c, 1, CHUNK)
            for p in range(model // 256):
                cols = slice(p * 256, (p + 1) * 256)
                turned = [
                    dat_ref[r // 2, :, r % 2 * model + p * 256 : r % 2 * model + (p + 1) * 256] for r in range(units // BLOCK)
                ]
                part_norm = dot(grad_low_ref[chunk_rows, :], jnp.concatenate(turned, axis=0))
                part_ffn = dot(low_ref[chunk_rows, :], w_outer_ref[:, cols])
                for m in range(pieces):
                    norm.put(c, m, part_norm[m * BLOCK : (m + 1) * BLOCK], cols)
                    feed.put(c, m, part_ffn[m * BLOCK : (m + 1) * BLOCK], cols)
            norm.start(c)

        @pl.when(t == 2)
        def _():
            att.forward(2)

        @pl.when(t == 3)
        def _():
            norm.middle(0)

        @pl.when(t == 6)
        def _():
            norm.middle(1)

        @pl.when(t == 7)
        def _():
            grad_of(0)

        return carry

    lax.fori_loop(0, chunks * steps, feed_step, 0)

    def weights_of(is_outer):
        for b in range(2):
            at = slice(b * half_model, (b + 1) * half_model)
            total = jnp.zeros((half_model, units), f32)
            for c in range(chunks):
                if is_outer:
                    left = jnp.concatenate([cot_ref[place(m, c), at] for m in range(pieces)], axis=0)
                    total = total + dot_tn(left, low_ref[run(c, 1, CHUNK), :])
                else:
                    total = total + dot_tn(nf_ref[run(c, 1, CHUNK), at], grad_low_ref[run(c, 1, CHUNK), :])
            if fast:
                (outer if is_outer else inner).put(b * half_model, total)
            else:
                (o_outer_ref if is_outer else o_inner_ref)[at, :] = total

    weights_of(True)
    if fast:
        outer.start()
    norm.middle(2)
    weights_of(False)
    if fast:
        inner.start()
    grad_of(1)
    wt_ref[...] = jnp.zeros_like(wt_ref)
    for k in range(3):
        for h in range(heads):
            wt_ref[h * 256 + k * 64 : h * 256 + (k + 1) * 64, :] = w_qkv_ref[k, h * 64 : (h + 1) * 64, :]

    def receive(c):
        grad_att.finish(c)
        at = run(c, 1, CHUNK)
        pairs, thirds = [], []
        for m in range(pieces):
            first = (c * 4 + m) * (BLOCK + BLOCK // 2)
            pairs.append(ga_ref[pl.ds(pl.multiple_of(first, BLOCK // 2), BLOCK), :])
            third = ga_ref[pl.ds(pl.multiple_of(first + BLOCK, BLOCK // 2), BLOCK // 2), :].astype(f32)
            thirds.extend([third, pltpu.roll(third, 64, 1)])
        received = [jnp.concatenate(pairs, axis=0).astype(f32), jnp.concatenate(thirds, axis=0)]
        for h in range(heads):
            pair = slice(h // 2 * BLOCK, h // 2 * BLOCK + BLOCK)
            grad = received[h // 2]
            out = att_ref[at, pair].astype(f32)
            if h % 2 == 1:
                grad = pltpu.roll(grad, 64, 1)
                out = pltpu.roll(out, 64, 1)
            high, middle, rest = split3(-jnp.sum(jnp.where(low, grad * out, 0.0), axis=1, keepdims=True))
            grad = jnp.where(
                low,
                grad,
                jnp.where(
                    lanes == FAR, high, jnp.where(lanes == FAR + 1, middle, jnp.where(lanes == FAR + 2, rest, 0.0))
                ),
            )
            da_ref[h, at, :] = grad.astype(bf16)
            dat_ref[h, :, at] = grad.T.astype(bf16)

    lines16 = lax.broadcasted_iota(jnp.int32, (16, rows), 0)
    block16 = lax.broadcasted_iota(jnp.int32, (16, rows), 1) // BLOCK
    start16 = jnp.clip(block16 - 1, 0, blocks - 3)
    real = lines16 < blocks
    tall_low = lax.broadcasted_iota(jnp.int32, (rows, BLOCK), 1) < 64

    def fold(value):
        total = value[:, :BLOCK]
        for b in range(1, value.shape[1] // BLOCK):
            total = total + value[:, b * BLOCK : (b + 1) * BLOCK]
        return jnp.sum(total, axis=0, keepdims=True)

    def mix(k):
        mixed_ref[run(k), :] = (hidden_ref[run(k), :] + feed.finish(k)).astype(bf16)

    def events(h, c, j):
        due = {
            (0, 0, 2): [lambda: grad_of(2)],
            (0, 1, 2): [lambda: grads.start(0)],
            (0, 2, 2): [lambda: grads.start(1)],
            (1, 0, 2): [lambda: grads.forward(0), lambda: grads.start(2), lambda: grads.forward(1)],
            (1, 1, 2): [lambda: feed.start(0), lambda: feed.start(1), lambda: feed.start(2)],
            (1, 2, 2): [lambda: grads.forward(2), lambda: feed.middle(0), lambda: feed.middle(1)],
            (2, 0, 2): [lambda: feed.middle(2)],
            (2, 1, 2): [lambda: mix(0), lambda: mix(1)],
            (2, 2, 2): [lambda: mix(2)],
        }
        if fast:
            for at, what in {
                (0, 2, 2): [outer.middle],
                (1, 1, 2): [outer.third, inner.middle],
                (1, 2, 2): [lambda: qkv(0).middle()],
                (2, 0, 2): [inner.third, lambda: qkv(0).third()],
                (2, 2, 2): [lambda: qkv(1).middle(), output.middle],
            }.items():
                due[at] = due.get(at, []) + what
        for (head_due, chunk_due, panel_due), what in due.items():
            if (chunk_due, panel_due) == (c, j):

                @pl.when(h == head_due)
                def _(what=what):
                    for each in what:
                        each()

    def leave(h, spread):
        grads_of = run(h, 1, 256)
        grad_qkv = dot_tn(nf_ref[:, grads_of], x1[...]).T
        if fast:
            spread.put(0, grad_qkv)
        else:
            o_qkv_ref[h] = grad_qkv
        if fast:
            spread.start()

    def leave_tables(h):
        band = roll_rows(bands_ref[...].T, False)
        spread = dqt_ref[:BLOCK, :]
        high = spread.astype(bf16)
        rest = (spread - high.astype(f32)).astype(bf16)
        plane = (dot(high, hot_ref[...]) + dot(rest, hot_ref[...])).T
        plane = jnp.where((square_rows < CODES) == (square_lanes < CODES), plane, 0.0)
        plane = roll_rows(plane, False)
        far = dqt_ref[BLOCK + FAR : BLOCK + FAR + 16, :]
        line = jnp.concatenate(
            [
                jnp.sum(band, axis=0, keepdims=True),
                jnp.sum(plane[:CODES], axis=0, keepdims=True),
                jnp.sum(plane[CODES:], axis=0, keepdims=True),
                fold(jnp.where(real & (lines16 < start16), far, 0.0)),
                fold(jnp.where(real & (lines16 > start16 + 2), far, 0.0)),
            ],
            axis=1,
        )
        sums_ref[...] += jnp.where(lax.broadcasted_iota(jnp.int32, sums_ref.shape, 0) == h, line, 0.0)

    def head(h, carry):
        dk_ref[...] = jnp.zeros_like(dk_ref)
        dv_ref[...] = jnp.zeros_like(dv_ref)
        bands_ref[...] = jnp.zeros_like(bands_ref)

        for c in range(chunks):

            @pl.when(h == 0)
            def _(c=c):
                receive(c)

            at = slice(c * CHUNK, (c + 1) * CHUNK)
            query = jnp.concatenate([qb_ref[h, place(m, c), :] for m in range(pieces)], axis=0)
            for j in range(chunks):
                keys = slice(j * CHUNK, (j + 1) * CHUNK)
                s = dot(jnp.concatenate([hot_ref[keys, :], k2_ref[h, keys, :]], axis=1), qt_ref[h, c])
                columns = []
                for m in range(pieces):
                    near, shift = window(m, c)
                    tiles = []
                    for b in range(pieces):
                        tile = s[b * BLOCK : (b + 1) * BLOCK, m * BLOCK : (m + 1) * BLOCK]
                        if j * pieces + b in near:
                            of = (j * pieces + b + shift) * BLOCK
                            tile = tile + band_t_ref[h, of : of + BLOCK, :].astype(f32)
                        tiles.append(tile)
                    columns.append(jnp.concatenate(tiles, axis=0))
                probs = jnp.exp(jnp.concatenate(columns, axis=1))
                probs_t = probs.astype(bf16)
                grad_t = (probs * dot(v_ref[h, keys, :], dat_ref[h, :, at])).astype(bf16)
                grad_low_ref[keys, :CHUNK] = grad_t
                dv_ref[keys, :] += dot(probs_t, da_ref[h, at, :])
                dk_ref[keys, :] += dot(grad_t, query)
                if j < chunks - 1:
                    events(h, c, j)
            dq = dot(jnp.concatenate([hot_t_ref[...], kt2_ref[h]], axis=0), grad_low_ref[:, :CHUNK])
            for m in range(pieces):
                dqt_ref[:, place(m, c)] = dq[:, m * BLOCK : (m + 1) * BLOCK]
                near, shift = window(m, c)
                of = slice((near.start + shift) * BLOCK, (near.stop + shift) * BLOCK)
                keys = slice(near.start * BLOCK, near.stop * BLOCK)
                bands_ref[of, :] += grad_low_ref[keys, m * BLOCK : (m + 1) * BLOCK].astype(f32)
            events(h, c, chunks - 1)

        dq = dqt_ref[BLOCK:, :].T * 0.125
        grads_of = run(h, 1, 256)
        nf_ref[:, grads_of] = jnp.concatenate(
            [jnp.where(tall_low, dq, pltpu.roll(dk_ref[...], 64, 1)), jnp.where(tall_low, dv_ref[...], 0.0)], axis=1
        ).astype(bf16)

        @pl.when(h < heads - 1)
        def _():
            leave(h, qkv(h) if fast else None)
            leave_tables(h)

        @pl.when(h == 1)
        def _():
            for c in range(chunks):
                grads.finish(c)
            grad_output = dot_tn(att_ref[...], ghl_ref[...]).T
            if fast:
                output.put(0, grad_output)
            else:
                o_output_ref[...] = grad_output[:, :width]
            if fast:
                output.start()

        return carry

    lax.fori_loop(0, heads, head, 0)

    credits = [(sibling, credit.at[0]), (across, credit.at[1])]
    for other, sem in credits:
        pl.semaphore_signal(
            sem, inc=1, device_id=(lax.axis_index("dp"), other), device_id_type=pl.DeviceIdType.MESH
        )
    leave(heads - 1, qkv_last if fast else None)
    loads[-1].start()
    for c in range(chunks):
        norm.drain(c)
    gain_total = jnp.zeros((1, model), f32)
    for c in range(chunks):
        at = [place(m, c) for m in range(pieces)]
        grad_rows = jnp.concatenate([nf_ref[rows_of, :] for rows_of in at], axis=0)
        sums = []
        for p in range(model // 256):
            cols = slice(p * 256, (p + 1) * 256)
            partial = dot(grad_rows, wt_ref[:, cols])
            normed_rows = jnp.concatenate([x1[rows_of, cols] for rows_of in at], axis=0)
            sums.append(jnp.sum(partial * normed_rows.astype(f32), axis=0, keepdims=True))
            for m in range(pieces):
                last.put(c, m, partial[m * BLOCK : (m + 1) * BLOCK], cols)
        gain_total = gain_total + jnp.concatenate(sums, axis=1)
        if c == 0:
            for _, sem in credits:
                pl.semaphore_wait(sem, 1)
        last.start(c)
        if c > 0:
            last.middle(c - 1)
    leave_tables(heads - 1)
    last.middle(chunks - 1)
    gain_total = gain_total / gain_a
    tables = sum(dot_nt(part.astype(bf16), collapse_ref[...]) for part in split3(sums_ref[...]))[:heads]
    if fast:
        lines = model // BLOCK
        small.value[0] = jnp.zeros_like(small.value[0])
        for i in range(lines):
            lane = slice(i * BLOCK, (i + 1) * BLOCK)
            small.value[0, i : i + 1, :] = gain_total[:, lane]
            small.value[0, lines + i : lines + i + 1, :] = gain_sum_ref[0:1, lane]
        small.value[0, 2 * lines : 2 * lines + heads, : 3 * BUCKETS] = tables
        small.start()
        output.third()
        qkv(1).third()
        o_outer_ref[...] = outer.finish()
        small.turn()
        o_output_ref[...] = output.finish()[:, :width].T
    loads[-1].wait()
    for c in range(chunks):
        x = cot_ref[run(c), :].astype(f32)
        grad_normed = last.finish(c)
        factor = factor_of(x)
        hat = x * factor
        scaled = grad_normed * gain_a
        back = factor * (scaled - hat * jnp.mean(scaled * hat, axis=-1, keepdims=True))
        input_ref[run(c), :] += back
    if fast:
        o_inner_ref[...] = inner.finish()
    if fast:
        low_each = lax.broadcasted_iota(jnp.int32, (model // 8, BLOCK), 1) < 64
        parts = [(qkv(h) if h < heads - 1 else qkv_last).finish() for h in range(heads)]
        for k in range(3):
            for h in range(0, heads, 2):
                at = slice(0, BLOCK) if k < 2 else slice(BLOCK, 2 * BLOCK)
                one = parts[h][:, at]
                one = pltpu.roll(one, 64, 1) if k == 1 else one
                if h + 1 < heads:
                    two = parts[h + 1][:, at]
                    two = two if k == 1 else pltpu.roll(two, 64, 1)
                    o_qkv_ref[k, :, h * 64 : (h + 2) * 64] = jnp.where(low_each, one, two)
                else:
                    o_qkv_ref[k, :, h * 64 :] = one[:, :64]
        totals = small.finish()
        for i in range(lines):
            o_gain_a_ref[i * BLOCK : (i + 1) * BLOCK] = totals[i : i + 1].reshape(BLOCK)
            o_gain_f_ref[i * BLOCK : (i + 1) * BLOCK] = totals[lines + i : lines + i + 1].reshape(BLOCK)
        o_tables_ref[...] = small.value[1, 2 * lines : 2 * lines + heads, : 3 * BUCKETS]
        outer.drain()
        inner.drain()
        output.drain()
        for h in range(heads - 1):
            qkv(h).drain()
        qkv_last.drain()
        small.drain()
    else:
        o_sums_ref[...] = jnp.zeros_like(o_sums_ref)
        o_sums_ref[0:1, :] = gain_total
        o_sums_ref[1:2, :] = gain_sum_ref[0:1, :]
        o_sums_ref[2 : 2 + heads, : 3 * BUCKETS] = tables
    wo.drain(0)
    for c in range(chunks):
        for each in (att, grad_att, grads, feed, last):
            each.drain(c)


def spread_scratch(rows, columns, lead=(), own_part=True):
    buffers = [pltpu.VMEM((*lead, 8 * rows, columns), bf16)] if own_part else []
    return buffers + [
        pltpu.VMEM((*lead, 4 * rows, columns), bf16),
        pltpu.VMEM((*lead, 2 * rows, columns), bf16),
        pltpu.VMEM((*lead, rows, columns), bf16),
        pltpu.SemaphoreType.DMA((*lead, 3)),
        pltpu.SemaphoreType.DMA((*lead, 3)),
    ]


def hand_over_kernel(*refs):
    count = len(refs) // 2
    for i in range(count):
        refs[count + i][...] = refs[i][...]


def hand_over(results):
    full = pl.BlockSpec(memory_space=pltpu.VMEM)
    return pl.pallas_call(
        hand_over_kernel,
        in_specs=[full] * len(results),
        out_specs=[full] * len(results),
        out_shape=[jax.ShapeDtypeStruct(each.shape, each.dtype) for each in results],
        name="hand_over",
    )(*results)


def local(
    fast,
    tokens, lengths, horizontal, vertical, gain_attn, w_qkv, bias_tables, w_output, gain_ffn, w_inner, w_outer, cotangent,
):
    rows, model = tokens.shape
    heads = bias_tables.shape[1]
    width = w_qkv.shape[2]
    units = w_inner.shape[1]
    share = rows // lax.axis_size("mp")
    chunks = rows // CHUNK
    each = model // 8
    sums = (8, WIDE + 4 * BLOCK)

    def dma(*shape):
        return pltpu.SemaphoreType.DMA(shape)

    def vmem(*shape, dtype=bf16):
        return pltpu.VMEM(shape, dtype)

    scratch = [
        vmem(rows, model), vmem(3, width, model), vmem(model, units), vmem(units, model),
        vmem(rows, model), dma(7 + 4 * chunks),
        vmem(8, rows, dtype=jnp.int32), vmem(heads, BLOCK, BLOCK), vmem(rows, BLOCK), vmem(BLOCK, rows), vmem(heads, rows, BLOCK),
        vmem(heads, rows, BLOCK), vmem(heads, rows, BLOCK), vmem(heads, BLOCK, rows), vmem(heads, rows, BLOCK),
        vmem(heads, BLOCK, WIDE), vmem(heads, WIDE, BLOCK),
        vmem(heads, chunks, 256, CHUNK),
        vmem(CHUNK, 256, dtype=f32), vmem(heads * CHUNK, BLOCK, dtype=f32), vmem(rows, BLOCK, dtype=f32),
        vmem(256, rows, dtype=f32), vmem(WIDE, BLOCK, dtype=f32), vmem(heads, BLOCK, rows),
        vmem(*sums, dtype=f32), vmem(8, model, dtype=f32), vmem(3 * BUCKETS, sums[1]),
        vmem(rows, 256), vmem(6 * rows, BLOCK), dma(chunks, 3), dma(chunks, 3),
        vmem(chunks * 9 * BLOCK // 2, BLOCK), vmem(chunks * 6 * BLOCK, BLOCK), dma(chunks, 3), dma(chunks, 3),
        vmem(4 * width, model), dma(1, 3), dma(1, 3), vmem(model, 4 * 256),
        vmem(rows, model),
        vmem(rows, model), dma(chunks, 3), dma(chunks, 3),
        vmem(rows, model), dma(chunks, 2), dma(chunks, 2), vmem(rows, model), dma(chunks, 2), dma(chunks, 2),
        dma(chunks, 2), dma(chunks, 2), vmem(rows // 2, model), vmem(share, model),
        pltpu.SemaphoreType.REGULAR((2,)),
        vmem(rows, units), vmem(rows, units), vmem(share, model, dtype=f32),
    ]
    outs = [((share, model), bf16), ((share, model), f32)]
    if fast:
        outs += [
            ((3, each, width), f32), ((width, each), f32), ((each, units), f32), ((each, units), f32),
            ((model,), f32), ((model,), f32), ((heads, 3 * BUCKETS), f32),
        ]
        scratch += [
            *spread_scratch(each, units, own_part=False), *spread_scratch(each, units), *spread_scratch(each, 256),
            *spread_scratch(each, 256, lead=(heads - 1,)),
            vmem(8 * each, 256), vmem(7 * each, 256), dma(7), dma(7),
            vmem(2, 16, BLOCK, dtype=f32), vmem(10, 16, BLOCK, dtype=f32), dma(10), dma(10),
        ]
    else:
        outs += [
            ((heads, model, 256), f32), ((model, width), f32), ((model, units), f32), ((model, units), f32), ((8, model), f32),
        ]
    full = pl.BlockSpec(memory_space=pltpu.VMEM)
    anywhere = pl.BlockSpec(memory_space=pl.ANY)
    results = pl.pallas_call(
        functools.partial(layer_kernel, fast),
        in_specs=[pl.BlockSpec(memory_space=pltpu.SMEM)] + [full] * 5 + [anywhere] * 6,
        out_specs=[full] * len(outs),
        out_shape=[jax.ShapeDtypeStruct(*out) for out in outs],
        scratch_shapes=scratch,
        compiler_params=pltpu.CompilerParams(vmem_limit_bytes=64 * MIB, collective_id=1, has_side_effects=True),
        name="layer",
    )(
        lengths, horizontal, vertical, gain_attn, gain_ffn, bias_tables.T,
        tokens, jnp.swapaxes(w_qkv, 1, 2), w_output, w_inner, w_outer, cotangent,
    )
    if fast:
        mixed, input_grad, qkv, output, inner, outer, gain_a, gain_f, tables = hand_over(results)
        return mixed, input_grad, qkv, output, inner, outer.T, gain_a, gain_f, tables.T
    mixed, input_grad, qkv, output, inner, outer, sums = results
    qkv = qkv[:, :, : 3 * 64].reshape(heads, model, 3, 64).transpose(2, 1, 0, 3).reshape(3, model, width)
    gains = lax.psum(sums[:2], ("dp", "mp"))
    tables = lax.psum(sums[2 : 2 + heads, : 3 * BUCKETS], "dp").T

    def spread(x, axis):
        return lax.psum_scatter(x, "dp", scatter_dimension=axis, tiled=True)

    return (
        mixed, input_grad, spread(qkv, 1), spread(output.T, 1), spread(inner, 0), spread(outer.T, 1),
        gains[0], gains[1], tables,
    )


def solution(mesh):
    fast = mesh.shape["dp"] == 8
    return jax.shard_map(
        functools.partial(local, fast),
        mesh=mesh,
        in_specs=(
            P("dp", None), P("dp"), P("dp"), P("dp"), P(), P(None, None, "mp"), P(None, "mp"), P("mp", None), P(),
            P(None, "mp"), P("mp", None), P("dp", None),
        ),
        out_specs=(
            P(("dp", "mp"), None), P(("dp", "mp"), None), P(None, "dp", "mp"), P("mp", "dp"), P("dp", "mp"),
            P("mp", "dp"), P(), P(), P(None, "mp"),
        ),
        check_vma=False,
    )
```
